32 devices in a mesh: row: 8 (over z, core), col: 4 (over y, x).
Axes of the slice: x: 2, y: 2, z: 4, core: 2. Of those that a mesh axis runs over, the one named last changes fastest.
Arguments:
- tokens: bfloat16 [16384, 2048], P('row', 'col'), may hold values from -6 to 6
- segments: int32 [16384], P('row'), may hold values from 0 to 10, as said below
- positions: int32 [16384], P('row'), may hold values from 0 to 3998, as said below
- gain_attn: float32 [2048], replicated, may hold values from 0.5 to 1.5
- w_query: bfloat16 [2048, 2048], P('row', 'col'), may hold values from -0.125 to 0.125
- key_weight_matrix: bfloat16 [2048, 1024], P('row', 'col'), may hold values from -0.125 to 0.125
- value_weight_matrix: bfloat16 [2048, 1024], P('row', 'col'), may hold values from -0.125 to 0.125
- gain_query: float32 [128], replicated, may hold values from 0.1 to 1.9
- gain_key: float32 [128], replicated, may hold values from 0.1 to 1.9
- w_out: bfloat16 [2048, 2048], P('col', 'row'), may hold values from -2 to 2
- gain_mlp: float32 [2048], replicated, may hold values from 0.5 to 1.5
- w_gate: bfloat16 [2048, 6144], P('row', 'col'), may hold values from -0.125 to 0.125
- w_up: bfloat16 [2048, 6144], P('row', 'col'), may hold values from -0.125 to 0.125
- w_down: bfloat16 [6144, 2048], P('col', 'row'), may hold values from -0.078125 to 0.078125
- cotangent: bfloat16 [16384, 2048], P('row', 'col'), may hold values from -6 to 6
Outputs:
- output: bfloat16 [16384, 2048], P('row', 'col')
- grad_tokens: float32 [16384, 2048], P('row', 'col')
- grad_gain_attn: float32 [2048], replicated
- grad_w_query: float32 [2048, 2048], P('row', 'col')
- grad_w_key: float32 [2048, 1024], P('row', 'col')
- grad_w_value: float32 [2048, 1024], P('row', 'col')
- grad_gain_query: float32 [128], replicated
- grad_gain_key: float32 [128], replicated
- grad_w_out: float32 [2048, 2048], P('col', 'row')
- grad_gain_mlp: float32 [2048], replicated
- grad_w_gate: float32 [2048, 6144], P('row', 'col')
- grad_w_up: float32 [2048, 6144], P('row', 'col')
- grad_w_down: float32 [6144, 2048], P('col', 'row')
The draws below stay inside these ranges and needn't reach their ends.
Inputs may be any that keep to these rules, and one draw needn't show every extreme that they name: `segments`: within each sequence segment ids start at 0 and rise by one at each document boundary; documents hold 200 to 2000 tokens, except that the last of a sequence may be cut shorter. Within a document positions rise by one from token to token; a document's first position is below 2000.
All inputs are finite; a program needn't handle non-finite values.
Results may differ from the reference program's by a relative error of at most 0.019.
Values may be sent and summed in bfloat16 or wider, within the bound.
A program may use at most 320 MiB of HBM per device.

```python
import math
import jax
import jax.numpy as jnp
from jax import lax

MODEL_WIDTH = 2048
QUERY_HEADS = 16
KEY_VALUE_HEADS = 8
HEAD_SIZE = 128
FF = 6144
TOK_ROW = 2048
DOC_MIN = 200
DOC_MAX = 2000
TOKENS = 16384


def documents(key):
    sequences = TOKENS // TOK_ROW
    count = TOK_ROW // DOC_MIN + 1
    pick_key = jax.random.fold_in(key, 11)
    long_pick = jax.random.randint(pick_key, (), 0, sequences).astype(jnp.int32)
    short_pick = ((long_pick + 1) % sequences).astype(jnp.int32)
    keys = jax.random.split(key, sequences)
    first_long = min(DOC_MAX, TOK_ROW)

    def one_sequence(sub, number):
        length_key, offset_key = jax.random.split(sub)
        slots = jnp.arange(count, dtype=jnp.int32)
        lengths = jax.random.randint(length_key, (count,), DOC_MIN, DOC_MAX + 1).astype(jnp.int32)
        lengths = jnp.where((number == long_pick) & (slots == 0), first_long, lengths)
        lengths = jnp.where(number == short_pick, DOC_MIN, lengths).astype(jnp.int32)
        offsets = jax.random.randint(offset_key, (count,), 0, DOC_MAX).astype(jnp.int32)
        offsets = jnp.where((number == long_pick) & (slots == 0), DOC_MAX - 1, offsets)
        offsets = jnp.where(number == short_pick, 0, offsets).astype(jnp.int32)
        ends = jnp.cumsum(lengths)
        places = jnp.arange(TOK_ROW, dtype=jnp.int32)
        passed = (ends[None, :] <= places[:, None]).astype(jnp.int32)
        segment = jnp.sum(passed, axis=1).astype(jnp.int32)
        begin = jnp.sum(passed * lengths[None, :], axis=1).astype(jnp.int32)
        picked = jnp.sum(jnp.where(slots[None, :] == segment[:, None], offsets[None, :], 0), axis=1).astype(jnp.int32)
        return (segment, (places - begin + picked).astype(jnp.int32))
    numbers = jnp.arange(sequences, dtype=jnp.int32)
    segment_all, position_all = jax.vmap(one_sequence)(keys, numbers)
    return (segment_all.reshape(-1), position_all.reshape(-1))


def draw_segments(key, part):
    return documents(key)[0]


def draw_positions(key, part):
    return documents(key)[1]


def shard_levels(stream_key, shape, cuts, least, high):
    level = 1.0
    for dim, parts in cuts:
        draws = jax.random.uniform(jax.random.fold_in(jax.random.fold_in(stream_key, 6), dim), (parts,), jnp.float32, least / len(cuts), high / len(cuts))
        level = level * jnp.repeat(jnp.exp(draws), shape[dim] // parts).reshape((-1,) + (1,) * (len(shape) - 1 - dim))
    return level


def centred(key, dims, deviation, limit, cuts=(), held_as=jnp.bfloat16):
    loudness = shard_levels(key, dims, cuts, -0.22, 0.18) if cuts else 1.0
    entries = jax.random.normal(key, dims, jnp.float32) * deviation * loudness
    return jnp.minimum(jnp.maximum(entries, -limit), limit).astype(held_as)


def setup_inputs(seed: int = 0) -> dict:
    arg_keys = jax.random.split(jax.random.key(seed), 16)
    return {
        "tokens": centred(arg_keys[0], (TOKENS, MODEL_WIDTH), 1.0, 6.0, ((0, 8), (1, 4))),
        "segments": draw_segments(jax.random.fold_in(arg_keys[15], 71), 0),
        "positions": draw_positions(jax.random.fold_in(arg_keys[15], 71), 0),
        "gain_attn": jnp.clip(1.0 + 0.1 * jax.random.normal(arg_keys[3], (MODEL_WIDTH,), jnp.float32), 0.5, 1.5),
        "w_query": centred(arg_keys[4], (MODEL_WIDTH, QUERY_HEADS * HEAD_SIZE), MODEL_WIDTH ** -0.5, 0.125, ((0, 8), (1, 4))),
        "key_weight_matrix": centred(arg_keys[5], (MODEL_WIDTH, KEY_VALUE_HEADS * HEAD_SIZE), MODEL_WIDTH ** -0.5, 0.125, ((0, 8), (1, 4))),
        "value_weight_matrix": centred(arg_keys[6], (MODEL_WIDTH, KEY_VALUE_HEADS * HEAD_SIZE), MODEL_WIDTH ** -0.5, 0.125, ((0, 8), (1, 4))),
        "gain_query": jnp.clip(1.0 + 0.18 * jax.random.normal(arg_keys[7], (HEAD_SIZE,), jnp.float32), 0.1, 1.9),
        "gain_key": jnp.clip(1.0 + 0.18 * jax.random.normal(arg_keys[8], (HEAD_SIZE,), jnp.float32), 0.1, 1.9),
        "w_out": centred(arg_keys[9], (QUERY_HEADS * HEAD_SIZE, MODEL_WIDTH), (QUERY_HEADS * HEAD_SIZE * 8 // DOC_MAX) ** -0.5, 2.0, ((0, 4), (1, 8))),
        "gain_mlp": jnp.clip(1.0 + 0.1 * jax.random.normal(arg_keys[10], (MODEL_WIDTH,), jnp.float32), 0.5, 1.5),
        "w_gate": centred(arg_keys[11], (MODEL_WIDTH, FF), MODEL_WIDTH ** -0.5, 0.125, ((0, 8), (1, 4))),
        "w_up": centred(arg_keys[12], (MODEL_WIDTH, FF), MODEL_WIDTH ** -0.5, 0.125, ((0, 8), (1, 4))),
        "w_down": centred(arg_keys[13], (FF, MODEL_WIDTH), FF ** -0.5, 0.078125, ((0, 4), (1, 8))),
        "cotangent": centred(arg_keys[14], (TOKENS, MODEL_WIDTH), 1.0, 6.0, ((0, 8), (1, 4))),
    }


EPS = 1e-06
THETA = 1000000.0
HIGH = lax.Precision.HIGHEST

@jax.custom_vjp
def low(v):
    return lax.optimization_barrier(v.astype(jnp.bfloat16)).astype(jnp.float32)

@jax.custom_vjp
def low_back(v):
    return v

def low_keep(v):
    return (low(v), None)

def low_pass(kept, grad):
    return (grad,)

def back_keep(v):
    return (v, None)

def back_low(kept, grad):
    return (low(grad),)
low.defvjp(low_keep, low_pass)
low_back.defvjp(back_keep, back_low)

def matrix_product(left, right):
    return jnp.dot(left, right, precision=HIGH)

def rms_norm(values, gain):
    return values * lax.rsqrt(lax.optimization_barrier(jnp.mean(values * values, axis=-1, keepdims=True)) + EPS) * gain

def swap_halves(values):
    half = values.shape[-1] // 2
    return jnp.concatenate([values[..., half:], values[..., :half]], axis=-1)

def rope_tables(positions):
    half = HEAD_SIZE // 2
    inverse = THETA ** (-(jnp.arange(half, dtype=jnp.float32) * 2.0 / HEAD_SIZE))
    angle = positions.astype(jnp.float32)[:, None] * inverse[None, :]
    cosine = jnp.concatenate([jnp.cos(angle), jnp.cos(angle)], axis=-1)
    sine = jnp.concatenate([-jnp.sin(angle), jnp.sin(angle)], axis=-1)
    return (cosine, sine)

def rotate(values, cosine, sine):
    return values * cosine[:, None, :] + swap_halves(values) * sine[:, None, :]

def attention(queries, keys, values, segments):
    length_total = queries.shape[0]
    rows = min(512, length_total)
    blocks = length_total // rows
    head_group = QUERY_HEADS // KEY_VALUE_HEADS
    keys_wide = jnp.repeat(keys, head_group, axis=1)
    values_wide = jnp.repeat(values, head_group, axis=1)
    key_place = jnp.arange(length_total, dtype=jnp.int32)
    scale = 1.0 / math.sqrt(HEAD_SIZE)

    def one_block(pieces):
        query_rows, query_segments, query_place = pieces
        raw = jnp.einsum('qhd,khd->hqk', query_rows, keys_wide, precision=HIGH)
        scores = low_back(raw) * scale
        allowed = (query_segments[:, None] == segments[None, :]) & (key_place[None, :] <= query_place[:, None])
        scores = jnp.where(allowed[None, :, :], scores, -1e+30)
        highest = lax.optimization_barrier(jnp.max(scores, axis=-1, keepdims=True))
        weights = jnp.exp(scores - highest)
        probs = weights / lax.optimization_barrier(jnp.sum(weights, axis=-1, keepdims=True))
        return jnp.einsum('hqk,khd->qhd', low(probs), values_wide, precision=HIGH)
    pieces = (queries.reshape(blocks, rows, QUERY_HEADS, HEAD_SIZE), segments.reshape(blocks, rows), key_place.reshape(blocks, rows))
    return lax.map(jax.checkpoint(one_block), pieces).reshape(length_total, QUERY_HEADS, HEAD_SIZE)

def layer(inputs, params, segments, cosine, sine):
    gain_attn, w_query, key_weight_matrix, value_weight_matrix, gain_query, gain_key, w_out, gain_mlp, w_gate, w_up, w_down = params
    length_total = inputs.shape[0]
    normalized_rows = low(rms_norm(inputs, gain_attn))
    query_proj = low_back(matrix_product(normalized_rows, w_query)).reshape(length_total, QUERY_HEADS, HEAD_SIZE)
    key_projected = low_back(matrix_product(normalized_rows, key_weight_matrix)).reshape(length_total, KEY_VALUE_HEADS, HEAD_SIZE)
    value_projected = low(low_back(matrix_product(normalized_rows, value_weight_matrix))).reshape(length_total, KEY_VALUE_HEADS, HEAD_SIZE)
    queries = low(rotate(rms_norm(query_proj, gain_query), cosine, sine))
    keys = low(rotate(rms_norm(key_projected, gain_key), cosine, sine))
    mixed = low(low_back(attention(queries, keys, value_projected, segments))).reshape(length_total, QUERY_HEADS * HEAD_SIZE)
    hidden = inputs + low_back(matrix_product(mixed, w_out))
    normed_mid = low(rms_norm(low(hidden), gain_mlp))
    gate = low_back(matrix_product(normed_mid, w_gate))
    up_part = low_back(matrix_product(normed_mid, w_up))
    active = low(jax.nn.silu(gate) * up_part)
    return hidden + low_back(matrix_product(active, w_down))

def reference(tokens, segments, positions, gain_attn, w_query, key_weight_matrix, value_weight_matrix, gain_query, gain_key, w_out, gain_mlp, w_gate, w_up, w_down, cotangent):
    params = (gain_attn, w_query.astype(jnp.float32), key_weight_matrix.astype(jnp.float32), value_weight_matrix.astype(jnp.float32), gain_query, gain_key, w_out.astype(jnp.float32), gain_mlp, w_gate.astype(jnp.float32), w_up.astype(jnp.float32), w_down.astype(jnp.float32))
    sequences = TOKENS // TOK_ROW
    inputs = tokens.astype(jnp.float32).reshape(sequences, TOK_ROW, MODEL_WIDTH)
    seg_rows = segments.reshape(sequences, TOK_ROW)
    pos_rows = positions.reshape(sequences, TOK_ROW)
    grad_rows = cotangent.astype(jnp.float32).reshape(sequences, TOK_ROW, MODEL_WIDTH)

    def per_sequence(sums, pieces):
        rows, seg_part, pos_part, grad_part = pieces
        cosine, sine = rope_tables(pos_part)

        def run(values, weights):
            return layer(values, weights, seg_part, cosine, sine)
        result, pull = jax.vjp(run, rows, params)
        grad_input, grad_params = pull(grad_part)
        sums = jax.tree.map(lambda left, right: left + right, sums, grad_params)
        return (sums, (result.astype(jnp.bfloat16), grad_input))
    start = jax.tree.map(jnp.zeros_like, params)
    sums, (outputs, grads) = lax.scan(per_sequence, start, (inputs, seg_rows, pos_rows, grad_rows))
    return (outputs.reshape(TOKENS, MODEL_WIDTH), grads.reshape(TOKENS, MODEL_WIDTH), sums[0], sums[1], sums[2], sums[3], sums[4], sums[5], sums[6], sums[7], sums[8], sums[9], sums[10])
```

```python
import functools
import math

import jax
import jax.numpy as jnp
from jax import lax
from jax.experimental import pallas as pl
from jax.experimental.pallas import tpu as pltpu
from jax.sharding import PartitionSpec as P

BF16 = jnp.bfloat16
F32 = jnp.float32
LOG2E = 1.4426950408889634
VMEM_LIMIT = 60 * 1024 * 1024


def dot_nt(left, right):
    return lax.dot_general(left, right, (((1,), (1,)), ((), ())), preferred_element_type=F32)


def dot_nn(left, right):
    return jnp.dot(left, right, preferred_element_type=F32)


def lane_repeat(column, width):
    return jnp.concatenate([column] * (width // column.shape[1]), axis=1)


def causal(bk, bq, shift):
    key_at = lax.broadcasted_iota(jnp.int32, (bk, bq), 0)
    query_at = lax.broadcasted_iota(jnp.int32, (bk, bq), 1)
    return key_at + shift <= query_at


def fwd_kernel(q0, bk, q_ref, k_ref, v_ref, seg_q_ref, seg_k_ref, out_ref, log_ref, vt):
    bq, wide = q_ref.shape
    dim = k_ref.shape[1]
    group = wide // dim
    step = pl.program_id(1)
    factor = LOG2E / math.sqrt(dim)

    @pl.when(step == 0)
    def _():
        for j in range(vt.shape[0]):
            vt[j] = v_ref[pl.ds(j * bk, bk), :].astype(F32).T.astype(BF16)

    seg_q = seg_q_ref[...]
    queries = [q_ref[:, h * dim : (h + 1) * dim] for h in range(group)]

    def block(j, carry, shift):
        key_rows = k_ref[pl.ds(pl.multiple_of(j * bk, bk), bk), :]
        seg_k = seg_k_ref[pl.ds(pl.multiple_of(j * bk, bk), bk), :]
        allowed = lane_repeat(seg_k, bq) == seg_q
        if shift is not None:
            allowed &= causal(bk, bq, shift)
        value_cols = vt[j]
        new = []
        for h in range(group):
            total, acc = carry[2 * h], carry[2 * h + 1]
            scores = dot_nt(key_rows, queries[h])
            weights = jnp.where(allowed, jnp.exp2(scores * factor), 0.0)
            total = total + jnp.sum(weights.reshape(bk // 8, 8, bq), axis=0)
            acc = acc + dot_nn(value_cols, weights.astype(BF16))
            new += [total, acc]
        return tuple(new)

    carry = (jnp.zeros((8, bq), F32), jnp.zeros((dim, bq), F32)) * group
    diag = bq // bk
    whole = q0 // bk + step * diag
    carry = lax.fori_loop(0, whole, lambda j, c: block(j, c, None), carry)
    for d in range(diag):
        carry = block(whole + d, carry, d * bk)
    for h in range(group):
        total = jnp.sum(carry[2 * h], axis=0, keepdims=True)
        mixed = carry[2 * h + 1] * (1.0 / total)
        out_ref[:, h * dim : (h + 1) * dim] = mixed.T.astype(BF16)
        log_ref[0, h : h + 1, :] = jnp.log2(total)


def attend(queries, keys, values, seg_row, seg_wide, q0, dim, bq, bk):
    rows, width = queries.shape
    span = keys.shape[0]
    kv = keys.shape[1] // dim
    group = width // dim // kv
    pairs = group * kv * rows * (span - rows / 2)
    return pl.pallas_call(
        functools.partial(fwd_kernel, q0, bk),
        grid=(kv, rows // bq),
        in_specs=[
            pl.BlockSpec((bq, group * dim), lambda k, i: (i, k)),
            pl.BlockSpec((span, dim), lambda k, i: (0, k)),
            pl.BlockSpec((span, dim), lambda k, i: (0, k)),
            pl.BlockSpec((1, bq), lambda k, i: (0, i + q0 // bq)),
            pl.BlockSpec((span, 128), lambda k, i: (0, 0)),
        ],
        out_specs=[
            pl.BlockSpec((bq, group * dim), lambda k, i: (i, k)),
            pl.BlockSpec((1, group, bq), lambda k, i: (k, 0, i)),
        ],
        out_shape=[
            jax.ShapeDtypeStruct((rows, width), BF16),
            jax.ShapeDtypeStruct((kv, group, rows), F32),
        ],
        scratch_shapes=[pltpu.VMEM((span // bk, dim, bk), BF16)],
        compiler_params=pltpu.CompilerParams(vmem_limit_bytes=VMEM_LIMIT),
        cost_estimate=pl.CostEstimate(
            flops=int(pairs * dim * 8), bytes_accessed=int(rows * width * 4), transcendentals=int(pairs)
        ),
        name="attend",
    )(queries, keys, values, seg_row, seg_wide)


def bwd_kernel(
    q0, bk, first, *refs
):
    if first:
        q_ref, k_ref, v_ref, g_ref, o_ref, log_ref, seg_q_ref, seg_k_ref = refs[:8]
        dq_ref, dk_ref, dv_ref, kt = refs[8:]
    else:
        q_ref, k_ref, v_ref, g_ref, o_ref, log_ref, seg_q_ref, seg_k_ref, dk_in, dv_in = refs[:10]
        dq_ref, dk_ref, dv_ref, kt = refs[10:]
    bq, wide = q_ref.shape
    dim = k_ref.shape[1]
    group = wide // dim
    step = pl.program_id(1)
    scale = 1.0 / math.sqrt(dim)
    factor = LOG2E * scale

    @pl.when(step == 0)
    def _():
        for j in range(kt.shape[0]):
            kt[j] = k_ref[pl.ds(j * bk, bk), :].astype(F32).T.astype(BF16)
        if first:
            dk_ref[...] = jnp.zeros_like(dk_ref)
            dv_ref[...] = jnp.zeros_like(dv_ref)
        else:
            dk_ref[...] = dk_in[...]
            dv_ref[...] = dv_in[...]

    seg_q = seg_q_ref[...]
    queries = [q_ref[:, h * dim : (h + 1) * dim] for h in range(group)]
    grads = [g_ref[:, h * dim : (h + 1) * dim] for h in range(group)]
    logs = [log_ref[0, h : h + 1, :] for h in range(group)]
    inner = []
    for h in range(group):
        product = grads[h].astype(F32) * o_ref[:, h * dim : (h + 1) * dim].astype(F32)
        inner.append(jnp.sum(product.T, axis=0, keepdims=True))

    def block(j, carry, shift):
        at = pl.ds(pl.multiple_of(j * bk, bk), bk)
        key_rows = k_ref[at, :]
        value_rows = v_ref[at, :]
        allowed = lane_repeat(seg_k_ref[at, :], bq) == seg_q
        if shift is not None:
            allowed &= causal(bk, bq, shift)
        key_cols = kt[j]
        new = []
        dk, dv = dk_ref[at, :], dv_ref[at, :]
        for h in range(group):
            scores = dot_nt(key_rows, queries[h])
            probs = jnp.where(allowed, jnp.exp2(scores * factor - logs[h]), 0.0)
            grad_probs = dot_nt(value_rows, grads[h])
            grad_scores = (probs * (grad_probs - inner[h])).astype(BF16)
            dv = dv + dot_nn(probs.astype(BF16), grads[h])
            dk = dk + dot_nn(grad_scores, queries[h])
            new.append(carry[h] + dot_nn(key_cols, grad_scores))
        dk_ref[at, :] = dk
        dv_ref[at, :] = dv
        return tuple(new)

    carry = (jnp.zeros((dim, bq), F32),) * group
    diag = bq // bk
    whole = q0 // bk + step * diag
    carry = lax.fori_loop(0, whole, lambda j, c: block(j, c, None), carry)
    for d in range(diag):
        carry = block(whole + d, carry, d * bk)
    for h in range(group):
        dq_ref[:, h * dim : (h + 1) * dim] = (carry[h] * scale).T


def attend_back(queries, keys, values, grads, mixed, logs, seg_row, seg_wide, q0, dim, bq, bk, sums=None):
    rows, width = queries.shape
    span = keys.shape[0]
    kv = keys.shape[1] // dim
    group = width // dim // kv
    pairs = group * kv * rows * (span - rows / 2)
    whole = pl.BlockSpec((span, dim), lambda k, i: (0, k))
    part = pl.BlockSpec((bq, group * dim), lambda k, i: (i, k))
    more = [] if sums is None else list(sums)
    return pl.pallas_call(
        functools.partial(bwd_kernel, q0, bk, sums is None),
        grid=(kv, rows // bq),
        in_specs=[
            part,
            whole,
            whole,
            part,
            part,
            pl.BlockSpec((1, group, bq), lambda k, i: (k, 0, i)),
            pl.BlockSpec((1, bq), lambda k, i: (0, i + q0 // bq)),
            pl.BlockSpec((span, 128), lambda k, i: (0, 0)),
        ]
        + [whole] * len(more),
        out_specs=[part, whole, whole],
        out_shape=[
            jax.ShapeDtypeStruct((rows, width), F32),
            jax.ShapeDtypeStruct((span, kv * dim), F32),
            jax.ShapeDtypeStruct((span, kv * dim), F32),
        ],
        scratch_shapes=[pltpu.VMEM((span // bk, dim, bk), BF16)],
        compiler_params=pltpu.CompilerParams(vmem_limit_bytes=VMEM_LIMIT),
        cost_estimate=pl.CostEstimate(
            flops=int(pairs * dim * 20), bytes_accessed=int(rows * width * 10), transcendentals=int(pairs)
        ),
        name="attend_back",
    )(queries, keys, values, grads, mixed, logs, seg_row, seg_wide, *more)


EPS = 1e-06
THETA = 1000000.0
CHUNKS = 2


def params(**more):
    return pltpu.CompilerParams(vmem_limit_bytes=VMEM_LIMIT, **more)


def resident(shape):
    return pl.BlockSpec(shape, lambda *_: (0,) * len(shape), pipeline_mode=pl.Buffered(1))


def tile_of(size, most):
    tile = most
    while size % tile:
        tile //= 2
    return tile


def swap(values):
    half = values.shape[-1] // 2
    return jnp.concatenate([values[:, half:], values[:, :half]], axis=1)


def row_scale(values):
    return lax.rsqrt(jnp.mean(values * values, axis=-1, keepdims=True) + EPS)


def qkv_kernel(kv, x_ref, gain_ref, w_ref, gq_ref, gk_ref, cos_ref, sin_ref, *refs):
    normed_ref, scale_ref, proj_ref, q_ref, k_ref, v_ref = refs[-6:]
    dim = gq_ref.shape[1]
    heads = q_ref.shape[1] // dim
    values = x_ref[...].astype(F32)
    scale = row_scale(values)
    normed = (values * scale * gain_ref[...]).astype(BF16)
    normed_ref[...] = normed
    scale_ref[...] = scale
    projected = dot_nn(normed, w_ref[...])
    cosine, sine = cos_ref[...], sin_ref[...]
    wide = (heads + kv) * dim
    proj_ref[...] = projected[:, :wide]
    for h in range(heads + kv):
        part = projected[:, h * dim : (h + 1) * dim]
        gain = gq_ref[...] if h < heads else gk_ref[...]
        part = part * row_scale(part) * gain
        turned = (part * cosine + swap(part) * sine).astype(BF16)
        if h < heads:
            q_ref[:, h * dim : (h + 1) * dim] = turned
        else:
            k_ref[:, (h - heads) * dim : (h - heads + 1) * dim] = turned
    v_ref[...] = projected[:, wide:].astype(BF16)


def project_qkv(x, gain, weights, gain_q, gain_k, cosine, sine, kv, chunk, total, kept):
    rows, width = x.shape
    cols = weights.shape[1]
    dim = gain_q.shape[1]
    heads = cols // dim - 2 * kv
    bt = tile_of(rows, 256)
    base = chunk * rows // bt
    wide = (heads + kv) * dim

    def here(w):
        return pl.BlockSpec((bt, w), lambda i: (i, 0))

    def there(w):
        return pl.BlockSpec((bt, w), lambda i: (i + base, 0))

    more = [] if kept is None else [kept]
    return pl.pallas_call(
        functools.partial(qkv_kernel, kv),
        grid=(rows // bt,),
        in_specs=[
            here(width),
            resident((1, width)),
            resident((width, cols)),
            resident((1, dim)),
            resident((1, dim)),
            there(dim),
            there(dim),
        ]
        + [pl.BlockSpec(memory_space=pl.ANY)] * len(more),
        out_specs=[there(width), here(1), here(wide), here(heads * dim), here(kv * dim), here(kv * dim)],
        out_shape=[
            jax.ShapeDtypeStruct((total, width), BF16),
            jax.ShapeDtypeStruct((rows, 1), F32),
            jax.ShapeDtypeStruct((rows, wide), F32),
            jax.ShapeDtypeStruct((rows, heads * dim), BF16),
            jax.ShapeDtypeStruct((rows, kv * dim), BF16),
            jax.ShapeDtypeStruct((rows, kv * dim), BF16),
        ],
        input_output_aliases={7: 0} if more else {},
        compiler_params=params(),
        cost_estimate=pl.CostEstimate(
            flops=2 * rows * width * cols, bytes_accessed=rows * width * 4 + width * cols * 2, transcendentals=0
        ),
        name="project_qkv",
    )(x, gain, weights, gain_q, gain_k, cosine, sine, *more)


def mlp_kernel(x_ref, gain_ref, wg_ref, wu_ref, wd_ref, cot_ref, *refs):
    normed_ref, scale_ref, active_ref, gg_ref, gu_ref = refs[-5:]

    @pl.when(pl.program_id(1) == 0)
    def _():
        values = x_ref[...].astype(F32)
        scale = row_scale(values)
        normed_ref[...] = (values * scale * gain_ref[...]).astype(BF16)
        scale_ref[...] = scale

    normed = normed_ref[...]
    gate = dot_nn(normed, wg_ref[...])
    up = dot_nn(normed, wu_ref[...])
    grad = dot_nt(cot_ref[...], wd_ref[...])
    sig = jax.nn.sigmoid(gate)
    silu = gate * sig
    active_ref[...] = (silu * up).astype(BF16)
    gu_ref[...] = (grad * silu).astype(BF16)
    gg_ref[...] = (grad * up * sig * (1.0 + gate * (1.0 - sig))).astype(BF16)


def mlp(x, gain, w_gate_up, w_down, cot, chunk, total, kept):
    rows, width = x.shape
    hidden = w_down.shape[0]
    bt = tile_of(rows, 512)
    bn = tile_of(hidden, 512)
    tiles = hidden // bn
    base = chunk * rows // bt
    more = [] if kept is None else list(kept)
    low = jax.ShapeDtypeStruct((total, hidden), BF16)
    tile = pl.BlockSpec((bt, bn), lambda i, j: (i + base, j))
    return pl.pallas_call(
        mlp_kernel,
        grid=(rows // bt, tiles),
        in_specs=[
            pl.BlockSpec((bt, width), lambda i, j: (i, 0)),
            resident((1, width)),
            pl.BlockSpec((width, bn), lambda i, j: (0, j)),
            pl.BlockSpec((width, bn), lambda i, j: (0, j + tiles)),
            pl.BlockSpec((bn, width), lambda i, j: (j, 0)),
            pl.BlockSpec((bt, width), lambda i, j: (i, 0)),
        ]
        + [pl.BlockSpec(memory_space=pl.ANY)] * len(more),
        out_specs=[
            pl.BlockSpec((bt, width), lambda i, j: (i + base, 0)),
            pl.BlockSpec((bt, 1), lambda i, j: (i, 0)),
            tile,
            tile,
            tile,
        ],
        out_shape=[
            jax.ShapeDtypeStruct((total, width), BF16),
            jax.ShapeDtypeStruct((rows, 1), F32),
            low,
            low,
            low,
        ],
        input_output_aliases={6: 0, 7: 2, 8: 3, 9: 4} if more else {},
        compiler_params=params(),
        cost_estimate=pl.CostEstimate(
            flops=6 * rows * width * hidden,
            bytes_accessed=rows * (width + hidden) * 6 + 6 * width * hidden,
            transcendentals=rows * hidden,
        ),
        name="mlp",
    )(x, gain, w_gate_up, w_gate_up, w_down, cot, *more)


def mid_kernel(gg_ref, gu_ref, w_ref, v_ref, scale_ref, gain_ref, part_ref, inner_ref, gain_out):
    hidden = gg_ref.shape[1]
    partial = dot_nt(gg_ref[...], w_ref[:, :hidden]) + dot_nt(gu_ref[...], w_ref[:, hidden:])
    part_ref[...] = partial.astype(BF16)
    product = partial * v_ref[...].astype(F32)
    gain_out[0] = jnp.sum(product * scale_ref[...], axis=0, keepdims=True)
    inner = jnp.sum(product * gain_ref[...], axis=1, keepdims=True)

    @pl.when(pl.program_id(1) == 0)
    def _():
        inner_ref[...] = inner

    @pl.when(pl.program_id(1) > 0)
    def _():
        inner_ref[...] += inner


def back_mid(gg, gu, weights, values, scale, gain, chunk):
    rows, width = values.shape
    hidden = gg.shape[1]
    bt = tile_of(rows, 512)
    bn = tile_of(width, 512)
    base = chunk * rows // bt
    return pl.pallas_call(
        mid_kernel,
        grid=(rows // bt, width // bn),
        in_specs=[
            pl.BlockSpec((bt, hidden), lambda i, j: (i + base, 0)),
            pl.BlockSpec((bt, hidden), lambda i, j: (i + base, 0)),
            pl.BlockSpec((bn, 2 * hidden), lambda i, j: (j, 0)),
            pl.BlockSpec((bt, bn), lambda i, j: (i, j)),
            pl.BlockSpec((bt, 1), lambda i, j: (i, 0)),
            pl.BlockSpec((1, bn), lambda i, j: (0, j)),
        ],
        out_specs=[
            pl.BlockSpec((bt, bn), lambda i, j: (i, j)),
            pl.BlockSpec((bt, 1), lambda i, j: (i, 0)),
            pl.BlockSpec((1, 1, bn), lambda i, j: (i, 0, j)),
        ],
        out_shape=[
            jax.ShapeDtypeStruct((rows, width), BF16),
            jax.ShapeDtypeStruct((rows, 1), F32),
            jax.ShapeDtypeStruct((rows // bt, 1, width), F32),
        ],
        compiler_params=params(),
        cost_estimate=pl.CostEstimate(
            flops=4 * rows * width * hidden, bytes_accessed=rows * (width + hidden) * 4, transcendentals=0
        ),
        name="back_mid",
    )(gg, gu, weights, values, scale, gain)


def qkv_back_kernel(
    kv, dq_ref, dk_ref, dv_ref, proj_ref, cos_ref, sin_ref, gq_ref, gk_ref, w_ref, v_ref, scale_ref, gain_ref, *refs
):
    low_ref, part_ref, inner_ref, gain_out, gq_out, gk_out = refs[-6:]
    dim = gq_ref.shape[1]
    heads = dq_ref.shape[1] // dim
    wide = (heads + kv) * dim
    cosine, sine = cos_ref[...], sin_ref[...]
    sums = [jnp.zeros((1, dim), F32), jnp.zeros((1, dim), F32)]
    for h in range(heads + kv):
        is_key = h >= heads
        if is_key:
            grad = dk_ref[:, (h - heads) * dim : (h - heads + 1) * dim] * (1.0 / math.sqrt(dim))
        else:
            grad = dq_ref[:, h * dim : (h + 1) * dim]
        grad = grad * cosine + swap(grad * sine)
        value = proj_ref[:, h * dim : (h + 1) * dim]
        scale = row_scale(value)
        sums[is_key] += jnp.sum(grad * value * scale, axis=0, keepdims=True)
        weighted = grad * (gk_ref[...] if is_key else gq_ref[...])
        mean = jnp.mean(weighted * value, axis=-1, keepdims=True)
        low_ref[:, h * dim : (h + 1) * dim] = (scale * (weighted - value * scale * scale * mean)).astype(BF16)
    low_ref[:, wide:] = dv_ref[...].astype(BF16)
    partial = dot_nt(low_ref[...], w_ref[...])
    part_ref[...] = partial.astype(BF16)
    product = partial * v_ref[...].astype(F32)
    inner_ref[...] = jnp.sum(product * gain_ref[...], axis=1, keepdims=True)
    gain_sum = jnp.sum(product * scale_ref[...], axis=0, keepdims=True)

    @pl.when(pl.program_id(0) == 0)
    def _():
        gain_out[...] = gain_sum
        gq_out[...] = sums[0]
        gk_out[...] = sums[1]

    @pl.when(pl.program_id(0) > 0)
    def _():
        gain_out[...] += gain_sum
        gq_out[...] += sums[0]
        gk_out[...] += sums[1]


def back_qkv(dq, dk, dv, proj, cosine, sine, gain_q, gain_k, weights, values, scale, gain, kv, chunk, total, kept):
    rows, width = values.shape
    cols = weights.shape[1]
    dim = gain_q.shape[1]
    bt = tile_of(rows, 256)
    base = chunk * rows // bt

    def here(w):
        return pl.BlockSpec((bt, w), lambda i: (i, 0))

    def there(w):
        return pl.BlockSpec((bt, w), lambda i: (i + base, 0))

    def once(w):
        return pl.BlockSpec((1, w), lambda i: (0, 0))

    more = [] if kept is None else [kept]
    return pl.pallas_call(
        functools.partial(qkv_back_kernel, kv),
        grid=(rows // bt,),
        in_specs=[
            here(dq.shape[1]),
            there(dk.shape[1]),
            there(dv.shape[1]),
            here(proj.shape[1]),
            there(dim),
            there(dim),
            resident((1, dim)),
            resident((1, dim)),
            resident((width, cols)),
            here(width),
            here(1),
            resident((1, width)),
        ]
        + [pl.BlockSpec(memory_space=pl.ANY)] * len(more),
        out_specs=[there(cols), here(width), here(1), once(width), once(dim), once(dim)],
        out_shape=[
            jax.ShapeDtypeStruct((total, cols), BF16),
            jax.ShapeDtypeStruct((rows, width), BF16),
            jax.ShapeDtypeStruct((rows, 1), F32),
            jax.ShapeDtypeStruct((1, width), F32),
            jax.ShapeDtypeStruct((1, dim), F32),
            jax.ShapeDtypeStruct((1, dim), F32),
        ],
        input_output_aliases={12: 0} if more else {},
        compiler_params=params(),
        cost_estimate=pl.CostEstimate(
            flops=2 * rows * width * cols, bytes_accessed=rows * width * 4 + rows * cols * 10, transcendentals=0
        ),
        name="back_qkv",
    )(dq, dk, dv, proj, cosine, sine, gain_q, gain_k, weights, values, scale, gain, *more)


def contract(left, right, left_dim, right_dim):
    return lax.dot_general(left, right, (((left_dim,), (right_dim,)), ((), ())), preferred_element_type=F32)


class Ring:
    def __init__(self, size):
        self.size = size
        order = [self.place(p) for p in range(size)]
        self.right = [(order[p], order[(p + 1) % size]) for p in range(size)]
        self.left = [(order[(p + 1) % size], order[p]) for p in range(size)]

    def place(self, index):
        half = self.size // 2
        if isinstance(index, int):
            return index if index < half else self.size + half - 1 - index
        return jnp.where(index < half, index, self.size + half - 1 - index)

    def owner(self, offset):
        return self.place(lax.rem(self.place(lax.axis_index("col")) + offset + self.size, self.size))

    def go(self, values, to_right):
        return lax.ppermute(values, "col", self.right if to_right else self.left)

    def gather(self, local):
        rows, width = local.shape
        half = rows // 2
        full = jnp.zeros((rows, width * self.size), local.dtype)

        def put(full, piece, offset, row=0):
            return lax.dynamic_update_slice(full, piece, (row, self.owner(offset) * width))

        from_left = from_right = local
        full = put(full, local, 0)
        for k in range(1, self.size // 2):
            from_left, from_right = self.go(from_left, True), self.go(from_right, False)
            full = put(put(full, from_left, -k), from_right, k)
        top = self.go(from_left[:half], True)
        bottom = self.go(from_right[half:], False)
        return put(put(full, top, self.size // 2), bottom, self.size // 2, half)

    def scatter(self, term):
        far = term(self.size // 2).astype(BF16)
        half = far.shape[0] // 2
        from_left, from_right = self.go(far[:half], True), self.go(far[half:], False)
        from_left = jnp.pad(from_left, ((0, half), (0, 0)))
        from_right = jnp.pad(from_right, ((half, 0), (0, 0)))
        for k in range(self.size // 2 - 1, 0, -1):
            to_right = (term(k) + from_left.astype(F32)).astype(BF16)
            to_left = (term(-k) + from_right.astype(F32)).astype(BF16)
            from_left, from_right = self.go(to_right, True), self.go(to_left, False)
        return term(0) + from_left.astype(F32) + from_right.astype(F32)


def rope_tables(positions, dim):
    half = dim // 2
    inverse = THETA ** (-(jnp.arange(half, dtype=F32) * 2.0 / dim))
    angle = positions.astype(F32)[:, None] * inverse[None, :]
    cosine, sine = jnp.cos(angle), jnp.sin(angle)
    return jnp.concatenate([cosine, cosine], axis=1), jnp.concatenate([-sine, sine], axis=1)


def body(
    tokens,
    segments,
    positions,
    gain_attn,
    w_query,
    key_weight_matrix,
    value_weight_matrix,
    gain_query,
    gain_key,
    w_out,
    gain_mlp,
    w_gate,
    w_up,
    w_down,
    cotangent,
):
    total, local = tokens.shape
    dim = gain_query.shape[0]
    query_cols, key_cols = w_query.shape[1], key_weight_matrix.shape[1]
    kv = key_cols // dim
    hidden_units = w_gate.shape[1]
    ring = Ring(lax.axis_size("col"))
    width = local * ring.size
    rows = total // CHUNKS
    parts = [slice(c * rows, (c + 1) * rows) for c in range(CHUNKS)]
    offset = lax.axis_index("col") * local
    gain_attn_local = lax.dynamic_slice_in_dim(gain_attn, offset, local)
    gain_mlp_local = lax.dynamic_slice_in_dim(gain_mlp, offset, local)
    gain_q, gain_k = gain_query[None], gain_key[None]
    bq = tile_of(rows, 512)

    w_qkv = lax.all_gather(
        jnp.concatenate([w_query, key_weight_matrix, value_weight_matrix], axis=1), "row", axis=0, tiled=True
    )
    w_out_full = lax.all_gather(w_out, "row", axis=1, tiled=True)
    w_gate_up = lax.all_gather(jnp.concatenate([w_gate, w_up], axis=1), "row", axis=0, tiled=True)
    w_down_full = lax.all_gather(w_down, "row", axis=1, tiled=True)

    cosine, sine = rope_tables(positions, dim)
    seg_row = segments[None]
    seg_wide = jnp.broadcast_to(segments[:, None], (total, 128))

    def block_of(matrix, k, axis=1):
        return lax.dynamic_slice_in_dim(matrix, ring.owner(k) * local, local, axis)

    x_full, normed, scale_attn, proj, queries = [], None, [], [], []
    key_all = value_all = None
    mixed, logs, hidden = [], [], []
    for c in range(CHUNKS):
        x_full.append(ring.gather(tokens[parts[c]]))
        normed, scale, pr, q, k, v = project_qkv(
            x_full[c], gain_attn[None], w_qkv, gain_q, gain_k, cosine, sine, kv, c, total, normed
        )
        scale_attn.append(scale)
        proj.append(pr)
        queries.append(q)
        key_all = k if c == 0 else jnp.concatenate([key_all, k])
        value_all = v if c == 0 else jnp.concatenate([value_all, v])
        span = (c + 1) * rows
        mx, lg = attend(q, key_all, value_all, seg_row, seg_wide[:span], c * rows, dim, bq, bq)
        mixed.append(mx)
        logs.append(lg)
        hidden.append(
            tokens[parts[c]].astype(F32) + ring.scatter(lambda k: jnp.dot(mx, block_of(w_out_full, k), preferred_element_type=F32))
        )

    kept = None
    mid_low, mid_full, cot_full, scale_mid = [], [], [], []
    for c in range(CHUNKS):
        mid_low.append(hidden[c].astype(BF16))
        mid_full.append(ring.gather(mid_low[c]))
        cot_full.append(ring.gather(cotangent[parts[c]]))
        nm, scale, active, gg, gu = mlp(
            mid_full[c], gain_mlp[None], w_gate_up, w_down_full, cot_full[c], c, total, kept
        )
        kept = (nm, active, gg, gu)
        scale_mid.append(scale)
    normed_mid, active, grad_gate, grad_up = kept

    grad_hidden, grad_hidden_full, gain_mlp_part, grad_mixed = [None] * CHUNKS, [None] * CHUNKS, 0.0, [None] * CHUNKS
    for c in reversed(range(CHUNKS)):
        partial, inner, gain_part = back_mid(
            grad_gate, grad_up, w_gate_up, mid_full[c], scale_mid[c], gain_mlp[None], c
        )
        gain_mlp_part = gain_mlp_part + jnp.sum(gain_part, axis=(0, 1))
        inner = lax.psum(inner[:, 0], "col")[:, None]
        grad_normed = ring.scatter(lambda k: block_of(partial, k).astype(F32))
        scale = scale_mid[c]
        grad_hidden[c] = cotangent[parts[c]].astype(F32) + scale * (
            grad_normed * gain_mlp_local - mid_low[c].astype(F32) * (scale * scale * inner / width)
        )
        grad_hidden_full[c] = ring.gather(grad_hidden[c].astype(BF16))
        grad_mixed[c] = contract(grad_hidden_full[c], w_out_full, 1, 1).astype(BF16)

    def scattered(partial, axis):
        return lax.psum_scatter(partial.astype(BF16), "row", scatter_dimension=axis, tiled=True).astype(F32)

    cot_all = jnp.concatenate(cot_full)
    grad_down = scattered(contract(active, cot_all, 0, 0), 1)
    grad_w_gate = scattered(contract(normed_mid, grad_gate, 0, 0), 0)
    grad_w_up = scattered(contract(normed_mid, grad_up, 0, 0), 0)
    grad_out = scattered(contract(jnp.concatenate(mixed), jnp.concatenate(grad_hidden_full), 0, 0), 1)

    output = []
    for c in range(CHUNKS):
        low = active[parts[c]]
        terms = ring.scatter(lambda k: jnp.dot(low, block_of(w_down_full, k), preferred_element_type=F32))
        output.append((hidden[c] + terms).astype(BF16))

    sums, low = None, None
    grad_tokens = [None] * CHUNKS
    gain_attn_part = gain_q_part = gain_k_part = 0.0
    for c in reversed(range(CHUNKS)):
        span = (c + 1) * rows
        dq, dk, dv = attend_back(
            queries[c], key_all[:span], value_all[:span], grad_mixed[c], mixed[c], logs[c], seg_row, seg_wide[:span],
            c * rows, dim, bq, bq, sums,
        )
        sums = (dk[: c * rows], dv[: c * rows])
        low, partial, inner, gain_part, gq_part, gk_part = back_qkv(
            dq, dk, dv, proj[c], cosine, sine, gain_q, gain_k, w_qkv, x_full[c], scale_attn[c], gain_attn[None],
            kv, c, total, low,
        )
        gain_attn_part, gain_q_part, gain_k_part = gain_attn_part + gain_part[0], gain_q_part + gq_part[0], gain_k_part + gk_part[0]
        inner = lax.psum(inner[:, 0], "col")[:, None]
        grad_normed = ring.scatter(lambda k: block_of(partial, k).astype(F32))
        scale = scale_attn[c]
        grad_tokens[c] = grad_hidden[c] + scale * (
            grad_normed * gain_attn_local - tokens[parts[c]].astype(F32) * (scale * scale * inner / width)
        )
    grad_qkv = scattered(contract(normed, low, 0, 0), 0)
    sum_attn, sum_mlp, sum_q, sum_k = lax.psum(
        (gain_attn_part, gain_mlp_part, gain_q_part, gain_k_part), ("row", "col")
    )
    return (
        jnp.concatenate(output),
        jnp.concatenate(grad_tokens),
        sum_attn,
        grad_qkv[:, :query_cols],
        grad_qkv[:, query_cols : query_cols + key_cols],
        grad_qkv[:, query_cols + key_cols :],
        sum_q,
        sum_k,
        grad_out,
        sum_mlp,
        grad_w_gate,
        grad_w_up,
        grad_down,
    )


def solution(mesh):
    both, split = P("row", "col"), P("col", "row")
    in_specs = (both, P("row"), P("row"), P(), both, both, both, P(), P(), split, P(), both, both, split, both)
    out_specs = (both, both, P(), both, both, both, P(), P(), split, P(), both, both, split)
    return jax.shard_map(body, mesh=mesh, in_specs=in_specs, out_specs=out_specs, check_vma=False)
```

```python
import functools
import math

import jax
import jax.numpy as jnp
from jax import lax
from jax.experimental import pallas as pl
from jax.experimental.pallas import tpu as pltpu
from jax.sharding import PartitionSpec as P

BF16 = jnp.bfloat16
F32 = jnp.float32
LOG2E = 1.4426950408889634
VMEM_LIMIT = 60 * 1024 * 1024


def dot_nt(left, right):
    return lax.dot_general(left, right, (((1,), (1,)), ((), ())), preferred_element_type=F32)


def dot_nn(left, right):
    return jnp.dot(left, right, preferred_element_type=F32)


def lane_repeat(column, width):
    return jnp.concatenate([column] * (width // column.shape[1]), axis=1)


def causal(bk, bq, shift):
    key_at = lax.broadcasted_iota(jnp.int32, (bk, bq), 0)
    query_at = lax.broadcasted_iota(jnp.int32, (bk, bq), 1)
    return key_at + shift <= query_at


def fwd_kernel(q0, bk, q_ref, k_ref, v_ref, seg_q_ref, seg_k_ref, out_ref, log_ref, vt):
    bq, wide = q_ref.shape
    dim = k_ref.shape[1]
    group = wide // dim
    step = pl.program_id(1)
    factor = LOG2E / math.sqrt(dim)

    @pl.when(step == 0)
    def _():
        for j in range(vt.shape[0]):
            vt[j] = v_ref[pl.ds(j * bk, bk), :].astype(F32).T.astype(BF16)

    seg_q = seg_q_ref[...]
    queries = [q_ref[:, h * dim : (h + 1) * dim] for h in range(group)]

    def block(j, carry, shift):
        key_rows = k_ref[pl.ds(pl.multiple_of(j * bk, bk), bk), :]
        seg_k = seg_k_ref[pl.ds(pl.multiple_of(j * bk, bk), bk), :]
        allowed = lane_repeat(seg_k, bq) == seg_q
        if shift is not None:
            allowed &= causal(bk, bq, shift)
        value_cols = vt[j]
        new = []
        for h in range(group):
            total, acc = carry[2 * h], carry[2 * h + 1]
            scores = dot_nt(key_rows, queries[h])
            weights = jnp.where(allowed, jnp.exp2(scores * factor), 0.0)
            total = total + jnp.sum(weights.reshape(bk // 8, 8, bq), axis=0)
            acc = acc + dot_nn(value_cols, weights.astype(BF16))
            new += [total, acc]
        return tuple(new)

    carry = (jnp.zeros((8, bq), F32), jnp.zeros((dim, bq), F32)) * group
    diag = bq // bk
    whole = q0 // bk + step * diag
    carry = lax.fori_loop(0, whole, lambda j, c: block(j, c, None), carry)
    for d in range(diag):
        carry = block(whole + d, carry, d * bk)
    for h in range(group):
        total = jnp.sum(carry[2 * h], axis=0, keepdims=True)
        mixed = carry[2 * h + 1] * (1.0 / total)
        out_ref[:, h * dim : (h + 1) * dim] = mixed.T.astype(BF16)
        log_ref[0, h : h + 1, :] = jnp.log2(total)


def attend(queries, keys, values, seg_row, seg_wide, q0, dim, bq, bk):
    rows, width = queries.shape
    span = keys.shape[0]
    kv = keys.shape[1] // dim
    group = width // dim // kv
    pairs = group * kv * rows * (span - rows / 2)
    return pl.pallas_call(
        functools.partial(fwd_kernel, q0, bk),
        grid=(kv, rows // bq),
        in_specs=[
            pl.BlockSpec((bq, group * dim), lambda k, i: (i, k)),
            pl.BlockSpec((span, dim), lambda k, i: (0, k)),
            pl.BlockSpec((span, dim), lambda k, i: (0, k)),
            pl.BlockSpec((1, bq), lambda k, i: (0, i + q0 // bq)),
            pl.BlockSpec((span, 128), lambda k, i: (0, 0)),
        ],
        out_specs=[
            pl.BlockSpec((bq, group * dim), lambda k, i: (i, k)),
            pl.BlockSpec((1, group, bq), lambda k, i: (k, 0, i)),
        ],
        out_shape=[
            jax.ShapeDtypeStruct((rows, width), BF16),
            jax.ShapeDtypeStruct((kv, group, rows), F32),
        ],
        scratch_shapes=[pltpu.VMEM((span // bk, dim, bk), BF16)],
        compiler_params=pltpu.CompilerParams(vmem_limit_bytes=VMEM_LIMIT),
        cost_estimate=pl.CostEstimate(
            flops=int(pairs * dim * 8), bytes_accessed=int(rows * width * 4), transcendentals=int(pairs)
        ),
        name="attend",
    )(queries, keys, values, seg_row, seg_wide)


def bwd_kernel(
    q0, bk, first, *refs
):
    if first:
        q_ref, k_ref, v_ref, g_ref, o_ref, log_ref, seg_q_ref, seg_k_ref = refs[:8]
        dq_ref, dk_ref, dv_ref, kt = refs[8:]
    else:
        q_ref, k_ref, v_ref, g_ref, o_ref, log_ref, seg_q_ref, seg_k_ref, dk_in, dv_in = refs[:10]
        dq_ref, dk_ref, dv_ref, kt = refs[10:]
    bq, wide = q_ref.shape
    dim = k_ref.shape[1]
    group = wide // dim
    step = pl.program_id(1)
    scale = 1.0 / math.sqrt(dim)
    factor = LOG2E * scale

    @pl.when(step == 0)
    def _():
        for j in range(kt.shape[0]):
            kt[j] = k_ref[pl.ds(j * bk, bk), :].astype(F32).T.astype(BF16)
        if first:
            dk_ref[...] = jnp.zeros_like(dk_ref)
            dv_ref[...] = jnp.zeros_like(dv_ref)
        else:
            dk_ref[...] = dk_in[...]
            dv_ref[...] = dv_in[...]

    seg_q = seg_q_ref[...]
    queries = [q_ref[:, h * dim : (h + 1) * dim] for h in range(group)]
    grads = [g_ref[:, h * dim : (h + 1) * dim] for h in range(group)]
    logs = [log_ref[0, h : h + 1, :] for h in range(group)]
    inner = []
    for h in range(group):
        product = grads[h].astype(F32) * o_ref[:, h * dim : (h + 1) * dim].astype(F32)
        inner.append(jnp.sum(product.T, axis=0, keepdims=True))

    def block(j, carry, shift):
        at = pl.ds(pl.multiple_of(j * bk, bk), bk)
        key_rows = k_ref[at, :]
        value_rows = v_ref[at, :]
        allowed = lane_repeat(seg_k_ref[at, :], bq) == seg_q
        if shift is not None:
            allowed &= causal(bk, bq, shift)
        key_cols = kt[j]
        new = []
        dk, dv = dk_ref[at, :], dv_ref[at, :]
        for h in range(group):
            scores = dot_nt(key_rows, queries[h])
            probs = jnp.where(allowed, jnp.exp2(scores * factor - logs[h]), 0.0)
            grad_probs = dot_nt(value_rows, grads[h])
            grad_scores = (probs * (grad_probs - inner[h])).astype(BF16)
            dv = dv + dot_nn(probs.astype(BF16), grads[h])
            dk = dk + dot_nn(grad_scores, queries[h])
            new.append(carry[h] + dot_nn(key_cols, grad_scores))
        dk_ref[at, :] = dk
        dv_ref[at, :] = dv
        return tuple(new)

    carry = (jnp.zeros((dim, bq), F32),) * group
    diag = bq // bk
    whole = q0 // bk + step * diag
    carry = lax.fori_loop(0, whole, lambda j, c: block(j, c, None), carry)
    for d in range(diag):
        carry = block(whole + d, carry, d * bk)
    for h in range(group):
        dq_ref[:, h * dim : (h + 1) * dim] = (carry[h] * scale).T


def attend_back(queries, keys, values, grads, mixed, logs, seg_row, seg_wide, q0, dim, bq, bk, sums=None):
    rows, width = queries.shape
    span = keys.shape[0]
    kv = keys.shape[1] // dim
    group = width // dim // kv
    pairs = group * kv * rows * (span - rows / 2)
    whole = pl.BlockSpec((span, dim), lambda k, i: (0, k))
    part = pl.BlockSpec((bq, group * dim), lambda k, i: (i, k))
    more = [] if sums is None else list(sums)
    return pl.pallas_call(
        functools.partial(bwd_kernel, q0, bk, sums is None),
        grid=(kv, rows // bq),
        in_specs=[
            part,
            whole,
            whole,
            part,
            part,
            pl.BlockSpec((1, group, bq), lambda k, i: (k, 0, i)),
            pl.BlockSpec((1, bq), lambda k, i: (0, i + q0 // bq)),
            pl.BlockSpec((span, 128), lambda k, i: (0, 0)),
        ]
        + [whole] * len(more),
        out_specs=[part, whole, whole],
        out_shape=[
            jax.ShapeDtypeStruct((rows, width), F32),
            jax.ShapeDtypeStruct((span, kv * dim), F32),
            jax.ShapeDtypeStruct((span, kv * dim), F32),
        ],
        scratch_shapes=[pltpu.VMEM((span // bk, dim, bk), BF16)],
        compiler_params=pltpu.CompilerParams(vmem_limit_bytes=VMEM_LIMIT),
        cost_estimate=pl.CostEstimate(
            flops=int(pairs * dim * 20), bytes_accessed=int(rows * width * 10), transcendentals=int(pairs)
        ),
        name="attend_back",
    )(queries, keys, values, grads, mixed, logs, seg_row, seg_wide, *more)


EPS = 1e-06
THETA = 1000000.0
CHUNKS = 2


def params(**more):
    return pltpu.CompilerParams(vmem_limit_bytes=VMEM_LIMIT, **more)


def resident(shape):
    return pl.BlockSpec(shape, lambda *_: (0,) * len(shape), pipeline_mode=pl.Buffered(1))


def tile_of(size, most):
    tile = most
    while size % tile:
        tile //= 2
    return tile


def swap(values):
    half = values.shape[-1] // 2
    return jnp.concatenate([values[:, half:], values[:, :half]], axis=1)


def row_scale(values):
    return lax.rsqrt(jnp.mean(values * values, axis=-1, keepdims=True) + EPS)


def qkv_kernel(kv, x_ref, gain_ref, w_ref, gq_ref, gk_ref, cos_ref, sin_ref, *refs):
    normed_ref, scale_ref, proj_ref, q_ref, k_ref, v_ref = refs[-6:]
    dim = gq_ref.shape[1]
    heads = q_ref.shape[1] // dim
    values = x_ref[...].astype(F32)
    scale = row_scale(values)
    normed = (values * scale * gain_ref[...]).astype(BF16)
    normed_ref[...] = normed
    scale_ref[...] = scale
    projected = dot_nn(normed, w_ref[...])
    cosine, sine = cos_ref[...], sin_ref[...]
    wide = (heads + kv) * dim
    proj_ref[...] = projected[:, :wide]
    for h in range(heads + kv):
        part = projected[:, h * dim : (h + 1) * dim]
        gain = gq_ref[...] if h < heads else gk_ref[...]
        part = part * row_scale(part) * gain
        turned = (part * cosine + swap(part) * sine).astype(BF16)
        if h < heads:
            q_ref[:, h * dim : (h + 1) * dim] = turned
        else:
            k_ref[:, (h - heads) * dim : (h - heads + 1) * dim] = turned
    v_ref[...] = projected[:, wide:].astype(BF16)


def project_qkv(x, gain, weights, gain_q, gain_k, cosine, sine, kv, chunk, rows, kept):
    total, width = x.shape
    cols = weights.shape[1]
    dim = gain_q.shape[1]
    heads = cols // dim - 2 * kv
    bt = tile_of(rows, 256)
    base = chunk * rows // bt
    wide = (heads + kv) * dim

    def here(w):
        return pl.BlockSpec((bt, w), lambda i: (i, 0))

    def there(w):
        return pl.BlockSpec((bt, w), lambda i: (i + base, 0))

    more = [] if kept is None else [kept]
    return pl.pallas_call(
        functools.partial(qkv_kernel, kv),
        grid=(rows // bt,),
        in_specs=[
            there(width),
            resident((1, width)),
            resident((width, cols)),
            resident((1, dim)),
            resident((1, dim)),
            there(dim),
            there(dim),
        ]
        + [pl.BlockSpec(memory_space=pl.ANY)] * len(more),
        out_specs=[there(width), here(1), here(wide), here(heads * dim), here(kv * dim), here(kv * dim)],
        out_shape=[
            jax.ShapeDtypeStruct((total, width), BF16),
            jax.ShapeDtypeStruct((rows, 1), F32),
            jax.ShapeDtypeStruct((rows, wide), F32),
            jax.ShapeDtypeStruct((rows, heads * dim), BF16),
            jax.ShapeDtypeStruct((rows, kv * dim), BF16),
            jax.ShapeDtypeStruct((rows, kv * dim), BF16),
        ],
        input_output_aliases={7: 0} if more else {},
        compiler_params=params(),
        cost_estimate=pl.CostEstimate(
            flops=2 * rows * width * cols, bytes_accessed=rows * width * 4 + width * cols * 2, transcendentals=0
        ),
        name="project_qkv",
    )(x, gain, weights, gain_q, gain_k, cosine, sine, *more)


def mlp_kernel(x_ref, gain_ref, wg_ref, wu_ref, wd_ref, cot_ref, *refs):
    normed_ref, scale_ref, active_ref, gg_ref, gu_ref, cot_out = refs[-6:]

    @pl.when(pl.program_id(1) == 0)
    def _():
        cot_out[...] = cot_ref[...]
        values = x_ref[...].astype(F32)
        scale = row_scale(values)
        normed_ref[...] = (values * scale * gain_ref[...]).astype(BF16)
        scale_ref[...] = scale

    normed = normed_ref[...]
    gate = dot_nn(normed, wg_ref[...])
    up = dot_nn(normed, wu_ref[...])
    grad = dot_nt(cot_ref[...], wd_ref[...])
    sig = jax.nn.sigmoid(gate)
    silu = gate * sig
    active_ref[...] = (silu * up).astype(BF16)
    gu_ref[...] = (grad * silu).astype(BF16)
    gg_ref[...] = (grad * up * sig * (1.0 + gate * (1.0 - sig))).astype(BF16)


def mlp(x, gain, w_gate_up, w_down, cot, chunk, total, kept):
    rows, width = x.shape
    hidden = w_down.shape[0]
    bt = tile_of(rows, 512)
    bn = tile_of(hidden, 512)
    tiles = hidden // bn
    base = chunk * rows // bt
    more = [] if kept is None else list(kept)
    low = jax.ShapeDtypeStruct((total, hidden), BF16)
    tile = pl.BlockSpec((bt, bn), lambda i, j: (i + base, j))
    return pl.pallas_call(
        mlp_kernel,
        grid=(rows // bt, tiles),
        in_specs=[
            pl.BlockSpec((bt, width), lambda i, j: (i, 0)),
            resident((1, width)),
            pl.BlockSpec((width, bn), lambda i, j: (0, j)),
            pl.BlockSpec((width, bn), lambda i, j: (0, j + tiles)),
            pl.BlockSpec((bn, width), lambda i, j: (j, 0)),
            pl.BlockSpec((bt, width), lambda i, j: (i, 0)),
        ]
        + [pl.BlockSpec(memory_space=pl.ANY)] * len(more),
        out_specs=[
            pl.BlockSpec((bt, width), lambda i, j: (i + base, 0)),
            pl.BlockSpec((bt, 1), lambda i, j: (i, 0)),
            tile,
            tile,
            tile,
            pl.BlockSpec((bt, width), lambda i, j: (i + base, 0)),
        ],
        out_shape=[
            jax.ShapeDtypeStruct((total, width), BF16),
            jax.ShapeDtypeStruct((rows, 1), F32),
            low,
            low,
            low,
            jax.ShapeDtypeStruct((total, width), BF16),
        ],
        input_output_aliases={6: 0, 7: 2, 8: 3, 9: 4, 10: 5} if more else {},
        compiler_params=params(),
        cost_estimate=pl.CostEstimate(
            flops=6 * rows * width * hidden,
            bytes_accessed=rows * (width + hidden) * 6 + 6 * width * hidden,
            transcendentals=rows * hidden,
        ),
        name="mlp",
    )(x, gain, w_gate_up, w_gate_up, w_down, cot, *more)


def row_of(column):
    return jnp.broadcast_to(column, (column.shape[0], 128)).T[:1]


def mid_kernel(gg_ref, gu_ref, w_ref, v_ref, scale_ref, gain_ref, part_ref, inner_ref, gain_out):
    hidden = gg_ref.shape[1]
    partial = dot_nt(gg_ref[...], w_ref[:, :hidden]) + dot_nt(gu_ref[...], w_ref[:, hidden:])
    part_ref[...] = partial.astype(BF16)
    product = partial * v_ref[...].astype(F32)
    gain_out[0] = jnp.sum(product * scale_ref[...], axis=0, keepdims=True)
    inner = row_of(jnp.sum(product * gain_ref[...], axis=1, keepdims=True))

    @pl.when(pl.program_id(1) == 0)
    def _():
        inner_ref[0] = inner

    @pl.when(pl.program_id(1) > 0)
    def _():
        inner_ref[0] += inner


def back_mid(gg, gu, weights, values, scale, gain, chunk):
    rows, width = values.shape
    hidden = gg.shape[1]
    bt = tile_of(rows, 512)
    bn = tile_of(width, 512)
    base = chunk * rows // bt
    return pl.pallas_call(
        mid_kernel,
        grid=(rows // bt, width // bn),
        in_specs=[
            pl.BlockSpec((bt, hidden), lambda i, j: (i + base, 0)),
            pl.BlockSpec((bt, hidden), lambda i, j: (i + base, 0)),
            pl.BlockSpec((bn, 2 * hidden), lambda i, j: (j, 0)),
            pl.BlockSpec((bt, bn), lambda i, j: (i, j)),
            pl.BlockSpec((bt, 1), lambda i, j: (i, 0)),
            pl.BlockSpec((1, bn), lambda i, j: (0, j)),
        ],
        out_specs=[
            pl.BlockSpec((bt, bn), lambda i, j: (i, j)),
            pl.BlockSpec((1, 1, bt), lambda i, j: (i, 0, 0)),
            pl.BlockSpec((1, 1, bn), lambda i, j: (i, 0, j)),
        ],
        out_shape=[
            jax.ShapeDtypeStruct((rows, width), BF16),
            jax.ShapeDtypeStruct((rows // bt, 1, bt), F32),
            jax.ShapeDtypeStruct((rows // bt, 1, width), F32),
        ],
        compiler_params=params(),
        cost_estimate=pl.CostEstimate(
            flops=4 * rows * width * hidden, bytes_accessed=rows * (width + hidden) * 4, transcendentals=0
        ),
        name="back_mid",
    )(gg, gu, weights, values, scale, gain)


def qkv_back_kernel(
    kv, dq_ref, dk_ref, dv_ref, proj_ref, cos_ref, sin_ref, gq_ref, gk_ref, w_ref, v_ref, scale_ref, gain_ref, *refs
):
    low_ref, part_ref, inner_ref, gain_out, gq_out, gk_out = refs[-6:]
    dim = gq_ref.shape[1]
    heads = dq_ref.shape[1] // dim
    wide = (heads + kv) * dim
    cosine, sine = cos_ref[...], sin_ref[...]
    sums = [jnp.zeros((1, dim), F32), jnp.zeros((1, dim), F32)]
    for h in range(heads + kv):
        is_key = h >= heads
        if is_key:
            grad = dk_ref[:, (h - heads) * dim : (h - heads + 1) * dim] * (1.0 / math.sqrt(dim))
        else:
            grad = dq_ref[:, h * dim : (h + 1) * dim]
        grad = grad * cosine + swap(grad * sine)
        value = proj_ref[:, h * dim : (h + 1) * dim]
        scale = row_scale(value)
        sums[is_key] += jnp.sum(grad * value * scale, axis=0, keepdims=True)
        weighted = grad * (gk_ref[...] if is_key else gq_ref[...])
        mean = jnp.mean(weighted * value, axis=-1, keepdims=True)
        low_ref[:, h * dim : (h + 1) * dim] = (scale * (weighted - value * scale * scale * mean)).astype(BF16)
    low_ref[:, wide:] = dv_ref[...].astype(BF16)
    partial = dot_nt(low_ref[...], w_ref[...])
    part_ref[...] = partial.astype(BF16)
    product = partial * v_ref[...].astype(F32)
    inner_ref[0] = row_of(jnp.sum(product * gain_ref[...], axis=1, keepdims=True))
    gain_sum = jnp.sum(product * scale_ref[...], axis=0, keepdims=True)

    @pl.when(pl.program_id(0) == 0)
    def _():
        gain_out[...] = gain_sum
        gq_out[...] = sums[0]
        gk_out[...] = sums[1]

    @pl.when(pl.program_id(0) > 0)
    def _():
        gain_out[...] += gain_sum
        gq_out[...] += sums[0]
        gk_out[...] += sums[1]


def back_qkv(dq, dk, dv, proj, cosine, sine, gain_q, gain_k, weights, values, scale, gain, kv, chunk, rows, kept):
    total, width = values.shape
    cols = weights.shape[1]
    dim = gain_q.shape[1]
    bt = tile_of(rows, 256)
    base = chunk * rows // bt

    def here(w):
        return pl.BlockSpec((bt, w), lambda i: (i, 0))

    def there(w):
        return pl.BlockSpec((bt, w), lambda i: (i + base, 0))

    def once(w):
        return pl.BlockSpec((1, w), lambda i: (0, 0))

    more = [] if kept is None else [kept]
    return pl.pallas_call(
        functools.partial(qkv_back_kernel, kv),
        grid=(rows // bt,),
        in_specs=[
            here(dq.shape[1]),
            there(dk.shape[1]),
            there(dv.shape[1]),
            here(proj.shape[1]),
            there(dim),
            there(dim),
            resident((1, dim)),
            resident((1, dim)),
            resident((width, cols)),
            there(width),
            here(1),
            resident((1, width)),
        ]
        + [pl.BlockSpec(memory_space=pl.ANY)] * len(more),
        out_specs=[
            there(cols),
            here(width),
            pl.BlockSpec((1, 1, bt), lambda i: (i, 0, 0)),
            once(width),
            once(dim),
            once(dim),
        ],
        out_shape=[
            jax.ShapeDtypeStruct((total, cols), BF16),
            jax.ShapeDtypeStruct((rows, width), BF16),
            jax.ShapeDtypeStruct((rows // bt, 1, bt), F32),
            jax.ShapeDtypeStruct((1, width), F32),
            jax.ShapeDtypeStruct((1, dim), F32),
            jax.ShapeDtypeStruct((1, dim), F32),
        ],
        input_output_aliases={12: 0} if more else {},
        compiler_params=params(),
        cost_estimate=pl.CostEstimate(
            flops=2 * rows * width * cols, bytes_accessed=rows * width * 4 + rows * cols * 10, transcendentals=0
        ),
        name="back_qkv",
    )(dq, dk, dv, proj, cosine, sine, gain_q, gain_k, weights, values, scale, gain, *more)


def contract(left, right, left_dim, right_dim):
    return lax.dot_general(left, right, (((left_dim,), (right_dim,)), ((), ())), preferred_element_type=F32)


class Ring:
    def __init__(self, size):
        self.size = size
        order = [self.place(p) for p in range(size)]
        self.right = [(order[p], order[(p + 1) % size]) for p in range(size)]
        self.left = [(order[(p + 1) % size], order[p]) for p in range(size)]

    def place(self, index):
        half = self.size // 2
        if isinstance(index, int):
            return index if index < half else self.size + half - 1 - index
        return jnp.where(index < half, index, self.size + half - 1 - index)

    def owner(self, offset):
        return self.place(lax.rem(self.place(lax.axis_index("col")) + offset + self.size, self.size))

    def go(self, values, to_right):
        return lax.ppermute(values, "col", self.right if to_right else self.left)

    def gather(self, local):
        half = local.shape[0] // 2
        from_left = from_right = local
        pieces = [(0, local)]
        for k in range(1, self.size // 2):
            from_left, from_right = self.go(from_left, True), self.go(from_right, False)
            pieces += [(-k, from_left), (k, from_right)]
            yield from_left, from_right
        top, bottom = self.go(from_left[:half], True), self.go(from_right[half:], False)
        yield top, bottom
        yield pieces, top, bottom

    def assemble(self, gathered, chunk=0, total=None, kept=None):
        pieces, top, bottom = gathered
        rows, width = pieces[0][1].shape
        total = total or rows
        bt = tile_of(rows // 2, 256)
        halves = rows // 2 // bt
        base = chunk * rows // bt
        offsets = [offset for offset, _ in pieces]

        def kernel(*refs):
            out = refs[-1]
            for offset, ref in zip(offsets, refs):
                out[:, pl.ds(pl.multiple_of(self.owner(offset) * width, 128), width)] = ref[...]
            far = pl.ds(pl.multiple_of(self.owner(self.size // 2) * width, 128), width)

            @pl.when(pl.program_id(0) < halves)
            def _():
                out[:, far] = refs[len(offsets)][...]

            @pl.when(pl.program_id(0) >= halves)
            def _():
                out[:, far] = refs[len(offsets) + 1][...]

        more = [] if kept is None else [kept]
        count = len(pieces) + 2
        return pl.pallas_call(
            kernel,
            grid=(rows // bt,),
            in_specs=[pl.BlockSpec((bt, width), lambda i: (i, 0))] * len(pieces)
            + [
                pl.BlockSpec((bt, width), lambda i: (jnp.minimum(i, halves - 1), 0)),
                pl.BlockSpec((bt, width), lambda i: (jnp.maximum(i - halves, 0), 0)),
            ]
            + [pl.BlockSpec(memory_space=pl.ANY)] * len(more),
            out_specs=pl.BlockSpec((bt, width * self.size), lambda i: (i + base, 0)),
            out_shape=jax.ShapeDtypeStruct((total, width * self.size), BF16),
            input_output_aliases={count: 0} if more else {},
            compiler_params=params(),
            cost_estimate=pl.CostEstimate(flops=0, bytes_accessed=rows * width * self.size * 4, transcendentals=0),
            name="assemble",
        )(*[piece for _, piece in pieces], top, bottom, *more)

    def scatter(self, term, half):
        far = term(self.size // 2).astype(BF16)
        rows = far.shape[0]
        from_left, from_right = self.go(far[:half], True), self.go(far[half:], False)
        yield far
        from_left = jnp.pad(from_left, ((0, rows - half), (0, 0)))
        from_right = jnp.pad(from_right, ((half, 0), (0, 0)))
        for k in range(self.size // 2 - 1, 0, -1):
            to_right = (term(k) + from_left.astype(F32)).astype(BF16)
            to_left = (term(-k) + from_right.astype(F32)).astype(BF16)
            from_left, from_right = self.go(to_right, True), self.go(to_left, False)
            yield (to_right, to_left)
        yield term(0) + from_left.astype(F32) + from_right.astype(F32)


def after(value, *others):
    return lax.optimization_barrier((value,) + others)[0]


def rope_tables(positions, dim):
    half = dim // 2
    inverse = THETA ** (-(jnp.arange(half, dtype=F32) * 2.0 / dim))
    angle = positions.astype(F32)[:, None] * inverse[None, :]
    cosine, sine = jnp.cos(angle), jnp.sin(angle)
    return jnp.concatenate([cosine, cosine], axis=1), jnp.concatenate([-sine, sine], axis=1)


def body(
    tokens,
    segments,
    positions,
    gain_attn,
    w_query,
    key_weight_matrix,
    value_weight_matrix,
    gain_query,
    gain_key,
    w_out,
    gain_mlp,
    w_gate,
    w_up,
    w_down,
    cotangent,
):
    total, local = tokens.shape
    dim = gain_query.shape[0]
    query_cols, key_cols = w_query.shape[1], key_weight_matrix.shape[1]
    kv = key_cols // dim
    hidden_units = w_gate.shape[1]
    ring = Ring(lax.axis_size("col"))
    width = local * ring.size
    rows = total // CHUNKS
    parts = [slice(c * rows, (c + 1) * rows) for c in range(CHUNKS)]
    offset = lax.axis_index("col") * local
    gain_attn_local = lax.dynamic_slice_in_dim(gain_attn, offset, local)
    gain_mlp_local = lax.dynamic_slice_in_dim(gain_mlp, offset, local)
    gain_q, gain_k = gain_query[None], gain_key[None]
    bq = tile_of(rows, 512)

    w_qkv = lax.all_gather(
        jnp.concatenate([w_query, key_weight_matrix, value_weight_matrix], axis=1), "row", axis=0, tiled=True
    )
    w_out_full = lax.all_gather(w_out, "row", axis=1, tiled=True)
    w_gate_up = lax.all_gather(jnp.concatenate([w_gate, w_up], axis=1), "row", axis=0, tiled=True)
    w_down_full = lax.all_gather(w_down, "row", axis=1, tiled=True)

    cosine, sine = rope_tables(positions, dim)
    seg_row = segments[None]
    seg_wide = jnp.broadcast_to(segments[:, None], (total, 128))

    def block_of(matrix, k, axis=1):
        return lax.dynamic_slice_in_dim(matrix, ring.owner(k) * local, local, axis)

    def term_of(left, matrix):
        return lambda k: jnp.dot(left, block_of(matrix, k), preferred_element_type=F32)

    def run(steps, count=1):
        for _ in range(count):
            made = next(steps)
        return made

    half = rows // 2
    hops = ring.size // 2 - 1

    def after_all(value, *others):
        return after(value, *jax.tree.leaves(others))

    def payload_of(partial, inner):
        extra = inner.reshape(-1, local).astype(BF16)
        extra = jnp.pad(extra, ((0, -extra.shape[0] % 16), (0, 0)))
        return lambda k: jnp.concatenate([block_of(partial, k), extra]).astype(F32)

    def unpack(payload):
        inner = payload[rows : rows + rows // local].reshape(rows, 1)
        return payload[:rows], inner

    def weight_grad(left, right):
        return contract(left, right, 0, 0).astype(BF16)

    def scattered(partial, axis):
        return lax.psum_scatter(partial, "row", scatter_dimension=axis, tiled=True).astype(F32)

    pair = lambda: [None] * 2
    proj, scale_attn, queries, keys, values = pair(), pair(), pair(), pair(), pair()
    mixed, logs, hidden, mid_low, mid_full, scale_mid = pair(), pair(), pair(), pair(), pair(), pair()
    sum_out, sum_down, sum_mid, sum_in = pair(), pair(), pair(), pair()
    get_cot, get_mid, get_grad = pair(), pair(), pair()
    gain_mlp_part, grad_hidden, grad_full, gains_in = pair(), pair(), pair(), pair()
    output, grad_tokens = pair(), pair()

    def project(c, normed, *before):
        normed, scale_attn[c], proj[c], queries[c], keys[c], values[c] = project_qkv(
            x_full, after_all(gain_attn[None], before), w_qkv, gain_q, gain_k, cosine, sine, kv, c, rows, normed
        )
        return normed

    def attention(c, *before):
        span = (c + 1) * rows
        mixed[c], logs[c] = attend(
            after_all(queries[c], before), jnp.concatenate(keys[: c + 1]), jnp.concatenate(values[: c + 1]), seg_row,
            seg_wide[:span], c * rows, dim, bq, bq,
        )
        return logs[c]

    def start_out(c, *before):
        sum_out[c] = ring.scatter(term_of(after_all(mixed[c], before), w_out_full), half)
        return run(sum_out[c])

    def end_out(c, *before):
        hidden[c] = after_all(tokens[parts[c]], before).astype(F32) + run(sum_out[c])
        mid_low[c] = hidden[c].astype(BF16)
        get_mid[c] = ring.gather(mid_low[c])
        return mid_low[c]

    def feed_forward(c, kept, mid, cot, *before):
        mid_full[c] = ring.assemble(mid)
        cot_full = ring.assemble(cot)
        nm, scale_mid[c], *rest = mlp(
            after_all(mid_full[c], before), gain_mlp[None], w_gate_up, w_down_full, cot_full, c, total, kept
        )
        return (nm, *rest)

    def start_down(c, active, *before):
        low = after_all(active[parts[c]], before)
        sum_down[c] = ring.scatter(term_of(low, w_down_full), half)
        return run(sum_down[c])

    def end_down(c, *before):
        output[c] = (after_all(hidden[c], before) + run(sum_down[c])).astype(BF16)
        return output[c]

    def back_middle(c, kept, *before):
        partial, inner, gain_part = back_mid(
            after_all(kept[2], before), kept[3], w_gate_up, mid_full[c], scale_mid[c], gain_mlp[None], c
        )
        gain_mlp_part[c] = jnp.sum(gain_part, axis=(0, 1))
        return partial, inner

    def start_sum(where, c, made, *before):
        where[c] = ring.scatter(payload_of(after_all(made[0], before), made[1]), half)
        return run(where[c])

    def end_mid(c, *before):
        grad_normed, inner = unpack(run(sum_mid[c]))
        scale = scale_mid[c]
        grad_hidden[c] = after_all(cotangent[parts[c]], before).astype(F32) + scale * (
            grad_normed * gain_mlp_local - mid_low[c].astype(F32) * (scale * scale * inner / width)
        )
        low = grad_hidden[c].astype(BF16)
        get_grad[c] = ring.gather(low)
        return low

    def end_in(c, *before):
        grad_normed, inner = unpack(run(sum_in[c]))
        scale = scale_attn[c]
        grad_tokens[c] = after_all(grad_hidden[c], before) + scale * (
            grad_normed * gain_attn_local - tokens[parts[c]].astype(F32) * (scale * scale * inner / width)
        )
        return grad_tokens[c]

    def grad_mix(c, gathered, *before):
        grad_full[c] = ring.assemble(gathered)
        return contract(after_all(grad_full[c], before), w_out_full, 1, 1).astype(BF16)

    def attention_back(c, grad_mixed, sums, *before):
        span = (c + 1) * rows
        return attend_back(
            after_all(queries[c], before), jnp.concatenate(keys[: c + 1]), jnp.concatenate(values[: c + 1]), grad_mixed,
            mixed[c], logs[c], seg_row, seg_wide[:span], c * rows, dim, bq, bq, sums,
        )

    def projection_back(c, grads, low_all, *before):
        low_all, partial, inner, *gains_in[c] = back_qkv(
            after_all(grads[0], before), grads[1], grads[2], proj[c], cosine, sine, gain_q, gain_k, w_qkv, x_full,
            scale_attn[c], gain_attn[None], kv, c, rows, low_all,
        )
        return low_all, (partial, inner)

    get_tok = ring.gather(tokens)
    tok_hops = [run(get_tok) for _ in range(hops + 1)]
    x_full = ring.assemble(run(get_tok))
    get_cot[1] = ring.gather(after_all(cotangent[parts[1]], tok_hops[-1]))
    hop = run(get_cot[1], hops)

    normed = project(0, None)
    at = attention(0, hop)
    hop = run(get_cot[1])
    at = start_out(0, at)
    normed = project(1, normed, at, hop)
    at = run(sum_out[0], hops)
    at = attention(1, at)
    at = start_out(1, at)
    at = end_out(0, at)
    mid_hop = run(get_mid[0], hops)
    at = run(sum_out[1], hops)
    at = end_out(1, at, mid_hop)
    run(get_mid[0])
    mid_hop = run(get_mid[1], hops)
    run(get_mid[1])
    get_cot[0] = ring.gather(after_all(cotangent[parts[0]], mid_hop))
    hop = run(get_cot[0], hops)
    run(get_cot[0])

    kept = feed_forward(1, None, run(get_mid[1]), run(get_cot[1]), hop)
    at = start_down(1, kept[1])
    made = back_middle(1, kept, at)
    at = run(sum_down[1], hops)
    at = start_sum(sum_mid, 1, made, at)
    kept = feed_forward(0, kept, run(get_mid[0]), run(get_cot[0]), at)
    normed_mid, active, grad_gate, grad_up, cot_all = kept
    at = run(sum_mid[1], hops)
    grad_down = weight_grad(after_all(active, at), cot_all)
    rs_down = scattered(grad_down, 1)
    at = end_mid(1, grad_down)
    hop = run(get_grad[1], hops)
    made = back_middle(0, kept, at)
    at = start_sum(sum_mid, 0, made, hop)
    grad_w_gate = weight_grad(after_all(normed_mid, at), grad_gate)
    rs_gate = scattered(grad_w_gate, 0)
    run(get_grad[1])
    at = run(sum_mid[0], hops)

    grads = attention_back(1, grad_mix(1, run(get_grad[1]), at, grad_w_gate), None)
    at = end_mid(0, grads[0])
    hop = run(get_grad[0], hops)
    low_all, made = projection_back(1, grads, None, at)
    at = start_sum(sum_in, 1, made, hop)
    run(get_grad[0])
    grad_w_up = weight_grad(after_all(normed_mid, at), grad_up)
    rs_up = scattered(grad_w_up, 0)
    grad_mixed = grad_mix(0, run(get_grad[0]), grad_w_up)
    at = run(sum_in[1], hops)
    grads = attention_back(0, grad_mixed, (grads[1][:rows], grads[2][:rows]), at, rs_down)
    at = start_down(0, active, grads[0])
    low_all, made = projection_back(0, grads, low_all, at)
    at = start_sum(sum_in, 0, made)
    at = run(sum_down[0], hops)
    grad_out = contract(after_all(mixed[0], at), grad_full[0], 0, 0) + contract(mixed[1], grad_full[1], 0, 0)
    rs_out = scattered(grad_out.astype(BF16), 1)
    at = run(sum_in[0], hops)
    at = end_in(1, at, grad_out)
    at = end_down(1, at)
    grad_qkv = weight_grad(after_all(normed, at, rs_gate), low_all)
    grad_qkv = scattered(grad_qkv, 0)
    at = end_down(0, at)
    at = end_in(0, at)

    both = [left + right for left, right in zip(*gains_in)]
    gains = jnp.concatenate([both[0][0], gain_mlp_part[0] + gain_mlp_part[1], both[1][0], both[2][0]])[None]
    for axis in ("col", "row"):
        step = 1
        while step < lax.axis_size(axis):
            gains = gains + lax.ppermute(gains, axis, [(i, i ^ step) for i in range(lax.axis_size(axis))])
            step *= 2
    gains = gains[0]
    return (
        jnp.concatenate(output),
        jnp.concatenate(grad_tokens),
        gains[:width],
        grad_qkv[:, :query_cols],
        grad_qkv[:, query_cols : query_cols + key_cols],
        grad_qkv[:, query_cols + key_cols :],
        gains[2 * width : 2 * width + dim],
        gains[2 * width + dim :],
        rs_out,
        gains[width : 2 * width],
        rs_gate,
        rs_up,
        rs_down,
    )


def solution(mesh):
    both, split = P("row", "col"), P("col", "row")
    in_specs = (both, P("row"), P("row"), P(), both, both, both, P(), P(), split, P(), both, both, split, both)
    out_specs = (both, both, P(), both, both, both, P(), P(), split, P(), both, both, split)
    return jax.shard_map(body, mesh=mesh, in_specs=in_specs, out_specs=out_specs, check_vma=False)
```

```python
import functools
import itertools
import math

import jax
import jax.numpy as jnp
from jax import lax
from jax.experimental import pallas as pl
from jax.experimental.pallas import tpu as pltpu
from jax.sharding import PartitionSpec as P

BF16 = jnp.bfloat16
F32 = jnp.float32
EPS = 1e-06
THETA = 1000000.0
LOG2E = 1.4426950408889634
VMEM_LIMIT = 60 * 1024 * 1024
ANY = pl.BlockSpec(memory_space=pl.ANY)


def dot_nt(left, right):
    return lax.dot_general(left, right, (((1,), (1,)), ((), ())), preferred_element_type=F32)


def dot_nn(left, right):
    return jnp.dot(left, right, preferred_element_type=F32)


def dot_tn(left, right):
    return lax.dot_general(left, right, (((0,), (0,)), ((), ())), preferred_element_type=F32)


def shape(dims, dtype):
    return jax.ShapeDtypeStruct(tuple(dims), dtype)


def resident(dims):
    return pl.BlockSpec(dims, lambda *_: (0,) * len(dims), pipeline_mode=pl.Buffered(1))


def held(dims, index):
    return pl.BlockSpec(dims, index, pipeline_mode=pl.Buffered(1))


def tile_of(size, most):
    tile = most
    while size % tile:
        tile //= 2
    return tile


def swap(values):
    half = values.shape[-1] // 2
    return jnp.concatenate([values[:, half:], values[:, :half]], axis=1)


def row_scale(values):
    return lax.rsqrt(jnp.mean(values * values, axis=-1, keepdims=True) + EPS)


def row_of(column):
    return jnp.broadcast_to(column, (column.shape[0], 128)).T[:1]


class Ring:
    def __init__(self, size):
        self.size = size
        self.stages = size // 2

    def place(self, index):
        half = self.size // 2
        return jnp.where(index < half, index, self.size + half - 1 - index)

    def owner(self, offset):
        return self.place(lax.rem(self.place(lax.axis_index("col")) + offset + self.size, self.size))

    def cols(self, offset, width):
        return pl.ds(pl.multiple_of(self.owner(offset) * width, 128), width)


class Gather:
    def __init__(self, ring, local, row, rows):
        self.ring, self.local, self.row, self.rows = ring, local, row, rows
        self.width = local.shape[1]
        self.stage, self.full = 0, None
        self.out = [shape((rows, self.width * ring.size), BF16)]
        self.offsets = [-1, 1]

    def prepare(self):
        self.stage += 1
        self.ins = [self.local] if self.stage == 1 else [self.full]
        self.alias = {} if self.stage == 1 else {0: 0}
        self.count = 3 if self.stage == 1 else 2
        self.bounce = [(self.rows, self.width)] if self.stage == 1 else []
        return self

    def copies(self, ins, outs):
        ring, full, width, half = self.ring, outs[0], self.width, self.rows // 2
        if self.stage == 1:
            source = ins[0].at[pl.ds(self.row, self.rows), :]
            mine = full.at[:, ring.cols(0, width)]
            return [(source, mine, 1), (source, mine, -1), (source, mine, None)]
        from_left, from_right = ring.cols(1 - self.stage, width), ring.cols(self.stage - 1, width)
        if self.stage < ring.stages:
            left, right = full.at[:, from_left], full.at[:, from_right]
        else:
            left, right = full.at[pl.ds(0, half), from_left], full.at[pl.ds(half, half), from_right]
        return [(left, left, 1), (right, right, -1)]

    def finish(self, outs):
        self.full = outs[0]


class Scatter:
    def __init__(self, ring, partial, inner=None):
        self.ring, self.partial, self.inner = ring, partial, inner
        self.rows, self.half = partial.shape[0], partial.shape[0] // 2
        self.width = partial.shape[1] // ring.size
        self.stage, self.inner_sum, self.bounce = 0, None, []
        self.offsets = [-1, 1]

    def block(self, offset, low):
        start = (self.half if low else 0, self.ring.owner(offset) * self.width)
        return lax.dynamic_slice(self.partial, start, (self.half, self.width)).astype(F32)

    def prepare(self):
        self.stage += 1
        stage, stages = self.stage, self.ring.stages
        whole = stage < stages
        self.alias = {}
        if stage == 1:
            self.ins = [self.partial]
        else:
            top = self.block(stages + 1 - stage, False) + self.got[0].astype(F32)
            bottom = self.block(stage - 1 - stages, True) + self.got[1].astype(F32)
            self.ins = [top.astype(BF16), bottom.astype(BF16)]
            if whole:
                low = self.block(stages - stage, True) + self.got[2].astype(F32)
                high = self.block(stage - stages, False) + self.got[3].astype(F32)
                self.ins += [low.astype(BF16), high.astype(BF16)]
            else:
                self.kept = self.got[2:]
        self.out = [shape((self.half, self.width), BF16)] * (4 if whole else 2)
        self.count = len(self.out)
        if stage == 1 and self.inner is not None:
            self.ins.append(self.inner)
            self.out.append(shape((self.ring.size - 1, *self.inner.shape), F32))
            self.count += self.ring.size - 1
            self.offsets = list(range(1, self.ring.size))
        else:
            self.offsets = [-1, 1]
        return self

    def copies(self, ins, outs):
        ring, width, half, stages = self.ring, self.width, self.half, self.ring.stages
        if self.stage > 1:
            return [(ref, out, way) for ref, out, way in zip(ins, outs, (1, -1, 1, -1))]
        top, bottom = pl.ds(0, half), pl.ds(half, half)
        far = ring.cols(stages, width)
        made = [
            (ins[0].at[top, far], outs[0], 1),
            (ins[0].at[bottom, far], outs[1], -1),
            (ins[0].at[bottom, ring.cols(stages - 1, width)], outs[2], 1),
            (ins[0].at[top, ring.cols(1 - stages, width)], outs[3], -1),
        ]
        if self.inner is not None:
            made += [(ins[1], outs[4].at[k - 1], k) for k in range(1, ring.size)]
        return made

    def finish(self, outs):
        if self.stage == 1 and self.inner is not None:
            self.inner_sum = (jnp.sum(outs[4], axis=0) + self.inner).reshape(self.rows, 1)
            outs = outs[:4]
        self.got = outs

    def total(self):
        mine = lax.dynamic_slice_in_dim(self.partial, lax.axis_index("col") * self.width, self.width, 1)
        left = jnp.concatenate([self.got[0], self.kept[0]]).astype(F32)
        right = jnp.concatenate([self.kept[1], self.got[1]]).astype(F32)
        return mine.astype(F32) + left + right


class Launcher:
    def __init__(self, ring):
        self.ring = ring
        self.ids = itertools.count()

    def __call__(self, kernel, args, in_specs, out_specs, out_shape, grid, name, cost, alias=None, scratch=(), carry=()):
        stages = [stage.prepare() for stage in carry]
        own_in, own_out = len(args), len(out_shape)
        args, in_specs, out_specs, out_shape = list(args), list(in_specs), list(out_specs), list(out_shape)
        alias, scratch = dict(alias or {}), list(scratch)
        own_scratch = len(scratch)
        spans = []
        for stage in stages:
            ins, outs = len(args), len(out_shape)
            alias.update({ins + i: outs + o for i, o in stage.alias.items()})
            args += stage.ins
            out_shape += stage.out
            spans.append((ins, len(args), outs, len(out_shape)))
        in_specs += [ANY] * (len(args) - own_in)
        out_specs += [ANY] * (len(out_shape) - own_out)
        more = {}
        if stages:
            count = sum(stage.count for stage in stages)
            scratch += [pltpu.SemaphoreType.DMA((count,)), pltpu.SemaphoreType.DMA((count,))]
            scratch += [pltpu.VMEM(dims, BF16) for stage in stages for dims in stage.bounce]
            more = dict(collective_id=next(self.ids), has_side_effects=True)
        offsets = sorted({o % self.ring.size for stage in stages for o in stage.offsets})
        ring = self.ring
        total_in, total_out = len(args), len(out_shape)

        def body(*refs):
            ins, outs, rest = refs[:total_in], refs[total_in : total_in + total_out], refs[total_in + total_out :]
            own = (*ins[:own_in], *outs[:own_out], *rest[:own_scratch])
            if not stages:
                kernel(*own)
                return
            send, receive, *bounce = rest[own_scratch:]

            def copies(part):
                made, at, held = [], 0, 0
                for stage, (a, b, c, d) in zip(stages, spans):
                    for source, target, way in stage.copies(ins[a:b], outs[c:d]):
                        if way is None:
                            if part == "in":
                                made.append(pltpu.make_async_copy(source, bounce[held], receive.at[at]))
                            elif part == "out":
                                made.append(pltpu.make_async_copy(bounce[held], target, send.at[at]))
                            held += 1
                        elif part == "remote":
                            made.append(
                                pltpu.make_async_remote_copy(
                                    source, target, send.at[at], receive.at[at], device_id={"col": ring.owner(way)},
                                    device_id_type=pl.DeviceIdType.MESH,
                                )
                            )
                        at += 1
                return made

            first = last = True
            for axis, size in enumerate(grid):
                first &= pl.program_id(axis) == 0
                last &= pl.program_id(axis) == size - 1
            barrier = pltpu.get_barrier_semaphore()

            @pl.when(first)
            def _():
                for offset in offsets:
                    pl.semaphore_signal(
                        barrier, 1, device_id={"col": ring.owner(offset)}, device_id_type=pl.DeviceIdType.MESH
                    )
                for copy in copies("in"):
                    copy.start()
                pl.semaphore_wait(barrier, len(offsets))
                for copy in copies("remote"):
                    copy.start()

            kernel(*own)

            @pl.when(first)
            def _():
                for inward, outward in zip(copies("in"), copies("out")):
                    inward.wait()
                    outward.start()

            @pl.when(last)
            def _():
                for copy in copies("out") + copies("remote"):
                    copy.wait()

        flops, moved, exps = cost
        made = pl.pallas_call(
            body,
            grid=grid,
            in_specs=in_specs,
            out_specs=out_specs,
            out_shape=out_shape,
            input_output_aliases=alias,
            scratch_shapes=scratch,
            compiler_params=pltpu.CompilerParams(vmem_limit_bytes=VMEM_LIMIT, **more),
            cost_estimate=pl.CostEstimate(flops=int(flops), bytes_accessed=int(moved), transcendentals=int(exps)),
            name=name,
        )(*args)
        for stage, (_, _, c, d) in zip(stages, spans):
            stage.finish(made[c:d])
        return made[:own_out]

    def alone(self, *stages):
        self(lambda *_: None, [], [], [], [], (1,), "exchange", (0, 0, 0), carry=stages)


def lane_repeat(column, width):
    return jnp.concatenate([column] * (width // column.shape[1]), axis=1)


def causal(bk, bq, shift):
    key_at = lax.broadcasted_iota(jnp.int32, (bk, bq), 0)
    query_at = lax.broadcasted_iota(jnp.int32, (bk, bq), 1)
    return key_at + shift <= query_at


def fwd_kernel(q0, bk, q_ref, k_ref, v_ref, seg_q_ref, seg_k_ref, out_ref, log_ref, vt):
    bq, wide = q_ref.shape
    dim = k_ref.shape[1]
    group = wide // dim
    step = pl.program_id(1)
    factor = LOG2E / math.sqrt(dim)

    @pl.when(step == 0)
    def _():
        for j in range(vt.shape[0]):
            vt[j] = v_ref[pl.ds(j * bk, bk), :].astype(F32).T.astype(BF16)

    seg_q = seg_q_ref[...]
    queries = [q_ref[:, h * dim : (h + 1) * dim] for h in range(group)]

    def block(j, carry, shift):
        key_rows = k_ref[pl.ds(pl.multiple_of(j * bk, bk), bk), :]
        seg_k = seg_k_ref[pl.ds(pl.multiple_of(j * bk, bk), bk), :]
        allowed = lane_repeat(seg_k, bq) == seg_q
        if shift is not None:
            allowed &= causal(bk, bq, shift)
        value_cols = vt[j]
        new = []
        for h in range(group):
            total, acc = carry[2 * h], carry[2 * h + 1]
            scores = dot_nt(key_rows, queries[h])
            weights = jnp.where(allowed, jnp.exp2(scores * factor), 0.0)
            total = total + jnp.sum(weights.reshape(bk // 8, 8, bq), axis=0)
            acc = acc + dot_nn(value_cols, weights.astype(BF16))
            new += [total, acc]
        return tuple(new)

    carry = (jnp.zeros((8, bq), F32), jnp.zeros((dim, bq), F32)) * group
    diag = bq // bk
    whole = q0 // bk + step * diag
    carry = lax.fori_loop(0, whole, lambda j, c: block(j, c, None), carry)
    for d in range(diag):
        carry = block(whole + d, carry, d * bk)
    for h in range(group):
        total = jnp.sum(carry[2 * h], axis=0, keepdims=True)
        mixed = carry[2 * h + 1] * (1.0 / total)
        out_ref[:, h * dim : (h + 1) * dim] = mixed.T.astype(BF16)
        log_ref[0, h : h + 1, :] = jnp.log2(total)


def attend(launch, queries, keys, values, seg_row, seg_wide, q0, rows, dim, bq, bk, carry=()):
    width = queries.shape[1]
    span = q0 + rows
    kv = keys.shape[1] // dim
    group = width // dim // kv
    pairs = group * kv * rows * (span - rows / 2)
    base = q0 // bq
    whole = pl.BlockSpec((span, dim), lambda k, i: (0, k))
    return launch(
        functools.partial(fwd_kernel, q0, bk),
        (queries, keys, values, seg_row, seg_wide),
        [
            pl.BlockSpec((bq, group * dim), lambda k, i: (i + base, k)),
            whole,
            whole,
            pl.BlockSpec((1, bq), lambda k, i: (0, i + base)),
            pl.BlockSpec((span, 128), lambda k, i: (0, 0)),
        ],
        [
            pl.BlockSpec((bq, group * dim), lambda k, i: (i, k)),
            pl.BlockSpec((1, group, bq), lambda k, i: (k, 0, i)),
        ],
        [shape((rows, width), BF16), shape((kv, group, rows), F32)],
        (kv, rows // bq),
        "attend",
        (pairs * dim * 8, rows * width * 4, pairs),
        scratch=[pltpu.VMEM((span // bk, dim, bk), BF16)],
        carry=carry,
    )


def bwd_kernel(q0, bk, first, *refs):
    q_ref, k_ref, v_ref, g_ref, o_ref, log_ref, seg_q_ref, seg_k_ref = refs[:8]
    dk_in, dv_in = (None, None) if first else refs[8:10]
    dq_ref, dk_ref, dv_ref, kt = refs[-4:]
    bq, wide = q_ref.shape
    dim = k_ref.shape[1]
    group = wide // dim
    step = pl.program_id(1)
    scale = 1.0 / math.sqrt(dim)
    factor = LOG2E * scale

    @pl.when(step == 0)
    def _():
        for j in range(kt.shape[0]):
            kt[j] = k_ref[pl.ds(j * bk, bk), :].astype(F32).T.astype(BF16)
        if first:
            dk_ref[...] = jnp.zeros_like(dk_ref)
            dv_ref[...] = jnp.zeros_like(dv_ref)
        else:
            dk_ref[...] = dk_in[...]
            dv_ref[...] = dv_in[...]

    seg_q = seg_q_ref[...]
    queries = [q_ref[:, h * dim : (h + 1) * dim] for h in range(group)]
    grads = [g_ref[:, h * dim : (h + 1) * dim] for h in range(group)]
    logs = [log_ref[0, h : h + 1, :] for h in range(group)]
    inner = []
    for h in range(group):
        product = grads[h].astype(F32) * o_ref[:, h * dim : (h + 1) * dim].astype(F32)
        inner.append(jnp.sum(product.T, axis=0, keepdims=True))

    def block(j, carry, shift):
        at = pl.ds(pl.multiple_of(j * bk, bk), bk)
        key_rows = k_ref[at, :]
        value_rows = v_ref[at, :]
        allowed = lane_repeat(seg_k_ref[at, :], bq) == seg_q
        if shift is not None:
            allowed &= causal(bk, bq, shift)
        key_cols = kt[j]
        new = []
        dk, dv = dk_ref[at, :], dv_ref[at, :]
        for h in range(group):
            scores = dot_nt(key_rows, queries[h])
            probs = jnp.where(allowed, jnp.exp2(scores * factor - logs[h]), 0.0)
            grad_probs = dot_nt(value_rows, grads[h])
            grad_scores = (probs * (grad_probs - inner[h])).astype(BF16)
            dv = dv + dot_nn(probs.astype(BF16), grads[h])
            dk = dk + dot_nn(grad_scores, queries[h])
            new.append(carry[h] + dot_nn(key_cols, grad_scores))
        dk_ref[at, :] = dk
        dv_ref[at, :] = dv
        return tuple(new)

    carry = (jnp.zeros((dim, bq), F32),) * group
    diag = bq // bk
    whole = q0 // bk + step * diag
    carry = lax.fori_loop(0, whole, lambda j, c: block(j, c, None), carry)
    for d in range(diag):
        carry = block(whole + d, carry, d * bk)
    for h in range(group):
        dq_ref[:, h * dim : (h + 1) * dim] = (carry[h] * scale).T


def attend_back(launch, queries, keys, values, grads, mixed, logs, seg_row, seg_wide, q0, dim, bq, bk, sums, carry=()):
    rows, width = grads.shape
    span = q0 + rows
    kv = keys.shape[1] // dim
    group = width // dim // kv
    pairs = group * kv * rows * (span - rows / 2)
    base = q0 // bq
    whole = pl.BlockSpec((span, dim), lambda k, i: (0, k))
    part = pl.BlockSpec((bq, group * dim), lambda k, i: (i, k))
    more = [] if sums is None else list(sums)
    return launch(
        functools.partial(bwd_kernel, q0, bk, sums is None),
        (queries, keys, values, grads, mixed, logs, seg_row, seg_wide, *more),
        [
            pl.BlockSpec((bq, group * dim), lambda k, i: (i + base, k)),
            whole,
            whole,
            part,
            part,
            pl.BlockSpec((1, group, bq), lambda k, i: (k, 0, i)),
            pl.BlockSpec((1, bq), lambda k, i: (0, i + base)),
            pl.BlockSpec((span, 128), lambda k, i: (0, 0)),
        ]
        + [whole] * len(more),
        [part, whole, whole],
        [shape((rows, width), F32), shape((span, kv * dim), F32), shape((span, kv * dim), F32)],
        (kv, rows // bq),
        "attend_back",
        (pairs * dim * 20, rows * width * 10, pairs),
        scratch=[pltpu.VMEM((span // bk, dim, bk), BF16)],
        carry=carry,
    )


def qkv_kernel(kv, x_ref, gain_ref, w_ref, gq_ref, gk_ref, cos_ref, sin_ref, *refs):
    normed_ref, scale_ref, proj_ref, q_ref, k_ref, v_ref = refs[-6:]
    dim = gq_ref.shape[1]
    heads = q_ref.shape[1] // dim
    values = x_ref[...].astype(F32)
    scale = row_scale(values)
    normed = (values * scale * gain_ref[...]).astype(BF16)
    normed_ref[...] = normed
    scale_ref[...] = scale
    projected = dot_nn(normed, w_ref[...])
    cosine, sine = cos_ref[...], sin_ref[...]
    wide = (heads + kv) * dim
    proj_ref[...] = projected[:, :wide]
    for h in range(heads + kv):
        part = projected[:, h * dim : (h + 1) * dim]
        gain = gq_ref[...] if h < heads else gk_ref[...]
        part = part * row_scale(part) * gain
        turned = (part * cosine + swap(part) * sine).astype(BF16)
        if h < heads:
            q_ref[:, h * dim : (h + 1) * dim] = turned
        else:
            k_ref[:, (h - heads) * dim : (h - heads + 1) * dim] = turned
    v_ref[...] = projected[:, wide:].astype(BF16)


def project_qkv(launch, x, gain, weights, gain_q, gain_k, cosine, sine, kv, carry=()):
    rows, width = x.shape
    cols = weights.shape[1]
    dim = gain_q.shape[1]
    heads = cols // dim - 2 * kv
    bt = tile_of(rows, 512)
    wide = (heads + kv) * dim

    def part(w):
        return pl.BlockSpec((bt, w), lambda i: (i, 0))

    return launch(
        functools.partial(qkv_kernel, kv),
        (x, gain, weights, gain_q, gain_k, cosine, sine),
        [
            part(width),
            resident((1, width)),
            resident((width, cols)),
            resident((1, dim)),
            resident((1, dim)),
            part(dim),
            part(dim),
        ],
        [part(width), part(1), part(wide), part(heads * dim), part(kv * dim), part(kv * dim)],
        [
            shape((rows, width), BF16),
            shape((rows, 1), F32),
            shape((rows, wide), F32),
            shape((rows, heads * dim), BF16),
            shape((rows, kv * dim), BF16),
            shape((rows, kv * dim), BF16),
        ],
        (rows // bt,),
        "project_qkv",
        (2 * rows * width * cols, rows * width * 4 + width * cols * 2, 0),
        carry=carry,
    )


def mlp_kernel(x_ref, gain_ref, wg_ref, wu_ref, wd_ref, cot_ref, *refs):
    normed_ref, scale_ref, active_ref, gg_ref, gu_ref, cot_out = refs[-6:]

    @pl.when(pl.program_id(1) == 0)
    def _():
        cot_out[...] = cot_ref[...]
        values = x_ref[...].astype(F32)
        scale = row_scale(values)
        normed_ref[...] = (values * scale * gain_ref[...]).astype(BF16)
        scale_ref[...] = scale

    normed = normed_ref[...]
    gate = dot_nn(normed, wg_ref[...])
    up = dot_nn(normed, wu_ref[...])
    grad = dot_nt(cot_ref[...], wd_ref[...])
    sig = jax.nn.sigmoid(gate)
    silu = gate * sig
    active_ref[...] = (silu * up).astype(BF16)
    gu_ref[...] = (grad * silu).astype(BF16)
    gg_ref[...] = (grad * up * (sig + silu * (1.0 - sig))).astype(BF16)


def mlp(launch, x, gain, w_gate_up, w_down, cot, chunk, total, kept, carry=()):
    rows, width = x.shape
    hidden = w_down.shape[0]
    bt = tile_of(rows, 1024)
    bn = tile_of(hidden, 512)
    tiles = hidden // bn
    base = chunk * rows // bt
    more = [] if kept is None else list(kept)
    tile = pl.BlockSpec((bt, bn), lambda i, j: (i + base, j))
    low = shape((total, hidden), BF16)
    big = shape((total, width), BF16)
    return launch(
        mlp_kernel,
        (x, gain, w_gate_up, w_gate_up, w_down, cot, *more),
        [
            held((bt, width), lambda i, j: (i, 0)),
            resident((1, width)),
            pl.BlockSpec((width, bn), lambda i, j: (0, j)),
            pl.BlockSpec((width, bn), lambda i, j: (0, j + tiles)),
            pl.BlockSpec((bn, width), lambda i, j: (j, 0)),
            held((bt, width), lambda i, j: (i, 0)),
        ]
        + [ANY] * len(more),
        [
            held((bt, width), lambda i, j: (i + base, 0)),
            pl.BlockSpec((bt, 1), lambda i, j: (i, 0)),
            tile,
            tile,
            tile,
            held((bt, width), lambda i, j: (i + base, 0)),
        ],
        [big, shape((rows, 1), F32), low, low, low, big],
        (rows // bt, tiles),
        "mlp",
        (6 * rows * width * hidden, rows * (width + hidden) * 6 + 6 * width * hidden, rows * hidden),
        alias={6: 0, 7: 2, 8: 3, 9: 4, 10: 5} if more else None,
        carry=carry,
    )


def mid_kernel(gg_ref, gu_ref, w_ref, v_ref, scale_ref, gain_ref, part_ref, inner_ref, gain_out):
    hidden = gg_ref.shape[1]
    partial = dot_nt(gg_ref[...], w_ref[:, :hidden]) + dot_nt(gu_ref[...], w_ref[:, hidden:])
    part_ref[...] = partial.astype(BF16)
    product = partial * v_ref[...].astype(F32)
    gain_out[0] = jnp.sum(product * scale_ref[...], axis=0, keepdims=True)
    inner = row_of(jnp.sum(product * gain_ref[...], axis=1, keepdims=True))

    @pl.when(pl.program_id(1) == 0)
    def _():
        inner_ref[0] = inner

    @pl.when(pl.program_id(1) > 0)
    def _():
        inner_ref[0] += inner


def back_mid(launch, gg, gu, weights, values, scale, gain, chunk, carry=()):
    rows, width = values.shape
    hidden = gg.shape[1]
    bt = tile_of(rows, 1024)
    bn = tile_of(width, 512)
    base = chunk * rows // bt
    return launch(
        mid_kernel,
        (gg, gu, weights, values, scale, gain),
        [
            held((bt, hidden), lambda i, j: (i + base, 0)),
            held((bt, hidden), lambda i, j: (i + base, 0)),
            pl.BlockSpec((bn, 2 * hidden), lambda i, j: (j, 0)),
            pl.BlockSpec((bt, bn), lambda i, j: (i, j)),
            pl.BlockSpec((bt, 1), lambda i, j: (i, 0)),
            pl.BlockSpec((1, bn), lambda i, j: (0, j)),
        ],
        [
            pl.BlockSpec((bt, bn), lambda i, j: (i, j)),
            pl.BlockSpec((1, 1, bt), lambda i, j: (i, 0, 0)),
            pl.BlockSpec((1, 1, bn), lambda i, j: (i, 0, j)),
        ],
        [shape((rows, width), BF16), shape((rows // bt, 1, bt), F32), shape((rows // bt, 1, width), F32)],
        (rows // bt, width // bn),
        "back_mid",
        (4 * rows * width * hidden, rows * (width + hidden) * 4 + 4 * width * hidden, 0),
        carry=carry,
    )


def qkv_back_kernel(
    kv, dq_ref, dk_ref, dv_ref, proj_ref, cos_ref, sin_ref, gq_ref, gk_ref, w_ref, v_ref, scale_ref, gain_ref, *refs
):
    low_ref, part_ref, inner_ref, gain_out, gq_out, gk_out = refs[-6:]
    dim = gq_ref.shape[1]
    heads = dq_ref.shape[1] // dim
    wide = (heads + kv) * dim

    @pl.when(pl.program_id(1) == 0)
    def _():
        cosine, sine = cos_ref[...], sin_ref[...]
        sums = [jnp.zeros((1, dim), F32), jnp.zeros((1, dim), F32)]
        for h in range(heads + kv):
            is_key = h >= heads
            if is_key:
                grad = dk_ref[:, (h - heads) * dim : (h - heads + 1) * dim] * (1.0 / math.sqrt(dim))
            else:
                grad = dq_ref[:, h * dim : (h + 1) * dim]
            grad = grad * cosine + swap(grad * sine)
            value = proj_ref[:, h * dim : (h + 1) * dim]
            scale = row_scale(value)
            sums[is_key] += jnp.sum(grad * value * scale, axis=0, keepdims=True)
            weighted = grad * (gk_ref[...] if is_key else gq_ref[...])
            mean = jnp.mean(weighted * value, axis=-1, keepdims=True)
            low_ref[:, h * dim : (h + 1) * dim] = (scale * (weighted - value * scale * scale * mean)).astype(BF16)
        low_ref[:, wide:] = dv_ref[...].astype(BF16)
        gq_out[0] = sums[0]
        gk_out[0] = sums[1]

    partial = dot_nt(low_ref[...], w_ref[...])
    part_ref[...] = partial.astype(BF16)
    product = partial * v_ref[...].astype(F32)
    gain_out[0] = jnp.sum(product * scale_ref[...], axis=0, keepdims=True)
    inner = row_of(jnp.sum(product * gain_ref[...], axis=1, keepdims=True))

    @pl.when(pl.program_id(1) == 0)
    def _():
        inner_ref[0] = inner

    @pl.when(pl.program_id(1) > 0)
    def _():
        inner_ref[0] += inner


def back_qkv(launch, dq, dk, dv, proj, cosine, sine, gain_q, gain_k, weights, values, scale, gain, kv, chunk, kept, carry=()):
    total, width = values.shape
    rows = dq.shape[0]
    cols = weights.shape[1]
    dim = gain_q.shape[1]
    bt = tile_of(rows, 1024)
    bn = tile_of(width, 512)
    base = chunk * rows // bt

    def here(w):
        return pl.BlockSpec((bt, w), lambda i, j: (i, 0))

    def there(w):
        return pl.BlockSpec((bt, w), lambda i, j: (i + base, 0))

    row = pl.BlockSpec((1, 1, dim), lambda i, j: (i, 0, 0))
    more = [] if kept is None else [kept]
    return launch(
        functools.partial(qkv_back_kernel, kv),
        (dq, dk, dv, proj, cosine, sine, gain_q, gain_k, weights, values, scale, gain, *more),
        [
            here(dq.shape[1]),
            there(dk.shape[1]),
            there(dv.shape[1]),
            there(proj.shape[1]),
            there(dim),
            there(dim),
            resident((1, dim)),
            resident((1, dim)),
            pl.BlockSpec((bn, cols), lambda i, j: (j, 0)),
            pl.BlockSpec((bt, bn), lambda i, j: (i + base, j)),
            there(1),
            pl.BlockSpec((1, bn), lambda i, j: (0, j)),
        ]
        + [ANY] * len(more),
        [
            there(cols),
            pl.BlockSpec((bt, bn), lambda i, j: (i, j)),
            pl.BlockSpec((1, 1, bt), lambda i, j: (i, 0, 0)),
            pl.BlockSpec((1, 1, bn), lambda i, j: (i, 0, j)),
            row,
            row,
        ],
        [
            shape((total, cols), BF16),
            shape((rows, width), BF16),
            shape((rows // bt, 1, bt), F32),
            shape((rows // bt, 1, width), F32),
            shape((rows // bt, 1, dim), F32),
            shape((rows // bt, 1, dim), F32),
        ],
        (rows // bt, width // bn),
        "back_qkv",
        (2 * rows * width * cols, rows * width * 4 + rows * cols * 10, 0),
        alias={12: 0} if more else None,
        carry=carry,
    )


def grad_kernel(left_ref, right_ref, out_ref):
    out_ref[...] = dot_tn(left_ref[...], right_ref[...]).astype(BF16)


def weight_grad(launch, left, right, carry=()):
    rows, width = left.shape
    cols = right.shape[1]
    bm = next(size for size in (1024, 768, 512, 256, 128) if width % size == 0)
    bn = tile_of(cols, 512)
    return launch(
        grad_kernel,
        (left, right),
        [pl.BlockSpec((rows, bm), lambda i, j: (0, i)), pl.BlockSpec((rows, bn), lambda i, j: (0, j))],
        [pl.BlockSpec((bm, bn), lambda i, j: (i, j))],
        [shape((width, cols), BF16)],
        (width // bm, cols // bn),
        "weight_grad",
        (2 * rows * width * cols, rows * (width + cols) * 2 + width * cols * 2, 0),
        carry=carry,
    )[0]


def rope_tables(positions, dim):
    half = dim // 2
    inverse = THETA ** (-(jnp.arange(half, dtype=F32) * 2.0 / dim))
    angle = positions.astype(F32)[:, None] * inverse[None, :]
    cosine, sine = jnp.cos(angle), jnp.sin(angle)
    return jnp.concatenate([cosine, cosine], axis=1), jnp.concatenate([-sine, sine], axis=1)


def after(value, *others):
    return lax.optimization_barrier((value, *jax.tree.leaves(others)))[0]


def body(
    tokens,
    segments,
    positions,
    gain_attn,
    w_query,
    key_weight_matrix,
    value_weight_matrix,
    gain_query,
    gain_key,
    w_out,
    gain_mlp,
    w_gate,
    w_up,
    w_down,
    cotangent,
):
    total, local = tokens.shape
    dim = gain_query.shape[0]
    query_cols, key_cols = w_query.shape[1], key_weight_matrix.shape[1]
    kv = key_cols // dim
    ring = Ring(lax.axis_size("col"))
    launch = Launcher(ring)
    width = local * ring.size
    rows = total // 2
    parts = [slice(0, rows), slice(rows, total)]
    offset = lax.axis_index("col") * local
    gain_attn_local = lax.dynamic_slice_in_dim(gain_attn, offset, local)
    gain_mlp_local = lax.dynamic_slice_in_dim(gain_mlp, offset, local)
    gain_q, gain_k = gain_query[None], gain_key[None]
    bq = tile_of(rows, 512)

    def gathered(weights, axis):
        return lax.all_gather(weights, "row", axis=axis, tiled=True)

    def scattered(partial, axis):
        return lax.psum_scatter(partial, "row", scatter_dimension=axis, tiled=True).astype(F32)

    def carried(first, *stages):
        for stage in stages:
            for _ in range(ring.stages - 2):
                launch.alone(stage)
        return first

    pair = lambda: [None] * 2
    mixed, logs, hidden, mid_low, scale_mid = pair(), pair(), pair(), pair(), pair()
    get_cot, get_mid, get_grad = pair(), pair(), pair()
    sum_out, sum_down, sum_mid, sum_in = pair(), pair(), pair(), pair()
    gain_mlp_part, grad_hidden, gains_in = pair(), pair(), pair()
    output, grad_tokens = pair(), pair()

    w_qkv = gathered(jnp.concatenate([w_query, key_weight_matrix, value_weight_matrix], axis=1), 0)
    w_out_full = gathered(w_out, 1)

    get_tok = Gather(ring, tokens, 0, total)
    launch.alone(get_tok)
    w_gate_up = gathered(jnp.concatenate([after(w_gate, get_tok.full), w_up], axis=1), 0)
    w_down_full = gathered(w_down, 1)
    cosine, sine = rope_tables(positions, dim)
    seg_row = segments[None]
    seg_wide = jnp.broadcast_to(segments[:, None], (total, 128))
    for _ in range(ring.stages - 1):
        launch.alone(get_tok)
    x_full = get_tok.full

    for c in (0, 1):
        get_cot[c] = Gather(ring, cotangent, c * rows, rows)
    normed, scale_attn, proj, queries, keys, values = project_qkv(
        launch, x_full, gain_attn[None], w_qkv, gain_q, gain_k, cosine, sine, kv, carry=[get_cot[1]]
    )

    def attention(c, at, carry):
        mixed[c], logs[c] = attend(
            launch, queries, keys, values, after(seg_row, at), seg_wide, c * rows, rows, dim, bq, bq, carry=carry
        )
        partial = jnp.dot(mixed[c], w_out_full, preferred_element_type=F32).astype(BF16)
        sum_out[c] = Scatter(ring, partial)
        return partial

    def end_out(c):
        hidden[c] = tokens[parts[c]].astype(F32) + sum_out[c].total()
        mid_low[c] = hidden[c].astype(BF16)
        get_mid[c] = Gather(ring, mid_low[c], 0, rows)

    carried(None, get_cot[1])
    at = attention(0, normed, [get_cot[1]])
    attention(1, at, [sum_out[0]])
    carried(None, sum_out[0])
    launch.alone(sum_out[0], sum_out[1])
    end_out(0)
    carried(None, sum_out[1])
    launch.alone(sum_out[1], get_mid[0])
    end_out(1)
    carried(None, get_mid[0])
    launch.alone(get_mid[0], get_mid[1])
    for _ in range(ring.stages - 1):
        launch.alone(get_mid[1])

    def feed_forward(c, kept, at, carry):
        nm, scale_mid[c], *rest = mlp(
            launch, get_mid[c].full, after(gain_mlp[None], at), w_gate_up, w_down_full, get_cot[c].full, c, total, kept,
            carry=carry,
        )
        return (nm, *rest)

    def back_middle(c, kept, at, carry):
        partial, inner, gain_part = back_mid(
            launch, kept[2], kept[3], w_gate_up, get_mid[c].full, scale_mid[c], after(gain_mlp[None], at), c, carry=carry
        )
        gain_mlp_part[c] = jnp.sum(gain_part, axis=(0, 1))
        sum_mid[c] = Scatter(ring, partial, inner)
        return partial

    def end_mid(c):
        scale = scale_mid[c]
        inner = sum_mid[c].inner_sum
        grad_hidden[c] = cotangent[parts[c]].astype(F32) + scale * (
            sum_mid[c].total() * gain_mlp_local - mid_low[c].astype(F32) * (scale * scale * inner / width)
        )
        low = grad_hidden[c].astype(BF16)
        get_grad[c] = Gather(ring, low, 0, rows)
        return low

    def start_down(c, active, at):
        partial = jnp.dot(after(active[parts[c]], at), w_down_full, preferred_element_type=F32).astype(BF16)
        sum_down[c] = Scatter(ring, partial)
        return partial

    def grad_mix(c):
        return lax.dot_general(
            get_grad[c].full, w_out_full, (((1,), (1,)), ((), ())), preferred_element_type=F32
        ).astype(BF16)

    kept = feed_forward(1, None, get_mid[1].full, [get_cot[0]])
    carried(None, get_cot[0])
    at = back_middle(1, kept, None, [get_cot[0]])
    kept = feed_forward(0, kept, at, [sum_mid[1]])
    normed_mid, active, grad_gate, grad_up, cot_all = kept
    carried(None, sum_mid[1])
    partial = weight_grad(launch, active, cot_all, carry=[sum_mid[1]])
    rs_down = scattered(partial, 1)
    low = end_mid(1)
    at = back_middle(0, kept, (partial, low), [get_grad[1]])
    carried(None, get_grad[1])
    partial = weight_grad(launch, after(normed_mid, at), grad_gate, carry=[get_grad[1], sum_mid[0]])
    rs_gate = scattered(partial, 0)
    at = start_down(1, active, partial)

    def attention_back(c, grad_mixed, sums, at, carry):
        return attend_back(
            launch, queries, keys, values, grad_mixed, mixed[c], logs[c], after(seg_row, at), seg_wide, c * rows, dim,
            bq, bq, sums, carry=carry,
        )

    def projection_back(c, grads, low_all, at, carry):
        low_all, partial, inner, *gains_in[c] = back_qkv(
            launch, *grads, proj, cosine, sine, gain_q, gain_k, w_qkv, x_full, scale_attn, after(gain_attn[None], at),
            kv, c, low_all, carry=carry,
        )
        sum_in[c] = Scatter(ring, partial, inner)
        return low_all, partial

    def end_in(c):
        scale = scale_attn[parts[c]]
        inner = sum_in[c].inner_sum
        grad_tokens[c] = grad_hidden[c] + scale * (
            sum_in[c].total() * gain_attn_local - tokens[parts[c]].astype(F32) * (scale * scale * inner / width)
        )
        return grad_tokens[c]

    def end_down(c):
        output[c] = (hidden[c] + sum_down[c].total()).astype(BF16)
        return output[c]

    carried(None, sum_mid[0])
    grads = attention_back(1, grad_mix(1), None, at, [sum_mid[0], sum_down[1]])
    low = end_mid(0)
    low_all, at = projection_back(1, grads, None, low, [get_grad[0]])
    carried(None, get_grad[0], sum_down[1])
    partial = weight_grad(launch, after(normed_mid, at), grad_up, carry=[get_grad[0], sum_down[1]])
    rs_up = scattered(partial, 0)
    at = start_down(0, active, (partial, rs_down))
    grads = attention_back(0, grad_mix(0), grads[1:], at, [sum_in[1]])
    carried(None, sum_in[1])
    low_all, at = projection_back(0, grads, low_all, end_down(1), [sum_in[1], sum_down[0]])
    grad_out = lax.dot_general(
        after(mixed[0], at), get_grad[0].full, (((0,), (0,)), ((), ())), preferred_element_type=F32
    ) + lax.dot_general(mixed[1], get_grad[1].full, (((0,), (0,)), ((), ())), preferred_element_type=F32)
    grad_out = grad_out.astype(BF16)
    rs_out = scattered(grad_out, 1)
    carried(None, sum_down[0])
    partial = weight_grad(launch, after(normed, grad_out, rs_gate), low_all, carry=[sum_in[0], sum_down[0]])
    grad_qkv = scattered(partial, 0)
    at = end_in(1)
    end_down(0)
    for _ in range(ring.stages - 1):
        launch.alone(sum_in[0])
    end_in(0)

    both = [jnp.sum(left, axis=(0, 1)) + jnp.sum(right, axis=(0, 1)) for left, right in zip(*gains_in)]
    gains = jnp.concatenate([both[0], gain_mlp_part[0] + gain_mlp_part[1], both[1], both[2]])[None]
    for axis in ("col", "row"):
        step = 1
        while step < lax.axis_size(axis):
            gains = gains + lax.ppermute(gains, axis, [(i, i ^ step) for i in range(lax.axis_size(axis))])
            step *= 2
    gains = gains[0]
    return (
        jnp.concatenate(output),
        jnp.concatenate(grad_tokens),
        gains[:width],
        grad_qkv[:, :query_cols],
        grad_qkv[:, query_cols : query_cols + key_cols],
        grad_qkv[:, query_cols + key_cols :],
        gains[2 * width : 2 * width + dim],
        gains[2 * width + dim :],
        rs_out,
        gains[width : 2 * width],
        rs_gate,
        rs_up,
        rs_down,
    )


def solution(mesh):
    both, split = P("row", "col"), P("col", "row")
    in_specs = (both, P("row"), P("row"), P(), both, both, both, P(), P(), split, P(), both, both, split, both)
    out_specs = (both, both, P(), both, both, both, P(), P(), split, P(), both, both, split)
    return jax.shard_map(body, mesh=mesh, in_specs=in_specs, out_specs=out_specs, check_vma=False)
```

```python
import functools
import itertools
import math

import jax
import jax.numpy as jnp
from jax import lax
from jax.experimental import pallas as pl
from jax.experimental.pallas import tpu as pltpu
from jax.sharding import PartitionSpec as P

BF16 = jnp.bfloat16
F32 = jnp.float32
EPS = 1e-06
THETA = 1000000.0
LOG2E = 1.4426950408889634
VMEM_LIMIT = 60 * 1024 * 1024
ANY = pl.BlockSpec(memory_space=pl.ANY)


def dot_nt(left, right):
    return lax.dot_general(left, right, (((1,), (1,)), ((), ())), preferred_element_type=F32)


def dot_nn(left, right):
    return jnp.dot(left, right, preferred_element_type=F32)


def dot_tn(left, right):
    return lax.dot_general(left, right, (((0,), (0,)), ((), ())), preferred_element_type=F32)


def shape(dims, dtype):
    return jax.ShapeDtypeStruct(tuple(dims), dtype)


def resident(dims):
    return pl.BlockSpec(dims, lambda *_: (0,) * len(dims), pipeline_mode=pl.Buffered(1))


def held(dims, index):
    return pl.BlockSpec(dims, index, pipeline_mode=pl.Buffered(1))


def tile_of(size, most):
    tile = most
    while size % tile:
        tile //= 2
    return tile


def swap(values):
    half = values.shape[-1] // 2
    return jnp.concatenate([values[:, half:], values[:, :half]], axis=1)


def row_scale(values):
    return lax.rsqrt(jnp.mean(values * values, axis=-1, keepdims=True) + EPS)


def row_of(column):
    return jnp.broadcast_to(column, (column.shape[0], 128)).T[:1]


class Held:
    def __init__(self, dims, row=0):
        self.dims, self.row = dims, row

    def of(self, ref):
        return ref.at[pl.ds(self.row, self.dims[0]), :]


class Ring:
    def __init__(self, size):
        self.size = size
        self.stages = size // 2

    def place(self, index):
        half = self.size // 2
        return jnp.where(index < half, index, self.size + half - 1 - index)

    def owner(self, offset):
        return self.place(lax.rem(self.place(lax.axis_index("col")) + offset + self.size, self.size))

    def cols(self, offset, width):
        return pl.ds(pl.multiple_of(self.owner(offset) * width, 128), width)


class Gather:
    def __init__(self, ring, local, row, rows):
        self.ring, self.local, self.row, self.rows = ring, local, row, rows
        self.width = local.shape[1]
        self.stage, self.full = 0, None
        self.out = [shape((rows, self.width * ring.size), BF16)]
        self.offsets = [-1, 1]

    def prepare(self):
        self.stage += 1
        self.ins = [self.local] if self.stage == 1 else [self.full]
        self.alias = {} if self.stage == 1 else {0: 0}
        self.count = 3 if self.stage == 1 else 2
        self.bounce = [(self.rows, self.width)] if self.stage == 1 else []
        return self

    def copies(self, ins, outs):
        ring, full, width, half = self.ring, outs[0], self.width, self.rows // 2
        if self.stage == 1:
            source = ins[0].at[pl.ds(self.row, self.rows), :]
            mine = full.at[:, ring.cols(0, width)]
            return [(source, mine, 1), (source, mine, -1), (source, mine, None)]
        from_left, from_right = ring.cols(1 - self.stage, width), ring.cols(self.stage - 1, width)
        if self.stage < ring.stages:
            left, right = full.at[:, from_left], full.at[:, from_right]
        else:
            left, right = full.at[pl.ds(0, half), from_left], full.at[pl.ds(half, half), from_right]
        return [(left, left, 1), (right, right, -1)]

    def finish(self, outs):
        self.full = outs[0]


class Scatter:
    def __init__(self, ring, partial, inner=None, split=False):
        self.ring, self.partial, self.inner, self.split = ring, partial, inner, split
        self.far = None
        self.rows, self.half = partial.shape[0], partial.shape[0] // 2
        self.width = partial.shape[1] // ring.size
        self.stage, self.inner_sum, self.bounce = 0, None, []
        self.offsets = [-1, 1]

    def block(self, offset, low):
        start = (self.half if low else 0, self.ring.owner(offset) * self.width)
        return lax.dynamic_slice(self.partial, start, (self.half, self.width)).astype(F32)

    def prepare(self):
        if not (self.split and self.stage == 1 and self.got is None):
            self.stage += 1
        stage, stages = self.stage, self.ring.stages
        whole = stage < stages
        self.alias = {}
        if stage == 1 and self.split:
            self.ins, self.out, self.count = [self.partial], [shape((self.half, self.width), BF16)] * 2, 2
            self.got, self.offsets = None, [-1, 1]
            if self.far is not None and self.inner is not None:
                self.add_inner()
            return self
        if stage == 1:
            self.ins = [self.partial]
        else:
            top = self.block(stages + 1 - stage, False) + self.got[0].astype(F32)
            bottom = self.block(stage - 1 - stages, True) + self.got[1].astype(F32)
            self.ins = [top.astype(BF16), bottom.astype(BF16)]
            if whole:
                low = self.block(stages - stage, True) + self.got[2].astype(F32)
                high = self.block(stage - stages, False) + self.got[3].astype(F32)
                self.ins += [low.astype(BF16), high.astype(BF16)]
            else:
                self.kept = self.got[2:]
        self.out = [shape((self.half, self.width), BF16)] * (4 if whole else 2)
        self.count = len(self.out)
        self.offsets = [-1, 1]
        if stage == 1 and self.inner is not None:
            self.add_inner()
        return self

    def add_inner(self):
        self.ins.append(self.inner)
        self.out.append(shape((self.ring.size - 1, *self.inner.shape), F32))
        self.count += self.ring.size - 1
        self.offsets = list(range(1, self.ring.size))

    def all_copies(self, ins, outs):
        ring, width, half, stages = self.ring, self.width, self.half, self.ring.stages
        if self.stage > 1:
            return [(ref, out, way) for ref, out, way in zip(ins, outs, (1, -1, 1, -1))]
        top, bottom = pl.ds(0, half), pl.ds(half, half)
        far = ring.cols(stages, width)
        made = [
            (ins[0].at[top, far], outs[0], 1),
            (ins[0].at[bottom, far], outs[1], -1),
            (ins[0].at[bottom, ring.cols(stages - 1, width)], outs[2], 1),
            (ins[0].at[top, ring.cols(1 - stages, width)], outs[3], -1),
        ]
        if len(ins) > 1:
            made += [(ins[1], outs[4].at[k - 1], k) for k in range(1, ring.size)]
        return made

    def copies(self, ins, outs):
        if not (self.split and self.stage == 1):
            return self.all_copies(ins, outs)
        if self.far is None:
            return self.all_copies(ins, [*outs, *outs])[:2]
        return self.all_copies(ins, [*outs[:2], *outs])[2:]

    def finish(self, outs):
        if self.split and self.stage == 1:
            if self.far is None:
                self.far = list(outs)
                return
            outs = self.far + list(outs)
        if self.stage == 1 and self.inner is not None:
            self.inner_sum = (jnp.sum(outs[4], axis=0) + self.inner).reshape(self.rows, 1)
            outs = outs[:4]
        self.got = outs

    def pieces(self):
        return self.got[0], self.kept[0], self.kept[1], self.got[1]

    def total(self):
        mine = lax.dynamic_slice_in_dim(self.partial, lax.axis_index("col") * self.width, self.width, 1)
        left = jnp.concatenate([self.got[0], self.kept[0]]).astype(F32)
        right = jnp.concatenate([self.kept[1], self.got[1]]).astype(F32)
        return mine.astype(F32) + left + right


class Share:
    def __init__(self, axis, row):
        self.axis, self.row = axis, row
        self.size = lax.axis_size(axis)
        self.bounce, self.alias = [], {}
        self.offsets = [(axis, k) for k in range(1, self.size)]

    def prepare(self):
        self.ins, self.out = [self.row], [shape((self.size, *self.row.shape), F32)]
        self.count = self.size - 1
        return self

    def copies(self, ins, outs):
        return [(ins[0], outs[0].at[lax.axis_index(self.axis)], offset) for offset in self.offsets]

    def finish(self, outs):
        here = lax.broadcasted_iota(jnp.int32, outs[0].shape, 0) == lax.axis_index(self.axis)
        self.sum = jnp.sum(jnp.where(here, self.row[None], outs[0]), axis=0)


class Launcher:
    def __init__(self, ring):
        self.ring = ring
        self.ids = itertools.count()

    def __call__(self, kernel, args, in_specs, out_specs, out_shape, grid, name, cost, alias=None, scratch=(), carry=()):
        stages = [stage.prepare() for stage in carry]
        own_in, own_out = len(args), len(out_shape)
        held_in = [(i, spec) for i, spec in enumerate(in_specs) if isinstance(spec, Held)]
        held_out = [(i, spec) for i, spec in enumerate(out_specs) if isinstance(spec, Held)]
        held_types = [args[i].dtype for i, _ in held_in] + [out_shape[i].dtype for i, _ in held_out]
        in_specs = [ANY if isinstance(spec, Held) else spec for spec in in_specs]
        out_specs = [ANY if isinstance(spec, Held) else spec for spec in out_specs]
        args, in_specs, out_specs, out_shape = list(args), list(in_specs), list(out_specs), list(out_shape)
        alias, scratch = dict(alias or {}), list(scratch)
        own_scratch = len(scratch)
        scratch += [pltpu.VMEM(spec.dims, kind) for (_, spec), kind in zip(held_in + held_out, held_types)]
        if held_types:
            scratch.append(pltpu.SemaphoreType.DMA((len(held_types),)))
        spans = []
        for stage in stages:
            ins, outs = len(args), len(out_shape)
            alias.update({ins + i: outs + o for i, o in stage.alias.items()})
            args += stage.ins
            out_shape += stage.out
            spans.append((ins, len(args), outs, len(out_shape)))
        in_specs += [ANY] * (len(args) - own_in)
        out_specs += [ANY] * (len(out_shape) - own_out)
        more = {}
        if stages:
            count = sum(stage.count for stage in stages)
            scratch += [pltpu.SemaphoreType.DMA((count,)), pltpu.SemaphoreType.DMA((count,))]
            scratch += [pltpu.VMEM(dims, BF16) for stage in stages for dims in stage.bounce]
            more = dict(collective_id=next(self.ids), has_side_effects=True)
        offsets = {o if isinstance(o, tuple) else ("col", o % self.ring.size) for stage in stages for o in stage.offsets}
        offsets = sorted(offsets)
        ring = self.ring

        def device(way):
            if not isinstance(way, tuple):
                way = ("col", way)
            axis, offset = way
            if axis == "col":
                return {axis: ring.owner(offset)}
            return {axis: lax.rem(lax.axis_index(axis) + offset, lax.axis_size(axis))}

        total_in, total_out = len(args), len(out_shape)

        def body(*refs):
            ins, outs, rest = refs[:total_in], refs[total_in : total_in + total_out], refs[total_in + total_out :]
            own_ins, own_outs = list(ins[:own_in]), list(outs[:own_out])
            own, rest = rest[:own_scratch], rest[own_scratch:]
            inward, outward = [], []
            if held_types:
                buffers, sems, rest = rest[: len(held_types)], rest[len(held_types)], rest[len(held_types) + 1 :]
                for k, (at, spec) in enumerate(held_in):
                    inward.append((spec.of(own_ins[at]), buffers[k], sems.at[k]))
                    own_ins[at] = buffers[k]
                for k, (at, spec) in enumerate(held_out, len(held_in)):
                    outward.append((buffers[k], spec.of(own_outs[at]), sems.at[k]))
                    own_outs[at] = buffers[k]
            own = (*own_ins, *own_outs, *own)
            send, receive, *bounce = rest if stages else (None, None)

            def copies(part):
                made, at, held = [], 0, 0
                for stage, (a, b, c, d) in zip(stages, spans):
                    for source, target, way in stage.copies(ins[a:b], outs[c:d]):
                        if way is None:
                            if part == "in":
                                made.append(pltpu.make_async_copy(source, bounce[held], receive.at[at]))
                            elif part == "out":
                                made.append(pltpu.make_async_copy(bounce[held], target, send.at[at]))
                            held += 1
                        elif part == "remote":
                            made.append(
                                pltpu.make_async_remote_copy(
                                    source, target, send.at[at], receive.at[at], device_id=device(way),
                                    device_id_type=pl.DeviceIdType.MESH,
                                )
                            )
                        at += 1
                return made

            first = last = True
            for axis, size in enumerate(grid):
                first &= pl.program_id(axis) == 0
                last &= pl.program_id(axis) == size - 1
            @pl.when(first)
            def _():
                if stages:
                    barrier = pltpu.get_barrier_semaphore()
                    for offset in offsets:
                        pl.semaphore_signal(
                            barrier, 1, device_id=device(offset), device_id_type=pl.DeviceIdType.MESH
                        )
                for copy in inward:
                    pltpu.make_async_copy(*copy).start()
                if stages:
                    for copy in copies("in"):
                        copy.start()
                    pl.semaphore_wait(barrier, len(offsets))
                    for copy in copies("remote"):
                        copy.start()
                for copy in inward:
                    pltpu.make_async_copy(*copy).wait()

            kernel(*own)

            @pl.when(first)
            def _():
                for copy in outward:
                    pltpu.make_async_copy(*copy).start()
                if stages:
                    for here, there in zip(copies("in"), copies("out")):
                        here.wait()
                        there.start()

            @pl.when(last)
            def _():
                for copy in outward:
                    pltpu.make_async_copy(*copy).wait()
                if stages:
                    for copy in copies("out") + copies("remote"):
                        copy.wait()

        flops, moved, exps = cost
        made = pl.pallas_call(
            body,
            grid=grid,
            in_specs=in_specs,
            out_specs=out_specs,
            out_shape=out_shape,
            input_output_aliases=alias,
            scratch_shapes=scratch,
            compiler_params=pltpu.CompilerParams(vmem_limit_bytes=VMEM_LIMIT, **more),
            cost_estimate=pl.CostEstimate(flops=int(flops), bytes_accessed=int(moved), transcendentals=int(exps)),
            name=name,
        )(*args)
        for stage, (_, _, c, d) in zip(stages, spans):
            stage.finish(made[c:d])
        return made[:own_out]

    def alone(self, *stages):
        self(lambda *_: None, [], [], [], [], (1,), "exchange", (0, 0, 0), carry=stages)


def lane_repeat(column, width):
    return jnp.concatenate([column] * (width // column.shape[1]), axis=1)


def causal(bk, bq, shift):
    key_at = lax.broadcasted_iota(jnp.int32, (bk, bq), 0)
    query_at = lax.broadcasted_iota(jnp.int32, (bk, bq), 1)
    return key_at + shift <= query_at


def fwd_kernel(q0, bk, q_ref, k_ref, v_ref, seg_q_ref, seg_k_ref, out_ref, log_ref, vt):
    bq, wide = q_ref.shape
    dim = k_ref.shape[1]
    group = wide // dim
    step = pl.program_id(1)
    factor = LOG2E / math.sqrt(dim)

    @pl.when(step == 0)
    def _():
        for j in range(vt.shape[0]):
            vt[j] = v_ref[pl.ds(j * bk, bk), :].astype(F32).T.astype(BF16)

    seg_q = seg_q_ref[...]
    queries = [q_ref[:, h * dim : (h + 1) * dim] for h in range(group)]

    def block(j, carry, shift):
        key_rows = k_ref[pl.ds(pl.multiple_of(j * bk, bk), bk), :]
        seg_k = seg_k_ref[pl.ds(pl.multiple_of(j * bk, bk), bk), :]
        allowed = lane_repeat(seg_k, bq) == seg_q
        if shift is not None:
            allowed &= causal(bk, bq, shift)
        value_cols = vt[j]
        new = []
        for h in range(group):
            total, acc = carry[2 * h], carry[2 * h + 1]
            scores = dot_nt(key_rows, queries[h])
            weights = jnp.where(allowed, jnp.exp2(scores * factor), 0.0)
            total = total + jnp.sum(weights.reshape(bk // 8, 8, bq), axis=0)
            acc = acc + dot_nn(value_cols, weights.astype(BF16))
            new += [total, acc]
        return tuple(new)

    carry = (jnp.zeros((8, bq), F32), jnp.zeros((dim, bq), F32)) * group
    diag = bq // bk
    whole = q0 // bk + step * diag
    carry = lax.fori_loop(0, whole, lambda j, c: block(j, c, None), carry)
    for d in range(diag):
        carry = block(whole + d, carry, d * bk)
    for h in range(group):
        total = jnp.sum(carry[2 * h], axis=0, keepdims=True)
        mixed = carry[2 * h + 1] * (1.0 / total)
        out_ref[:, h * dim : (h + 1) * dim] = mixed.T.astype(BF16)
        log_ref[0, h : h + 1, :] = jnp.log2(total)


def attend(launch, queries, keys, values, seg_row, seg_wide, q0, rows, dim, bq, bk, carry=()):
    width = queries.shape[1]
    span = q0 + rows
    kv = keys.shape[1] // dim
    group = width // dim // kv
    pairs = group * kv * rows * (span - rows / 2)
    base = q0 // bq
    whole = pl.BlockSpec((span, dim), lambda k, i: (0, k))
    return launch(
        functools.partial(fwd_kernel, q0, bk),
        (queries, keys, values, seg_row, seg_wide),
        [
            pl.BlockSpec((bq, group * dim), lambda k, i: (i + base, k)),
            whole,
            whole,
            pl.BlockSpec((1, bq), lambda k, i: (0, i + base)),
            pl.BlockSpec((span, 128), lambda k, i: (0, 0)),
        ],
        [
            pl.BlockSpec((bq, group * dim), lambda k, i: (i, k)),
            pl.BlockSpec((1, group, bq), lambda k, i: (k, 0, i)),
        ],
        [shape((rows, width), BF16), shape((kv, group, rows), F32)],
        (kv, rows // bq),
        "attend",
        (pairs * dim * 8, rows * width * 4, pairs),
        scratch=[pltpu.VMEM((span // bk, dim, bk), BF16)],
        carry=carry,
    )


def bwd_kernel(q0, bk, first, *refs):
    q_ref, k_ref, v_ref, g_ref, o_ref, log_ref, seg_q_ref, seg_k_ref = refs[:8]
    dk_in, dv_in = (None, None) if first else refs[8:10]
    dq_ref, dk_ref, dv_ref, kt = refs[-4:]
    bq, wide = q_ref.shape
    dim = k_ref.shape[1]
    group = wide // dim
    step = pl.program_id(1)
    scale = 1.0 / math.sqrt(dim)
    factor = LOG2E * scale

    @pl.when(step == 0)
    def _():
        for j in range(kt.shape[0]):
            kt[j] = k_ref[pl.ds(j * bk, bk), :].astype(F32).T.astype(BF16)
        if first:
            dk_ref[...] = jnp.zeros_like(dk_ref)
            dv_ref[...] = jnp.zeros_like(dv_ref)
        else:
            dk_ref[...] = dk_in[...]
            dv_ref[...] = dv_in[...]

    seg_q = seg_q_ref[...]
    queries = [q_ref[:, h * dim : (h + 1) * dim] for h in range(group)]
    grads = [g_ref[:, h * dim : (h + 1) * dim] for h in range(group)]
    logs = [log_ref[0, h : h + 1, :] for h in range(group)]
    inner = []
    for h in range(group):
        product = grads[h].astype(F32) * o_ref[:, h * dim : (h + 1) * dim].astype(F32)
        inner.append(jnp.sum(product.T, axis=0, keepdims=True))

    def block(j, carry, shift):
        at = pl.ds(pl.multiple_of(j * bk, bk), bk)
        key_rows = k_ref[at, :]
        value_rows = v_ref[at, :]
        allowed = lane_repeat(seg_k_ref[at, :], bq) == seg_q
        if shift is not None:
            allowed &= causal(bk, bq, shift)
        key_cols = kt[j]
        new = []
        dk, dv = dk_ref[at, :], dv_ref[at, :]
        for h in range(group):
            scores = dot_nt(key_rows, queries[h])
            probs = jnp.where(allowed, jnp.exp2(scores * factor - logs[h]), 0.0)
            grad_probs = dot_nt(value_rows, grads[h])
            grad_scores = (probs * (grad_probs - inner[h])).astype(BF16)
            dv = dv + dot_nn(probs.astype(BF16), grads[h])
            dk = dk + dot_nn(grad_scores, queries[h])
            new.append(carry[h] + dot_nn(key_cols, grad_scores))
        dk_ref[at, :] = dk
        dv_ref[at, :] = dv
        return tuple(new)

    carry = (jnp.zeros((dim, bq), F32),) * group
    diag = bq // bk
    whole = q0 // bk + step * diag
    carry = lax.fori_loop(0, whole, lambda j, c: block(j, c, None), carry)
    for d in range(diag):
        carry = block(whole + d, carry, d * bk)
    for h in range(group):
        dq_ref[:, h * dim : (h + 1) * dim] = (carry[h] * scale).T


def attend_back(launch, queries, keys, values, grads, mixed, logs, seg_row, seg_wide, q0, dim, bq, bk, sums, carry=()):
    rows, width = grads.shape
    span = q0 + rows
    kv = keys.shape[1] // dim
    group = width // dim // kv
    pairs = group * kv * rows * (span - rows / 2)
    base = q0 // bq
    whole = pl.BlockSpec((span, dim), lambda k, i: (0, k))
    part = pl.BlockSpec((bq, group * dim), lambda k, i: (i, k))
    more = [] if sums is None else list(sums)
    return launch(
        functools.partial(bwd_kernel, q0, bk, sums is None),
        (queries, keys, values, grads, mixed, logs, seg_row, seg_wide, *more),
        [
            pl.BlockSpec((bq, group * dim), lambda k, i: (i + base, k)),
            whole,
            whole,
            part,
            part,
            pl.BlockSpec((1, group, bq), lambda k, i: (k, 0, i)),
            pl.BlockSpec((1, bq), lambda k, i: (0, i + base)),
            pl.BlockSpec((span, 128), lambda k, i: (0, 0)),
        ]
        + [whole] * len(more),
        [part, whole, whole],
        [shape((rows, width), F32), shape((span, kv * dim), F32), shape((span, kv * dim), F32)],
        (kv, rows // bq),
        "attend_back",
        (pairs * dim * 20, rows * width * 10, pairs),
        scratch=[pltpu.VMEM((span // bk, dim, bk), BF16)],
        carry=carry,
    )


def qkv_kernel(kv, x_ref, gain_ref, w_ref, gq_ref, gk_ref, cos_ref, sin_ref, *refs):
    normed_ref, scale_ref, proj_ref, q_ref, k_ref, v_ref = refs[-6:]
    dim = gq_ref.shape[1]
    heads = q_ref.shape[1] // dim
    values = x_ref[...].astype(F32)
    scale = row_scale(values)
    normed = (values * scale * gain_ref[...]).astype(BF16)
    normed_ref[...] = normed
    scale_ref[...] = scale
    projected = dot_nn(normed, w_ref[...])
    cosine, sine = cos_ref[...], sin_ref[...]
    wide = (heads + kv) * dim
    proj_ref[...] = projected[:, :wide]
    for h in range(heads + kv):
        part = projected[:, h * dim : (h + 1) * dim]
        gain = gq_ref[...] if h < heads else gk_ref[...]
        part = part * row_scale(part) * gain
        turned = (part * cosine + swap(part) * sine).astype(BF16)
        if h < heads:
            q_ref[:, h * dim : (h + 1) * dim] = turned
        else:
            k_ref[:, (h - heads) * dim : (h - heads + 1) * dim] = turned
    v_ref[...] = projected[:, wide:].astype(BF16)


def project_qkv(launch, x, gain, weights, gain_q, gain_k, cosine, sine, kv, carry=()):
    rows, width = x.shape
    cols = weights.shape[1]
    dim = gain_q.shape[1]
    heads = cols // dim - 2 * kv
    bt = tile_of(rows, 512)
    wide = (heads + kv) * dim

    def part(w):
        return pl.BlockSpec((bt, w), lambda i: (i, 0))

    return launch(
        functools.partial(qkv_kernel, kv),
        (x, gain, weights, gain_q, gain_k, cosine, sine),
        [
            part(width),
            resident((1, width)),
            resident((width, cols)),
            resident((1, dim)),
            resident((1, dim)),
            part(dim),
            part(dim),
        ],
        [part(width), part(1), part(wide), part(heads * dim), part(kv * dim), part(kv * dim)],
        [
            shape((rows, width), BF16),
            shape((rows, 1), F32),
            shape((rows, wide), F32),
            shape((rows, heads * dim), BF16),
            shape((rows, kv * dim), BF16),
            shape((rows, kv * dim), BF16),
        ],
        (rows // bt,),
        "project_qkv",
        (2 * rows * width * cols, rows * width * 4 + width * cols * 2, 0),
        carry=carry,
    )


def mlp_kernel(x_ref, gain_ref, wg_ref, wu_ref, wd_ref, cot_ref, *refs):
    normed_ref, scale_ref, active_ref, gg_ref, gu_ref = refs[-5:]

    @pl.when(pl.program_id(1) == 0)
    def _():
        values = x_ref[...].astype(F32)
        scale = row_scale(values)
        normed_ref[...] = (values * scale * gain_ref[...]).astype(BF16)
        scale_ref[...] = scale

    normed = normed_ref[...]
    gate = dot_nn(normed, wg_ref[...])
    up = dot_nn(normed, wu_ref[...])
    grad = dot_nt(cot_ref[...], wd_ref[...])
    sig = jax.nn.sigmoid(gate)
    silu = gate * sig
    active_ref[...] = (silu * up).astype(BF16)
    gu_ref[...] = (grad * silu).astype(BF16)
    gg_ref[...] = (grad * up * (sig + silu * (1.0 - sig))).astype(BF16)


def mlp(launch, x, gain, w_gate_up, w_down, cot, chunk, total, kept, carry=()):
    rows, width = x.shape
    hidden = w_down.shape[0]
    bn = tile_of(hidden, 512)
    tiles = hidden // bn
    more = [] if kept is None else list(kept)
    tile = pl.BlockSpec((rows, bn), lambda i, j: (chunk, j))
    low = shape((total, hidden), BF16)
    return launch(
        mlp_kernel,
        (x, gain, w_gate_up, w_gate_up, w_down, cot, *more),
        [
            Held((rows, width)),
            resident((1, width)),
            pl.BlockSpec((width, bn), lambda i, j: (0, j)),
            pl.BlockSpec((width, bn), lambda i, j: (0, j + tiles)),
            pl.BlockSpec((bn, width), lambda i, j: (j, 0)),
            Held((rows, width)),
        ]
        + [ANY] * len(more),
        [Held((rows, width), chunk * rows), pl.BlockSpec((rows, 1), lambda i, j: (0, 0)), tile, tile, tile],
        [shape((total, width), BF16), shape((rows, 1), F32), low, low, low],
        (1, tiles),
        "mlp",
        (6 * rows * width * hidden, rows * (width + hidden) * 6 + 6 * width * hidden, rows * hidden),
        alias={6: 0, 7: 2, 8: 3, 9: 4} if more else None,
        carry=carry,
    )


def mid_kernel(gg_ref, gu_ref, w_ref, v_ref, scale_ref, gain_ref, part_ref, inner_ref, gain_out):
    hidden = gg_ref.shape[1]
    partial = dot_nt(gg_ref[...], w_ref[:, :hidden]) + dot_nt(gu_ref[...], w_ref[:, hidden:])
    part_ref[...] = partial.astype(BF16)
    product = partial * v_ref[...].astype(F32)
    gain_out[0] = jnp.sum(product * scale_ref[...], axis=0, keepdims=True)
    inner = row_of(jnp.sum(product * gain_ref[...], axis=1, keepdims=True))

    @pl.when(pl.program_id(1) == 0)
    def _():
        inner_ref[0] = inner

    @pl.when(pl.program_id(1) > 0)
    def _():
        inner_ref[0] += inner


def back_mid(launch, gg, gu, weights, values, scale, gain, chunk, carry=()):
    rows, width = values.shape
    hidden = gg.shape[1]
    bn = tile_of(width, 512)
    return launch(
        mid_kernel,
        (gg, gu, weights, values, scale, gain),
        [
            Held((rows, hidden), chunk * rows),
            Held((rows, hidden), chunk * rows),
            pl.BlockSpec((bn, 2 * hidden), lambda i, j: (j, 0)),
            pl.BlockSpec((rows, bn), lambda i, j: (0, j)),
            pl.BlockSpec((rows, 1), lambda i, j: (0, 0)),
            pl.BlockSpec((1, bn), lambda i, j: (0, j)),
        ],
        [
            pl.BlockSpec((rows, bn), lambda i, j: (0, j)),
            pl.BlockSpec((1, 1, rows), lambda i, j: (0, 0, 0)),
            pl.BlockSpec((1, 1, bn), lambda i, j: (0, 0, j)),
        ],
        [shape((rows, width), BF16), shape((1, 1, rows), F32), shape((1, 1, width), F32)],
        (1, width // bn),
        "back_mid",
        (4 * rows * width * hidden, rows * (width + hidden) * 4 + 4 * width * hidden, 0),
        carry=carry,
    )


def qkv_back_kernel(
    kv, dq_ref, dk_ref, dv_ref, proj_ref, cos_ref, sin_ref, gq_ref, gk_ref, w_ref, v_ref, scale_ref, gain_ref, *refs
):
    low_ref, part_ref, inner_ref, gain_out, gq_out, gk_out = refs[-6:]
    dim = gq_ref.shape[1]
    heads = dq_ref.shape[1] // dim
    wide = (heads + kv) * dim

    @pl.when(pl.program_id(1) == 0)
    def _():
        cosine, sine = cos_ref[...], sin_ref[...]
        sums = [jnp.zeros((1, dim), F32), jnp.zeros((1, dim), F32)]
        for h in range(heads + kv):
            is_key = h >= heads
            if is_key:
                grad = dk_ref[:, (h - heads) * dim : (h - heads + 1) * dim] * (1.0 / math.sqrt(dim))
            else:
                grad = dq_ref[:, h * dim : (h + 1) * dim]
            grad = grad * cosine + swap(grad * sine)
            value = proj_ref[:, h * dim : (h + 1) * dim]
            scale = row_scale(value)
            sums[is_key] += jnp.sum(grad * value * scale, axis=0, keepdims=True)
            weighted = grad * (gk_ref[...] if is_key else gq_ref[...])
            mean = jnp.mean(weighted * value, axis=-1, keepdims=True)
            low_ref[:, h * dim : (h + 1) * dim] = (scale * (weighted - value * scale * scale * mean)).astype(BF16)
        low_ref[:, wide:] = dv_ref[...].astype(BF16)
        gq_out[0] = sums[0]
        gk_out[0] = sums[1]

    partial = dot_nt(low_ref[...], w_ref[...])
    part_ref[...] = partial.astype(BF16)
    product = partial * v_ref[...].astype(F32)
    gain_out[0] = jnp.sum(product * scale_ref[...], axis=0, keepdims=True)
    inner = row_of(jnp.sum(product * gain_ref[...], axis=1, keepdims=True))

    @pl.when(pl.program_id(1) == 0)
    def _():
        inner_ref[0] = inner

    @pl.when(pl.program_id(1) > 0)
    def _():
        inner_ref[0] += inner


def back_qkv(launch, dq, dk, dv, proj, cosine, sine, gain_q, gain_k, weights, values, scale, gain, kv, chunk, kept, carry=()):
    total, width = values.shape
    rows = dq.shape[0]
    cols = weights.shape[1]
    dim = gain_q.shape[1]
    bt = rows
    bn = tile_of(width, 512)
    base = chunk

    def here(w):
        return Held((rows, w))

    def there(w):
        return Held((rows, w), chunk * rows)

    row = pl.BlockSpec((1, 1, dim), lambda i, j: (i, 0, 0))
    more = [] if kept is None else [kept]
    return launch(
        functools.partial(qkv_back_kernel, kv),
        (dq, dk, dv, proj, cosine, sine, gain_q, gain_k, weights, values, scale, gain, *more),
        [
            here(dq.shape[1]),
            there(dk.shape[1]),
            there(dv.shape[1]),
            there(proj.shape[1]),
            there(dim),
            there(dim),
            resident((1, dim)),
            resident((1, dim)),
            pl.BlockSpec((bn, cols), lambda i, j: (j, 0)),
            pl.BlockSpec((bt, bn), lambda i, j: (i + base, j)),
            pl.BlockSpec((rows, 1), lambda i, j: (chunk, 0)),
            pl.BlockSpec((1, bn), lambda i, j: (0, j)),
        ]
        + [ANY] * len(more),
        [
            there(cols),
            pl.BlockSpec((bt, bn), lambda i, j: (i, j)),
            pl.BlockSpec((1, 1, bt), lambda i, j: (i, 0, 0)),
            pl.BlockSpec((1, 1, bn), lambda i, j: (i, 0, j)),
            row,
            row,
        ],
        [
            shape((total, cols), BF16),
            shape((rows, width), BF16),
            shape((rows // bt, 1, bt), F32),
            shape((rows // bt, 1, width), F32),
            shape((rows // bt, 1, dim), F32),
            shape((rows // bt, 1, dim), F32),
        ],
        (rows // bt, width // bn),
        "back_qkv",
        (2 * rows * width * cols, rows * width * 4 + rows * cols * 10, 0),
        alias={12: 0} if more else None,
        carry=carry,
    )


def pair_kernel(low_ref, high_ref, first_ref, second_ref, out_ref):
    out_ref[...] = (dot_tn(low_ref[...], first_ref[...]) + dot_tn(high_ref[...], second_ref[...])).astype(BF16)


def weight_grad_pair(launch, lefts, rights, rows_at, carry=()):
    rows, cols = rights[0].shape
    width = lefts[0].shape[1]
    bm = next(size for size in (1024, 768, 512, 256, 128) if width % size == 0)
    bn = tile_of(cols, 512)

    def left(k):
        return pl.BlockSpec((rows, bm), lambda i, j: (rows_at[k], i))

    right = pl.BlockSpec((rows, bn), lambda i, j: (0, j))
    return launch(
        pair_kernel,
        (*lefts, *rights),
        [left(0), left(1), right, right],
        [pl.BlockSpec((bm, bn), lambda i, j: (i, j))],
        [shape((width, cols), BF16)],
        (width // bm, cols // bn),
        "weight_grad",
        (4 * rows * width * cols, rows * (width + cols) * 4 + width * cols * 2, 0),
        carry=carry,
    )[0]


def grad_kernel(tiles, left_ref, *refs):
    rights, out_ref = refs[:-1], refs[-1]
    for k, right in enumerate(rights):
        @pl.when(pl.program_id(1) // tiles == k)
        def _():
            out_ref[...] = dot_tn(left_ref[...], right[...]).astype(BF16)


def weight_grad(launch, left, *rights, carry=()):
    rows, width = left.shape
    cols = rights[0].shape[1]
    bm = next(size for size in (1024, 768, 512, 256, 128) if width % size == 0)
    bn = next(size for size in (512, 384, 256, 128) if cols % size == 0)
    tiles = cols // bn

    def part(k):
        return pl.BlockSpec((rows, bn), lambda i, j: (0, jnp.clip(j - k * tiles, 0, tiles - 1)))

    return launch(
        functools.partial(grad_kernel, tiles),
        (left, *rights),
        [pl.BlockSpec((rows, bm), lambda i, j: (0, i))] + [part(k) for k in range(len(rights))],
        [pl.BlockSpec((bm, bn), lambda i, j: (i, j))],
        [shape((width, cols * len(rights)), BF16)],
        (width // bm, tiles * len(rights)),
        "weight_grad",
        (2 * rows * width * cols * len(rights), rows * (width + cols) * 2 + width * cols * 4, 0),
        carry=carry,
    )[0]


def down_kernel(left_ref, right_ref, out_ref):
    out_ref[...] = dot_nn(left_ref[...], right_ref[...]).astype(BF16)


def project_down(launch, active, weights, chunk, rows, carry=()):
    hidden, width = weights.shape
    bn = tile_of(width, 512)
    return launch(
        down_kernel,
        (active, weights),
        [Held((rows, hidden), chunk * rows), pl.BlockSpec((hidden, bn), lambda i, j: (0, j))],
        [pl.BlockSpec((rows, bn), lambda i, j: (0, j))],
        [shape((rows, width), BF16)],
        (1, width // bn),
        "project_down",
        (2 * rows * width * hidden, rows * (width + hidden) * 2 + width * hidden * 2, 0),
        carry=carry,
    )[0]


def settle_kernel(steps, factor, *refs):
    first = (pl.program_id(0) // (steps // 4)) % 2 == 0
    second_chunk = pl.program_id(0) >= steps // 2
    output, grad_out = refs[-2:]
    tokens, scale, gain = refs[-5:-2]

    def one(hidden, down, d0, d1, d2, d3, grad, term, t0, t1, t2, t3, inner):
        def side(low, high):
            return jnp.where(first, low[...].astype(F32), high[...].astype(F32))

        total = down[...].astype(F32) + side(d0, d1) + side(d2, d3)
        output[...] = (hidden[...] + total).astype(BF16)
        total = term[...].astype(F32) + side(t0, t1) + side(t2, t3)
        scales = scale[...]
        grad_out[...] = grad[...] + scales * (
            total * gain[...] - tokens[...].astype(F32) * (scales * scales * inner[...] * factor)
        )

    count = (len(refs) - 5) // 2
    pl.when(jnp.logical_not(second_chunk))(lambda: one(*refs[:count]))
    pl.when(second_chunk)(lambda: one(*refs[count : 2 * count]))


def settle(launch, hidden, sum_down, grad_hidden, sum_in, tokens, scale, gain):
    rows, local = hidden[0].shape
    total = tokens.shape[0]
    steps = 8
    bt = total // steps
    per = rows // bt
    args, specs = [], []
    for c in (0, 1):
        def at(count, start, wide=local, last=None, c=c):
            def index(i):
                return jnp.clip(i - c * per - start, 0, count - 1), 0 if last is None else last()

            return pl.BlockSpec((bt, wide), index)

        here = at(per, 0)
        mine = at(per, 0, last=lambda: lax.axis_index("col"))
        piece = [at(per // 2, 0), at(per // 2, per // 2)] * 2
        args += [hidden[c], sum_down[c].partial, *sum_down[c].pieces()]
        args += [grad_hidden[c], sum_in[c].partial, *sum_in[c].pieces(), sum_in[c].inner_sum]
        specs += [here, mine, *piece, here, mine, *piece, at(per, 0, 1)]
    whole = pl.BlockSpec((bt, local), lambda i: (i, 0))
    return launch(
        functools.partial(settle_kernel, steps, 1.0 / (local * launch.ring.size)),
        (*args, tokens, scale, gain[None]),
        [*specs, whole, pl.BlockSpec((bt, 1), lambda i: (i, 0)), resident((1, local))],
        [whole, whole],
        [shape((total, local), BF16), shape((total, local), F32)],
        (steps,),
        "settle",
        (0, total * local * 24, 0),
    )


def rope_tables(positions, dim):
    half = dim // 2
    inverse = THETA ** (-(jnp.arange(half, dtype=F32) * 2.0 / dim))
    angle = positions.astype(F32)[:, None] * inverse[None, :]
    cosine, sine = jnp.cos(angle), jnp.sin(angle)
    return jnp.concatenate([cosine, cosine], axis=1), jnp.concatenate([-sine, sine], axis=1)


def after(value, *others):
    return lax.optimization_barrier((value, *jax.tree.leaves(others)))[0]


def body(
    tokens,
    segments,
    positions,
    gain_attn,
    w_query,
    key_weight_matrix,
    value_weight_matrix,
    gain_query,
    gain_key,
    w_out,
    gain_mlp,
    w_gate,
    w_up,
    w_down,
    cotangent,
):
    total, local = tokens.shape
    dim = gain_query.shape[0]
    query_cols, key_cols = w_query.shape[1], key_weight_matrix.shape[1]
    kv = key_cols // dim
    hidden_units = w_gate.shape[1]
    ring = Ring(lax.axis_size("col"))
    launch = Launcher(ring)
    width = local * ring.size
    rows = total // 2
    parts = [slice(0, rows), slice(rows, total)]
    offset = lax.axis_index("col") * local
    gain_attn_local = lax.dynamic_slice_in_dim(gain_attn, offset, local)
    gain_mlp_local = lax.dynamic_slice_in_dim(gain_mlp, offset, local)
    gain_q, gain_k = gain_query[None], gain_key[None]
    bq = tile_of(rows, 512)

    def gathered(weights, axis):
        return lax.all_gather(weights, "row", axis=axis, tiled=True)

    def scattered(partial, axis):
        return lax.psum_scatter(partial, "row", scatter_dimension=axis, tiled=True)

    def carried(*stages):
        for stage in stages:
            for _ in range(ring.stages - 2):
                launch.alone(stage)

    pair = lambda: [None] * 2
    mixed, logs, hidden, mid_low, scale_mid = pair(), pair(), pair(), pair(), pair()
    get_cot, get_mid, get_grad = pair(), pair(), pair()
    sum_out, sum_down, sum_mid, sum_in = pair(), pair(), pair(), pair()
    gain_mlp_part, grad_hidden, gains_in = pair(), pair(), pair()

    w_qkv = gathered(jnp.concatenate([w_query, key_weight_matrix, value_weight_matrix], axis=1), 0)
    w_out_full = gathered(w_out, 1)

    get_tok = Gather(ring, tokens, 0, total)
    launch.alone(get_tok)
    w_gate_up = gathered(jnp.concatenate([after(w_gate, get_tok.full), w_up], axis=1), 0)
    w_down_full = gathered(w_down, 1)
    cosine, sine = rope_tables(positions, dim)
    seg_row = segments[None]
    seg_wide = jnp.broadcast_to(segments[:, None], (total, 128))
    for _ in range(ring.stages - 1):
        launch.alone(get_tok)
    x_full = get_tok.full

    for c in (0, 1):
        get_cot[c] = Gather(ring, cotangent, c * rows, rows)
    normed, scale_attn, proj, queries, keys, values = project_qkv(
        launch, x_full, gain_attn[None], w_qkv, gain_q, gain_k, cosine, sine, kv, carry=[get_cot[1]]
    )

    def attention(c, at, carry):
        mixed[c], logs[c] = attend(
            launch, queries, keys, values, after(seg_row, at), seg_wide, c * rows, rows, dim, bq, bq, carry=carry
        )
        partial = jnp.dot(mixed[c], w_out_full, preferred_element_type=F32).astype(BF16)
        sum_out[c] = Scatter(ring, partial)
        return partial

    def end_out(c):
        hidden[c] = tokens[parts[c]].astype(F32) + sum_out[c].total()
        mid_low[c] = hidden[c].astype(BF16)
        get_mid[c] = Gather(ring, mid_low[c], 0, rows)

    carried(get_cot[1])
    at = attention(1, normed, [get_cot[1]])
    attention(0, at, [sum_out[1]])
    carried(sum_out[1])
    launch.alone(sum_out[1])
    end_out(1)
    launch.alone(get_mid[1])
    carried(get_mid[1])
    launch.alone(get_mid[1], sum_out[0])
    carried(sum_out[0])
    launch.alone(sum_out[0], get_cot[0])
    end_out(0)

    def feed_forward(c, kept, at, carry):
        nm, scale_mid[c], *rest = mlp(
            launch, get_mid[c].full, after(gain_mlp[None], at), w_gate_up, w_down_full, get_cot[c].full, c, total, kept,
            carry=carry,
        )
        return (nm, *rest)

    def back_middle(c, kept, at, carry):
        partial, inner, gain_part = back_mid(
            launch, kept[2], kept[3], w_gate_up, get_mid[c].full, scale_mid[c], after(gain_mlp[None], at), c, carry=carry
        )
        gain_mlp_part[c] = jnp.sum(gain_part, axis=(0, 1))
        sum_mid[c] = Scatter(ring, partial, inner)
        return partial

    def end_mid(c):
        scale = scale_mid[c]
        inner = sum_mid[c].inner_sum
        grad_hidden[c] = cotangent[parts[c]].astype(F32) + scale * (
            sum_mid[c].total() * gain_mlp_local - mid_low[c].astype(F32) * (scale * scale * inner / width)
        )
        low = grad_hidden[c].astype(BF16)
        get_grad[c] = Gather(ring, low, 0, rows)
        return low

    def start_down(c, active, at, carry=()):
        partial = project_down(launch, after(active, at), w_down_full, c, rows, carry=carry)
        sum_down[c] = Scatter(ring, partial, split=True)
        return partial

    def grad_mix(c):
        return lax.dot_general(
            get_grad[c].full, w_out_full, (((1,), (1,)), ((), ())), preferred_element_type=F32
        ).astype(BF16)

    kept = feed_forward(1, None, get_mid[1].full, [get_mid[0]])
    carried(get_mid[0], get_cot[0])
    at = start_down(1, kept[1], kept[0])
    at = back_middle(1, kept, at, [get_mid[0], get_cot[0]])
    kept = feed_forward(0, kept, at, [sum_mid[1], sum_down[1]])
    normed_mid, active, grad_gate, grad_up = kept
    carried(sum_mid[1])
    partial = weight_grad_pair(
        launch, (active, active), (get_cot[0].full, get_cot[1].full), (0, 1), carry=[sum_mid[1], sum_down[1]]
    )
    rs_down = scattered(partial, 1)
    low = end_mid(1)
    at = back_middle(0, kept, (partial, low), [get_grad[1]])
    carried(get_grad[1])
    partial = weight_grad(launch, after(normed_mid, at), grad_gate, grad_up, carry=[get_grad[1], sum_mid[0]])
    rs_gate_up = scattered(partial, 0)
    carried(sum_mid[0])
    at = start_down(0, active, partial, [sum_mid[0]])
    low = end_mid(0)

    def attention_back(c, grad_mixed, sums, at, carry):
        return attend_back(
            launch, queries, keys, values, grad_mixed, mixed[c], logs[c], after(seg_row, at), seg_wide, c * rows, dim,
            bq, bq, sums, carry=carry,
        )

    def projection_back(c, grads, low_all, at, carry):
        low_all, partial, inner, *gains_in[c] = back_qkv(
            launch, *grads, proj, cosine, sine, gain_q, gain_k, w_qkv, x_full, scale_attn, after(gain_attn[None], at),
            kv, c, low_all, carry=carry,
        )
        sum_in[c] = Scatter(ring, partial, inner, split=c == 0)
        return low_all, partial

    grads = attention_back(1, grad_mix(1), None, (at, low), [get_grad[0], sum_down[0]])
    carried(get_grad[0], sum_down[1])
    low_all, at = projection_back(1, grads, None, None, [get_grad[0], sum_down[1]])
    grads = attention_back(0, grad_mix(0), grads[1:], (at, rs_down), [sum_in[1], sum_down[0]])
    grad_out = weight_grad_pair(
        launch, (after(mixed[0], grads[0]), mixed[1]), (get_grad[0].full, get_grad[1].full), (0, 0)
    )
    rs_out = scattered(grad_out, 1)
    carried(sum_in[1], sum_down[0])
    low_all, at = projection_back(0, grads, low_all, grad_out, [sum_in[1], sum_down[0]])
    partial = weight_grad(launch, after(normed, at, rs_gate_up), low_all, carry=[sum_in[0]])
    grad_qkv = scattered(after(partial, rs_out), 0)

    sums = [jnp.sum(left, axis=(0, 1)) + jnp.sum(right, axis=(0, 1)) for left, right in zip(*gains_in)]
    gains = Share("col", jnp.concatenate([sums[0], gain_mlp_part[0] + gain_mlp_part[1], sums[1], sums[2]])[None])
    launch.alone(sum_in[0], gains)
    gains = Share("row", gains.sum)
    carried(sum_in[0])
    launch.alone(sum_in[0], gains)
    gains = gains.sum[0]
    output, grad_tokens = settle(
        launch, hidden, sum_down, grad_hidden, sum_in, tokens, scale_attn, gain_attn_local
    )
    return (
        output,
        grad_tokens,
        gains[:width],
        grad_qkv[:, :query_cols].astype(F32),
        grad_qkv[:, query_cols : query_cols + key_cols].astype(F32),
        grad_qkv[:, query_cols + key_cols :].astype(F32),
        gains[2 * width : 2 * width + dim],
        gains[2 * width + dim :],
        rs_out.astype(F32),
        gains[width : 2 * width],
        rs_gate_up[:, :hidden_units].astype(F32),
        rs_gate_up[:, hidden_units:].astype(F32),
        rs_down.astype(F32),
    )


def solution(mesh):
    both, split = P("row", "col"), P("col", "row")
    in_specs = (both, P("row"), P("row"), P(), both, both, both, P(), P(), split, P(), both, both, split, both)
    out_specs = (both, both, P(), both, both, both, P(), P(), split, P(), both, both, split)
    return jax.shard_map(body, mesh=mesh, in_specs=in_specs, out_specs=out_specs, check_vma=False)
```

```python
import functools
import itertools
import math

import jax
import jax.numpy as jnp
from jax import lax
from jax.experimental import pallas as pl
from jax.experimental.pallas import tpu as pltpu
from jax.sharding import PartitionSpec as P

BF16 = jnp.bfloat16
F32 = jnp.float32
EPS = 1e-06
THETA = 1000000.0
LOG2E = 1.4426950408889634
VMEM_LIMIT = 60 * 1024 * 1024
ANY = pl.BlockSpec(memory_space=pl.ANY)


def dot_nt(left, right):
    return lax.dot_general(left, right, (((1,), (1,)), ((), ())), preferred_element_type=F32)


def dot_nn(left, right):
    return jnp.dot(left, right, preferred_element_type=F32)


def dot_tn(left, right):
    return lax.dot_general(left, right, (((0,), (0,)), ((), ())), preferred_element_type=F32)


def shape(dims, dtype):
    return jax.ShapeDtypeStruct(tuple(dims), dtype)


def resident(dims):
    return pl.BlockSpec(dims, lambda *_: (0,) * len(dims), pipeline_mode=pl.Buffered(1))


def held(dims, index):
    return pl.BlockSpec(dims, index, pipeline_mode=pl.Buffered(1))


def tile_of(size, most):
    tile = most
    while size % tile:
        tile //= 2
    return tile


def swap(values):
    half = values.shape[-1] // 2
    return jnp.concatenate([values[:, half:], values[:, :half]], axis=1)


def row_scale(values):
    return lax.rsqrt(jnp.mean(values * values, axis=-1, keepdims=True) + EPS)


def row_of(column):
    return jnp.broadcast_to(column, (column.shape[0], 128)).T[:1]


class Held:
    def __init__(self, dims, row=0, col=0):
        self.dims, self.row, self.col = dims, row, col

    def of(self, ref):
        return ref.at[pl.ds(self.row, self.dims[0]), pl.ds(self.col, self.dims[1])]


class Ring:
    def __init__(self, size):
        self.size = size
        self.stages = size // 2

    def place(self, index):
        half = self.size // 2
        return jnp.where(index < half, index, self.size + half - 1 - index)

    def owner(self, offset):
        return self.place(lax.rem(self.place(lax.axis_index("col")) + offset + self.size, self.size))

    def cols(self, offset, width):
        return pl.ds(pl.multiple_of(self.owner(offset) * width, 128), width)


class Gather:
    def __init__(self, ring, local, row, rows, split=False):
        self.ring, self.local, self.row, self.rows = ring, local, row, rows
        self.width = local.shape[1]
        self.stage, self.full, self.part = 0, None, 2 if split else 0
        self.out = [shape((rows, self.width * ring.size), BF16)]
        self.offsets = [-1, 1]

    def prepare(self):
        if self.stage == 0 or self.part == 0:
            self.stage += 1
        self.ins = [self.full] if self.full is not None else []
        self.alias = {0: 0} if self.ins else {}
        self.count, self.bounce, self.span = 2, [], None
        if self.stage == 1:
            start, size = self.row, self.rows
            if self.part:
                size //= 2
                start += (2 - self.part) * size
                self.part -= 1
            self.span = start, size
            self.ins = self.ins + [self.local]
            self.count, self.bounce = 3, [(size, self.width)]
        return self

    def copies(self, ins, outs):
        ring, full, width, half = self.ring, outs[0], self.width, self.rows // 2
        if self.stage == 1:
            start, size = self.span
            source = ins[-1].at[pl.ds(start, size), :]
            mine = full.at[pl.ds(start - self.row, size), ring.cols(0, width)]
            return [(source, mine, 1), (source, mine, -1), (source, mine, None)]
        from_left, from_right = ring.cols(1 - self.stage, width), ring.cols(self.stage - 1, width)
        if self.stage < ring.stages:
            left, right = full.at[:, from_left], full.at[:, from_right]
        else:
            left, right = full.at[pl.ds(0, half), from_left], full.at[pl.ds(half, half), from_right]
        return [(left, left, 1), (right, right, -1)]

    def finish(self, outs):
        self.full = outs[0]


class Scatter:
    def __init__(self, ring, partial, inner=None, split=False):
        self.ring, self.partial, self.inner = ring, partial, inner
        self.split = split and ring.stages == 2
        self.rows, self.half = partial.shape[0], partial.shape[0] // 2
        self.width = partial.shape[1] // ring.size
        self.stage, self.inner_others, self.bounce, self.alias = 0, None, [], {}
        self.near = Near(self)

    def block(self, offset, low):
        start = (self.half if low else 0, self.ring.owner(offset) * self.width)
        return lax.dynamic_slice(self.partial, start, (self.half, self.width)).astype(F32)

    def prepare(self):
        self.stage += 1
        stage, stages = self.stage, self.ring.stages
        whole = stage < stages
        self.offsets = [-1, 1]
        if stage == 1:
            self.ins = [self.partial]
        else:
            top = self.block(stages + 1 - stage, False) + self.got[0].astype(F32)
            bottom = self.block(stage - 1 - stages, True) + self.got[1].astype(F32)
            self.ins = [top.astype(BF16), bottom.astype(BF16)]
            if whole:
                low = self.block(stages - stage, True) + self.got[2].astype(F32)
                high = self.block(stage - stages, False) + self.got[3].astype(F32)
                self.ins += [low.astype(BF16), high.astype(BF16)]
            elif not self.split:
                self.kept = self.got[2:]
        self.out = [shape((self.half, self.width), BF16)] * (4 if whole and not self.split else 2)
        self.count = len(self.out)
        if stage == 1 and not self.split:
            self.near.add_inner(self)
        return self

    def far_copies(self, ins, outs):
        top, bottom = pl.ds(0, self.half), pl.ds(self.half, self.half)
        far = self.ring.cols(self.ring.stages, self.width)
        return [(ins[0].at[top, far], outs[0], 1), (ins[0].at[bottom, far], outs[1], -1)]

    def copies(self, ins, outs):
        if self.stage > 1:
            return [(ref, out, way) for ref, out, way in zip(ins, outs, (1, -1, 1, -1))]
        made = self.far_copies(ins, outs)
        if not self.split:
            made += self.near.near_copies(ins, outs[2:])
        return made

    def finish(self, outs):
        if self.stage == 1 and not self.split:
            outs = [*outs[:2], *self.near.take(outs[2:])]
        self.got = outs

    def pieces(self):
        return self.got[0], self.kept[0], self.kept[1], self.got[1]

    def total(self):
        mine = lax.dynamic_slice_in_dim(self.partial, lax.axis_index("col") * self.width, self.width, 1)
        left = jnp.concatenate([self.got[0], self.kept[0]]).astype(F32)
        right = jnp.concatenate([self.kept[1], self.got[1]]).astype(F32)
        return mine.astype(F32) + left + right


class Near:
    def __init__(self, whole):
        self.whole = whole
        self.bounce, self.alias = [], {}

    @property
    def empty(self):
        return not self.whole.split

    def add_inner(self, stage):
        whole = self.whole
        if whole.inner is not None:
            others = whole.ring.size - 1
            stage.ins = stage.ins + [whole.inner]
            stage.out = stage.out + [shape((others, *whole.inner.shape), F32)]
            stage.count += others
            stage.offsets = list(range(1, whole.ring.size))

    def prepare(self):
        whole = self.whole
        self.ins, self.offsets, self.count = [whole.partial], [-1, 1], 2
        self.out = [shape((whole.half, whole.width), BF16)] * 2
        self.add_inner(self)
        return self

    def near_copies(self, ins, outs):
        whole, ring = self.whole, self.whole.ring
        top, bottom = pl.ds(0, whole.half), pl.ds(whole.half, whole.half)
        made = [
            (ins[0].at[bottom, ring.cols(ring.stages - 1, whole.width)], outs[0], 1),
            (ins[0].at[top, ring.cols(1 - ring.stages, whole.width)], outs[1], -1),
        ]
        if whole.inner is not None:
            made += [(ins[1], outs[2].at[k - 1], k) for k in range(1, ring.size)]
        return made

    def copies(self, ins, outs):
        return self.near_copies(ins, outs)

    def take(self, outs):
        whole = self.whole
        if whole.inner is not None:
            whole.inner_others = outs[2]
        return outs[:2]

    def finish(self, outs):
        self.whole.kept = self.take(outs)


class Share:
    def __init__(self, axis, *arrays):
        self.axis, self.arrays = axis, arrays
        self.size = lax.axis_size(axis)
        self.bounce, self.alias = [], {}
        self.offsets = [(axis, k) for k in range(1, self.size)]

    def prepare(self):
        self.ins, self.out = list(self.arrays), [shape((self.size, *a.shape), F32) for a in self.arrays]
        self.count = (self.size - 1) * len(self.arrays)
        return self

    def copies(self, ins, outs):
        here = lax.axis_index(self.axis)
        return [(a, out.at[here], offset) for a, out in zip(ins, outs) for offset in self.offsets]

    def finish(self, outs):
        self.sums = []
        for mine, out in zip(self.arrays, outs):
            here = lax.broadcasted_iota(jnp.int32, out.shape, 0) == lax.axis_index(self.axis)
            self.sums.append(jnp.sum(jnp.where(here, mine[None], out), axis=0))


class Launcher:
    def __init__(self, ring):
        self.ring = ring
        self.ids = itertools.count()

    def __call__(self, kernel, args, in_specs, out_specs, out_shape, grid, name, cost, alias=None, scratch=(), carry=()):
        stages = [stage.prepare() for stage in carry if not getattr(stage, "empty", False)]
        own_in, own_out = len(args), len(out_shape)
        held_in = [(i, spec) for i, spec in enumerate(in_specs) if isinstance(spec, Held)]
        held_out = [(i, spec) for i, spec in enumerate(out_specs) if isinstance(spec, Held)]
        held_types = [args[i].dtype for i, _ in held_in] + [out_shape[i].dtype for i, _ in held_out]
        in_specs = [ANY if isinstance(spec, Held) else spec for spec in in_specs]
        out_specs = [ANY if isinstance(spec, Held) else spec for spec in out_specs]
        args, in_specs, out_specs, out_shape = list(args), list(in_specs), list(out_specs), list(out_shape)
        alias, scratch = dict(alias or {}), list(scratch)
        own_scratch = len(scratch)
        scratch += [pltpu.VMEM(spec.dims, kind) for (_, spec), kind in zip(held_in + held_out, held_types)]
        if held_types:
            scratch.append(pltpu.SemaphoreType.DMA((len(held_types),)))
        spans = []
        for stage in stages:
            ins, outs = len(args), len(out_shape)
            alias.update({ins + i: outs + o for i, o in stage.alias.items()})
            args += stage.ins
            out_shape += stage.out
            spans.append((ins, len(args), outs, len(out_shape)))
        in_specs += [ANY] * (len(args) - own_in)
        out_specs += [ANY] * (len(out_shape) - own_out)
        more = {}
        if stages:
            count = sum(stage.count for stage in stages)
            scratch += [pltpu.SemaphoreType.DMA((count,)), pltpu.SemaphoreType.DMA((count,))]
            scratch += [pltpu.VMEM(dims, BF16) for stage in stages for dims in stage.bounce]
            more = dict(collective_id=next(self.ids), has_side_effects=True)
        offsets = {o if isinstance(o, tuple) else ("col", o % self.ring.size) for stage in stages for o in stage.offsets}
        offsets = sorted(offsets)
        ring = self.ring

        def device(way):
            if not isinstance(way, tuple):
                way = ("col", way)
            axis, offset = way
            if axis == "col":
                return {axis: ring.owner(offset)}
            return {axis: lax.rem(lax.axis_index(axis) + offset, lax.axis_size(axis))}

        total_in, total_out = len(args), len(out_shape)

        def body(*refs):
            ins, outs, rest = refs[:total_in], refs[total_in : total_in + total_out], refs[total_in + total_out :]
            own_ins, own_outs = list(ins[:own_in]), list(outs[:own_out])
            own, rest = rest[:own_scratch], rest[own_scratch:]
            inward, outward = [], []
            if held_types:
                buffers, sems, rest = rest[: len(held_types)], rest[len(held_types)], rest[len(held_types) + 1 :]
                for k, (at, spec) in enumerate(held_in):
                    inward.append((spec.of(own_ins[at]), buffers[k], sems.at[k]))
                    own_ins[at] = buffers[k]
                for k, (at, spec) in enumerate(held_out, len(held_in)):
                    outward.append((buffers[k], spec.of(own_outs[at]), sems.at[k]))
                    own_outs[at] = buffers[k]
            own = (*own_ins, *own_outs, *own)
            send, receive, *bounce = rest if stages else (None, None)

            def copies(part):
                made, at, held = [], 0, 0
                for stage, (a, b, c, d) in zip(stages, spans):
                    for source, target, way in stage.copies(ins[a:b], outs[c:d]):
                        if way is None:
                            if part == "in":
                                made.append(pltpu.make_async_copy(source, bounce[held], receive.at[at]))
                            elif part == "out":
                                made.append(pltpu.make_async_copy(bounce[held], target, send.at[at]))
                            held += 1
                        elif part == "remote":
                            made.append(
                                pltpu.make_async_remote_copy(
                                    source, target, send.at[at], receive.at[at], device_id=device(way),
                                    device_id_type=pl.DeviceIdType.MESH,
                                )
                            )
                        at += 1
                return made

            first = last = True
            for axis, size in enumerate(grid):
                first &= pl.program_id(axis) == 0
                last &= pl.program_id(axis) == size - 1
            @pl.when(first)
            def _():
                if stages:
                    barrier = pltpu.get_barrier_semaphore()
                    for offset in offsets:
                        pl.semaphore_signal(
                            barrier, 1, device_id=device(offset), device_id_type=pl.DeviceIdType.MESH
                        )
                for copy in inward:
                    pltpu.make_async_copy(*copy).start()
                if stages:
                    for copy in copies("in"):
                        copy.start()
                    pl.semaphore_wait(barrier, len(offsets))
                    for copy in copies("remote"):
                        copy.start()
                for copy in inward:
                    pltpu.make_async_copy(*copy).wait()

            kernel(*own)

            @pl.when(first)
            def _():
                for copy in outward:
                    pltpu.make_async_copy(*copy).start()
                if stages:
                    for here, there in zip(copies("in"), copies("out")):
                        here.wait()
                        there.start()

            @pl.when(last)
            def _():
                for copy in outward:
                    pltpu.make_async_copy(*copy).wait()
                if stages:
                    for copy in copies("out") + copies("remote"):
                        copy.wait()

        flops, moved, exps = cost
        made = pl.pallas_call(
            body,
            grid=grid,
            in_specs=in_specs,
            out_specs=out_specs,
            out_shape=out_shape,
            input_output_aliases=alias,
            scratch_shapes=scratch,
            compiler_params=pltpu.CompilerParams(vmem_limit_bytes=VMEM_LIMIT, **more),
            cost_estimate=pl.CostEstimate(flops=int(flops), bytes_accessed=int(moved), transcendentals=int(exps)),
            name=name,
        )(*args)
        for stage, (_, _, c, d) in zip(stages, spans):
            stage.finish(made[c:d])
        return made[:own_out]

    def alone(self, *stages):
        self(lambda *_: None, [], [], [], [], (1,), "exchange", (0, 0, 0), carry=stages)


def lane_repeat(column, width):
    return jnp.concatenate([column] * (width // column.shape[1]), axis=1)


def causal(bk, bq, shift):
    key_at = lax.broadcasted_iota(jnp.int32, (bk, bq), 0)
    query_at = lax.broadcasted_iota(jnp.int32, (bk, bq), 1)
    return key_at + shift <= query_at


def fwd_kernel(q0, bk, q_ref, k_ref, v_ref, seg_q_ref, seg_k_ref, out_ref, log_ref, vt):
    bq, wide = q_ref.shape
    dim = k_ref.shape[1]
    group = wide // dim
    step = pl.program_id(1)
    factor = LOG2E / math.sqrt(dim)

    @pl.when(step == 0)
    def _():
        for j in range(vt.shape[0]):
            vt[j] = v_ref[pl.ds(j * bk, bk), :].astype(F32).T.astype(BF16)

    seg_q = seg_q_ref[...]
    queries = [q_ref[:, h * dim : (h + 1) * dim] for h in range(group)]

    def block(j, carry, shift):
        key_rows = k_ref[pl.ds(pl.multiple_of(j * bk, bk), bk), :]
        seg_k = seg_k_ref[pl.ds(pl.multiple_of(j * bk, bk), bk), :]
        allowed = lane_repeat(seg_k, bq) == seg_q
        if shift is not None:
            allowed &= causal(bk, bq, shift)
        value_cols = vt[j]
        new = []
        for h in range(group):
            total, acc = carry[2 * h], carry[2 * h + 1]
            scores = dot_nt(key_rows, queries[h])
            weights = jnp.where(allowed, jnp.exp2(scores * factor), 0.0)
            total = total + jnp.sum(weights.reshape(bk // 8, 8, bq), axis=0)
            acc = acc + dot_nn(value_cols, weights.astype(BF16))
            new += [total, acc]
        return tuple(new)

    carry = (jnp.zeros((8, bq), F32), jnp.zeros((dim, bq), F32)) * group
    diag = bq // bk
    whole = q0 // bk + step * diag
    carry = lax.fori_loop(0, whole, lambda j, c: block(j, c, None), carry)
    for d in range(diag):
        carry = block(whole + d, carry, d * bk)
    for h in range(group):
        total = jnp.sum(carry[2 * h], axis=0, keepdims=True)
        mixed = carry[2 * h + 1] * (1.0 / total)
        out_ref[:, h * dim : (h + 1) * dim] = mixed.T.astype(BF16)
        log_ref[0, h : h + 1, :] = jnp.log2(total)


def attend(launch, queries, keys, values, seg_row, seg_wide, q0, rows, dim, bq, bk, carry=()):
    width = queries.shape[1]
    span = q0 + rows
    kv = keys.shape[1] // dim
    group = width // dim // kv
    pairs = group * kv * rows * (span - rows / 2)
    base = q0 // bq
    whole = pl.BlockSpec((span, dim), lambda k, i: (0, k))
    return launch(
        functools.partial(fwd_kernel, q0, bk),
        (queries, keys, values, seg_row, seg_wide),
        [
            pl.BlockSpec((bq, group * dim), lambda k, i: (i + base, k)),
            whole,
            whole,
            pl.BlockSpec((1, bq), lambda k, i: (0, i + base)),
            pl.BlockSpec((span, 128), lambda k, i: (0, 0)),
        ],
        [
            pl.BlockSpec((bq, group * dim), lambda k, i: (i, k)),
            pl.BlockSpec((1, group, bq), lambda k, i: (k, 0, i)),
        ],
        [shape((rows, width), BF16), shape((kv, group, rows), F32)],
        (kv, rows // bq),
        "attend",
        (pairs * dim * 8, rows * width * 4, pairs),
        scratch=[pltpu.VMEM((span // bk, dim, bk), BF16)],
        carry=carry,
    )


def bwd_kernel(q0, bk, first, *refs):
    q_ref, k_ref, v_ref, g_ref, o_ref, log_ref, seg_q_ref, seg_k_ref = refs[:8]
    dk_in, dv_in = (None, None) if first else refs[8:10]
    dq_ref, dk_ref, dv_ref, kt = refs[-4:]
    bq, wide = q_ref.shape
    dim = k_ref.shape[1]
    group = wide // dim
    step = pl.program_id(1)
    scale = 1.0 / math.sqrt(dim)
    factor = LOG2E * scale

    @pl.when(step == 0)
    def _():
        for j in range(kt.shape[0]):
            kt[j] = k_ref[pl.ds(j * bk, bk), :].astype(F32).T.astype(BF16)
        if first:
            dk_ref[...] = jnp.zeros_like(dk_ref)
            dv_ref[...] = jnp.zeros_like(dv_ref)
        else:
            dk_ref[...] = dk_in[...]
            dv_ref[...] = dv_in[...]

    seg_q = seg_q_ref[...]
    queries = [q_ref[:, h * dim : (h + 1) * dim] for h in range(group)]
    grads = [g_ref[:, h * dim : (h + 1) * dim] for h in range(group)]
    logs = [log_ref[0, h : h + 1, :] for h in range(group)]
    inner = []
    for h in range(group):
        product = grads[h].astype(F32) * o_ref[:, h * dim : (h + 1) * dim].astype(F32)
        inner.append(jnp.sum(product.T, axis=0, keepdims=True))

    def block(j, carry, shift):
        at = pl.ds(pl.multiple_of(j * bk, bk), bk)
        key_rows = k_ref[at, :]
        value_rows = v_ref[at, :]
        allowed = lane_repeat(seg_k_ref[at, :], bq) == seg_q
        if shift is not None:
            allowed &= causal(bk, bq, shift)
        key_cols = kt[j]
        new = []
        dk, dv = dk_ref[at, :], dv_ref[at, :]
        for h in range(group):
            scores = dot_nt(key_rows, queries[h])
            probs = jnp.where(allowed, jnp.exp2(scores * factor - logs[h]), 0.0)
            grad_probs = dot_nt(value_rows, grads[h])
            grad_scores = (probs * (grad_probs - inner[h])).astype(BF16)
            dv = dv + dot_nn(probs.astype(BF16), grads[h])
            dk = dk + dot_nn(grad_scores, queries[h])
            new.append(carry[h] + dot_nn(key_cols, grad_scores))
        dk_ref[at, :] = dk
        dv_ref[at, :] = dv
        return tuple(new)

    carry = (jnp.zeros((dim, bq), F32),) * group
    diag = bq // bk
    whole = q0 // bk + step * diag
    carry = lax.fori_loop(0, whole, lambda j, c: block(j, c, None), carry)
    for d in range(diag):
        carry = block(whole + d, carry, d * bk)
    for h in range(group):
        dq_ref[:, h * dim : (h + 1) * dim] = (carry[h] * scale).T


def attend_back(launch, queries, keys, values, grads, mixed, logs, seg_row, seg_wide, q0, dim, bq, bk, sums, carry=()):
    rows, width = grads.shape
    span = q0 + rows
    kv = keys.shape[1] // dim
    group = width // dim // kv
    pairs = group * kv * rows * (span - rows / 2)
    base = q0 // bq
    whole = pl.BlockSpec((span, dim), lambda k, i: (0, k))
    part = pl.BlockSpec((bq, group * dim), lambda k, i: (i, k))
    more = [] if sums is None else list(sums)
    return launch(
        functools.partial(bwd_kernel, q0, bk, sums is None),
        (queries, keys, values, grads, mixed, logs, seg_row, seg_wide, *more),
        [
            pl.BlockSpec((bq, group * dim), lambda k, i: (i + base, k)),
            whole,
            whole,
            part,
            part,
            pl.BlockSpec((1, group, bq), lambda k, i: (k, 0, i)),
            pl.BlockSpec((1, bq), lambda k, i: (0, i + base)),
            pl.BlockSpec((span, 128), lambda k, i: (0, 0)),
        ]
        + [whole] * len(more),
        [part, whole, whole],
        [shape((rows, width), F32), shape((span, kv * dim), F32), shape((span, kv * dim), F32)],
        (kv, rows // bq),
        "attend_back",
        (pairs * dim * 20, rows * width * 10, pairs),
        scratch=[pltpu.VMEM((span // bk, dim, bk), BF16)],
        carry=carry,
    )


def qkv_kernel(kv, x_ref, gain_ref, w_ref, gq_ref, gk_ref, cos_ref, sin_ref, *refs):
    normed_ref, scale_ref, proj_ref, q_ref, k_ref, v_ref = refs[-6:]
    dim = gq_ref.shape[1]
    heads = q_ref.shape[1] // dim
    values = x_ref[...].astype(F32)
    scale = row_scale(values)
    normed = (values * scale * gain_ref[...]).astype(BF16)
    normed_ref[...] = normed
    scale_ref[...] = scale
    projected = dot_nn(normed, w_ref[...])
    cosine, sine = cos_ref[...], sin_ref[...]
    wide = (heads + kv) * dim
    proj_ref[...] = projected[:, :wide]
    for h in range(heads + kv):
        part = projected[:, h * dim : (h + 1) * dim]
        gain = gq_ref[...] if h < heads else gk_ref[...]
        part = part * row_scale(part) * gain
        turned = (part * cosine + swap(part) * sine).astype(BF16)
        if h < heads:
            q_ref[:, h * dim : (h + 1) * dim] = turned
        else:
            k_ref[:, (h - heads) * dim : (h - heads + 1) * dim] = turned
    v_ref[...] = projected[:, wide:].astype(BF16)


def project_qkv(launch, x, gain, weights, cols, gain_q, gain_k, cosine, sine, kv, carry=()):
    rows, width = x.shape
    dim = gain_q.shape[1]
    heads = cols // dim - 2 * kv
    bt = tile_of(rows, 512)
    wide = (heads + kv) * dim

    def part(w):
        return pl.BlockSpec((bt, w), lambda i: (i, 0))

    return launch(
        functools.partial(qkv_kernel, kv),
        (x, gain, weights, gain_q, gain_k, cosine, sine),
        [
            part(width),
            resident((1, width)),
            Held((width, cols)),
            resident((1, dim)),
            resident((1, dim)),
            part(dim),
            part(dim),
        ],
        [part(width), part(1), part(wide), part(heads * dim), part(kv * dim), part(kv * dim)],
        [
            shape((rows, width), BF16),
            shape((rows, 1), F32),
            shape((rows, wide), F32),
            shape((rows, heads * dim), BF16),
            shape((rows, kv * dim), BF16),
            shape((rows, kv * dim), BF16),
        ],
        (rows // bt,),
        "project_qkv",
        (2 * rows * width * cols, rows * width * 4 + width * cols * 2, 0),
        carry=carry,
    )


def mlp_kernel(x_ref, gain_ref, wg_ref, wu_ref, wd_ref, cot_ref, *refs):
    normed_ref, scale_ref, active_ref, gg_ref, gu_ref = refs[-5:]

    @pl.when(pl.program_id(1) == 0)
    def _():
        values = x_ref[...].astype(F32)
        scale = row_scale(values)
        normed_ref[...] = (values * scale * gain_ref[...]).astype(BF16)
        scale_ref[...] = scale

    normed = normed_ref[...]
    gate = dot_nn(normed, wg_ref[...])
    up = dot_nn(normed, wu_ref[...])
    grad = dot_nn(cot_ref[...], wd_ref[...])
    sig = jax.nn.sigmoid(gate)
    silu = gate * sig
    active_ref[...] = (silu * up).astype(BF16)
    gu_ref[...] = (grad * silu).astype(BF16)
    gg_ref[...] = (grad * up * (sig + silu * (1.0 - sig))).astype(BF16)


def mlp(launch, x, gain, weights, cot, chunk, total, kept, carry=()):
    rows, width = x.shape
    hidden = weights.shape[1] // 3
    bn = tile_of(hidden, 512)
    tiles = hidden // bn
    more = [] if kept is None else list(kept)
    tile = pl.BlockSpec((rows, bn), lambda i, j: (chunk, j))
    low = shape((total, hidden), BF16)
    return launch(
        mlp_kernel,
        (x, gain, weights, weights, weights, cot, *more),
        [
            Held((rows, width)),
            resident((1, width)),
            pl.BlockSpec((width, bn), lambda i, j: (0, j)),
            pl.BlockSpec((width, bn), lambda i, j: (0, j + tiles)),
            pl.BlockSpec((width, bn), lambda i, j: (0, j + 2 * tiles)),
            Held((rows, width)),
        ]
        + [ANY] * len(more),
        [Held((rows, width), chunk * rows), pl.BlockSpec((rows, 1), lambda i, j: (0, 0)), tile, tile, tile],
        [shape((total, width), BF16), shape((rows, 1), F32), low, low, low],
        (1, tiles),
        "mlp",
        (6 * rows * width * hidden, rows * (width + hidden) * 6 + 6 * width * hidden, rows * hidden),
        alias={6: 0, 7: 2, 8: 3, 9: 4} if more else None,
        carry=carry,
    )


def mid_kernel(gg_ref, gu_ref, w_ref, v_ref, scale_ref, gain_ref, part_ref, inner_ref, gain_out):
    hidden = gg_ref.shape[1]
    partial = dot_nt(gg_ref[...], w_ref[:, :hidden]) + dot_nt(gu_ref[...], w_ref[:, hidden:])
    part_ref[...] = partial.astype(BF16)
    product = partial * v_ref[...].astype(F32)
    gain_out[0] = jnp.sum(product * scale_ref[...], axis=0, keepdims=True)
    inner = row_of(jnp.sum(product * gain_ref[...], axis=1, keepdims=True))

    @pl.when(pl.program_id(1) == 0)
    def _():
        inner_ref[0] = inner

    @pl.when(pl.program_id(1) > 0)
    def _():
        inner_ref[0] += inner


def back_mid(launch, gg, gu, weights, values, scale, gain, chunk, carry=()):
    rows, width = values.shape
    hidden = gg.shape[1]
    bn = tile_of(width, 512)
    return launch(
        mid_kernel,
        (gg, gu, weights, values, scale, gain),
        [
            Held((rows, hidden), chunk * rows),
            Held((rows, hidden), chunk * rows),
            pl.BlockSpec((bn, 2 * hidden), lambda i, j: (j, 0)),
            pl.BlockSpec((rows, bn), lambda i, j: (0, j)),
            pl.BlockSpec((rows, 1), lambda i, j: (0, 0)),
            pl.BlockSpec((1, bn), lambda i, j: (0, j)),
        ],
        [
            pl.BlockSpec((rows, bn), lambda i, j: (0, j)),
            pl.BlockSpec((1, 1, rows), lambda i, j: (0, 0, 0)),
            pl.BlockSpec((1, 1, bn), lambda i, j: (0, 0, j)),
        ],
        [shape((rows, width), BF16), shape((1, 1, rows), F32), shape((1, 1, width), F32)],
        (1, width // bn),
        "back_mid",
        (4 * rows * width * hidden, rows * (width + hidden) * 4 + 4 * width * hidden, 0),
        carry=carry,
    )


def qkv_back_kernel(
    kv, dq_ref, dk_ref, dv_ref, proj_ref, cos_ref, sin_ref, gq_ref, gk_ref, w_ref, v_ref, scale_ref, gain_ref, *refs
):
    low_ref, part_ref, inner_ref, gain_out, gq_out, gk_out = refs[-6:]
    dim = gq_ref.shape[1]
    heads = dq_ref.shape[1] // dim
    wide = (heads + kv) * dim

    @pl.when(pl.program_id(1) == 0)
    def _():
        cosine, sine = cos_ref[...], sin_ref[...]
        sums = [jnp.zeros((1, dim), F32), jnp.zeros((1, dim), F32)]
        for h in range(heads + kv):
            is_key = h >= heads
            if is_key:
                grad = dk_ref[:, (h - heads) * dim : (h - heads + 1) * dim] * (1.0 / math.sqrt(dim))
            else:
                grad = dq_ref[:, h * dim : (h + 1) * dim]
            grad = grad * cosine + swap(grad * sine)
            value = proj_ref[:, h * dim : (h + 1) * dim]
            scale = row_scale(value)
            sums[is_key] += jnp.sum(grad * value * scale, axis=0, keepdims=True)
            weighted = grad * (gk_ref[...] if is_key else gq_ref[...])
            mean = jnp.mean(weighted * value, axis=-1, keepdims=True)
            low_ref[:, h * dim : (h + 1) * dim] = (scale * (weighted - value * scale * scale * mean)).astype(BF16)
        low_ref[:, wide:] = dv_ref[...].astype(BF16)
        gq_out[0] = sums[0]
        gk_out[0] = sums[1]

    partial = dot_nt(low_ref[...], w_ref[...])
    part_ref[...] = partial.astype(BF16)
    product = partial * v_ref[...].astype(F32)
    gain_out[0] = jnp.sum(product * scale_ref[...], axis=0, keepdims=True)
    inner = row_of(jnp.sum(product * gain_ref[...], axis=1, keepdims=True))

    @pl.when(pl.program_id(1) == 0)
    def _():
        inner_ref[0] = inner

    @pl.when(pl.program_id(1) > 0)
    def _():
        inner_ref[0] += inner


def back_qkv(launch, dq, dk, dv, proj, cosine, sine, gain_q, gain_k, weights, cols, values, scale, gain, kv, chunk, kept, carry=()):
    total, width = values.shape
    rows = dq.shape[0]
    dim = gain_q.shape[1]
    bt = rows
    bn = tile_of(width, 512)
    base = chunk

    def here(w):
        return Held((rows, w))

    def there(w):
        return Held((rows, w), chunk * rows)

    row = pl.BlockSpec((1, 1, dim), lambda i, j: (i, 0, 0))
    more = [] if kept is None else [kept]
    return launch(
        functools.partial(qkv_back_kernel, kv),
        (dq, dk, dv, proj, cosine, sine, gain_q, gain_k, weights, values, scale, gain, *more),
        [
            here(dq.shape[1]),
            there(dk.shape[1]),
            there(dv.shape[1]),
            there(proj.shape[1]),
            there(dim),
            there(dim),
            resident((1, dim)),
            resident((1, dim)),
            pl.BlockSpec((bn, cols), lambda i, j: (j, 0)),
            pl.BlockSpec((bt, bn), lambda i, j: (i + base, j)),
            pl.BlockSpec((rows, 1), lambda i, j: (chunk, 0)),
            pl.BlockSpec((1, bn), lambda i, j: (0, j)),
        ]
        + [ANY] * len(more),
        [
            there(cols),
            pl.BlockSpec((bt, bn), lambda i, j: (i, j)),
            pl.BlockSpec((1, 1, bt), lambda i, j: (i, 0, 0)),
            pl.BlockSpec((1, 1, bn), lambda i, j: (i, 0, j)),
            row,
            row,
        ],
        [
            shape((total, cols), BF16),
            shape((rows, width), BF16),
            shape((rows // bt, 1, bt), F32),
            shape((rows // bt, 1, width), F32),
            shape((rows // bt, 1, dim), F32),
            shape((rows // bt, 1, dim), F32),
        ],
        (rows // bt, width // bn),
        "back_qkv",
        (2 * rows * width * cols, rows * width * 4 + rows * cols * 10, 0),
        alias={12: 0} if more else None,
        carry=carry,
    )


def pair_kernel(low_ref, high_ref, first_ref, second_ref, out_ref):
    out_ref[...] = (dot_tn(low_ref[...], first_ref[...]) + dot_tn(high_ref[...], second_ref[...])).astype(BF16)


def weight_grad_pair(launch, lefts, rights, rows_at, carry=()):
    rows, cols = rights[0].shape
    width = lefts[0].shape[1]
    bm = next(size for size in (1024, 768, 512, 256, 128) if width % size == 0)
    bn = tile_of(cols, 512)

    def left(k):
        return pl.BlockSpec((rows, bm), lambda i, j: (rows_at[k], i))

    right = pl.BlockSpec((rows, bn), lambda i, j: (0, j))
    return launch(
        pair_kernel,
        (*lefts, *rights),
        [left(0), left(1), right, right],
        [pl.BlockSpec((bm, bn), lambda i, j: (i, j))],
        [shape((width, cols), BF16)],
        (width // bm, cols // bn),
        "weight_grad",
        (4 * rows * width * cols, rows * (width + cols) * 4 + width * cols * 2, 0),
        carry=carry,
    )[0]


def grad_kernel(tiles, left_ref, *refs):
    rights, out_ref = refs[:-1], refs[-1]
    for k, right in enumerate(rights):
        @pl.when(pl.program_id(1) // tiles == k)
        def _():
            out_ref[...] = dot_tn(left_ref[...], right[...]).astype(BF16)


def weight_grad(launch, left, *rights, carry=()):
    rows, width = left.shape
    cols = rights[0].shape[1]
    bm = next(size for size in (1024, 768, 512, 256, 128) if width % size == 0)
    bn = next(size for size in (512, 384, 256, 128) if cols % size == 0)
    tiles = cols // bn

    def part(k):
        return pl.BlockSpec((rows, bn), lambda i, j: (0, jnp.clip(j - k * tiles, 0, tiles - 1)))

    return launch(
        functools.partial(grad_kernel, tiles),
        (left, *rights),
        [pl.BlockSpec((rows, bm), lambda i, j: (0, i))] + [part(k) for k in range(len(rights))],
        [pl.BlockSpec((bm, bn), lambda i, j: (i, j))],
        [shape((width, cols * len(rights)), BF16)],
        (width // bm, tiles * len(rights)),
        "weight_grad",
        (2 * rows * width * cols * len(rights), rows * (width + cols) * 2 + width * cols * 4, 0),
        carry=carry,
    )[0]


def out_kernel(left_ref, right_ref, out_ref):
    out_ref[...] = dot_nt(left_ref[...], right_ref[...]).astype(BF16)


def project_out(launch, left, weights, chunk, rows, carry=()):
    width, hidden = weights.shape[0], left.shape[1]
    bn = tile_of(width, 512)
    last = weights.shape[1] // hidden - 1
    return launch(
        out_kernel,
        (left, weights),
        [Held((rows, hidden), chunk * rows), pl.BlockSpec((bn, hidden), lambda i, j: (j, last))],
        [pl.BlockSpec((rows, bn), lambda i, j: (0, j))],
        [shape((rows, width), BF16)],
        (1, width // bn),
        "project_out",
        (2 * rows * width * hidden, rows * (width + hidden) * 2 + width * hidden * 2, 0),
        carry=carry,
    )[0]


def mix_kernel(left_ref, right_ref, out_ref):
    out_ref[...] = dot_nn(left_ref[...], right_ref[...]).astype(BF16)


def grad_mix(launch, grads, weights, cols):
    rows, width = grads.shape
    bt = tile_of(rows, 512)
    return launch(
        mix_kernel,
        (grads, weights),
        [pl.BlockSpec((bt, width), lambda i: (i, 0)), Held((width, cols), 0, weights.shape[1] - cols)],
        [pl.BlockSpec((bt, cols), lambda i: (i, 0))],
        [shape((rows, cols), BF16)],
        (rows // bt,),
        "grad_mix",
        (2 * rows * width * cols, (rows * width + rows * cols + width * cols) * 2, 0),
    )[0]


def tables_kernel(position_ref, segment_ref, inverse_ref, cos_ref, sin_ref, wide_ref):
    def column(row):
        return jnp.broadcast_to(row.astype(F32), (128, row.shape[1])).T

    angle = column(position_ref[...]) * inverse_ref[...]
    half = lax.broadcasted_iota(jnp.int32, angle.shape, 1) < angle.shape[1] // 2
    sine = jnp.sin(angle)
    cos_ref[...] = jnp.cos(angle)
    sin_ref[...] = jnp.where(half, -sine, sine)
    wide_ref[...] = column(segment_ref[...]).astype(jnp.int32)


def tables(launch, positions, segments, dim, carry=()):
    rows = positions.shape[0]
    bt = tile_of(rows, 512)
    inverse = THETA ** (-(jnp.arange(dim // 2, dtype=F32) * 2.0 / dim))
    row = pl.BlockSpec((1, bt), lambda i: (0, i))
    wide = pl.BlockSpec((bt, 128), lambda i: (i, 0))
    return launch(
        tables_kernel,
        (positions[None], segments[None], jnp.concatenate([inverse, inverse])[None]),
        [row, row, resident((1, dim))],
        [wide, wide, wide],
        [shape((rows, dim), F32), shape((rows, dim), F32), shape((rows, 128), jnp.int32)],
        (rows // bt,),
        "tables",
        (0, rows * dim * 12, rows * dim * 2),
        carry=carry,
    )


def side(first, low, high):
    return jnp.where(first, low[...].astype(F32), high[...].astype(F32))


def grad_block(factor, first, base, term, t0, t1, t2, t3, values, scale, inner, others, gain):
    row = inner[0] + jnp.sum(others[:, 0, 0, :], axis=0, keepdims=True)
    inner = jnp.broadcast_to(row, (128, row.shape[1])).T[:, :1]
    scales = scale[...]
    total = term[...].astype(F32) + side(first, t0, t1) + side(first, t2, t3)
    return base[...].astype(F32) + scales * (
        total * gain[...] - values[...].astype(F32) * (scales * scales * inner * factor)
    )


def grad_operands(base, summed, values, scale, gain, base_at, values_at, scale_at, start=0):
    local = base.shape[1]
    bt = summed.half

    def step(i):
        return jnp.clip(i - start, 0, 1)

    def at(chunk, wide):
        return pl.BlockSpec((bt, wide), lambda i: (step(i) + 2 * chunk, 0))

    mine = pl.BlockSpec((bt, local), lambda i: (step(i), lax.axis_index("col")))
    others = summed.inner_others
    args = (base, summed.partial, *summed.pieces(), values, scale, summed.inner, others, gain[None])
    specs = [at(base_at, local), mine, *([Held((bt, local))] * 4), at(values_at, local), at(scale_at, 1)]
    specs += [
        pl.BlockSpec((1, 1, bt), lambda i: (0, 0, step(i))),
        pl.BlockSpec((others.shape[0], 1, 1, bt), lambda i: (0, 0, 0, step(i))),
        resident((1, local)),
    ]
    return args, specs, at


def hidden_kernel(factor, *refs):
    grad = grad_block(factor, pl.program_id(0) == 0, *refs[:-2])
    refs[-2][...] = grad
    refs[-1][...] = grad.astype(BF16)


def hidden_grad(launch, base, summed, values, scale, gain, chunk):
    args, specs, at = grad_operands(base, summed, values, scale, gain, chunk, 0, 0)
    rows, local = summed.rows, base.shape[1]
    return launch(
        functools.partial(hidden_kernel, 1.0 / (local * launch.ring.size)),
        args,
        specs,
        [at(0, local), at(0, local)],
        [shape((rows, local), F32), shape((rows, local), BF16)],
        (2,),
        "hidden_grad",
        (0, rows * local * 18, 0),
    )


def settle_kernel(*refs):
    step = pl.program_id(0)
    output = refs[-1]

    def one(hidden, down, p0, p1, p2, p3):
        first = step % 2 == 0
        output[...] = (hidden[...] + (down[...].astype(F32) + side(first, p0, p1) + side(first, p2, p3))).astype(BF16)

    pl.when(step < 2)(lambda: one(*refs[:6]))
    pl.when(step >= 2)(lambda: one(*refs[6:12]))


def settle(launch, hidden, sums, carry=()):
    rows, local = hidden[0].shape
    bt = rows // 2
    args, specs = [], []
    for c in (0, 1):
        here = pl.BlockSpec((bt, local), lambda i, c=c: (jnp.clip(i - 2 * c, 0, 1), 0))
        mine = pl.BlockSpec((bt, local), lambda i, c=c: (jnp.clip(i - 2 * c, 0, 1), lax.axis_index("col")))
        args += [hidden[c], sums[c].partial, *sums[c].pieces()]
        specs += [here, mine] + [Held((bt, local))] * 4
    return launch(
        settle_kernel,
        args,
        specs,
        [pl.BlockSpec((bt, local), lambda i: (i, 0))],
        [shape((2 * rows, local), BF16)],
        (4,),
        "settle",
        (0, rows * local * 24, 0),
        carry=carry,
    )[0]


def last_kernel(factor, *refs):
    step = pl.program_id(0)
    count = (len(refs) - 1) // 2

    @pl.when(step < 2)
    def _():
        refs[-1][...] = grad_block(factor, step == 0, *refs[:count])

    @pl.when(step >= 2)
    def _():
        refs[-1][...] = grad_block(factor, step == 2, *refs[count:-1])


def settle_last(launch, grad_hidden, sums, tokens, scale, gain, carry=()):
    args, specs = [], []
    for c in (0, 1):
        more, more_specs, _ = grad_operands(grad_hidden[c], sums[c], tokens, scale, gain, 0, c, c, 2 * c)
        args += more
        specs += more_specs
    total, local = tokens.shape
    return launch(
        functools.partial(last_kernel, 1.0 / (local * launch.ring.size)),
        args,
        specs,
        [pl.BlockSpec((total // 4, local), lambda i: (i, 0))],
        [shape((total, local), F32)],
        (4,),
        "settle_last",
        (0, total * local * 24, 0),
        carry=carry,
    )[0]


def after(value, *others):
    return lax.optimization_barrier((value, *jax.tree.leaves(others)))[0]


def body(
    tokens,
    segments,
    positions,
    gain_attn,
    w_query,
    key_weight_matrix,
    value_weight_matrix,
    gain_query,
    gain_key,
    w_out,
    gain_mlp,
    w_gate,
    w_up,
    w_down,
    cotangent,
):
    total, local = tokens.shape
    dim = gain_query.shape[0]
    query_cols, key_cols = w_query.shape[1], key_weight_matrix.shape[1]
    kv = key_cols // dim
    hidden_units = w_gate.shape[1]
    ring = Ring(lax.axis_size("col"))
    launch = Launcher(ring)
    width = local * ring.size
    rows = total // 2
    parts = [slice(0, rows), slice(rows, total)]
    offset = lax.axis_index("col") * local
    gain_attn_local = lax.dynamic_slice_in_dim(gain_attn, offset, local)
    gain_mlp_local = lax.dynamic_slice_in_dim(gain_mlp, offset, local)
    gain_q, gain_k = gain_query[None], gain_key[None]
    bq = tile_of(rows, 512)

    def gathered(weights, axis):
        return lax.all_gather(weights, "row", axis=axis, tiled=True)

    def scattered(partial, axis):
        return lax.psum_scatter(partial, "row", scatter_dimension=axis, tiled=True)

    def carried(*stages):
        for stage in stages:
            for _ in range(ring.stages - 2):
                launch.alone(stage)

    pair = lambda: [None] * 2
    mixed, logs, hidden, mid_low, scale_mid = pair(), pair(), pair(), pair(), pair()
    get_cot, get_mid, get_grad = pair(), pair(), pair()
    sum_out, sum_down, sum_mid, sum_in = pair(), pair(), pair(), pair()
    gain_mlp_part, grad_hidden, gains_in = pair(), pair(), pair()

    qkv_cols = query_cols + 2 * key_cols
    w_attn = gathered(jnp.concatenate([w_query, key_weight_matrix, value_weight_matrix, w_out.T], axis=1), 0)

    get_tok = Gather(ring, tokens, 0, total)
    launch.alone(get_tok)
    w_mlp = gathered(jnp.concatenate([after(w_gate, get_tok.full), w_up, w_down.T], axis=1), 0)
    seg_row = segments[None]
    for _ in range(ring.stages - 2):
        launch.alone(get_tok)
    cosine, sine, seg_wide = tables(launch, positions, segments, dim, [get_tok])
    x_full = get_tok.full

    for c in (0, 1):
        get_cot[c] = Gather(ring, cotangent, c * rows, rows, split=c == 0)
    normed, scale_attn, proj, queries, keys, values = project_qkv(
        launch, x_full, gain_attn[None], w_attn, qkv_cols, gain_q, gain_k, cosine, sine, kv, carry=[get_cot[1]]
    )

    def attention(c, at, carry):
        mixed[c], logs[c] = attend(
            launch, queries, keys, values, after(seg_row, at), seg_wide, c * rows, rows, dim, bq, bq, carry=carry
        )
        return logs[c]

    def start_out(c, at, carry):
        partial = project_out(launch, after(mixed[c], at), w_attn, 0, rows, carry=carry)
        sum_out[c] = Scatter(ring, partial)
        return partial

    def end_out(c):
        hidden[c] = tokens[parts[c]].astype(F32) + sum_out[c].total()
        mid_low[c] = hidden[c].astype(BF16)
        get_mid[c] = Gather(ring, mid_low[c], 0, rows)

    carried(get_cot[1])
    at = attention(1, normed, [get_cot[1]])
    at = start_out(1, at, [get_cot[0]])
    at = attention(0, at, [sum_out[1]])
    carried(sum_out[1])
    launch.alone(sum_out[1])
    end_out(1)
    launch.alone(get_mid[1])
    carried(get_mid[1])
    start_out(0, get_mid[1].full, [get_mid[1]])
    launch.alone(sum_out[0])
    carried(sum_out[0])
    launch.alone(sum_out[0], get_cot[0])
    end_out(0)

    def feed_forward(c, kept, at, carry):
        nm, scale_mid[c], *rest = mlp(
            launch, get_mid[c].full, after(gain_mlp[None], at), w_mlp, get_cot[c].full, c, total, kept,
            carry=carry,
        )
        return (nm, *rest)

    def back_middle(c, kept, at, carry):
        partial, inner, gain_part = back_mid(
            launch, kept[2], kept[3], w_mlp, get_mid[c].full, scale_mid[c], after(gain_mlp[None], at), c, carry=carry
        )
        gain_mlp_part[c] = jnp.sum(gain_part, axis=(0, 1))
        sum_mid[c] = Scatter(ring, partial, inner)
        return partial

    def end_mid(c):
        grad_hidden[c], low = hidden_grad(
            launch, cotangent, sum_mid[c], mid_low[c], scale_mid[c], gain_mlp_local, c
        )
        get_grad[c] = Gather(ring, low, 0, rows)
        return low

    def start_down(c, active, at, carry=()):
        partial = project_out(launch, after(active, at), w_mlp, c, rows, carry=carry)
        sum_down[c] = Scatter(ring, partial, split=True)
        return partial

    kept = feed_forward(1, None, get_mid[1].full, [get_mid[0]])
    carried(get_mid[0], get_cot[0])
    at = start_down(1, kept[1], kept[0], [get_mid[0]])
    at = back_middle(1, kept, at, [get_cot[0], sum_down[1]])
    kept = feed_forward(0, kept, at, [sum_mid[1]])
    normed_mid, active, grad_gate, grad_up = kept
    carried(sum_mid[1])
    partial = weight_grad_pair(
        launch, (active, active), (get_cot[0].full, get_cot[1].full), (0, 1), carry=[sum_mid[1], sum_down[1].near]
    )
    rs_down = scattered(partial, 1)
    low = end_mid(1)
    at = back_middle(0, kept, (partial, low), [get_grad[1]])
    carried(get_grad[1])
    partial = weight_grad(launch, after(normed_mid, at), grad_gate, grad_up, carry=[get_grad[1], sum_mid[0]])
    rs_gate_up = scattered(partial, 0)
    carried(sum_mid[0])
    at = start_down(0, active, partial, [sum_mid[0]])
    low = end_mid(0)

    def mix(c):
        return jnp.dot(get_grad[c].full, w_attn[:, qkv_cols:], preferred_element_type=F32).astype(BF16)

    def attention_back(c, grad_mixed, sums, at, carry):
        return attend_back(
            launch, queries, keys, values, grad_mixed, mixed[c], logs[c], after(seg_row, at), seg_wide, c * rows, dim,
            bq, bq, sums, carry=carry,
        )

    def projection_back(c, grads, low_all, at, carry):
        low_all, partial, inner, *gains_in[c] = back_qkv(
            launch, *grads, proj, cosine, sine, gain_q, gain_k, w_attn, qkv_cols, x_full, scale_attn, after(gain_attn[None], at),
            kv, c, low_all, carry=carry,
        )
        sum_in[c] = Scatter(ring, partial, inner, split=True)
        return low_all, partial

    grads = attention_back(1, mix(1), None, (at, low), [get_grad[0], sum_down[0]])
    carried(get_grad[0])
    low_all, at = projection_back(1, grads, None, None, [get_grad[0], sum_down[0].near])
    grad_mixed = mix(0)
    early = Share("col", *gains_in[1], (gain_mlp_part[0] + gain_mlp_part[1])[None])
    grads = attention_back(0, grad_mixed, grads[1:], (at, rs_down), [sum_in[1], early])
    carried(sum_down[1])
    grad_out = weight_grad_pair(
        launch, (after(mixed[0], grads[0]), mixed[1]), (get_grad[0].full, get_grad[1].full), (0, 0), carry=[sum_down[1]]
    )
    rs_out = scattered(grad_out, 1)
    carried(sum_in[1], sum_down[0])
    low_all, at = projection_back(0, grads, low_all, grad_out, [sum_in[1], sum_down[0]])
    gains = Share("col", *gains_in[0])
    partial = weight_grad(launch, after(normed, at, rs_gate_up), low_all, carry=[sum_in[0], sum_in[1].near, gains])

    grad_qkv = scattered(after(partial, rs_out), 0)
    gains = jnp.concatenate([part.reshape(-1) for part in (*gains.sums, *early.sums)])[None]
    gains = Share("row", gains)
    carried(sum_in[0])
    output = settle(launch, hidden, sum_down, [sum_in[0], sum_in[0].near])
    grad_tokens = settle_last(launch, grad_hidden, sum_in, tokens, scale_attn, gain_attn_local, [gains])
    sum_attn, sum_q, sum_k, more_attn, more_q, more_k, sum_mlp = jnp.split(
        gains.sums[0][0], list(itertools.accumulate([width, dim, dim, width, dim, dim]))
    )
    return (
        output,
        grad_tokens,
        sum_attn + more_attn,
        grad_qkv[:, :query_cols].astype(F32),
        grad_qkv[:, query_cols : query_cols + key_cols].astype(F32),
        grad_qkv[:, query_cols + key_cols :].astype(F32),
        sum_q + more_q,
        sum_k + more_k,
        rs_out.astype(F32),
        sum_mlp,
        rs_gate_up[:, :hidden_units].astype(F32),
        rs_gate_up[:, hidden_units:].astype(F32),
        rs_down.astype(F32),
    )


def solution(mesh):
    both, split = P("row", "col"), P("col", "row")
    in_specs = (both, P("row"), P("row"), P(), both, both, both, P(), P(), split, P(), both, both, split, both)
    out_specs = (both, both, P(), both, both, both, P(), P(), split, P(), both, both, split)
    return jax.shard_map(body, mesh=mesh, in_specs=in_specs, out_specs=out_specs, check_vma=False)
```

```python
import functools
import itertools
import math

import jax
import jax.numpy as jnp
from jax import lax
from jax.experimental import pallas as pl
from jax.experimental.pallas import tpu as pltpu
from jax.sharding import PartitionSpec as P

BF16 = jnp.bfloat16
F32 = jnp.float32
EPS = 1e-06
THETA = 1000000.0
LOG2E = 1.4426950408889634
VMEM_LIMIT = 60 * 1024 * 1024
ANY = pl.BlockSpec(memory_space=pl.ANY)


def dot_nt(left, right):
    return lax.dot_general(left, right, (((1,), (1,)), ((), ())), preferred_element_type=F32)


def dot_nn(left, right):
    return jnp.dot(left, right, preferred_element_type=F32)


def dot_tn(left, right):
    return lax.dot_general(left, right, (((0,), (0,)), ((), ())), preferred_element_type=F32)


def shape(dims, dtype):
    return jax.ShapeDtypeStruct(tuple(dims), dtype)


def resident(dims):
    return pl.BlockSpec(dims, lambda *_: (0,) * len(dims), pipeline_mode=pl.Buffered(1))


def held(dims, index):
    return pl.BlockSpec(dims, index, pipeline_mode=pl.Buffered(1))


def tile_of(size, most):
    tile = most
    while size % tile:
        tile //= 2
    return tile


def swap(values):
    half = values.shape[-1] // 2
    return jnp.concatenate([values[:, half:], values[:, :half]], axis=1)


def row_scale(values):
    return lax.rsqrt(jnp.mean(values * values, axis=-1, keepdims=True) + EPS)


def row_of(column):
    return jnp.broadcast_to(column, (column.shape[0], 128)).T[:1]


class Held:
    def __init__(self, dims, row=0, col=0):
        self.dims, self.row, self.col = dims, row, col

    def of(self, ref):
        return ref.at[pl.ds(self.row, self.dims[0]), pl.ds(self.col, self.dims[1])]


class Ring:
    def __init__(self, size):
        self.size = size
        self.stages = size // 2

    def place(self, index):
        half = self.size // 2
        return jnp.where(index < half, index, self.size + half - 1 - index)

    def owner(self, offset):
        return self.place(lax.rem(self.place(lax.axis_index("col")) + offset + self.size, self.size))

    def cols(self, offset, width):
        return pl.ds(pl.multiple_of(self.owner(offset) * width, 128), width)


class Gather:
    def __init__(self, ring, local, row, rows, split=False):
        self.ring, self.local, self.row, self.rows = ring, local, row, rows
        self.width = local.shape[1]
        self.stage, self.full, self.part = 0, None, 2 if split else 0
        self.out = [shape((rows, self.width * ring.size), BF16)]
        self.offsets = [-1, 1]

    def prepare(self):
        if self.stage == 0 or self.part == 0:
            self.stage += 1
        self.ins = [self.full] if self.full is not None else []
        self.alias = {0: 0} if self.ins else {}
        self.count, self.bounce, self.span = 2, [], None
        if self.stage == 1:
            start, size = self.row, self.rows
            if self.part:
                size //= 2
                start += (2 - self.part) * size
                self.part -= 1
            self.span = start, size
            self.ins = self.ins + [self.local]
            self.count, self.bounce = 3, [(size, self.width)]
        return self

    def copies(self, ins, outs):
        ring, full, width, half = self.ring, outs[0], self.width, self.rows // 2
        if self.stage == 1:
            start, size = self.span
            source = ins[-1].at[pl.ds(start, size), :]
            mine = full.at[pl.ds(start - self.row, size), ring.cols(0, width)]
            return [(source, mine, 1), (source, mine, -1), (source, mine, None)]
        from_left, from_right = ring.cols(1 - self.stage, width), ring.cols(self.stage - 1, width)
        if self.stage < ring.stages:
            left, right = full.at[:, from_left], full.at[:, from_right]
        else:
            left, right = full.at[pl.ds(0, half), from_left], full.at[pl.ds(half, half), from_right]
        return [(left, left, 1), (right, right, -1)]

    def finish(self, outs):
        self.full = outs[0]


class Scatter:
    def __init__(self, ring, partial, inner=None, split=False):
        self.ring, self.partial, self.inner = ring, partial, inner
        self.split = split and ring.stages == 2
        self.rows, self.half = partial.shape[0], partial.shape[0] // 2
        self.width = partial.shape[1] // ring.size
        self.stage, self.inner_others, self.bounce, self.alias = 0, None, [], {}
        self.near = Near(self)
        self.scratch = []

    def block(self, offset, low):
        start = (self.half if low else 0, self.ring.owner(offset) * self.width)
        return lax.dynamic_slice(self.partial, start, (self.half, self.width)).astype(F32)

    def prepare(self):
        self.stage += 1
        stage, stages = self.stage, self.ring.stages
        whole = stage < stages
        self.offsets = [-1, 1]
        if stage == 1:
            self.ins = [self.partial]
        elif stages == 2:
            self.ins, self.scratch = [self.partial, *self.got[:2]], [(self.half, self.width)] * 4
            if not self.split:
                self.kept = self.got[2:]
        else:
            top = self.block(stages + 1 - stage, False) + self.got[0].astype(F32)
            bottom = self.block(stage - 1 - stages, True) + self.got[1].astype(F32)
            self.ins = [top.astype(BF16), bottom.astype(BF16)]
            if whole:
                low = self.block(stages - stage, True) + self.got[2].astype(F32)
                high = self.block(stage - stages, False) + self.got[3].astype(F32)
                self.ins += [low.astype(BF16), high.astype(BF16)]
            elif not self.split:
                self.kept = self.got[2:]
        self.out = [shape((self.half, self.width), BF16)] * (4 if whole and not self.split else 2)
        self.count = len(self.out)
        if stage == 1 and not self.split:
            self.near.add_inner(self)
        return self

    def far_copies(self, ins, outs):
        top, bottom = pl.ds(0, self.half), pl.ds(self.half, self.half)
        far = self.ring.cols(self.ring.stages, self.width)
        return [(ins[0].at[top, far], outs[0], 1), (ins[0].at[bottom, far], outs[1], -1)]

    def loads(self, ins, held):
        top, bottom = pl.ds(0, self.half), pl.ds(self.half, self.half)
        right, left = self.ring.cols(1, self.width), self.ring.cols(-1, self.width)
        sources = [ins[0].at[top, right], ins[0].at[bottom, left], ins[1], ins[2]]
        self.held = held
        return list(zip(sources, held))

    def combine(self):
        for term, others in zip(self.held[:2], self.held[2:]):
            term[...] = (term[...].astype(F32) + others[...].astype(F32)).astype(BF16)

    def copies(self, ins, outs):
        if self.scratch:
            return [(self.held[0], outs[0], 1), (self.held[1], outs[1], -1)]
        if self.stage > 1:
            return [(ref, out, way) for ref, out, way in zip(ins, outs, (1, -1, 1, -1))]
        made = self.far_copies(ins, outs)
        if not self.split:
            made += self.near.near_copies(ins, outs[2:])
        return made

    def finish(self, outs):
        if self.stage == 1 and not self.split:
            outs = [*outs[:2], *self.near.take(outs[2:])]
        self.got = outs

    def pieces(self):
        return self.got[0], self.kept[0], self.kept[1], self.got[1]

    def total(self):
        mine = lax.dynamic_slice_in_dim(self.partial, lax.axis_index("col") * self.width, self.width, 1)
        left = jnp.concatenate([self.got[0], self.kept[0]]).astype(F32)
        right = jnp.concatenate([self.kept[1], self.got[1]]).astype(F32)
        return mine.astype(F32) + left + right


class Near:
    def __init__(self, whole):
        self.whole = whole
        self.bounce, self.alias = [], {}

    @property
    def empty(self):
        return not self.whole.split

    def add_inner(self, stage):
        whole = self.whole
        if whole.inner is not None:
            others = whole.ring.size - 1
            stage.ins = stage.ins + [whole.inner]
            stage.out = stage.out + [shape((others, *whole.inner.shape), F32)]
            stage.count += others
            stage.offsets = list(range(1, whole.ring.size))

    def prepare(self):
        whole = self.whole
        self.ins, self.offsets, self.count = [whole.partial], [-1, 1], 2
        self.out = [shape((whole.half, whole.width), BF16)] * 2
        self.add_inner(self)
        return self

    def near_copies(self, ins, outs):
        whole, ring = self.whole, self.whole.ring
        top, bottom = pl.ds(0, whole.half), pl.ds(whole.half, whole.half)
        made = [
            (ins[0].at[bottom, ring.cols(ring.stages - 1, whole.width)], outs[0], 1),
            (ins[0].at[top, ring.cols(1 - ring.stages, whole.width)], outs[1], -1),
        ]
        if whole.inner is not None:
            made += [(ins[1], outs[2].at[k - 1], k) for k in range(1, ring.size)]
        return made

    def copies(self, ins, outs):
        return self.near_copies(ins, outs)

    def take(self, outs):
        whole = self.whole
        if whole.inner is not None:
            whole.inner_others = outs[2]
        return outs[:2]

    def finish(self, outs):
        self.whole.kept = self.take(outs)


class Share:
    def __init__(self, axis, *arrays):
        self.axis, self.arrays = axis, arrays
        self.size = lax.axis_size(axis)
        self.bounce, self.alias = [], {}
        self.offsets = [(axis, k) for k in range(1, self.size)]

    def prepare(self):
        self.ins, self.out = list(self.arrays), [shape((self.size, *a.shape), F32) for a in self.arrays]
        self.count = (self.size - 1) * len(self.arrays)
        return self

    def copies(self, ins, outs):
        here = lax.axis_index(self.axis)
        return [(a, out.at[here], offset) for a, out in zip(ins, outs) for offset in self.offsets]

    def finish(self, outs):
        self.sums = []
        for mine, out in zip(self.arrays, outs):
            here = lax.broadcasted_iota(jnp.int32, out.shape, 0) == lax.axis_index(self.axis)
            self.sums.append(jnp.sum(jnp.where(here, mine[None], out), axis=0))


class Launcher:
    def __init__(self, ring):
        self.ring = ring
        self.ids = itertools.count()

    def __call__(self, kernel, args, in_specs, out_specs, out_shape, grid, name, cost, alias=None, scratch=(), carry=()):
        stages = [stage.prepare() for stage in carry if not getattr(stage, "empty", False)]
        own_in, own_out = len(args), len(out_shape)
        held_in = [(i, spec) for i, spec in enumerate(in_specs) if isinstance(spec, Held)]
        held_out = [(i, spec) for i, spec in enumerate(out_specs) if isinstance(spec, Held)]
        held_types = [args[i].dtype for i, _ in held_in] + [out_shape[i].dtype for i, _ in held_out]
        in_specs = [ANY if isinstance(spec, Held) else spec for spec in in_specs]
        out_specs = [ANY if isinstance(spec, Held) else spec for spec in out_specs]
        args, in_specs, out_specs, out_shape = list(args), list(in_specs), list(out_specs), list(out_shape)
        alias, scratch = dict(alias or {}), list(scratch)
        own_scratch = len(scratch)
        scratch += [pltpu.VMEM(spec.dims, kind) for (_, spec), kind in zip(held_in + held_out, held_types)]
        if held_types:
            scratch.append(pltpu.SemaphoreType.DMA((len(held_types),)))
        spans = []
        for stage in stages:
            ins, outs = len(args), len(out_shape)
            alias.update({ins + i: outs + o for i, o in stage.alias.items()})
            args += stage.ins
            out_shape += stage.out
            spans.append((ins, len(args), outs, len(out_shape)))
        in_specs += [ANY] * (len(args) - own_in)
        out_specs += [ANY] * (len(out_shape) - own_out)
        more = {}
        if stages:
            count = sum(stage.count for stage in stages)
            scratch += [pltpu.SemaphoreType.DMA((count,)), pltpu.SemaphoreType.DMA((count,))]
            more = dict(collective_id=next(self.ids), has_side_effects=True)
            scratch += [pltpu.VMEM(dims, BF16) for stage in stages for dims in stage.bounce]
        summed = [stage for stage in stages if getattr(stage, "scratch", None)]
        if summed:
            scratch += [pltpu.VMEM(dims, BF16) for stage in summed for dims in stage.scratch]
            scratch.append(pltpu.SemaphoreType.DMA((4 * len(summed),)))
        offsets = {o if isinstance(o, tuple) else ("col", o % self.ring.size) for stage in stages for o in stage.offsets}
        offsets = sorted(offsets)
        ring = self.ring

        def device(way):
            if not isinstance(way, tuple):
                way = ("col", way)
            axis, offset = way
            if axis == "col":
                return {axis: ring.owner(offset)}
            return {axis: lax.rem(lax.axis_index(axis) + offset, lax.axis_size(axis))}

        total_in, total_out = len(args), len(out_shape)

        def body(*refs):
            ins, outs, rest = refs[:total_in], refs[total_in : total_in + total_out], refs[total_in + total_out :]
            own_ins, own_outs = list(ins[:own_in]), list(outs[:own_out])
            own, rest = rest[:own_scratch], rest[own_scratch:]
            inward, outward = [], []
            if held_types:
                buffers, sems, rest = rest[: len(held_types)], rest[len(held_types)], rest[len(held_types) + 1 :]
                for k, (at, spec) in enumerate(held_in):
                    inward.append((spec.of(own_ins[at]), buffers[k], sems.at[k]))
                    own_ins[at] = buffers[k]
                for k, (at, spec) in enumerate(held_out, len(held_in)):
                    outward.append((buffers[k], spec.of(own_outs[at]), sems.at[k]))
                    own_outs[at] = buffers[k]
            own = (*own_ins, *own_outs, *own)
            loads = []
            if summed:
                *rest, buffers, sems = (*rest[: -4 * len(summed) - 1], rest[-4 * len(summed) - 1 : -1], rest[-1])
                for stage, (a, b, _, _) in zip(stages, spans):
                    if stage in summed:
                        k = 4 * summed.index(stage)
                        for at, pair in enumerate(stage.loads(ins[a:b], buffers[k : k + 4]), k):
                            loads.append((*pair, sems.at[at]))
            send, receive, *bounce = rest if stages else (None, None)

            def copies(part, which=(False, True)):
                made, at, held = [], 0, 0
                for stage, (a, b, c, d) in zip(stages, spans):
                    for source, target, way in stage.copies(ins[a:b], outs[c:d]):
                        if way is None:
                            if part == "in":
                                made.append(pltpu.make_async_copy(source, bounce[held], receive.at[at]))
                            elif part == "out":
                                made.append(pltpu.make_async_copy(bounce[held], target, send.at[at]))
                            held += 1
                        elif part == "remote" and (stage in summed) in which:
                            made.append(
                                pltpu.make_async_remote_copy(
                                    source, target, send.at[at], receive.at[at], device_id=device(way),
                                    device_id_type=pl.DeviceIdType.MESH,
                                )
                            )
                        at += 1
                return made

            first = last = True
            for axis, size in enumerate(grid):
                first &= pl.program_id(axis) == 0
                last &= pl.program_id(axis) == size - 1
            @pl.when(first)
            def _():
                if stages:
                    barrier = pltpu.get_barrier_semaphore()
                    for offset in offsets:
                        pl.semaphore_signal(
                            barrier, 1, device_id=device(offset), device_id_type=pl.DeviceIdType.MESH
                        )
                for copy in inward:
                    pltpu.make_async_copy(*copy).start()
                if stages:
                    for copy in copies("in"):
                        copy.start()
                    for copy in loads:
                        pltpu.make_async_copy(*copy).start()
                    pl.semaphore_wait(barrier, len(offsets))
                    for copy in copies("remote", (False,)):
                        copy.start()
                    for copy in loads:
                        pltpu.make_async_copy(*copy).wait()
                    for stage in summed:
                        stage.combine()
                    for copy in copies("remote", (True,)):
                        copy.start()
                for copy in inward:
                    pltpu.make_async_copy(*copy).wait()

            kernel(*own)

            @pl.when(first)
            def _():
                for copy in outward:
                    pltpu.make_async_copy(*copy).start()
                if stages:
                    for here, there in zip(copies("in"), copies("out")):
                        here.wait()
                        there.start()

            @pl.when(last)
            def _():
                for copy in outward:
                    pltpu.make_async_copy(*copy).wait()
                if stages:
                    for copy in copies("out") + copies("remote"):
                        copy.wait()

        flops, moved, exps = cost
        made = pl.pallas_call(
            body,
            grid=grid,
            in_specs=in_specs,
            out_specs=out_specs,
            out_shape=out_shape,
            input_output_aliases=alias,
            scratch_shapes=scratch,
            compiler_params=pltpu.CompilerParams(vmem_limit_bytes=VMEM_LIMIT, **more),
            cost_estimate=pl.CostEstimate(flops=int(flops), bytes_accessed=int(moved), transcendentals=int(exps)),
            name=name,
        )(*args)
        for stage, (_, _, c, d) in zip(stages, spans):
            stage.finish(made[c:d])
        return made[:own_out]

    def alone(self, *stages):
        self(lambda *_: None, [], [], [], [], (1,), "exchange", (0, 0, 0), carry=stages)


def lane_repeat(column, width):
    return jnp.concatenate([column] * (width // column.shape[1]), axis=1)


def causal(bk, bq, shift):
    key_at = lax.broadcasted_iota(jnp.int32, (bk, bq), 0)
    query_at = lax.broadcasted_iota(jnp.int32, (bk, bq), 1)
    return key_at + shift <= query_at


def fwd_kernel(q0, bk, q_ref, k_ref, v_ref, seg_q_ref, seg_k_ref, out_ref, log_ref, vt):
    bq, wide = q_ref.shape
    dim = k_ref.shape[1]
    group = wide // dim
    step = pl.program_id(1)
    factor = LOG2E / math.sqrt(dim)

    @pl.when(step == 0)
    def _():
        for j in range(vt.shape[0]):
            vt[j] = v_ref[pl.ds(j * bk, bk), :].astype(F32).T.astype(BF16)

    seg_q = seg_q_ref[...]
    queries = [q_ref[:, h * dim : (h + 1) * dim] for h in range(group)]

    def block(j, carry, shift):
        key_rows = k_ref[pl.ds(pl.multiple_of(j * bk, bk), bk), :]
        seg_k = seg_k_ref[pl.ds(pl.multiple_of(j * bk, bk), bk), :]
        allowed = lane_repeat(seg_k, bq) == seg_q
        if shift is not None:
            allowed &= causal(bk, bq, shift)
        value_cols = vt[j]
        new = []
        for h in range(group):
            total, acc = carry[2 * h], carry[2 * h + 1]
            scores = dot_nt(key_rows, queries[h])
            weights = jnp.where(allowed, jnp.exp2(scores * factor), 0.0)
            total = total + jnp.sum(weights.reshape(bk // 8, 8, bq), axis=0)
            acc = acc + dot_nn(value_cols, weights.astype(BF16))
            new += [total, acc]
        return tuple(new)

    carry = (jnp.zeros((8, bq), F32), jnp.zeros((dim, bq), F32)) * group
    diag = bq // bk
    whole = q0 // bk + step * diag
    carry = lax.fori_loop(0, whole, lambda j, c: block(j, c, None), carry)
    for d in range(diag):
        carry = block(whole + d, carry, d * bk)
    for h in range(group):
        total = jnp.sum(carry[2 * h], axis=0, keepdims=True)
        mixed = carry[2 * h + 1] * (1.0 / total)
        out_ref[:, h * dim : (h + 1) * dim] = mixed.T.astype(BF16)
        log_ref[0, h : h + 1, :] = jnp.log2(total)


def attend(launch, queries, keys, values, seg_row, seg_wide, q0, rows, dim, bq, bk, carry=()):
    width = queries.shape[1]
    span = q0 + rows
    kv = keys.shape[1] // dim
    group = width // dim // kv
    pairs = group * kv * rows * (span - rows / 2)
    base = q0 // bq
    whole = pl.BlockSpec((span, dim), lambda k, i: (0, k))
    return launch(
        functools.partial(fwd_kernel, q0, bk),
        (queries, keys, values, seg_row, seg_wide),
        [
            pl.BlockSpec((bq, group * dim), lambda k, i: (i + base, k)),
            whole,
            whole,
            pl.BlockSpec((1, bq), lambda k, i: (0, i + base)),
            pl.BlockSpec((span, 128), lambda k, i: (0, 0)),
        ],
        [
            pl.BlockSpec((bq, group * dim), lambda k, i: (i, k)),
            pl.BlockSpec((1, group, bq), lambda k, i: (k, 0, i)),
        ],
        [shape((rows, width), BF16), shape((kv, group, rows), F32)],
        (kv, rows // bq),
        "attend",
        (pairs * dim * 8, rows * width * 4, pairs),
        scratch=[pltpu.VMEM((span // bk, dim, bk), BF16)],
        carry=carry,
    )


def bwd_kernel(q0, bk, first, *refs):
    q_ref, k_ref, v_ref, g_ref, o_ref, log_ref, seg_q_ref, seg_k_ref = refs[:8]
    dk_in, dv_in = (None, None) if first else refs[8:10]
    dq_ref, dk_ref, dv_ref, kt = refs[-4:]
    bq, wide = q_ref.shape
    dim = k_ref.shape[1]
    group = wide // dim
    step = pl.program_id(1)
    scale = 1.0 / math.sqrt(dim)
    factor = LOG2E * scale

    @pl.when(step == 0)
    def _():
        for j in range(kt.shape[0]):
            kt[j] = k_ref[pl.ds(j * bk, bk), :].astype(F32).T.astype(BF16)
        if first:
            dk_ref[...] = jnp.zeros_like(dk_ref)
            dv_ref[...] = jnp.zeros_like(dv_ref)
        else:
            dk_ref[...] = dk_in[...]
            dv_ref[...] = dv_in[...]

    seg_q = seg_q_ref[...]
    queries = [q_ref[:, h * dim : (h + 1) * dim] for h in range(group)]
    grads = [g_ref[:, h * dim : (h + 1) * dim] for h in range(group)]
    logs = [log_ref[0, h : h + 1, :] for h in range(group)]
    inner = []
    for h in range(group):
        product = grads[h].astype(F32) * o_ref[:, h * dim : (h + 1) * dim].astype(F32)
        inner.append(jnp.sum(product.T, axis=0, keepdims=True))

    def block(j, carry, shift):
        at = pl.ds(pl.multiple_of(j * bk, bk), bk)
        key_rows = k_ref[at, :]
        value_rows = v_ref[at, :]
        allowed = lane_repeat(seg_k_ref[at, :], bq) == seg_q
        if shift is not None:
            allowed &= causal(bk, bq, shift)
        key_cols = kt[j]
        new = []
        dk, dv = dk_ref[at, :], dv_ref[at, :]
        for h in range(group):
            scores = dot_nt(key_rows, queries[h])
            probs = jnp.where(allowed, jnp.exp2(scores * factor - logs[h]), 0.0)
            grad_probs = dot_nt(value_rows, grads[h])
            grad_scores = (probs * (grad_probs - inner[h])).astype(BF16)
            dv = dv + dot_nn(probs.astype(BF16), grads[h])
            dk = dk + dot_nn(grad_scores, queries[h])
            new.append(carry[h] + dot_nn(key_cols, grad_scores))
        dk_ref[at, :] = dk
        dv_ref[at, :] = dv
        return tuple(new)

    carry = (jnp.zeros((dim, bq), F32),) * group
    diag = bq // bk
    whole = q0 // bk + step * diag
    carry = lax.fori_loop(0, whole, lambda j, c: block(j, c, None), carry)
    for d in range(diag):
        carry = block(whole + d, carry, d * bk)
    for h in range(group):
        dq_ref[:, h * dim : (h + 1) * dim] = (carry[h] * scale).T


def attend_back(launch, queries, keys, values, grads, mixed, logs, seg_row, seg_wide, q0, dim, bq, bk, sums, carry=()):
    rows, width = grads.shape
    span = q0 + rows
    kv = keys.shape[1] // dim
    group = width // dim // kv
    pairs = group * kv * rows * (span - rows / 2)
    base = q0 // bq
    whole = pl.BlockSpec((span, dim), lambda k, i: (0, k))
    part = pl.BlockSpec((bq, group * dim), lambda k, i: (i, k))
    more = [] if sums is None else list(sums)
    return launch(
        functools.partial(bwd_kernel, q0, bk, sums is None),
        (queries, keys, values, grads, mixed, logs, seg_row, seg_wide, *more),
        [
            pl.BlockSpec((bq, group * dim), lambda k, i: (i + base, k)),
            whole,
            whole,
            part,
            part,
            pl.BlockSpec((1, group, bq), lambda k, i: (k, 0, i)),
            pl.BlockSpec((1, bq), lambda k, i: (0, i + base)),
            pl.BlockSpec((span, 128), lambda k, i: (0, 0)),
        ]
        + [whole] * len(more),
        [part, whole, whole],
        [shape((rows, width), F32), shape((span, kv * dim), F32), shape((span, kv * dim), F32)],
        (kv, rows // bq),
        "attend_back",
        (pairs * dim * 20, rows * width * 10, pairs),
        scratch=[pltpu.VMEM((span // bk, dim, bk), BF16)],
        carry=carry,
    )


def qkv_kernel(kv, x_ref, gain_ref, w_ref, gq_ref, gk_ref, cos_ref, sin_ref, *refs):
    normed_ref, scale_ref, proj_ref, q_ref, k_ref, v_ref = refs[-6:]
    dim = gq_ref.shape[1]
    heads = q_ref.shape[1] // dim
    values = x_ref[...].astype(F32)
    scale = row_scale(values)
    normed = (values * scale * gain_ref[...]).astype(BF16)
    normed_ref[...] = normed
    scale_ref[...] = scale
    projected = dot_nn(normed, w_ref[...])
    cosine, sine = cos_ref[...], sin_ref[...]
    wide = (heads + kv) * dim
    proj_ref[...] = projected[:, :wide]
    for h in range(heads + kv):
        part = projected[:, h * dim : (h + 1) * dim]
        gain = gq_ref[...] if h < heads else gk_ref[...]
        part = part * row_scale(part) * gain
        turned = (part * cosine + swap(part) * sine).astype(BF16)
        if h < heads:
            q_ref[:, h * dim : (h + 1) * dim] = turned
        else:
            k_ref[:, (h - heads) * dim : (h - heads + 1) * dim] = turned
    v_ref[...] = projected[:, wide:].astype(BF16)


def project_qkv(launch, x, gain, weights, cols, gain_q, gain_k, cosine, sine, kv, carry=()):
    rows, width = x.shape
    dim = gain_q.shape[1]
    heads = cols // dim - 2 * kv
    bt = tile_of(rows, 512)
    wide = (heads + kv) * dim

    def part(w):
        return pl.BlockSpec((bt, w), lambda i: (i, 0))

    return launch(
        functools.partial(qkv_kernel, kv),
        (x, gain, weights, gain_q, gain_k, cosine, sine),
        [
            part(width),
            resident((1, width)),
            Held((width, cols)),
            resident((1, dim)),
            resident((1, dim)),
            part(dim),
            part(dim),
        ],
        [part(width), part(1), part(wide), part(heads * dim), part(kv * dim), part(kv * dim)],
        [
            shape((rows, width), BF16),
            shape((rows, 1), F32),
            shape((rows, wide), F32),
            shape((rows, heads * dim), BF16),
            shape((rows, kv * dim), BF16),
            shape((rows, kv * dim), BF16),
        ],
        (rows // bt,),
        "project_qkv",
        (2 * rows * width * cols, rows * width * 4 + width * cols * 2, 0),
        carry=carry,
    )


def mlp_kernel(x_ref, gain_ref, wg_ref, wu_ref, wd_ref, cot_ref, *refs):
    normed_ref, scale_ref, active_ref, gg_ref, gu_ref = refs[-5:]

    @pl.when(pl.program_id(1) == 0)
    def _():
        values = x_ref[...].astype(F32)
        scale = row_scale(values)
        normed_ref[...] = (values * scale * gain_ref[...]).astype(BF16)
        scale_ref[...] = scale

    normed = normed_ref[...]
    gate = dot_nn(normed, wg_ref[...])
    up = dot_nn(normed, wu_ref[...])
    grad = dot_nn(cot_ref[...], wd_ref[...])
    sig = jax.nn.sigmoid(gate)
    silu = gate * sig
    active_ref[...] = (silu * up).astype(BF16)
    gu_ref[...] = (grad * silu).astype(BF16)
    gg_ref[...] = (grad * up * (sig + silu * (1.0 - sig))).astype(BF16)


def mlp(launch, x, gain, weights, cot, chunk, total, kept, carry=()):
    rows, width = x.shape
    hidden = weights.shape[1] // 3
    bn = tile_of(hidden, 512)
    tiles = hidden // bn
    more = [] if kept is None else list(kept)
    tile = pl.BlockSpec((rows, bn), lambda i, j: (chunk, j))
    low = shape((total, hidden), BF16)
    return launch(
        mlp_kernel,
        (x, gain, weights, weights, weights, cot, *more),
        [
            Held((rows, width)),
            resident((1, width)),
            pl.BlockSpec((width, bn), lambda i, j: (0, j)),
            pl.BlockSpec((width, bn), lambda i, j: (0, j + tiles)),
            pl.BlockSpec((width, bn), lambda i, j: (0, j + 2 * tiles)),
            Held((rows, width)),
        ]
        + [ANY] * len(more),
        [Held((rows, width), chunk * rows), pl.BlockSpec((rows, 1), lambda i, j: (0, 0)), tile, tile, tile],
        [shape((total, width), BF16), shape((rows, 1), F32), low, low, low],
        (1, tiles),
        "mlp",
        (6 * rows * width * hidden, rows * (width + hidden) * 6 + 6 * width * hidden, rows * hidden),
        alias={6: 0, 7: 2, 8: 3, 9: 4} if more else None,
        carry=carry,
    )


def mid_kernel(gg_ref, gu_ref, w_ref, v_ref, scale_ref, gain_ref, part_ref, inner_ref, gain_out):
    hidden = gg_ref.shape[1]
    partial = dot_nt(gg_ref[...], w_ref[:, :hidden]) + dot_nt(gu_ref[...], w_ref[:, hidden:])
    part_ref[...] = partial.astype(BF16)
    product = partial * v_ref[...].astype(F32)
    gain_out[0] = jnp.sum(product * scale_ref[...], axis=0, keepdims=True)
    inner = row_of(jnp.sum(product * gain_ref[...], axis=1, keepdims=True))

    @pl.when(pl.program_id(1) == 0)
    def _():
        inner_ref[0] = inner

    @pl.when(pl.program_id(1) > 0)
    def _():
        inner_ref[0] += inner


def back_mid(launch, gg, gu, weights, values, scale, gain, chunk, carry=()):
    rows, width = values.shape
    hidden = gg.shape[1]
    bn = tile_of(width, 512)
    return launch(
        mid_kernel,
        (gg, gu, weights, values, scale, gain),
        [
            Held((rows, hidden), chunk * rows),
            Held((rows, hidden), chunk * rows),
            pl.BlockSpec((bn, 2 * hidden), lambda i, j: (j, 0)),
            pl.BlockSpec((rows, bn), lambda i, j: (0, j)),
            pl.BlockSpec((rows, 1), lambda i, j: (0, 0)),
            pl.BlockSpec((1, bn), lambda i, j: (0, j)),
        ],
        [
            pl.BlockSpec((rows, bn), lambda i, j: (0, j)),
            pl.BlockSpec((1, 1, rows), lambda i, j: (0, 0, 0)),
            pl.BlockSpec((1, 1, bn), lambda i, j: (0, 0, j)),
        ],
        [shape((rows, width), BF16), shape((1, 1, rows), F32), shape((1, 1, width), F32)],
        (1, width // bn),
        "back_mid",
        (4 * rows * width * hidden, rows * (width + hidden) * 4 + 4 * width * hidden, 0),
        carry=carry,
    )


def qkv_back_kernel(
    kv, dq_ref, dk_ref, dv_ref, proj_ref, cos_ref, sin_ref, gq_ref, gk_ref, w_ref, v_ref, scale_ref, gain_ref, *refs
):
    low_ref, part_ref, inner_ref, gain_out, gq_out, gk_out = refs[-6:]
    dim = gq_ref.shape[1]
    heads = dq_ref.shape[1] // dim
    wide = (heads + kv) * dim

    @pl.when(pl.program_id(1) == 0)
    def _():
        cosine, sine = cos_ref[...], sin_ref[...]
        sums = [jnp.zeros((1, dim), F32), jnp.zeros((1, dim), F32)]
        for h in range(heads + kv):
            is_key = h >= heads
            if is_key:
                grad = dk_ref[:, (h - heads) * dim : (h - heads + 1) * dim] * (1.0 / math.sqrt(dim))
            else:
                grad = dq_ref[:, h * dim : (h + 1) * dim]
            grad = grad * cosine + swap(grad * sine)
            value = proj_ref[:, h * dim : (h + 1) * dim]
            scale = row_scale(value)
            sums[is_key] += jnp.sum(grad * value * scale, axis=0, keepdims=True)
            weighted = grad * (gk_ref[...] if is_key else gq_ref[...])
            mean = jnp.mean(weighted * value, axis=-1, keepdims=True)
            low_ref[:, h * dim : (h + 1) * dim] = (scale * (weighted - value * scale * scale * mean)).astype(BF16)
        low_ref[:, wide:] = dv_ref[...].astype(BF16)
        gq_out[0] = sums[0]
        gk_out[0] = sums[1]

    partial = dot_nt(low_ref[...], w_ref[...])
    part_ref[...] = partial.astype(BF16)
    product = partial * v_ref[...].astype(F32)
    gain_out[0] = jnp.sum(product * scale_ref[...], axis=0, keepdims=True)
    inner = row_of(jnp.sum(product * gain_ref[...], axis=1, keepdims=True))

    @pl.when(pl.program_id(1) == 0)
    def _():
        inner_ref[0] = inner

    @pl.when(pl.program_id(1) > 0)
    def _():
        inner_ref[0] += inner


def back_qkv(launch, dq, dk, dv, proj, cosine, sine, gain_q, gain_k, weights, cols, values, scale, gain, kv, chunk, kept, carry=()):
    total, width = values.shape
    rows = dq.shape[0]
    dim = gain_q.shape[1]
    bt = rows
    bn = tile_of(width, 512)
    base = chunk

    def here(w):
        return Held((rows, w))

    def there(w):
        return Held((rows, w), chunk * rows)

    row = pl.BlockSpec((1, 1, dim), lambda i, j: (i, 0, 0))
    more = [] if kept is None else [kept]
    return launch(
        functools.partial(qkv_back_kernel, kv),
        (dq, dk, dv, proj, cosine, sine, gain_q, gain_k, weights, values, scale, gain, *more),
        [
            here(dq.shape[1]),
            there(dk.shape[1]),
            there(dv.shape[1]),
            there(proj.shape[1]),
            there(dim),
            there(dim),
            resident((1, dim)),
            resident((1, dim)),
            pl.BlockSpec((bn, cols), lambda i, j: (j, 0)),
            pl.BlockSpec((bt, bn), lambda i, j: (i + base, j)),
            pl.BlockSpec((rows, 1), lambda i, j: (chunk, 0)),
            pl.BlockSpec((1, bn), lambda i, j: (0, j)),
        ]
        + [ANY] * len(more),
        [
            there(cols),
            pl.BlockSpec((bt, bn), lambda i, j: (i, j)),
            pl.BlockSpec((1, 1, bt), lambda i, j: (i, 0, 0)),
            pl.BlockSpec((1, 1, bn), lambda i, j: (i, 0, j)),
            row,
            row,
        ],
        [
            shape((total, cols), BF16),
            shape((rows, width), BF16),
            shape((rows // bt, 1, bt), F32),
            shape((rows // bt, 1, width), F32),
            shape((rows // bt, 1, dim), F32),
            shape((rows // bt, 1, dim), F32),
        ],
        (rows // bt, width // bn),
        "back_qkv",
        (2 * rows * width * cols, rows * width * 4 + rows * cols * 10, 0),
        alias={12: 0} if more else None,
        carry=carry,
    )


def pair_kernel(low_ref, high_ref, first_ref, second_ref, out_ref):
    out_ref[...] = (dot_tn(low_ref[...], first_ref[...]) + dot_tn(high_ref[...], second_ref[...])).astype(BF16)


def weight_grad_pair(launch, lefts, rights, rows_at, carry=()):
    rows, cols = rights[0].shape
    width = lefts[0].shape[1]
    bm = next(size for size in (1024, 768, 512, 256, 128) if width % size == 0)
    bn = tile_of(cols, 512)

    def left(k):
        return pl.BlockSpec((rows, bm), lambda i, j: (rows_at[k], i))

    right = pl.BlockSpec((rows, bn), lambda i, j: (0, j))
    return launch(
        pair_kernel,
        (*lefts, *rights),
        [left(0), left(1), right, right],
        [pl.BlockSpec((bm, bn), lambda i, j: (i, j))],
        [shape((width, cols), BF16)],
        (width // bm, cols // bn),
        "weight_grad",
        (4 * rows * width * cols, rows * (width + cols) * 4 + width * cols * 2, 0),
        carry=carry,
    )[0]


def grad_kernel(tiles, left_ref, *refs):
    rights, out_ref = refs[:-1], refs[-1]
    for k, right in enumerate(rights):
        @pl.when(pl.program_id(1) // tiles == k)
        def _():
            out_ref[...] = dot_tn(left_ref[...], right[...]).astype(BF16)


def weight_grad(launch, left, *rights, carry=()):
    rows, width = left.shape
    cols = rights[0].shape[1]
    bm = next(size for size in (1024, 768, 512, 256, 128) if width % size == 0)
    bn = next(size for size in (512, 384, 256, 128) if cols % size == 0)
    tiles = cols // bn

    def part(k):
        return pl.BlockSpec((rows, bn), lambda i, j: (0, jnp.clip(j - k * tiles, 0, tiles - 1)))

    return launch(
        functools.partial(grad_kernel, tiles),
        (left, *rights),
        [pl.BlockSpec((rows, bm), lambda i, j: (0, i))] + [part(k) for k in range(len(rights))],
        [pl.BlockSpec((bm, bn), lambda i, j: (i, j))],
        [shape((width, cols * len(rights)), BF16)],
        (width // bm, tiles * len(rights)),
        "weight_grad",
        (2 * rows * width * cols * len(rights), rows * (width + cols) * 2 + width * cols * 4, 0),
        carry=carry,
    )[0]


def out_kernel(left_ref, right_ref, out_ref):
    out_ref[...] = dot_nt(left_ref[...], right_ref[...]).astype(BF16)


def project_out(launch, left, weights, chunk, rows, carry=()):
    width, hidden = weights.shape[0], left.shape[1]
    bn = tile_of(width, 512)
    last = weights.shape[1] // hidden - 1
    return launch(
        out_kernel,
        (left, weights),
        [Held((rows, hidden), chunk * rows), pl.BlockSpec((bn, hidden), lambda i, j: (j, last))],
        [pl.BlockSpec((rows, bn), lambda i, j: (0, j))],
        [shape((rows, width), BF16)],
        (1, width // bn),
        "project_out",
        (2 * rows * width * hidden, rows * (width + hidden) * 2 + width * hidden * 2, 0),
        carry=carry,
    )[0]


def mix_kernel(left_ref, right_ref, out_ref):
    out_ref[...] = dot_nn(left_ref[...], right_ref[...]).astype(BF16)


def grad_mix(launch, grads, weights, cols):
    rows, width = grads.shape
    bt = tile_of(rows, 512)
    return launch(
        mix_kernel,
        (grads, weights),
        [pl.BlockSpec((bt, width), lambda i: (i, 0)), Held((width, cols), 0, weights.shape[1] - cols)],
        [pl.BlockSpec((bt, cols), lambda i: (i, 0))],
        [shape((rows, cols), BF16)],
        (rows // bt,),
        "grad_mix",
        (2 * rows * width * cols, (rows * width + rows * cols + width * cols) * 2, 0),
    )[0]


def tables_kernel(position_ref, segment_ref, inverse_ref, cos_ref, sin_ref, wide_ref):
    def column(row):
        return jnp.broadcast_to(row.astype(F32), (128, row.shape[1])).T

    angle = column(position_ref[...]) * inverse_ref[...]
    half = lax.broadcasted_iota(jnp.int32, angle.shape, 1) < angle.shape[1] // 2
    sine = jnp.sin(angle)
    cos_ref[...] = jnp.cos(angle)
    sin_ref[...] = jnp.where(half, -sine, sine)
    wide_ref[...] = column(segment_ref[...]).astype(jnp.int32)


def tables(launch, positions, segments, dim, carry=()):
    rows = positions.shape[0]
    bt = tile_of(rows, 512)
    inverse = THETA ** (-(jnp.arange(dim // 2, dtype=F32) * 2.0 / dim))
    row = pl.BlockSpec((1, bt), lambda i: (0, i))
    wide = pl.BlockSpec((bt, 128), lambda i: (i, 0))
    return launch(
        tables_kernel,
        (positions[None], segments[None], jnp.concatenate([inverse, inverse])[None]),
        [row, row, resident((1, dim))],
        [wide, wide, wide],
        [shape((rows, dim), F32), shape((rows, dim), F32), shape((rows, 128), jnp.int32)],
        (rows // bt,),
        "tables",
        (0, rows * dim * 12, rows * dim * 2),
        carry=carry,
    )


def side(first, low, high):
    return jnp.where(first, low[...].astype(F32), high[...].astype(F32))


def grad_block(factor, first, base, term, t0, t1, t2, t3, values, scale, inner, others, gain):
    row = inner[0] + jnp.sum(others[:, 0, 0, :], axis=0, keepdims=True)
    inner = jnp.broadcast_to(row, (128, row.shape[1])).T[:, :1]
    scales = scale[...]
    total = term[...].astype(F32) + side(first, t0, t1) + side(first, t2, t3)
    return base[...].astype(F32) + scales * (
        total * gain[...] - values[...].astype(F32) * (scales * scales * inner * factor)
    )


def grad_operands(base, summed, values, scale, gain, base_at, values_at, scale_at, start=0):
    local = base.shape[1]
    bt = summed.half // 2

    def step(i):
        return jnp.clip(i - start, 0, 3)

    def at(chunk, wide):
        return pl.BlockSpec((bt, wide), lambda i: (step(i) + 4 * chunk, 0))

    mine = pl.BlockSpec((bt, local), lambda i: (step(i), lax.axis_index("col")))
    low = pl.BlockSpec((bt, local), lambda i: (jnp.minimum(step(i), 1), 0))
    high = pl.BlockSpec((bt, local), lambda i: (jnp.maximum(step(i) - 2, 0), 0))
    others = summed.inner_others
    args = (base, summed.partial, *summed.pieces(), values, scale, summed.inner, others, gain[None])
    specs = [at(base_at, local), mine, low, high, low, high, at(values_at, local), at(scale_at, 1)]
    specs += [
        pl.BlockSpec((1, 1, bt), lambda i: (0, 0, step(i))),
        pl.BlockSpec((others.shape[0], 1, 1, bt), lambda i: (0, 0, 0, step(i))),
        resident((1, local)),
    ]
    return args, specs, at


def hidden_kernel(factor, *refs):
    grad = grad_block(factor, pl.program_id(0) < 2, *refs[:-2])
    refs[-2][...] = grad
    refs[-1][...] = grad.astype(BF16)


def hidden_grad(launch, base, summed, values, scale, gain, chunk):
    args, specs, at = grad_operands(base, summed, values, scale, gain, chunk, 0, 0)
    rows, local = summed.rows, base.shape[1]
    return launch(
        functools.partial(hidden_kernel, 1.0 / (local * launch.ring.size)),
        args,
        specs,
        [at(0, local), at(0, local)],
        [shape((rows, local), F32), shape((rows, local), BF16)],
        (4,),
        "hidden_grad",
        (0, rows * local * 18, 0),
    )


def settle_kernel(*refs):
    step = pl.program_id(0)
    output = refs[-1]

    def one(hidden, down, p0, p1, p2, p3):
        first = step % 2 == 0
        output[...] = (hidden[...] + (down[...].astype(F32) + side(first, p0, p1) + side(first, p2, p3))).astype(BF16)

    pl.when(step < 2)(lambda: one(*refs[:6]))
    pl.when(step >= 2)(lambda: one(*refs[6:12]))


def settle(launch, hidden, sums, carry=()):
    rows, local = hidden[0].shape
    bt = rows // 2
    args, specs = [], []
    for c in (0, 1):
        here = pl.BlockSpec((bt, local), lambda i, c=c: (jnp.clip(i - 2 * c, 0, 1), 0))
        mine = pl.BlockSpec((bt, local), lambda i, c=c: (jnp.clip(i - 2 * c, 0, 1), lax.axis_index("col")))
        args += [hidden[c], sums[c].partial, *sums[c].pieces()]
        specs += [here, mine] + [Held((bt, local))] * 4
    return launch(
        settle_kernel,
        args,
        specs,
        [pl.BlockSpec((bt, local), lambda i: (i, 0))],
        [shape((2 * rows, local), BF16)],
        (4,),
        "settle",
        (0, rows * local * 24, 0),
        carry=carry,
    )[0]


def last_kernel(factor, *refs):
    step = pl.program_id(0)
    count = (len(refs) - 1) // 2

    @pl.when(step < 4)
    def _():
        refs[-1][...] = grad_block(factor, step < 2, *refs[:count])

    @pl.when(step >= 4)
    def _():
        refs[-1][...] = grad_block(factor, step < 6, *refs[count:-1])


def settle_last(launch, grad_hidden, sums, tokens, scale, gain, carry=()):
    args, specs = [], []
    for c in (0, 1):
        more, more_specs, _ = grad_operands(grad_hidden[c], sums[c], tokens, scale, gain, 0, c, c, 4 * c)
        args += more
        specs += more_specs
    total, local = tokens.shape
    return launch(
        functools.partial(last_kernel, 1.0 / (local * launch.ring.size)),
        args,
        specs,
        [pl.BlockSpec((total // 8, local), lambda i: (i, 0))],
        [shape((total, local), F32)],
        (8,),
        "settle_last",
        (0, total * local * 24, 0),
        carry=carry,
    )[0]


def after(value, *others):
    return lax.optimization_barrier((value, *jax.tree.leaves(others)))[0]


def body(
    tokens,
    segments,
    positions,
    gain_attn,
    w_query,
    key_weight_matrix,
    value_weight_matrix,
    gain_query,
    gain_key,
    w_out,
    gain_mlp,
    w_gate,
    w_up,
    w_down,
    cotangent,
):
    total, local = tokens.shape
    dim = gain_query.shape[0]
    query_cols, key_cols = w_query.shape[1], key_weight_matrix.shape[1]
    kv = key_cols // dim
    hidden_units = w_gate.shape[1]
    ring = Ring(lax.axis_size("col"))
    launch = Launcher(ring)
    width = local * ring.size
    rows = total // 2
    parts = [slice(0, rows), slice(rows, total)]
    offset = lax.axis_index("col") * local
    gain_attn_local = lax.dynamic_slice_in_dim(gain_attn, offset, local)
    gain_mlp_local = lax.dynamic_slice_in_dim(gain_mlp, offset, local)
    gain_q, gain_k = gain_query[None], gain_key[None]
    bq = tile_of(rows, 512)

    def gathered(weights, axis):
        return lax.all_gather(weights, "row", axis=axis, tiled=True)

    def scattered(partial, axis):
        return lax.psum_scatter(partial, "row", scatter_dimension=axis, tiled=True)

    def carried(*stages):
        for stage in stages:
            for _ in range(ring.stages - 2):
                launch.alone(stage)

    pair = lambda: [None] * 2
    mixed, logs, hidden, mid_low, scale_mid = pair(), pair(), pair(), pair(), pair()
    get_cot, get_mid, get_grad = pair(), pair(), pair()
    sum_out, sum_down, sum_mid, sum_in = pair(), pair(), pair(), pair()
    gain_mlp_part, grad_hidden, gains_in = pair(), pair(), pair()

    qkv_cols = query_cols + 2 * key_cols
    w_attn = gathered(jnp.concatenate([w_query, key_weight_matrix, value_weight_matrix, w_out.T], axis=1), 0)

    get_tok = Gather(ring, tokens, 0, total)
    launch.alone(get_tok)
    w_mlp = gathered(jnp.concatenate([after(w_gate, get_tok.full), w_up, w_down.T], axis=1), 0)
    seg_row = segments[None]
    for _ in range(ring.stages - 2):
        launch.alone(get_tok)
    cosine, sine, seg_wide = tables(launch, positions, segments, dim, [get_tok])
    x_full = get_tok.full

    for c in (0, 1):
        get_cot[c] = Gather(ring, cotangent, c * rows, rows, split=c == 0)
    normed, scale_attn, proj, queries, keys, values = project_qkv(
        launch, x_full, gain_attn[None], w_attn, qkv_cols, gain_q, gain_k, cosine, sine, kv, carry=[get_cot[1]]
    )

    def attention(c, at, carry):
        mixed[c], logs[c] = attend(
            launch, queries, keys, values, after(seg_row, at), seg_wide, c * rows, rows, dim, bq, bq, carry=carry
        )
        return logs[c]

    def start_out(c, at, carry):
        partial = project_out(launch, after(mixed[c], at), w_attn, 0, rows, carry=carry)
        sum_out[c] = Scatter(ring, partial)
        return partial

    def end_out(c):
        hidden[c] = tokens[parts[c]].astype(F32) + sum_out[c].total()
        mid_low[c] = hidden[c].astype(BF16)
        get_mid[c] = Gather(ring, mid_low[c], 0, rows)

    carried(get_cot[1])
    at = attention(1, normed, [get_cot[1]])
    at = start_out(1, at, [get_cot[0]])
    at = attention(0, at, [sum_out[1]])
    carried(sum_out[1])
    launch.alone(sum_out[1])
    end_out(1)
    launch.alone(get_mid[1])
    carried(get_mid[1])
    start_out(0, get_mid[1].full, [get_mid[1]])
    launch.alone(sum_out[0])
    carried(sum_out[0])
    launch.alone(sum_out[0], get_cot[0])
    end_out(0)

    def feed_forward(c, kept, at, carry):
        nm, scale_mid[c], *rest = mlp(
            launch, get_mid[c].full, after(gain_mlp[None], at), w_mlp, get_cot[c].full, c, total, kept,
            carry=carry,
        )
        return (nm, *rest)

    def back_middle(c, kept, at, carry):
        partial, inner, gain_part = back_mid(
            launch, kept[2], kept[3], w_mlp, get_mid[c].full, scale_mid[c], after(gain_mlp[None], at), c, carry=carry
        )
        gain_mlp_part[c] = jnp.sum(gain_part, axis=(0, 1))
        sum_mid[c] = Scatter(ring, partial, inner)
        return partial

    def end_mid(c):
        grad_hidden[c], low = hidden_grad(
            launch, cotangent, sum_mid[c], mid_low[c], scale_mid[c], gain_mlp_local, c
        )
        get_grad[c] = Gather(ring, low, 0, rows)
        return low

    def start_down(c, active, at, carry=()):
        partial = project_out(launch, after(active, at), w_mlp, c, rows, carry=carry)
        sum_down[c] = Scatter(ring, partial, split=True)
        return partial

    kept = feed_forward(1, None, get_mid[1].full, [get_mid[0]])
    carried(get_mid[0], get_cot[0])
    at = start_down(1, kept[1], kept[0], [get_mid[0]])
    at = back_middle(1, kept, at, [get_cot[0], sum_down[1]])
    kept = feed_forward(0, kept, at, [sum_mid[1]])
    normed_mid, active, grad_gate, grad_up = kept
    carried(sum_mid[1])
    partial = weight_grad_pair(
        launch, (active, active), (get_cot[0].full, get_cot[1].full), (0, 1), carry=[sum_mid[1], sum_down[1].near]
    )
    rs_down = scattered(partial, 1)
    low = end_mid(1)
    at = back_middle(0, kept, (partial, low), [get_grad[1]])
    carried(get_grad[1])
    partial = weight_grad(launch, after(normed_mid, at), grad_gate, grad_up, carry=[get_grad[1], sum_mid[0]])
    rs_gate_up = scattered(partial, 0)
    carried(sum_mid[0])
    at = start_down(0, active, partial, [sum_mid[0]])
    low = end_mid(0)

    def mix(c):
        return jnp.dot(get_grad[c].full, w_attn[:, qkv_cols:], preferred_element_type=F32).astype(BF16)

    def attention_back(c, grad_mixed, sums, at, carry):
        return attend_back(
            launch, queries, keys, values, grad_mixed, mixed[c], logs[c], after(seg_row, at), seg_wide, c * rows, dim,
            bq, bq, sums, carry=carry,
        )

    def projection_back(c, grads, low_all, at, carry):
        low_all, partial, inner, *gains_in[c] = back_qkv(
            launch, *grads, proj, cosine, sine, gain_q, gain_k, w_attn, qkv_cols, x_full, scale_attn, after(gain_attn[None], at),
            kv, c, low_all, carry=carry,
        )
        sum_in[c] = Scatter(ring, partial, inner, split=True)
        return low_all, partial

    grads = attention_back(1, mix(1), None, (at, low), [get_grad[0], sum_down[0]])
    carried(get_grad[0])
    low_all, at = projection_back(1, grads, None, None, [get_grad[0], sum_down[0].near])
    grad_mixed = mix(0)
    early = Share("col", *gains_in[1], (gain_mlp_part[0] + gain_mlp_part[1])[None])
    grads = attention_back(0, grad_mixed, grads[1:], (at, rs_down), [sum_in[1], early])
    carried(sum_down[1])
    grad_out = weight_grad_pair(
        launch, (after(mixed[0], grads[0]), mixed[1]), (get_grad[0].full, get_grad[1].full), (0, 0), carry=[sum_down[1]]
    )
    rs_out = scattered(grad_out, 1)
    carried(sum_in[1], sum_down[0])
    low_all, at = projection_back(0, grads, low_all, grad_out, [sum_in[1], sum_down[0]])
    gains = Share("col", *gains_in[0])
    partial = weight_grad(launch, after(normed, at, rs_gate_up), low_all, carry=[sum_in[0], sum_in[1].near, gains])

    grad_qkv = scattered(after(partial, rs_out), 0)
    gains = jnp.concatenate([part.reshape(-1) for part in (*gains.sums, *early.sums)])[None]
    gains = Share("row", gains)
    carried(sum_in[0])
    output = settle(launch, hidden, sum_down, [sum_in[0], sum_in[0].near])
    grad_tokens = settle_last(launch, grad_hidden, sum_in, tokens, scale_attn, gain_attn_local, [gains])
    sum_attn, sum_q, sum_k, more_attn, more_q, more_k, sum_mlp = jnp.split(
        gains.sums[0][0], list(itertools.accumulate([width, dim, dim, width, dim, dim]))
    )
    return (
        output,
        grad_tokens,
        sum_attn + more_attn,
        grad_qkv[:, :query_cols].astype(F32),
        grad_qkv[:, query_cols : query_cols + key_cols].astype(F32),
        grad_qkv[:, query_cols + key_cols :].astype(F32),
        sum_q + more_q,
        sum_k + more_k,
        rs_out.astype(F32),
        sum_mlp,
        rs_gate_up[:, :hidden_units].astype(F32),
        rs_gate_up[:, hidden_units:].astype(F32),
        rs_down.astype(F32),
    )


def solution(mesh):
    both, split = P("row", "col"), P("col", "row")
    in_specs = (both, P("row"), P("row"), P(), both, both, both, P(), P(), split, P(), both, both, split, both)
    out_specs = (both, both, P(), both, both, both, P(), P(), split, P(), both, both, split)
    return jax.shard_map(body, mesh=mesh, in_specs=in_specs, out_specs=out_specs, check_vma=False)
```

```python
import functools
import itertools
import math

import jax
import jax.numpy as jnp
from jax import lax
from jax.experimental import pallas as pl
from jax.experimental.pallas import tpu as pltpu
from jax.sharding import PartitionSpec as P

BF16 = jnp.bfloat16
F32 = jnp.float32
EPS = 1e-06
THETA = 1000000.0
LOG2E = 1.4426950408889634
VMEM_LIMIT = 60 * 1024 * 1024
ANY = pl.BlockSpec(memory_space=pl.ANY)


def dot_nt(left, right):
    return lax.dot_general(left, right, (((1,), (1,)), ((), ())), preferred_element_type=F32)


def dot_nn(left, right):
    return jnp.dot(left, right, preferred_element_type=F32)


def dot_tn(left, right):
    return lax.dot_general(left, right, (((0,), (0,)), ((), ())), preferred_element_type=F32)


def shape(dims, dtype):
    return jax.ShapeDtypeStruct(tuple(dims), dtype)


def resident(dims):
    return pl.BlockSpec(dims, lambda *_: (0,) * len(dims), pipeline_mode=pl.Buffered(1))


def held(dims, index):
    return pl.BlockSpec(dims, index, pipeline_mode=pl.Buffered(1))


def tile_of(size, most):
    tile = most
    while size % tile:
        tile //= 2
    return tile


def swap(values):
    half = values.shape[-1] // 2
    return jnp.concatenate([values[:, half:], values[:, :half]], axis=1)


def row_scale(values):
    return lax.rsqrt(jnp.mean(values * values, axis=-1, keepdims=True) + EPS)


def row_of(column):
    return jnp.broadcast_to(column, (column.shape[0], 128)).T[:1]


class Held:
    def __init__(self, dims, row=0, col=0):
        self.dims, self.row, self.col = dims, row, col

    def of(self, ref):
        return ref.at[pl.ds(self.row, self.dims[0]), pl.ds(self.col, self.dims[1])]


class Ring:
    def __init__(self, size):
        self.size = size
        self.stages = size // 2

    def place(self, index):
        half = self.size // 2
        return jnp.where(index < half, index, self.size + half - 1 - index)

    def owner(self, offset):
        return self.place(lax.rem(self.place(lax.axis_index("col")) + offset + self.size, self.size))

    def cols(self, offset, width):
        return pl.ds(pl.multiple_of(self.owner(offset) * width, 128), width)


class Gather:
    def __init__(self, ring, local, row, rows, split=False):
        self.ring, self.local, self.row, self.rows = ring, local, row, rows
        self.width = local.shape[1]
        self.stage, self.full, self.part = 0, None, 2 if split else 0
        self.out = [shape((rows, self.width * ring.size), BF16)]
        self.offsets = [-1, 1]

    def prepare(self):
        if self.stage == 0 or self.part == 0:
            self.stage += 1
        self.ins = [self.full] if self.full is not None else []
        self.alias = {0: 0} if self.ins else {}
        self.count, self.bounce, self.span = 2, [], None
        if self.stage == 1:
            start, size = self.row, self.rows
            if self.part:
                size //= 2
                start += (2 - self.part) * size
                self.part -= 1
            self.span = start, size
            self.ins = self.ins + [self.local]
            self.count, self.bounce = 3, [(size, self.width)]
        return self

    def copies(self, ins, outs):
        ring, full, width, half = self.ring, outs[0], self.width, self.rows // 2
        if self.stage == 1:
            start, size = self.span
            source = ins[-1].at[pl.ds(start, size), :]
            mine = full.at[pl.ds(start - self.row, size), ring.cols(0, width)]
            return [(source, mine, 1), (source, mine, -1), (source, mine, None)]
        from_left, from_right = ring.cols(1 - self.stage, width), ring.cols(self.stage - 1, width)
        if self.stage < ring.stages:
            left, right = full.at[:, from_left], full.at[:, from_right]
        else:
            left, right = full.at[pl.ds(0, half), from_left], full.at[pl.ds(half, half), from_right]
        return [(left, left, 1), (right, right, -1)]

    def finish(self, outs):
        self.full = outs[0]


class Scatter:
    def __init__(self, ring, partial, inner=None, split=False):
        self.ring, self.partial, self.inner = ring, partial, inner
        self.split = split and ring.stages == 2
        self.rows, self.half = partial.shape[0], partial.shape[0] // 2
        self.width = partial.shape[1] // ring.size
        self.stage, self.inner_others, self.bounce, self.alias = 0, None, [], {}
        self.near = Near(self)
        self.scratch = []

    def block(self, offset, low):
        start = (self.half if low else 0, self.ring.owner(offset) * self.width)
        return lax.dynamic_slice(self.partial, start, (self.half, self.width)).astype(F32)

    def prepare(self):
        self.stage += 1
        stage, stages = self.stage, self.ring.stages
        whole = stage < stages
        self.offsets = [-1, 1]
        if stage == 1:
            self.ins = [self.partial]
        elif stages == 2:
            self.ins, self.scratch = [self.partial, *self.got[:2]], [(self.half, self.width)] * 4
            if not self.split:
                self.kept = self.got[2:]
        else:
            top = self.block(stages + 1 - stage, False) + self.got[0].astype(F32)
            bottom = self.block(stage - 1 - stages, True) + self.got[1].astype(F32)
            self.ins = [top.astype(BF16), bottom.astype(BF16)]
            if whole:
                low = self.block(stages - stage, True) + self.got[2].astype(F32)
                high = self.block(stage - stages, False) + self.got[3].astype(F32)
                self.ins += [low.astype(BF16), high.astype(BF16)]
            elif not self.split:
                self.kept = self.got[2:]
        self.out = [shape((self.half, self.width), BF16)] * (4 if whole and not self.split else 2)
        self.count = len(self.out)
        if stage == 1 and not self.split:
            self.near.add_inner(self)
        return self

    def far_copies(self, ins, outs):
        top, bottom = pl.ds(0, self.half), pl.ds(self.half, self.half)
        far = self.ring.cols(self.ring.stages, self.width)
        return [(ins[0].at[top, far], outs[0], 1), (ins[0].at[bottom, far], outs[1], -1)]

    def loads(self, ins, held):
        top, bottom = pl.ds(0, self.half), pl.ds(self.half, self.half)
        right, left = self.ring.cols(1, self.width), self.ring.cols(-1, self.width)
        sources = [ins[0].at[top, right], ins[0].at[bottom, left], ins[1], ins[2]]
        self.held = held
        return list(zip(sources, held))

    def combine(self):
        for term, others in zip(self.held[:2], self.held[2:]):
            term[...] = (term[...].astype(F32) + others[...].astype(F32)).astype(BF16)

    def copies(self, ins, outs):
        if self.scratch:
            return [(self.held[0], outs[0], 1), (self.held[1], outs[1], -1)]
        if self.stage > 1:
            return [(ref, out, way) for ref, out, way in zip(ins, outs, (1, -1, 1, -1))]
        made = self.far_copies(ins, outs)
        if not self.split:
            made += self.near.near_copies(ins, outs[2:])
        return made

    def finish(self, outs):
        if self.stage == 1 and not self.split:
            outs = [*outs[:2], *self.near.take(outs[2:])]
        self.got = outs

    def pieces(self):
        return self.got[0], self.kept[0], self.kept[1], self.got[1]

    def total(self):
        mine = lax.dynamic_slice_in_dim(self.partial, lax.axis_index("col") * self.width, self.width, 1)
        left = jnp.concatenate([self.got[0], self.kept[0]]).astype(F32)
        right = jnp.concatenate([self.kept[1], self.got[1]]).astype(F32)
        return mine.astype(F32) + left + right


class Near:
    def __init__(self, whole):
        self.whole = whole
        self.bounce, self.alias = [], {}

    @property
    def empty(self):
        return not self.whole.split

    def add_inner(self, stage):
        whole = self.whole
        if whole.inner is not None:
            others = whole.ring.size - 1
            stage.ins = stage.ins + [whole.inner]
            stage.out = stage.out + [shape((others, *whole.inner.shape), F32)]
            stage.count += others
            stage.offsets = list(range(1, whole.ring.size))

    def prepare(self):
        whole = self.whole
        self.ins, self.offsets, self.count = [whole.partial], [-1, 1], 2
        self.out = [shape((whole.half, whole.width), BF16)] * 2
        self.add_inner(self)
        return self

    def near_copies(self, ins, outs):
        whole, ring = self.whole, self.whole.ring
        top, bottom = pl.ds(0, whole.half), pl.ds(whole.half, whole.half)
        made = [
            (ins[0].at[bottom, ring.cols(ring.stages - 1, whole.width)], outs[0], 1),
            (ins[0].at[top, ring.cols(1 - ring.stages, whole.width)], outs[1], -1),
        ]
        if whole.inner is not None:
            made += [(ins[1], outs[2].at[k - 1], k) for k in range(1, ring.size)]
        return made

    def copies(self, ins, outs):
        return self.near_copies(ins, outs)

    def take(self, outs):
        whole = self.whole
        if whole.inner is not None:
            whole.inner_others = outs[2]
        return outs[:2]

    def finish(self, outs):
        self.whole.kept = self.take(outs)


class Share:
    def __init__(self, axis, *arrays):
        self.axis, self.arrays = axis, arrays
        self.size = lax.axis_size(axis)
        self.bounce, self.alias = [], {}
        self.offsets = [(axis, k) for k in range(1, self.size)]

    def prepare(self):
        self.ins, self.out = list(self.arrays), [shape((self.size, *a.shape), F32) for a in self.arrays]
        self.count = (self.size - 1) * len(self.arrays)
        return self

    def copies(self, ins, outs):
        here = lax.axis_index(self.axis)
        return [(a, out.at[here], offset) for a, out in zip(ins, outs) for offset in self.offsets]

    def finish(self, outs):
        self.sums = []
        for mine, out in zip(self.arrays, outs):
            here = lax.broadcasted_iota(jnp.int32, out.shape, 0) == lax.axis_index(self.axis)
            self.sums.append(jnp.sum(jnp.where(here, mine[None], out), axis=0))


class Launcher:
    def __init__(self, ring):
        self.ring = ring
        self.ids = itertools.count()

    def __call__(self, kernel, args, in_specs, out_specs, out_shape, grid, name, cost, alias=None, scratch=(), carry=()):
        stages = [stage.prepare() for stage in carry if not getattr(stage, "empty", False)]
        own_in, own_out = len(args), len(out_shape)
        held_in = [(i, spec) for i, spec in enumerate(in_specs) if isinstance(spec, Held)]
        held_out = [(i, spec) for i, spec in enumerate(out_specs) if isinstance(spec, Held)]
        held_types = [args[i].dtype for i, _ in held_in] + [out_shape[i].dtype for i, _ in held_out]
        in_specs = [ANY if isinstance(spec, Held) else spec for spec in in_specs]
        out_specs = [ANY if isinstance(spec, Held) else spec for spec in out_specs]
        args, in_specs, out_specs, out_shape = list(args), list(in_specs), list(out_specs), list(out_shape)
        alias, scratch = dict(alias or {}), list(scratch)
        own_scratch = len(scratch)
        scratch += [pltpu.VMEM(spec.dims, kind) for (_, spec), kind in zip(held_in + held_out, held_types)]
        if held_types:
            scratch.append(pltpu.SemaphoreType.DMA((len(held_types),)))
        spans = []
        for stage in stages:
            ins, outs = len(args), len(out_shape)
            alias.update({ins + i: outs + o for i, o in stage.alias.items()})
            args += stage.ins
            out_shape += stage.out
            spans.append((ins, len(args), outs, len(out_shape)))
        in_specs += [ANY] * (len(args) - own_in)
        out_specs += [ANY] * (len(out_shape) - own_out)
        more = {}
        if stages:
            count = sum(stage.count for stage in stages)
            scratch += [pltpu.SemaphoreType.DMA((count,)), pltpu.SemaphoreType.DMA((count,))]
            more = dict(collective_id=next(self.ids), has_side_effects=True)
            scratch += [pltpu.VMEM(dims, BF16) for stage in stages for dims in stage.bounce]
        summed = [stage for stage in stages if getattr(stage, "scratch", None)]
        if summed:
            scratch += [pltpu.VMEM(dims, BF16) for stage in summed for dims in stage.scratch]
            scratch.append(pltpu.SemaphoreType.DMA((4 * len(summed),)))
        offsets = {o if isinstance(o, tuple) else ("col", o % self.ring.size) for stage in stages for o in stage.offsets}
        offsets = sorted(offsets)
        ring = self.ring

        def device(way):
            if not isinstance(way, tuple):
                way = ("col", way)
            axis, offset = way
            if axis == "col":
                return {axis: ring.owner(offset)}
            return {axis: lax.rem(lax.axis_index(axis) + offset, lax.axis_size(axis))}

        total_in, total_out = len(args), len(out_shape)

        def body(*refs):
            ins, outs, rest = refs[:total_in], refs[total_in : total_in + total_out], refs[total_in + total_out :]
            own_ins, own_outs = list(ins[:own_in]), list(outs[:own_out])
            own, rest = rest[:own_scratch], rest[own_scratch:]
            inward, outward = [], []
            if held_types:
                buffers, sems, rest = rest[: len(held_types)], rest[len(held_types)], rest[len(held_types) + 1 :]
                for k, (at, spec) in enumerate(held_in):
                    inward.append((spec.of(own_ins[at]), buffers[k], sems.at[k]))
                    own_ins[at] = buffers[k]
                for k, (at, spec) in enumerate(held_out, len(held_in)):
                    outward.append((buffers[k], spec.of(own_outs[at]), sems.at[k]))
                    own_outs[at] = buffers[k]
            own = (*own_ins, *own_outs, *own)
            loads = []
            if summed:
                *rest, buffers, sems = (*rest[: -4 * len(summed) - 1], rest[-4 * len(summed) - 1 : -1], rest[-1])
                for stage, (a, b, _, _) in zip(stages, spans):
                    if stage in summed:
                        k = 4 * summed.index(stage)
                        for at, pair in enumerate(stage.loads(ins[a:b], buffers[k : k + 4]), k):
                            loads.append((*pair, sems.at[at]))
            send, receive, *bounce = rest if stages else (None, None)

            def copies(part, which=(False, True)):
                made, at, held = [], 0, 0
                for stage, (a, b, c, d) in zip(stages, spans):
                    for source, target, way in stage.copies(ins[a:b], outs[c:d]):
                        if way is None:
                            if part == "in":
                                made.append(pltpu.make_async_copy(source, bounce[held], receive.at[at]))
                            elif part == "out":
                                made.append(pltpu.make_async_copy(bounce[held], target, send.at[at]))
                            held += 1
                        elif part == "remote" and (stage in summed) in which:
                            made.append(
                                pltpu.make_async_remote_copy(
                                    source, target, send.at[at], receive.at[at], device_id=device(way),
                                    device_id_type=pl.DeviceIdType.MESH,
                                )
                            )
                        at += 1
                return made

            first = last = True
            for axis, size in enumerate(grid):
                first &= pl.program_id(axis) == 0
                last &= pl.program_id(axis) == size - 1
            @pl.when(first)
            def _():
                if stages:
                    barrier = pltpu.get_barrier_semaphore()
                    for offset in offsets:
                        pl.semaphore_signal(
                            barrier, 1, device_id=device(offset), device_id_type=pl.DeviceIdType.MESH
                        )
                for copy in inward:
                    pltpu.make_async_copy(*copy).start()
                if stages:
                    for copy in copies("in"):
                        copy.start()
                    for copy in loads:
                        pltpu.make_async_copy(*copy).start()
                    pl.semaphore_wait(barrier, len(offsets))
                    for copy in copies("remote", (False,)):
                        copy.start()
                    for copy in loads:
                        pltpu.make_async_copy(*copy).wait()
                    for stage in summed:
                        stage.combine()
                    for copy in copies("remote", (True,)):
                        copy.start()
                for copy in inward:
                    pltpu.make_async_copy(*copy).wait()

            kernel(*own)

            @pl.when(first)
            def _():
                for copy in outward:
                    pltpu.make_async_copy(*copy).start()
                if stages:
                    for here, there in zip(copies("in"), copies("out")):
                        here.wait()
                        there.start()

            @pl.when(last)
            def _():
                for copy in outward:
                    pltpu.make_async_copy(*copy).wait()
                if stages:
                    for copy in copies("out") + copies("remote"):
                        copy.wait()

        flops, moved, exps = cost
        made = pl.pallas_call(
            body,
            grid=grid,
            in_specs=in_specs,
            out_specs=out_specs,
            out_shape=out_shape,
            input_output_aliases=alias,
            scratch_shapes=scratch,
            compiler_params=pltpu.CompilerParams(vmem_limit_bytes=VMEM_LIMIT, **more),
            cost_estimate=pl.CostEstimate(flops=int(flops), bytes_accessed=int(moved), transcendentals=int(exps)),
            name=name,
        )(*args)
        for stage, (_, _, c, d) in zip(stages, spans):
            stage.finish(made[c:d])
        return made[:own_out]

    def alone(self, *stages):
        self(lambda *_: None, [], [], [], [], (1,), "exchange", (0, 0, 0), carry=stages)


def lane_repeat(column, width):
    return jnp.concatenate([column] * (width // column.shape[1]), axis=1)


def causal(bk, bq, shift):
    key_at = lax.broadcasted_iota(jnp.int32, (bk, bq), 0)
    query_at = lax.broadcasted_iota(jnp.int32, (bk, bq), 1)
    return key_at + shift <= query_at


def fwd_kernel(q0, bk, q_ref, k_ref, v_ref, seg_q_ref, seg_k_ref, out_ref, log_ref, vt):
    bq, wide = q_ref.shape
    dim = k_ref.shape[1]
    group = wide // dim
    step = pl.program_id(1)
    factor = LOG2E / math.sqrt(dim)

    @pl.when(step == 0)
    def _():
        for j in range(vt.shape[0]):
            vt[j] = v_ref[pl.ds(j * bk, bk), :].astype(F32).T.astype(BF16)

    seg_q = seg_q_ref[...]
    queries = [q_ref[:, h * dim : (h + 1) * dim] for h in range(group)]

    def block(j, carry, shift):
        key_rows = k_ref[pl.ds(pl.multiple_of(j * bk, bk), bk), :]
        seg_k = seg_k_ref[pl.ds(pl.multiple_of(j * bk, bk), bk), :]
        allowed = lane_repeat(seg_k, bq) == seg_q
        if shift is not None:
            allowed &= causal(bk, bq, shift)
        value_cols = vt[j]
        new = []
        for h in range(group):
            total, acc = carry[2 * h], carry[2 * h + 1]
            scores = dot_nt(key_rows, queries[h])
            weights = jnp.where(allowed, jnp.exp2(scores * factor), 0.0)
            total = total + jnp.sum(weights.reshape(bk // 8, 8, bq), axis=0)
            acc = acc + dot_nn(value_cols, weights.astype(BF16))
            new += [total, acc]
        return tuple(new)

    carry = (jnp.zeros((8, bq), F32), jnp.zeros((dim, bq), F32)) * group
    diag = bq // bk
    whole = q0 // bk + step * diag
    carry = lax.fori_loop(0, whole, lambda j, c: block(j, c, None), carry)
    for d in range(diag):
        carry = block(whole + d, carry, d * bk)
    for h in range(group):
        total = jnp.sum(carry[2 * h], axis=0, keepdims=True)
        mixed = carry[2 * h + 1] * (1.0 / total)
        out_ref[:, h * dim : (h + 1) * dim] = mixed.T.astype(BF16)
        log_ref[0, h : h + 1, :] = jnp.log2(total)


def attend(launch, queries, keys, values, seg_row, seg_wide, q0, rows, dim, bq, bk, carry=()):
    width = queries.shape[1]
    span = q0 + rows
    kv = keys.shape[1] // dim
    group = width // dim // kv
    pairs = group * kv * rows * (span - rows / 2)
    base = q0 // bq
    whole = pl.BlockSpec((span, dim), lambda k, i: (0, k))
    return launch(
        functools.partial(fwd_kernel, q0, bk),
        (queries, keys, values, seg_row, seg_wide),
        [
            pl.BlockSpec((bq, group * dim), lambda k, i: (i + base, k)),
            whole,
            whole,
            pl.BlockSpec((1, bq), lambda k, i: (0, i + base)),
            pl.BlockSpec((span, 128), lambda k, i: (0, 0)),
        ],
        [
            pl.BlockSpec((bq, group * dim), lambda k, i: (i, k)),
            pl.BlockSpec((1, group, bq), lambda k, i: (k, 0, i)),
        ],
        [shape((rows, width), BF16), shape((kv, group, rows), F32)],
        (kv, rows // bq),
        "attend",
        (pairs * dim * 8, rows * width * 4, pairs),
        scratch=[pltpu.VMEM((span // bk, dim, bk), BF16)],
        carry=carry,
    )


def bwd_kernel(q0, bk, first, *refs):
    q_ref, k_ref, v_ref, g_ref, o_ref, log_ref, seg_q_ref, seg_k_ref = refs[:8]
    dk_in, dv_in = (None, None) if first else refs[8:10]
    dq_ref, dk_ref, dv_ref, kt = refs[-4:]
    bq, wide = q_ref.shape
    dim = k_ref.shape[1]
    group = wide // dim
    step = pl.program_id(1)
    scale = 1.0 / math.sqrt(dim)
    factor = LOG2E * scale

    @pl.when(step == 0)
    def _():
        for j in range(kt.shape[0]):
            kt[j] = k_ref[pl.ds(j * bk, bk), :].astype(F32).T.astype(BF16)
        if first:
            dk_ref[...] = jnp.zeros_like(dk_ref)
            dv_ref[...] = jnp.zeros_like(dv_ref)
        else:
            dk_ref[...] = dk_in[...]
            dv_ref[...] = dv_in[...]

    seg_q = seg_q_ref[...]
    queries = [q_ref[:, h * dim : (h + 1) * dim] for h in range(group)]
    grads = [g_ref[:, h * dim : (h + 1) * dim] for h in range(group)]
    logs = [log_ref[0, h : h + 1, :] for h in range(group)]
    inner = []
    for h in range(group):
        product = grads[h].astype(F32) * o_ref[:, h * dim : (h + 1) * dim].astype(F32)
        inner.append(jnp.sum(product.T, axis=0, keepdims=True))

    def block(j, carry, shift):
        at = pl.ds(pl.multiple_of(j * bk, bk), bk)
        key_rows = k_ref[at, :]
        value_rows = v_ref[at, :]
        allowed = lane_repeat(seg_k_ref[at, :], bq) == seg_q
        if shift is not None:
            allowed &= causal(bk, bq, shift)
        key_cols = kt[j]
        new = []
        dk, dv = dk_ref[at, :], dv_ref[at, :]
        for h in range(group):
            scores = dot_nt(key_rows, queries[h])
            probs = jnp.where(allowed, jnp.exp2(scores * factor - logs[h]), 0.0)
            grad_probs = dot_nt(value_rows, grads[h])
            grad_scores = (probs * (grad_probs - inner[h])).astype(BF16)
            dv = dv + dot_nn(probs.astype(BF16), grads[h])
            dk = dk + dot_nn(grad_scores, queries[h])
            new.append(carry[h] + dot_nn(key_cols, grad_scores))
        dk_ref[at, :] = dk
        dv_ref[at, :] = dv
        return tuple(new)

    carry = (jnp.zeros((dim, bq), F32),) * group
    diag = bq // bk
    whole = q0 // bk + step * diag
    carry = lax.fori_loop(0, whole, lambda j, c: block(j, c, None), carry)
    for d in range(diag):
        carry = block(whole + d, carry, d * bk)
    for h in range(group):
        dq_ref[:, h * dim : (h + 1) * dim] = (carry[h] * scale).T


def attend_back(launch, queries, keys, values, grads, mixed, logs, seg_row, seg_wide, q0, dim, bq, bk, sums, carry=()):
    rows, width = grads.shape
    span = q0 + rows
    kv = keys.shape[1] // dim
    group = width // dim // kv
    pairs = group * kv * rows * (span - rows / 2)
    base = q0 // bq
    whole = pl.BlockSpec((span, dim), lambda k, i: (0, k))
    part = pl.BlockSpec((bq, group * dim), lambda k, i: (i, k))
    more = [] if sums is None else list(sums)
    return launch(
        functools.partial(bwd_kernel, q0, bk, sums is None),
        (queries, keys, values, grads, mixed, logs, seg_row, seg_wide, *more),
        [
            pl.BlockSpec((bq, group * dim), lambda k, i: (i + base, k)),
            whole,
            whole,
            part,
            part,
            pl.BlockSpec((1, group, bq), lambda k, i: (k, 0, i)),
            pl.BlockSpec((1, bq), lambda k, i: (0, i + base)),
            pl.BlockSpec((span, 128), lambda k, i: (0, 0)),
        ]
        + [whole] * len(more),
        [part, whole, whole],
        [shape((rows, width), F32), shape((span, kv * dim), F32), shape((span, kv * dim), F32)],
        (kv, rows // bq),
        "attend_back",
        (pairs * dim * 20, rows * width * 10, pairs),
        scratch=[pltpu.VMEM((span // bk, dim, bk), BF16)],
        carry=carry,
    )


def qkv_kernel(kv, x_ref, gain_ref, w_ref, gq_ref, gk_ref, cos_ref, sin_ref, *refs):
    normed_ref, scale_ref, proj_ref, q_ref, k_ref, v_ref = refs[-6:]
    dim = gq_ref.shape[1]
    heads = q_ref.shape[1] // dim
    values = x_ref[...].astype(F32)
    scale = row_scale(values)
    normed = (values * scale * gain_ref[...]).astype(BF16)
    normed_ref[...] = normed
    scale_ref[...] = scale
    projected = dot_nn(normed, w_ref[...])
    cosine, sine = cos_ref[...], sin_ref[...]
    wide = (heads + kv) * dim
    proj_ref[...] = projected[:, :wide]
    for h in range(heads + kv):
        part = projected[:, h * dim : (h + 1) * dim]
        gain = gq_ref[...] if h < heads else gk_ref[...]
        part = part * row_scale(part) * gain
        turned = (part * cosine + swap(part) * sine).astype(BF16)
        if h < heads:
            q_ref[:, h * dim : (h + 1) * dim] = turned
        else:
            k_ref[:, (h - heads) * dim : (h - heads + 1) * dim] = turned
    v_ref[...] = projected[:, wide:].astype(BF16)


def project_qkv(launch, x, gain, weights, cols, gain_q, gain_k, cosine, sine, kv, carry=()):
    rows, width = x.shape
    dim = gain_q.shape[1]
    heads = cols // dim - 2 * kv
    bt = tile_of(rows, 512)
    wide = (heads + kv) * dim

    def part(w):
        return pl.BlockSpec((bt, w), lambda i: (i, 0))

    return launch(
        functools.partial(qkv_kernel, kv),
        (x, gain, weights, gain_q, gain_k, cosine, sine),
        [
            part(width),
            resident((1, width)),
            Held((width, cols)),
            resident((1, dim)),
            resident((1, dim)),
            part(dim),
            part(dim),
        ],
        [part(width), part(1), part(wide), part(heads * dim), part(kv * dim), part(kv * dim)],
        [
            shape((rows, width), BF16),
            shape((rows, 1), F32),
            shape((rows, wide), F32),
            shape((rows, heads * dim), BF16),
            shape((rows, kv * dim), BF16),
            shape((rows, kv * dim), BF16),
        ],
        (rows // bt,),
        "project_qkv",
        (2 * rows * width * cols, rows * width * 4 + width * cols * 2, 0),
        carry=carry,
    )


def mlp_kernel(x_ref, gain_ref, wg_ref, wu_ref, wd_ref, cot_ref, *refs):
    normed_ref, scale_ref, active_ref, gg_ref, gu_ref = refs[-5:]

    @pl.when(pl.program_id(1) == 0)
    def _():
        values = x_ref[...].astype(F32)
        scale = row_scale(values)
        normed_ref[...] = (values * scale * gain_ref[...]).astype(BF16)
        scale_ref[...] = scale

    normed = normed_ref[...]
    gate = dot_nn(normed, wg_ref[...])
    up = dot_nn(normed, wu_ref[...])
    grad = dot_nn(cot_ref[...], wd_ref[...])
    sig = jax.nn.sigmoid(gate)
    silu = gate * sig
    active_ref[...] = (silu * up).astype(BF16)
    gu_ref[...] = (grad * silu).astype(BF16)
    gg_ref[...] = (grad * up * (sig + silu * (1.0 - sig))).astype(BF16)


def mlp(launch, x, gain, weights, cot, chunk, total, kept, carry=()):
    rows, width = x.shape
    hidden = weights.shape[1] // 3
    bn = tile_of(hidden, 512)
    tiles = hidden // bn
    more = [] if kept is None else list(kept)
    tile = pl.BlockSpec((rows, bn), lambda i, j: (chunk, j))
    low = shape((total, hidden), BF16)
    return launch(
        mlp_kernel,
        (x, gain, weights, weights, weights, cot, *more),
        [
            Held((rows, width)),
            resident((1, width)),
            pl.BlockSpec((width, bn), lambda i, j: (0, j)),
            pl.BlockSpec((width, bn), lambda i, j: (0, j + tiles)),
            pl.BlockSpec((width, bn), lambda i, j: (0, j + 2 * tiles)),
            Held((rows, width)),
        ]
        + [ANY] * len(more),
        [Held((rows, width), chunk * rows), pl.BlockSpec((rows, 1), lambda i, j: (0, 0)), tile, tile, tile],
        [shape((total, width), BF16), shape((rows, 1), F32), low, low, low],
        (1, tiles),
        "mlp",
        (6 * rows * width * hidden, rows * (width + hidden) * 6 + 6 * width * hidden, rows * hidden),
        alias={6: 0, 7: 2, 8: 3, 9: 4} if more else None,
        carry=carry,
    )


def mid_kernel(gg_ref, gu_ref, w_ref, v_ref, scale_ref, gain_ref, part_ref, inner_ref, gain_out):
    hidden = gg_ref.shape[1]
    partial = dot_nt(gg_ref[...], w_ref[:, :hidden]) + dot_nt(gu_ref[...], w_ref[:, hidden:])
    part_ref[...] = partial.astype(BF16)
    product = partial * v_ref[...].astype(F32)
    gain_out[0] = jnp.sum(product * scale_ref[...], axis=0, keepdims=True)
    inner = row_of(jnp.sum(product * gain_ref[...], axis=1, keepdims=True))

    @pl.when(pl.program_id(1) == 0)
    def _():
        inner_ref[0] = inner

    @pl.when(pl.program_id(1) > 0)
    def _():
        inner_ref[0] += inner


def back_mid(launch, gg, gu, weights, values, scale, gain, chunk, carry=()):
    rows, width = values.shape
    hidden = gg.shape[1]
    bn = tile_of(width, 512)
    return launch(
        mid_kernel,
        (gg, gu, weights, values, scale, gain),
        [
            Held((rows, hidden), chunk * rows),
            Held((rows, hidden), chunk * rows),
            pl.BlockSpec((bn, 2 * hidden), lambda i, j: (j, 0)),
            pl.BlockSpec((rows, bn), lambda i, j: (0, j)),
            pl.BlockSpec((rows, 1), lambda i, j: (0, 0)),
            pl.BlockSpec((1, bn), lambda i, j: (0, j)),
        ],
        [
            pl.BlockSpec((rows, bn), lambda i, j: (0, j)),
            pl.BlockSpec((1, 1, rows), lambda i, j: (0, 0, 0)),
            pl.BlockSpec((1, 1, bn), lambda i, j: (0, 0, j)),
        ],
        [shape((rows, width), BF16), shape((1, 1, rows), F32), shape((1, 1, width), F32)],
        (1, width // bn),
        "back_mid",
        (4 * rows * width * hidden, rows * (width + hidden) * 4 + 4 * width * hidden, 0),
        carry=carry,
    )


def qkv_back_kernel(
    kv, dq_ref, dk_ref, dv_ref, proj_ref, cos_ref, sin_ref, gq_ref, gk_ref, w_ref, v_ref, scale_ref, gain_ref, *refs
):
    low_ref, part_ref, inner_ref, gain_out, gq_out, gk_out = refs[-6:]
    dim = gq_ref.shape[1]
    heads = dq_ref.shape[1] // dim
    wide = (heads + kv) * dim

    @pl.when(pl.program_id(1) == 0)
    def _():
        cosine, sine = cos_ref[...], sin_ref[...]
        sums = [jnp.zeros((1, dim), F32), jnp.zeros((1, dim), F32)]
        for h in range(heads + kv):
            is_key = h >= heads
            if is_key:
                grad = dk_ref[:, (h - heads) * dim : (h - heads + 1) * dim] * (1.0 / math.sqrt(dim))
            else:
                grad = dq_ref[:, h * dim : (h + 1) * dim]
            grad = grad * cosine + swap(grad * sine)
            value = proj_ref[:, h * dim : (h + 1) * dim]
            scale = row_scale(value)
            sums[is_key] += jnp.sum(grad * value * scale, axis=0, keepdims=True)
            weighted = grad * (gk_ref[...] if is_key else gq_ref[...])
            mean = jnp.mean(weighted * value, axis=-1, keepdims=True)
            low_ref[:, h * dim : (h + 1) * dim] = (scale * (weighted - value * scale * scale * mean)).astype(BF16)
        low_ref[:, wide:] = dv_ref[...].astype(BF16)
        gq_out[0] = sums[0]
        gk_out[0] = sums[1]

    partial = dot_nt(low_ref[...], w_ref[...])
    part_ref[...] = partial.astype(BF16)
    product = partial * v_ref[...].astype(F32)
    gain_out[0] = jnp.sum(product * scale_ref[...], axis=0, keepdims=True)
    inner = row_of(jnp.sum(product * gain_ref[...], axis=1, keepdims=True))

    @pl.when(pl.program_id(1) == 0)
    def _():
        inner_ref[0] = inner

    @pl.when(pl.program_id(1) > 0)
    def _():
        inner_ref[0] += inner


def back_qkv(launch, dq, dk, dv, proj, cosine, sine, gain_q, gain_k, weights, cols, values, scale, gain, kv, chunk, kept, carry=()):
    total, width = values.shape
    rows = dq.shape[0]
    dim = gain_q.shape[1]
    bt = rows
    bn = tile_of(width, 512)
    base = chunk

    def here(w):
        return Held((rows, w))

    def there(w):
        return Held((rows, w), chunk * rows)

    row = pl.BlockSpec((1, 1, dim), lambda i, j: (i, 0, 0))
    more = [] if kept is None else [kept]
    return launch(
        functools.partial(qkv_back_kernel, kv),
        (dq, dk, dv, proj, cosine, sine, gain_q, gain_k, weights, values, scale, gain, *more),
        [
            here(dq.shape[1]),
            there(dk.shape[1]),
            there(dv.shape[1]),
            there(proj.shape[1]),
            there(dim),
            there(dim),
            resident((1, dim)),
            resident((1, dim)),
            pl.BlockSpec((bn, cols), lambda i, j: (j, 0)),
            pl.BlockSpec((bt, bn), lambda i, j: (i + base, j)),
            pl.BlockSpec((rows, 1), lambda i, j: (chunk, 0)),
            pl.BlockSpec((1, bn), lambda i, j: (0, j)),
        ]
        + [ANY] * len(more),
        [
            there(cols),
            pl.BlockSpec((bt, bn), lambda i, j: (i, j)),
            pl.BlockSpec((1, 1, bt), lambda i, j: (i, 0, 0)),
            pl.BlockSpec((1, 1, bn), lambda i, j: (i, 0, j)),
            row,
            row,
        ],
        [
            shape((total, cols), BF16),
            shape((rows, width), BF16),
            shape((rows // bt, 1, bt), F32),
            shape((rows // bt, 1, width), F32),
            shape((rows // bt, 1, dim), F32),
            shape((rows // bt, 1, dim), F32),
        ],
        (rows // bt, width // bn),
        "back_qkv",
        (2 * rows * width * cols, rows * width * 4 + rows * cols * 10, 0),
        alias={12: 0} if more else None,
        carry=carry,
    )


def pair_kernel(low_ref, high_ref, first_ref, second_ref, out_ref):
    out_ref[...] = (dot_tn(low_ref[...], first_ref[...]) + dot_tn(high_ref[...], second_ref[...])).astype(BF16)


def weight_grad_pair(launch, lefts, rights, rows_at, carry=()):
    rows, cols = rights[0].shape
    width = lefts[0].shape[1]
    bm = next(size for size in (1024, 768, 512, 256, 128) if width % size == 0)
    bn = tile_of(cols, 512)

    def left(k):
        return pl.BlockSpec((rows, bm), lambda i, j: (rows_at[k], i))

    right = pl.BlockSpec((rows, bn), lambda i, j: (0, j))
    return launch(
        pair_kernel,
        (*lefts, *rights),
        [left(0), left(1), right, right],
        [pl.BlockSpec((bm, bn), lambda i, j: (i, j))],
        [shape((width, cols), BF16)],
        (width // bm, cols // bn),
        "weight_grad",
        (4 * rows * width * cols, rows * (width + cols) * 4 + width * cols * 2, 0),
        carry=carry,
    )[0]


def grad_kernel(tiles, left_ref, *refs):
    rights, out_ref = refs[:-1], refs[-1]
    for k, right in enumerate(rights):
        @pl.when(pl.program_id(1) // tiles == k)
        def _():
            out_ref[...] = dot_tn(left_ref[...], right[...]).astype(BF16)


def weight_grad(launch, left, *rights, carry=()):
    rows, width = left.shape
    cols = rights[0].shape[1]
    bm = next(size for size in (1024, 768, 512, 256, 128) if width % size == 0)
    bn = next(size for size in (512, 384, 256, 128) if cols % size == 0)
    tiles = cols // bn

    def part(k):
        return pl.BlockSpec((rows, bn), lambda i, j: (0, jnp.clip(j - k * tiles, 0, tiles - 1)))

    return launch(
        functools.partial(grad_kernel, tiles),
        (left, *rights),
        [pl.BlockSpec((rows, bm), lambda i, j: (0, i))] + [part(k) for k in range(len(rights))],
        [pl.BlockSpec((bm, bn), lambda i, j: (i, j))],
        [shape((width, cols * len(rights)), BF16)],
        (width // bm, tiles * len(rights)),
        "weight_grad",
        (2 * rows * width * cols * len(rights), rows * (width + cols) * 2 + width * cols * 4, 0),
        carry=carry,
    )[0]


def out_kernel(left_ref, right_ref, out_ref):
    out_ref[...] = dot_nt(left_ref[...], right_ref[...]).astype(BF16)


def project_out(launch, left, weights, chunk, rows, carry=()):
    width, hidden = weights.shape[0], left.shape[1]
    bn = tile_of(width, 512)
    last = weights.shape[1] // hidden - 1
    return launch(
        out_kernel,
        (left, weights),
        [Held((rows, hidden), chunk * rows), pl.BlockSpec((bn, hidden), lambda i, j: (j, last))],
        [pl.BlockSpec((rows, bn), lambda i, j: (0, j))],
        [shape((rows, width), BF16)],
        (1, width // bn),
        "project_out",
        (2 * rows * width * hidden, rows * (width + hidden) * 2 + width * hidden * 2, 0),
        carry=carry,
    )[0]


def mix_kernel(left_ref, right_ref, out_ref):
    out_ref[...] = dot_nn(left_ref[...], right_ref[...]).astype(BF16)


def grad_mix(launch, grads, weights, cols):
    rows, width = grads.shape
    bt = tile_of(rows, 512)
    return launch(
        mix_kernel,
        (grads, weights),
        [pl.BlockSpec((bt, width), lambda i: (i, 0)), Held((width, cols), 0, weights.shape[1] - cols)],
        [pl.BlockSpec((bt, cols), lambda i: (i, 0))],
        [shape((rows, cols), BF16)],
        (rows // bt,),
        "grad_mix",
        (2 * rows * width * cols, (rows * width + rows * cols + width * cols) * 2, 0),
    )[0]


def tables_kernel(position_ref, segment_ref, inverse_ref, cos_ref, sin_ref, wide_ref):
    def column(row):
        return jnp.broadcast_to(row.astype(F32), (128, row.shape[1])).T

    angle = column(position_ref[...]) * inverse_ref[...]
    half = lax.broadcasted_iota(jnp.int32, angle.shape, 1) < angle.shape[1] // 2
    sine = jnp.sin(angle)
    cos_ref[...] = jnp.cos(angle)
    sin_ref[...] = jnp.where(half, -sine, sine)
    wide_ref[...] = column(segment_ref[...]).astype(jnp.int32)


def tables(launch, positions, segments, dim, carry=()):
    rows = positions.shape[0]
    bt = tile_of(rows, 512)
    inverse = THETA ** (-(jnp.arange(dim // 2, dtype=F32) * 2.0 / dim))
    row = pl.BlockSpec((1, bt), lambda i: (0, i))
    wide = pl.BlockSpec((bt, 128), lambda i: (i, 0))
    return launch(
        tables_kernel,
        (positions[None], segments[None], jnp.concatenate([inverse, inverse])[None]),
        [row, row, resident((1, dim))],
        [wide, wide, wide],
        [shape((rows, dim), F32), shape((rows, dim), F32), shape((rows, 128), jnp.int32)],
        (rows // bt,),
        "tables",
        (0, rows * dim * 12, rows * dim * 2),
        carry=carry,
    )


def side(first, low, high):
    return jnp.where(first, low[...].astype(F32), high[...].astype(F32))


def grad_block(factor, first, base, term, t0, t1, t2, t3, values, scale, inner, others, gain):
    row = inner[0] + jnp.sum(others[:, 0, 0, :], axis=0, keepdims=True)
    inner = jnp.broadcast_to(row, (128, row.shape[1])).T[:, :1]
    scales = scale[...]
    total = term[...].astype(F32) + side(first, t0, t1) + side(first, t2, t3)
    return base[...].astype(F32) + scales * (
        total * gain[...] - values[...].astype(F32) * (scales * scales * inner * factor)
    )


def grad_operands(base, summed, values, scale, gain, base_at, values_at, scale_at, start=0):
    local = base.shape[1]
    bt = summed.half // 2

    def step(i):
        return jnp.clip(i - start, 0, 3)

    def at(chunk, wide):
        return pl.BlockSpec((bt, wide), lambda i: (step(i) + 4 * chunk, 0))

    mine = pl.BlockSpec((bt, local), lambda i: (step(i), lax.axis_index("col")))
    low = pl.BlockSpec((bt, local), lambda i: (jnp.minimum(step(i), 1), 0))
    high = pl.BlockSpec((bt, local), lambda i: (jnp.maximum(step(i) - 2, 0), 0))
    others = summed.inner_others
    args = (base, summed.partial, *summed.pieces(), values, scale, summed.inner, others, gain[None])
    specs = [at(base_at, local), mine, low, high, low, high, at(values_at, local), at(scale_at, 1)]
    specs += [
        pl.BlockSpec((1, 1, bt), lambda i: (0, 0, step(i))),
        pl.BlockSpec((others.shape[0], 1, 1, bt), lambda i: (0, 0, 0, step(i))),
        resident((1, local)),
    ]
    return args, specs, at


def hidden_kernel(factor, *refs):
    grad = grad_block(factor, pl.program_id(0) < 2, *refs[:-2])
    refs[-2][...] = grad
    refs[-1][...] = grad.astype(BF16)


def hidden_grad(launch, base, summed, values, scale, gain, chunk):
    args, specs, at = grad_operands(base, summed, values, scale, gain, chunk, 0, 0)
    rows, local = summed.rows, base.shape[1]
    return launch(
        functools.partial(hidden_kernel, 1.0 / (local * launch.ring.size)),
        args,
        specs,
        [at(0, local), at(0, local)],
        [shape((rows, local), F32), shape((rows, local), BF16)],
        (4,),
        "hidden_grad",
        (0, rows * local * 18, 0),
    )


def settle_kernel(*refs):
    step = pl.program_id(0)
    output = refs[-1]

    def one(hidden, down, p0, p1, p2, p3):
        first = step % 2 == 0
        output[...] = (hidden[...] + (down[...].astype(F32) + side(first, p0, p1) + side(first, p2, p3))).astype(BF16)

    pl.when(step < 2)(lambda: one(*refs[:6]))
    pl.when(step >= 2)(lambda: one(*refs[6:12]))


def settle(launch, hidden, sums, carry=()):
    rows, local = hidden[0].shape
    bt = rows // 2
    args, specs = [], []
    for c in (0, 1):
        here = pl.BlockSpec((bt, local), lambda i, c=c: (jnp.clip(i - 2 * c, 0, 1), 0))
        mine = pl.BlockSpec((bt, local), lambda i, c=c: (jnp.clip(i - 2 * c, 0, 1), lax.axis_index("col")))
        args += [hidden[c], sums[c].partial, *sums[c].pieces()]
        specs += [here, mine] + [Held((bt, local))] * 4
    return launch(
        settle_kernel,
        args,
        specs,
        [pl.BlockSpec((bt, local), lambda i: (i, 0))],
        [shape((2 * rows, local), BF16)],
        (4,),
        "settle",
        (0, rows * local * 24, 0),
        carry=carry,
    )[0]


def last_kernel(factor, *refs):
    step = pl.program_id(0)
    count = (len(refs) - 1) // 2

    @pl.when(step < 4)
    def _():
        refs[-1][...] = grad_block(factor, step < 2, *refs[:count])

    @pl.when(step >= 4)
    def _():
        refs[-1][...] = grad_block(factor, step < 6, *refs[count:-1])


def settle_last(launch, grad_hidden, sums, tokens, scale, gain, carry=()):
    args, specs = [], []
    for c in (0, 1):
        more, more_specs, _ = grad_operands(grad_hidden[c], sums[c], tokens, scale, gain, 0, c, c, 4 * c)
        args += more
        specs += more_specs
    total, local = tokens.shape
    return launch(
        functools.partial(last_kernel, 1.0 / (local * launch.ring.size)),
        args,
        specs,
        [pl.BlockSpec((total // 8, local), lambda i: (i, 0))],
        [shape((total, local), F32)],
        (8,),
        "settle_last",
        (0, total * local * 24, 0),
        carry=carry,
    )[0]


def hand_on_kernel(*refs):
    half = len(refs) // 2
    for source, target in zip(refs[:half], refs[half:]):
        target[...] = source[...]


def hand_on(launch, *arrays):
    steps = 4
    specs = [pl.BlockSpec((a.shape[0] // steps, a.shape[1]), lambda i: (i, 0)) for a in arrays]
    return launch(
        hand_on_kernel, arrays, specs, specs, [shape(a.shape, a.dtype) for a in arrays], (steps,), "hand_on",
        (0, sum(a.size * a.dtype.itemsize * 2 for a in arrays), 0),
    )


def widen_kernel(source, *targets):
    at = 0
    for target in targets:
        target[...] = source[:, at : at + target.shape[1]].astype(F32)
        at += target.shape[1]


def widen(launch, source, *cols):
    rows = source.shape[0]
    whole = [pl.BlockSpec((rows, n), lambda i: (0, 0)) for n in (source.shape[1], *cols)]
    return launch(
        widen_kernel, [source], whole[:1], whole[1:], [shape((rows, n), F32) for n in cols], (1,), "widen",
        (0, source.size * 6, 0),
    )


def after(value, *others):
    return lax.optimization_barrier((value, *jax.tree.leaves(others)))[0]


def body(
    tokens,
    segments,
    positions,
    gain_attn,
    w_query,
    key_weight_matrix,
    value_weight_matrix,
    gain_query,
    gain_key,
    w_out,
    gain_mlp,
    w_gate,
    w_up,
    w_down,
    cotangent,
):
    total, local = tokens.shape
    dim = gain_query.shape[0]
    query_cols, key_cols = w_query.shape[1], key_weight_matrix.shape[1]
    kv = key_cols // dim
    hidden_units = w_gate.shape[1]
    ring = Ring(lax.axis_size("col"))
    launch = Launcher(ring)
    width = local * ring.size
    rows = total // 2
    parts = [slice(0, rows), slice(rows, total)]
    offset = lax.axis_index("col") * local
    gain_attn_local = lax.dynamic_slice_in_dim(gain_attn, offset, local)
    gain_mlp_local = lax.dynamic_slice_in_dim(gain_mlp, offset, local)
    gain_q, gain_k = gain_query[None], gain_key[None]
    bq = tile_of(rows, 512)

    def gathered(weights, axis):
        return lax.all_gather(weights, "row", axis=axis, tiled=True)

    def scattered(partial, axis):
        return lax.psum_scatter(partial, "row", scatter_dimension=axis, tiled=True)

    def carried(*stages):
        for stage in stages:
            for _ in range(ring.stages - 2):
                launch.alone(stage)

    pair = lambda: [None] * 2
    mixed, logs, hidden, mid_low, scale_mid = pair(), pair(), pair(), pair(), pair()
    get_cot, get_mid, get_grad = pair(), pair(), pair()
    sum_out, sum_down, sum_mid, sum_in = pair(), pair(), pair(), pair()
    gain_mlp_part, grad_hidden, gains_in = pair(), pair(), pair()

    qkv_cols = query_cols + 2 * key_cols
    w_attn = gathered(jnp.concatenate([w_query, key_weight_matrix, value_weight_matrix, w_out.T], axis=1), 0)

    get_tok = Gather(ring, tokens, 0, total)
    launch.alone(get_tok)
    w_mlp = gathered(jnp.concatenate([after(w_gate, get_tok.full), w_up, w_down.T], axis=1), 0)
    seg_row = segments[None]
    for _ in range(ring.stages - 2):
        launch.alone(get_tok)
    cosine, sine, seg_wide = tables(launch, positions, segments, dim, [get_tok])
    x_full = get_tok.full

    for c in (0, 1):
        get_cot[c] = Gather(ring, cotangent, c * rows, rows, split=c == 0)
    normed, scale_attn, proj, queries, keys, values = project_qkv(
        launch, x_full, gain_attn[None], w_attn, qkv_cols, gain_q, gain_k, cosine, sine, kv, carry=[get_cot[1]]
    )

    def attention(c, at, carry):
        mixed[c], logs[c] = attend(
            launch, queries, keys, values, after(seg_row, at), seg_wide, c * rows, rows, dim, bq, bq, carry=carry
        )
        return logs[c]

    def start_out(c, at, carry):
        partial = project_out(launch, after(mixed[c], at), w_attn, 0, rows, carry=carry)
        sum_out[c] = Scatter(ring, partial)
        return partial

    def end_out(c):
        hidden[c] = tokens[parts[c]].astype(F32) + sum_out[c].total()
        mid_low[c] = hidden[c].astype(BF16)
        get_mid[c] = Gather(ring, mid_low[c], 0, rows)

    carried(get_cot[1])
    at = attention(1, normed, [get_cot[1]])
    at = start_out(1, at, [get_cot[0]])
    at = attention(0, at, [sum_out[1]])
    carried(sum_out[1])
    launch.alone(sum_out[1])
    end_out(1)
    launch.alone(get_mid[1])
    carried(get_mid[1])
    start_out(0, get_mid[1].full, [get_mid[1]])
    launch.alone(sum_out[0])
    carried(sum_out[0])
    launch.alone(sum_out[0], get_cot[0])
    end_out(0)

    def feed_forward(c, kept, at, carry):
        nm, scale_mid[c], *rest = mlp(
            launch, get_mid[c].full, after(gain_mlp[None], at), w_mlp, get_cot[c].full, c, total, kept,
            carry=carry,
        )
        return (nm, *rest)

    def back_middle(c, kept, at, carry):
        partial, inner, gain_part = back_mid(
            launch, kept[2], kept[3], w_mlp, get_mid[c].full, scale_mid[c], after(gain_mlp[None], at), c, carry=carry
        )
        gain_mlp_part[c] = jnp.sum(gain_part, axis=(0, 1))
        sum_mid[c] = Scatter(ring, partial, inner)
        return partial

    def end_mid(c):
        grad_hidden[c], low = hidden_grad(
            launch, cotangent, sum_mid[c], mid_low[c], scale_mid[c], gain_mlp_local, c
        )
        get_grad[c] = Gather(ring, low, 0, rows)
        return low

    def start_down(c, active, at, carry=()):
        partial = project_out(launch, after(active, at), w_mlp, c, rows, carry=carry)
        sum_down[c] = Scatter(ring, partial, split=True)
        return partial

    kept = feed_forward(1, None, get_mid[1].full, [get_mid[0]])
    carried(get_mid[0], get_cot[0])
    at = start_down(1, kept[1], kept[0], [get_mid[0]])
    at = back_middle(1, kept, at, [get_cot[0], sum_down[1]])
    kept = feed_forward(0, kept, at, [sum_mid[1]])
    normed_mid, active, grad_gate, grad_up = kept
    carried(sum_mid[1])
    partial = weight_grad_pair(
        launch, (active, active), (get_cot[0].full, get_cot[1].full), (0, 1), carry=[sum_mid[1], sum_down[1].near]
    )
    rs_down = scattered(partial, 1)
    low = end_mid(1)
    at = back_middle(0, kept, (partial, low), [get_grad[1]])
    carried(get_grad[1])
    partial = weight_grad(launch, after(normed_mid, at), grad_gate, grad_up, carry=[get_grad[1], sum_mid[0]])
    rs_gate_up = scattered(partial, 0)
    carried(sum_mid[0])
    at = start_down(0, active, partial, [sum_mid[0]])
    low = end_mid(0)

    def mix(c):
        return jnp.dot(get_grad[c].full, w_attn[:, qkv_cols:], preferred_element_type=F32).astype(BF16)

    def attention_back(c, grad_mixed, sums, at, carry):
        return attend_back(
            launch, queries, keys, values, grad_mixed, mixed[c], logs[c], after(seg_row, at), seg_wide, c * rows, dim,
            bq, bq, sums, carry=carry,
        )

    def projection_back(c, grads, low_all, at, carry):
        low_all, partial, inner, *gains_in[c] = back_qkv(
            launch, *grads, proj, cosine, sine, gain_q, gain_k, w_attn, qkv_cols, x_full, scale_attn, after(gain_attn[None], at),
            kv, c, low_all, carry=carry,
        )
        sum_in[c] = Scatter(ring, partial, inner, split=True)
        return low_all, partial

    grads = attention_back(1, mix(1), None, (at, low), [get_grad[0], sum_down[0]])
    carried(get_grad[0])
    low_all, at = projection_back(1, grads, None, None, [get_grad[0], sum_down[0].near])
    grad_mixed = mix(0)
    early = Share("col", *gains_in[1], (gain_mlp_part[0] + gain_mlp_part[1])[None])
    grads = attention_back(0, grad_mixed, grads[1:], (at, rs_down), [sum_in[1], early])
    carried(sum_down[1])
    grad_out = weight_grad_pair(
        launch, (after(mixed[0], grads[0]), mixed[1]), (get_grad[0].full, get_grad[1].full), (0, 0), carry=[sum_down[1]]
    )
    rs_out = scattered(grad_out, 1)
    carried(sum_in[1], sum_down[0])
    low_all, at = projection_back(0, grads, low_all, grad_out, [sum_in[1], sum_down[0]])
    gains = Share("col", *gains_in[0])
    partial = weight_grad(launch, after(normed, at, rs_gate_up), low_all, carry=[sum_in[0], sum_in[1].near, gains])

    grad_qkv = scattered(after(partial, rs_out), 0)
    gains = jnp.concatenate([part.reshape(-1) for part in (*gains.sums, *early.sums)])[None]
    gains = Share("row", gains)
    carried(sum_in[0])
    output = settle(launch, hidden, sum_down, [sum_in[0], sum_in[0].near])
    grad_tokens = settle_last(launch, grad_hidden, sum_in, tokens, scale_attn, gain_attn_local, [gains])
    sum_attn, sum_q, sum_k, more_attn, more_q, more_k, sum_mlp = jnp.split(
        gains.sums[0][0], list(itertools.accumulate([width, dim, dim, width, dim, dim]))
    )
    output, grad_tokens = hand_on(launch, output, grad_tokens)
    grad_query, grad_key, grad_value = widen(launch, grad_qkv, query_cols, key_cols, key_cols)
    return (
        output,
        grad_tokens,
        sum_attn + more_attn,
        grad_query,
        grad_key,
        grad_value,
        sum_q + more_q,
        sum_k + more_k,
        rs_out.astype(F32),
        sum_mlp,
        rs_gate_up[:, :hidden_units].astype(F32),
        rs_gate_up[:, hidden_units:].astype(F32),
        rs_down.astype(F32),
    )


def solution(mesh):
    both, split = P("row", "col"), P("col", "row")
    in_specs = (both, P("row"), P("row"), P(), both, both, both, P(), P(), split, P(), both, both, split, both)
    out_specs = (both, both, P(), both, both, both, P(), P(), split, P(), both, both, split)
    return jax.shard_map(body, mesh=mesh, in_specs=in_specs, out_specs=out_specs, check_vma=False)
```

```python
import functools
import itertools
import math

import jax
import jax.numpy as jnp
from jax import lax
from jax.experimental import pallas as pl
from jax.experimental.pallas import tpu as pltpu
from jax.sharding import PartitionSpec as P

BF16 = jnp.bfloat16
F32 = jnp.float32
EPS = 1e-06
THETA = 1000000.0
LOG2E = 1.4426950408889634
VMEM_LIMIT = 60 * 1024 * 1024
ANY = pl.BlockSpec(memory_space=pl.ANY)


def dot_nt(left, right):
    return lax.dot_general(left, right, (((1,), (1,)), ((), ())), preferred_element_type=F32)


def dot_nn(left, right):
    return jnp.dot(left, right, preferred_element_type=F32)


def dot_tn(left, right):
    return lax.dot_general(left, right, (((0,), (0,)), ((), ())), preferred_element_type=F32)


def shape(dims, dtype):
    return jax.ShapeDtypeStruct(tuple(dims), dtype)


def resident(dims):
    return pl.BlockSpec(dims, lambda *_: (0,) * len(dims), pipeline_mode=pl.Buffered(1))


def held(dims, index):
    return pl.BlockSpec(dims, index, pipeline_mode=pl.Buffered(1))


def tile_of(size, most):
    tile = most
    while size % tile:
        tile //= 2
    return tile


def swap(values):
    half = values.shape[-1] // 2
    return jnp.concatenate([values[:, half:], values[:, :half]], axis=1)


def row_scale(values):
    return lax.rsqrt(jnp.mean(values * values, axis=-1, keepdims=True) + EPS)


def row_of(column):
    return jnp.broadcast_to(column, (column.shape[0], 128)).T[:1]


class Held:
    def __init__(self, dims, row=0, col=0):
        self.dims, self.row, self.col = dims, row, col

    def of(self, ref):
        return ref.at[pl.ds(self.row, self.dims[0]), pl.ds(self.col, self.dims[1])]


class Ring:
    def __init__(self, size):
        self.size = size
        self.stages = size // 2

    def place(self, index):
        half = self.size // 2
        return jnp.where(index < half, index, self.size + half - 1 - index)

    def owner(self, offset):
        return self.place(lax.rem(self.place(lax.axis_index("col")) + offset + self.size, self.size))

    def cols(self, offset, width):
        return pl.ds(pl.multiple_of(self.owner(offset) * width, 128), width)


class Gather:
    def __init__(self, ring, local, row, rows, split=False):
        self.ring, self.local, self.row, self.rows = ring, local, row, rows
        self.width = local.shape[1]
        self.stage, self.full, self.part = 0, None, 2 if split else 0
        self.out = [shape((rows, self.width * ring.size), BF16)]
        self.offsets = [-1, 1]

    def prepare(self):
        if self.stage == 0 or self.part == 0:
            self.stage += 1
        self.ins = [self.full] if self.full is not None else []
        self.alias = {0: 0} if self.ins else {}
        self.count, self.bounce, self.span = 2, [], None
        if self.stage == 1:
            start, size = self.row, self.rows
            if self.part:
                size //= 2
                start += (2 - self.part) * size
                self.part -= 1
            self.span = start, size
            self.ins = self.ins + [self.local]
            self.count, self.bounce = 3, [(size, self.width)]
        return self

    def copies(self, ins, outs):
        ring, full, width, half = self.ring, outs[0], self.width, self.rows // 2
        if self.stage == 1:
            start, size = self.span
            source = ins[-1].at[pl.ds(start, size), :]
            mine = full.at[pl.ds(start - self.row, size), ring.cols(0, width)]
            return [(source, mine, 1), (source, mine, -1), (source, mine, None)]
        from_left, from_right = ring.cols(1 - self.stage, width), ring.cols(self.stage - 1, width)
        if self.stage < ring.stages:
            left, right = full.at[:, from_left], full.at[:, from_right]
        else:
            left, right = full.at[pl.ds(0, half), from_left], full.at[pl.ds(half, half), from_right]
        return [(left, left, 1), (right, right, -1)]

    def finish(self, outs):
        self.full = outs[0]


class Scatter:
    def __init__(self, ring, partial, inner=None, split=False):
        self.ring, self.partial, self.inner = ring, partial, inner
        self.split = split and ring.stages == 2
        self.rows, self.half = partial.shape[0], partial.shape[0] // 2
        self.width = partial.shape[1] // ring.size
        self.stage, self.inner_others, self.bounce, self.alias = 0, None, [], {}
        self.near = Near(self)
        self.scratch = []

    def block(self, offset, low):
        start = (self.half if low else 0, self.ring.owner(offset) * self.width)
        return lax.dynamic_slice(self.partial, start, (self.half, self.width)).astype(F32)

    def prepare(self):
        self.stage += 1
        stage, stages = self.stage, self.ring.stages
        whole = stage < stages
        self.offsets = [-1, 1]
        if stage == 1:
            self.ins = [self.partial]
        elif stages == 2:
            self.ins, self.scratch = [self.partial, *self.got[:2]], [(self.half, self.width)] * 4
            if not self.split:
                self.kept = self.got[2:]
        else:
            top = self.block(stages + 1 - stage, False) + self.got[0].astype(F32)
            bottom = self.block(stage - 1 - stages, True) + self.got[1].astype(F32)
            self.ins = [top.astype(BF16), bottom.astype(BF16)]
            if whole:
                low = self.block(stages - stage, True) + self.got[2].astype(F32)
                high = self.block(stage - stages, False) + self.got[3].astype(F32)
                self.ins += [low.astype(BF16), high.astype(BF16)]
            elif not self.split:
                self.kept = self.got[2:]
        self.out = [shape((self.half, self.width), BF16)] * (4 if whole and not self.split else 2)
        self.count = len(self.out)
        if stage == 1 and not self.split:
            self.near.add_inner(self)
        return self

    def far_copies(self, ins, outs):
        top, bottom = pl.ds(0, self.half), pl.ds(self.half, self.half)
        far = self.ring.cols(self.ring.stages, self.width)
        return [(ins[0].at[top, far], outs[0], 1), (ins[0].at[bottom, far], outs[1], -1)]

    def loads(self, ins, held):
        top, bottom = pl.ds(0, self.half), pl.ds(self.half, self.half)
        right, left = self.ring.cols(1, self.width), self.ring.cols(-1, self.width)
        sources = [ins[0].at[top, right], ins[0].at[bottom, left], ins[1], ins[2]]
        self.held = held
        return list(zip(sources, held))

    def combine(self):
        for term, others in zip(self.held[:2], self.held[2:]):
            term[...] = (term[...].astype(F32) + others[...].astype(F32)).astype(BF16)

    def copies(self, ins, outs):
        if self.scratch:
            return [(self.held[0], outs[0], 1), (self.held[1], outs[1], -1)]
        if self.stage > 1:
            return [(ref, out, way) for ref, out, way in zip(ins, outs, (1, -1, 1, -1))]
        made = self.far_copies(ins, outs)
        if not self.split:
            made += self.near.near_copies(ins, outs[2:])
        return made

    def finish(self, outs):
        if self.stage == 1 and not self.split:
            outs = [*outs[:2], *self.near.take(outs[2:])]
        self.got = outs

    def pieces(self):
        return self.got[0], self.kept[0], self.kept[1], self.got[1]

    def total(self):
        mine = lax.dynamic_slice_in_dim(self.partial, lax.axis_index("col") * self.width, self.width, 1)
        left = jnp.concatenate([self.got[0], self.kept[0]]).astype(F32)
        right = jnp.concatenate([self.kept[1], self.got[1]]).astype(F32)
        return mine.astype(F32) + left + right


class Near:
    def __init__(self, whole):
        self.whole = whole
        self.bounce, self.alias = [], {}

    @property
    def empty(self):
        return not self.whole.split

    def add_inner(self, stage):
        whole = self.whole
        if whole.inner is not None:
            others = whole.ring.size - 1
            stage.ins = stage.ins + [whole.inner]
            stage.out = stage.out + [shape((others, *whole.inner.shape), F32)]
            stage.count += others
            stage.offsets = list(range(1, whole.ring.size))

    def prepare(self):
        whole = self.whole
        self.ins, self.offsets, self.count = [whole.partial], [-1, 1], 2
        self.out = [shape((whole.half, whole.width), BF16)] * 2
        self.add_inner(self)
        return self

    def near_copies(self, ins, outs):
        whole, ring = self.whole, self.whole.ring
        top, bottom = pl.ds(0, whole.half), pl.ds(whole.half, whole.half)
        made = [
            (ins[0].at[bottom, ring.cols(ring.stages - 1, whole.width)], outs[0], 1),
            (ins[0].at[top, ring.cols(1 - ring.stages, whole.width)], outs[1], -1),
        ]
        if whole.inner is not None:
            made += [(ins[1], outs[2].at[k - 1], k) for k in range(1, ring.size)]
        return made

    def copies(self, ins, outs):
        return self.near_copies(ins, outs)

    def take(self, outs):
        whole = self.whole
        if whole.inner is not None:
            whole.inner_others = outs[2]
        return outs[:2]

    def finish(self, outs):
        self.whole.kept = self.take(outs)


class Share:
    def __init__(self, axis, *arrays):
        self.axis, self.arrays = axis, arrays
        self.size = lax.axis_size(axis)
        self.bounce, self.alias = [], {}
        self.offsets = [(axis, k) for k in range(1, self.size)]

    def prepare(self):
        self.ins, self.out = list(self.arrays), [shape((self.size, *a.shape), F32) for a in self.arrays]
        self.count = (self.size - 1) * len(self.arrays)
        return self

    def copies(self, ins, outs):
        here = lax.axis_index(self.axis)
        return [(a, out.at[here], offset) for a, out in zip(ins, outs) for offset in self.offsets]

    def finish(self, outs):
        self.sums = []
        for mine, out in zip(self.arrays, outs):
            here = lax.broadcasted_iota(jnp.int32, out.shape, 0) == lax.axis_index(self.axis)
            self.sums.append(jnp.sum(jnp.where(here, mine[None], out), axis=0))


class Launcher:
    def __init__(self, ring):
        self.ring = ring
        self.ids = itertools.count()

    def __call__(self, kernel, args, in_specs, out_specs, out_shape, grid, name, cost, alias=None, scratch=(), carry=()):
        stages = [stage.prepare() for stage in carry if not getattr(stage, "empty", False)]
        own_in, own_out = len(args), len(out_shape)
        held_in = [(i, spec) for i, spec in enumerate(in_specs) if isinstance(spec, Held)]
        held_out = [(i, spec) for i, spec in enumerate(out_specs) if isinstance(spec, Held)]
        held_types = [args[i].dtype for i, _ in held_in] + [out_shape[i].dtype for i, _ in held_out]
        in_specs = [ANY if isinstance(spec, Held) else spec for spec in in_specs]
        out_specs = [ANY if isinstance(spec, Held) else spec for spec in out_specs]
        args, in_specs, out_specs, out_shape = list(args), list(in_specs), list(out_specs), list(out_shape)
        alias, scratch = dict(alias or {}), list(scratch)
        own_scratch = len(scratch)
        scratch += [pltpu.VMEM(spec.dims, kind) for (_, spec), kind in zip(held_in + held_out, held_types)]
        if held_types:
            scratch.append(pltpu.SemaphoreType.DMA((len(held_types),)))
        spans = []
        for stage in stages:
            ins, outs = len(args), len(out_shape)
            alias.update({ins + i: outs + o for i, o in stage.alias.items()})
            args += stage.ins
            out_shape += stage.out
            spans.append((ins, len(args), outs, len(out_shape)))
        in_specs += [ANY] * (len(args) - own_in)
        out_specs += [ANY] * (len(out_shape) - own_out)
        more = {}
        if stages:
            count = sum(stage.count for stage in stages)
            scratch += [pltpu.SemaphoreType.DMA((count,)), pltpu.SemaphoreType.DMA((count,))]
            more = dict(collective_id=next(self.ids), has_side_effects=True)
            scratch += [pltpu.VMEM(dims, BF16) for stage in stages for dims in stage.bounce]
        summed = [stage for stage in stages if getattr(stage, "scratch", None)]
        if summed:
            scratch += [pltpu.VMEM(dims, BF16) for stage in summed for dims in stage.scratch]
            scratch.append(pltpu.SemaphoreType.DMA((4 * len(summed),)))
        offsets = {o if isinstance(o, tuple) else ("col", o % self.ring.size) for stage in stages for o in stage.offsets}
        offsets = sorted(offsets)
        ring = self.ring

        def device(way):
            if not isinstance(way, tuple):
                way = ("col", way)
            axis, offset = way
            if axis == "col":
                return {axis: ring.owner(offset)}
            return {axis: lax.rem(lax.axis_index(axis) + offset, lax.axis_size(axis))}

        total_in, total_out = len(args), len(out_shape)

        def body(*refs):
            ins, outs, rest = refs[:total_in], refs[total_in : total_in + total_out], refs[total_in + total_out :]
            own_ins, own_outs = list(ins[:own_in]), list(outs[:own_out])
            own, rest = rest[:own_scratch], rest[own_scratch:]
            inward, outward = [], []
            if held_types:
                buffers, sems, rest = rest[: len(held_types)], rest[len(held_types)], rest[len(held_types) + 1 :]
                for k, (at, spec) in enumerate(held_in):
                    inward.append((spec.of(own_ins[at]), buffers[k], sems.at[k]))
                    own_ins[at] = buffers[k]
                for k, (at, spec) in enumerate(held_out, len(held_in)):
                    outward.append((buffers[k], spec.of(own_outs[at]), sems.at[k]))
                    own_outs[at] = buffers[k]
            own = (*own_ins, *own_outs, *own)
            loads = []
            if summed:
                *rest, buffers, sems = (*rest[: -4 * len(summed) - 1], rest[-4 * len(summed) - 1 : -1], rest[-1])
                for stage, (a, b, _, _) in zip(stages, spans):
                    if stage in summed:
                        k = 4 * summed.index(stage)
                        for at, pair in enumerate(stage.loads(ins[a:b], buffers[k : k + 4]), k):
                            loads.append((*pair, sems.at[at]))
            send, receive, *bounce = rest if stages else (None, None)

            def copies(part, which=(False, True)):
                made, at, held = [], 0, 0
                for stage, (a, b, c, d) in zip(stages, spans):
                    for source, target, way in stage.copies(ins[a:b], outs[c:d]):
                        if way is None:
                            if part == "in":
                                made.append(pltpu.make_async_copy(source, bounce[held], receive.at[at]))
                            elif part == "out":
                                made.append(pltpu.make_async_copy(bounce[held], target, send.at[at]))
                            held += 1
                        elif part == "remote" and (stage in summed) in which:
                            made.append(
                                pltpu.make_async_remote_copy(
                                    source, target, send.at[at], receive.at[at], device_id=device(way),
                                    device_id_type=pl.DeviceIdType.MESH,
                                )
                            )
                        at += 1
                return made

            first = last = True
            for axis, size in enumerate(grid):
                first &= pl.program_id(axis) == 0
                last &= pl.program_id(axis) == size - 1
            @pl.when(first)
            def _():
                if stages:
                    barrier = pltpu.get_barrier_semaphore()
                    for offset in offsets:
                        pl.semaphore_signal(
                            barrier, 1, device_id=device(offset), device_id_type=pl.DeviceIdType.MESH
                        )
                for copy in inward:
                    pltpu.make_async_copy(*copy).start()
                if stages:
                    for copy in copies("in"):
                        copy.start()
                    for copy in loads:
                        pltpu.make_async_copy(*copy).start()
                    pl.semaphore_wait(barrier, len(offsets))
                    for copy in copies("remote", (False,)):
                        copy.start()
                    for copy in loads:
                        pltpu.make_async_copy(*copy).wait()
                    for stage in summed:
                        stage.combine()
                    for copy in copies("remote", (True,)):
                        copy.start()
                for copy in inward:
                    pltpu.make_async_copy(*copy).wait()

            kernel(*own)

            @pl.when(first)
            def _():
                for copy in outward:
                    pltpu.make_async_copy(*copy).start()
                if stages:
                    for here, there in zip(copies("in"), copies("out")):
                        here.wait()
                        there.start()

            @pl.when(last)
            def _():
                for copy in outward:
                    pltpu.make_async_copy(*copy).wait()
                if stages:
                    for copy in copies("out") + copies("remote"):
                        copy.wait()

        flops, moved, exps = cost
        made = pl.pallas_call(
            body,
            grid=grid,
            in_specs=in_specs,
            out_specs=out_specs,
            out_shape=out_shape,
            input_output_aliases=alias,
            scratch_shapes=scratch,
            compiler_params=pltpu.CompilerParams(vmem_limit_bytes=VMEM_LIMIT, **more),
            cost_estimate=pl.CostEstimate(flops=int(flops), bytes_accessed=int(moved), transcendentals=int(exps)),
            name=name,
        )(*args)
        for stage, (_, _, c, d) in zip(stages, spans):
            stage.finish(made[c:d])
        return made[:own_out]

    def alone(self, *stages):
        self(lambda *_: None, [], [], [], [], (1,), "exchange", (0, 0, 0), carry=stages)


def lane_repeat(column, width):
    return jnp.concatenate([column] * (width // column.shape[1]), axis=1)


def causal(bk, bq, shift):
    key_at = lax.broadcasted_iota(jnp.int32, (bk, bq), 0)
    query_at = lax.broadcasted_iota(jnp.int32, (bk, bq), 1)
    return key_at + shift <= query_at


def fwd_kernel(q0, bk, q_ref, k_ref, v_ref, seg_q_ref, seg_k_ref, out_ref, log_ref, vt):
    bq, wide = q_ref.shape
    dim = k_ref.shape[1]
    group = wide // dim
    step = pl.program_id(1)
    factor = LOG2E / math.sqrt(dim)

    @pl.when(step == 0)
    def _():
        for j in range(vt.shape[0]):
            vt[j] = v_ref[pl.ds(j * bk, bk), :].astype(F32).T.astype(BF16)

    seg_q = seg_q_ref[...]
    queries = [q_ref[:, h * dim : (h + 1) * dim] for h in range(group)]

    def block(j, carry, shift):
        key_rows = k_ref[pl.ds(pl.multiple_of(j * bk, bk), bk), :]
        seg_k = seg_k_ref[pl.ds(pl.multiple_of(j * bk, bk), bk), :]
        allowed = lane_repeat(seg_k, bq) == seg_q
        if shift is not None:
            allowed &= causal(bk, bq, shift)
        value_cols = vt[j]
        new = []
        for h in range(group):
            total, acc = carry[2 * h], carry[2 * h + 1]
            scores = dot_nt(key_rows, queries[h])
            weights = jnp.where(allowed, jnp.exp2(scores * factor), 0.0)
            total = total + jnp.sum(weights.reshape(bk // 8, 8, bq), axis=0)
            acc = acc + dot_nn(value_cols, weights.astype(BF16))
            new += [total, acc]
        return tuple(new)

    carry = (jnp.zeros((8, bq), F32), jnp.zeros((dim, bq), F32)) * group
    diag = bq // bk
    whole = q0 // bk + step * diag
    carry = lax.fori_loop(0, whole, lambda j, c: block(j, c, None), carry)
    for d in range(diag):
        carry = block(whole + d, carry, d * bk)
    for h in range(group):
        total = jnp.sum(carry[2 * h], axis=0, keepdims=True)
        mixed = carry[2 * h + 1] * (1.0 / total)
        out_ref[:, h * dim : (h + 1) * dim] = mixed.T.astype(BF16)
        log_ref[0, h : h + 1, :] = jnp.log2(total)


def attend(launch, queries, keys, values, seg_row, seg_wide, q0, rows, dim, bq, bk, carry=()):
    width = queries.shape[1]
    span = q0 + rows
    kv = keys.shape[1] // dim
    group = width // dim // kv
    pairs = group * kv * rows * (span - rows / 2)
    base = q0 // bq
    whole = pl.BlockSpec((span, dim), lambda k, i: (0, k))
    return launch(
        functools.partial(fwd_kernel, q0, bk),
        (queries, keys, values, seg_row, seg_wide),
        [
            pl.BlockSpec((bq, group * dim), lambda k, i: (i + base, k)),
            whole,
            whole,
            pl.BlockSpec((1, bq), lambda k, i: (0, i + base)),
            pl.BlockSpec((span, 128), lambda k, i: (0, 0)),
        ],
        [
            pl.BlockSpec((bq, group * dim), lambda k, i: (i, k)),
            pl.BlockSpec((1, group, bq), lambda k, i: (k, 0, i)),
        ],
        [shape((rows, width), BF16), shape((kv, group, rows), F32)],
        (kv, rows // bq),
        "attend",
        (pairs * dim * 8, rows * width * 4, pairs),
        scratch=[pltpu.VMEM((span // bk, dim, bk), BF16)],
        carry=carry,
    )


def bwd_kernel(q0, bk, first, *refs):
    q_ref, k_ref, v_ref, g_ref, o_ref, log_ref, seg_q_ref, seg_k_ref = refs[:8]
    dk_in, dv_in = (None, None) if first else refs[8:10]
    dq_ref, dk_ref, dv_ref, kt = refs[-4:]
    bq, wide = q_ref.shape
    dim = k_ref.shape[1]
    group = wide // dim
    step = pl.program_id(1)
    scale = 1.0 / math.sqrt(dim)
    factor = LOG2E * scale

    @pl.when(step == 0)
    def _():
        for j in range(kt.shape[0]):
            kt[j] = k_ref[pl.ds(j * bk, bk), :].astype(F32).T.astype(BF16)
        if first:
            dk_ref[...] = jnp.zeros_like(dk_ref)
            dv_ref[...] = jnp.zeros_like(dv_ref)
        else:
            dk_ref[...] = dk_in[...]
            dv_ref[...] = dv_in[...]

    seg_q = seg_q_ref[...]
    queries = [q_ref[:, h * dim : (h + 1) * dim] for h in range(group)]
    grads = [g_ref[:, h * dim : (h + 1) * dim] for h in range(group)]
    logs = [log_ref[0, h : h + 1, :] for h in range(group)]
    inner = []
    for h in range(group):
        product = grads[h].astype(F32) * o_ref[:, h * dim : (h + 1) * dim].astype(F32)
        inner.append(jnp.sum(product.T, axis=0, keepdims=True))

    def block(j, carry, shift):
        at = pl.ds(pl.multiple_of(j * bk, bk), bk)
        key_rows = k_ref[at, :]
        value_rows = v_ref[at, :]
        allowed = lane_repeat(seg_k_ref[at, :], bq) == seg_q
        if shift is not None:
            allowed &= causal(bk, bq, shift)
        key_cols = kt[j]
        new = []
        dk, dv = dk_ref[at, :], dv_ref[at, :]
        for h in range(group):
            scores = dot_nt(key_rows, queries[h])
            probs = jnp.where(allowed, jnp.exp2(scores * factor - logs[h]), 0.0)
            grad_probs = dot_nt(value_rows, grads[h])
            grad_scores = (probs * (grad_probs - inner[h])).astype(BF16)
            dv = dv + dot_nn(probs.astype(BF16), grads[h])
            dk = dk + dot_nn(grad_scores, queries[h])
            new.append(carry[h] + dot_nn(key_cols, grad_scores))
        dk_ref[at, :] = dk
        dv_ref[at, :] = dv
        return tuple(new)

    carry = (jnp.zeros((dim, bq), F32),) * group
    diag = bq // bk
    whole = q0 // bk + step * diag
    carry = lax.fori_loop(0, whole, lambda j, c: block(j, c, None), carry)
    for d in range(diag):
        carry = block(whole + d, carry, d * bk)
    for h in range(group):
        dq_ref[:, h * dim : (h + 1) * dim] = (carry[h] * scale).T


def attend_back(launch, queries, keys, values, grads, mixed, logs, seg_row, seg_wide, q0, dim, bq, bk, sums, carry=()):
    rows, width = grads.shape
    span = q0 + rows
    kv = keys.shape[1] // dim
    group = width // dim // kv
    pairs = group * kv * rows * (span - rows / 2)
    base = q0 // bq
    whole = pl.BlockSpec((span, dim), lambda k, i: (0, k))
    part = pl.BlockSpec((bq, group * dim), lambda k, i: (i, k))
    more = [] if sums is None else list(sums)
    return launch(
        functools.partial(bwd_kernel, q0, bk, sums is None),
        (queries, keys, values, grads, mixed, logs, seg_row, seg_wide, *more),
        [
            pl.BlockSpec((bq, group * dim), lambda k, i: (i + base, k)),
            whole,
            whole,
            part,
            part,
            pl.BlockSpec((1, group, bq), lambda k, i: (k, 0, i)),
            pl.BlockSpec((1, bq), lambda k, i: (0, i + base)),
            pl.BlockSpec((span, 128), lambda k, i: (0, 0)),
        ]
        + [whole] * len(more),
        [part, whole, whole],
        [shape((rows, width), F32), shape((span, kv * dim), F32), shape((span, kv * dim), F32)],
        (kv, rows // bq),
        "attend_back",
        (pairs * dim * 20, rows * width * 10, pairs),
        scratch=[pltpu.VMEM((span // bk, dim, bk), BF16)],
        carry=carry,
    )


def qkv_kernel(kv, x_ref, gain_ref, w_ref, gq_ref, gk_ref, cos_ref, sin_ref, *refs):
    normed_ref, scale_ref, proj_ref, q_ref, k_ref, v_ref = refs[-6:]
    dim = gq_ref.shape[1]
    heads = q_ref.shape[1] // dim
    values = x_ref[...].astype(F32)
    scale = row_scale(values)
    normed = (values * scale * gain_ref[...]).astype(BF16)
    normed_ref[...] = normed
    scale_ref[...] = scale
    projected = dot_nn(normed, w_ref[...])
    cosine, sine = cos_ref[...], sin_ref[...]
    wide = (heads + kv) * dim
    proj_ref[...] = projected[:, :wide]
    for h in range(heads + kv):
        part = projected[:, h * dim : (h + 1) * dim]
        gain = gq_ref[...] if h < heads else gk_ref[...]
        part = part * row_scale(part) * gain
        turned = (part * cosine + swap(part) * sine).astype(BF16)
        if h < heads:
            q_ref[:, h * dim : (h + 1) * dim] = turned
        else:
            k_ref[:, (h - heads) * dim : (h - heads + 1) * dim] = turned
    v_ref[...] = projected[:, wide:].astype(BF16)


def project_qkv(launch, x, gain, weights, cols, gain_q, gain_k, cosine, sine, kv, carry=()):
    rows, width = x.shape
    dim = gain_q.shape[1]
    heads = cols // dim - 2 * kv
    bt = tile_of(rows, 512)
    wide = (heads + kv) * dim

    def part(w):
        return pl.BlockSpec((bt, w), lambda i: (i, 0))

    return launch(
        functools.partial(qkv_kernel, kv),
        (x, gain, weights, gain_q, gain_k, cosine, sine),
        [
            part(width),
            resident((1, width)),
            Held((width, cols)),
            resident((1, dim)),
            resident((1, dim)),
            part(dim),
            part(dim),
        ],
        [part(width), part(1), part(wide), part(heads * dim), part(kv * dim), part(kv * dim)],
        [
            shape((rows, width), BF16),
            shape((rows, 1), F32),
            shape((rows, wide), F32),
            shape((rows, heads * dim), BF16),
            shape((rows, kv * dim), BF16),
            shape((rows, kv * dim), BF16),
        ],
        (rows // bt,),
        "project_qkv",
        (2 * rows * width * cols, rows * width * 4 + width * cols * 2, 0),
        carry=carry,
    )


def mlp_kernel(x_ref, gain_ref, wg_ref, wu_ref, wd_ref, cot_ref, *refs):
    normed_ref, scale_ref, active_ref, gg_ref, gu_ref = refs[-5:]

    @pl.when(pl.program_id(1) == 0)
    def _():
        values = x_ref[...].astype(F32)
        scale = row_scale(values)
        normed_ref[...] = (values * scale * gain_ref[...]).astype(BF16)
        scale_ref[...] = scale

    normed = normed_ref[...]
    gate = dot_nn(normed, wg_ref[...])
    up = dot_nn(normed, wu_ref[...])
    grad = dot_nn(cot_ref[...], wd_ref[...])
    sig = jax.nn.sigmoid(gate)
    silu = gate * sig
    active_ref[...] = (silu * up).astype(BF16)
    gu_ref[...] = (grad * silu).astype(BF16)
    gg_ref[...] = (grad * up * (sig + silu * (1.0 - sig))).astype(BF16)


def mlp(launch, x, gain, weights, cot, chunk, total, kept, carry=()):
    rows, width = x.shape
    hidden = weights.shape[1] // 3
    bn = tile_of(hidden, 256)
    tiles = hidden // bn
    more = [] if kept is None else list(kept)
    tile = pl.BlockSpec((rows, bn), lambda i, j: (chunk, j))
    low = shape((total, hidden), BF16)
    return launch(
        mlp_kernel,
        (x, gain, weights, weights, weights, cot, *more),
        [
            Held((rows, width)),
            resident((1, width)),
            pl.BlockSpec((width, bn), lambda i, j: (0, j)),
            pl.BlockSpec((width, bn), lambda i, j: (0, j + tiles)),
            pl.BlockSpec((width, bn), lambda i, j: (0, j + 2 * tiles)),
            Held((rows, width)),
        ]
        + [ANY] * len(more),
        [Held((rows, width), chunk * rows), pl.BlockSpec((rows, 1), lambda i, j: (0, 0)), tile, tile, tile],
        [shape((total, width), BF16), shape((rows, 1), F32), low, low, low],
        (1, tiles),
        "mlp",
        (6 * rows * width * hidden, rows * (width + hidden) * 6 + 6 * width * hidden, rows * hidden),
        alias={6: 0, 7: 2, 8: 3, 9: 4} if more else None,
        carry=carry,
    )


def mid_kernel(gg_ref, gu_ref, w_ref, v_ref, scale_ref, gain_ref, part_ref, inner_ref, gain_out):
    hidden = gg_ref.shape[1]
    partial = dot_nt(gg_ref[...], w_ref[:, :hidden]) + dot_nt(gu_ref[...], w_ref[:, hidden:])
    part_ref[...] = partial.astype(BF16)
    product = partial * v_ref[...].astype(F32)
    gain_out[0] = jnp.sum(product * scale_ref[...], axis=0, keepdims=True)
    inner = row_of(jnp.sum(product * gain_ref[...], axis=1, keepdims=True))

    @pl.when(pl.program_id(1) == 0)
    def _():
        inner_ref[0] = inner

    @pl.when(pl.program_id(1) > 0)
    def _():
        inner_ref[0] += inner


def back_mid(launch, gg, gu, weights, values, scale, gain, chunk, carry=()):
    rows, width = values.shape
    hidden = gg.shape[1]
    bn = tile_of(width, 512)
    return launch(
        mid_kernel,
        (gg, gu, weights, values, scale, gain),
        [
            Held((rows, hidden), chunk * rows),
            Held((rows, hidden), chunk * rows),
            pl.BlockSpec((bn, 2 * hidden), lambda i, j: (j, 0)),
            pl.BlockSpec((rows, bn), lambda i, j: (0, j)),
            pl.BlockSpec((rows, 1), lambda i, j: (0, 0)),
            pl.BlockSpec((1, bn), lambda i, j: (0, j)),
        ],
        [
            pl.BlockSpec((rows, bn), lambda i, j: (0, j)),
            pl.BlockSpec((1, 1, rows), lambda i, j: (0, 0, 0)),
            pl.BlockSpec((1, 1, bn), lambda i, j: (0, 0, j)),
        ],
        [shape((rows, width), BF16), shape((1, 1, rows), F32), shape((1, 1, width), F32)],
        (1, width // bn),
        "back_mid",
        (4 * rows * width * hidden, rows * (width + hidden) * 4 + 4 * width * hidden, 0),
        carry=carry,
    )


def qkv_back_kernel(
    kv, dq_ref, dk_ref, dv_ref, proj_ref, cos_ref, sin_ref, gq_ref, gk_ref, w_ref, v_ref, scale_ref, gain_ref, *refs
):
    low_ref, part_ref, inner_ref, gain_out, gq_out, gk_out = refs[-6:]
    dim = gq_ref.shape[1]
    heads = dq_ref.shape[1] // dim
    wide = (heads + kv) * dim

    @pl.when(pl.program_id(1) == 0)
    def _():
        cosine, sine = cos_ref[...], sin_ref[...]
        sums = [jnp.zeros((1, dim), F32), jnp.zeros((1, dim), F32)]
        for h in range(heads + kv):
            is_key = h >= heads
            if is_key:
                grad = dk_ref[:, (h - heads) * dim : (h - heads + 1) * dim] * (1.0 / math.sqrt(dim))
            else:
                grad = dq_ref[:, h * dim : (h + 1) * dim]
            grad = grad * cosine + swap(grad * sine)
            value = proj_ref[:, h * dim : (h + 1) * dim]
            scale = row_scale(value)
            sums[is_key] += jnp.sum(grad * value * scale, axis=0, keepdims=True)
            weighted = grad * (gk_ref[...] if is_key else gq_ref[...])
            mean = jnp.mean(weighted * value, axis=-1, keepdims=True)
            low_ref[:, h * dim : (h + 1) * dim] = (scale * (weighted - value * scale * scale * mean)).astype(BF16)
        low_ref[:, wide:] = dv_ref[...].astype(BF16)
        gq_out[0] = sums[0]
        gk_out[0] = sums[1]

    partial = dot_nt(low_ref[...], w_ref[...])
    part_ref[...] = partial.astype(BF16)
    product = partial * v_ref[...].astype(F32)
    gain_out[0] = jnp.sum(product * scale_ref[...], axis=0, keepdims=True)
    inner = row_of(jnp.sum(product * gain_ref[...], axis=1, keepdims=True))

    @pl.when(pl.program_id(1) == 0)
    def _():
        inner_ref[0] = inner

    @pl.when(pl.program_id(1) > 0)
    def _():
        inner_ref[0] += inner


def back_qkv(launch, dq, dk, dv, proj, cosine, sine, gain_q, gain_k, weights, cols, values, scale, gain, kv, chunk, kept, carry=()):
    total, width = values.shape
    rows = dq.shape[0]
    dim = gain_q.shape[1]
    bt = rows
    bn = tile_of(width, 512)
    base = chunk

    def here(w):
        return Held((rows, w))

    def there(w):
        return Held((rows, w), chunk * rows)

    row = pl.BlockSpec((1, 1, dim), lambda i, j: (i, 0, 0))
    more = [] if kept is None else [kept]
    return launch(
        functools.partial(qkv_back_kernel, kv),
        (dq, dk, dv, proj, cosine, sine, gain_q, gain_k, weights, values, scale, gain, *more),
        [
            here(dq.shape[1]),
            there(dk.shape[1]),
            there(dv.shape[1]),
            there(proj.shape[1]),
            there(dim),
            there(dim),
            resident((1, dim)),
            resident((1, dim)),
            pl.BlockSpec((bn, cols), lambda i, j: (j, 0)),
            pl.BlockSpec((bt, bn), lambda i, j: (i + base, j)),
            pl.BlockSpec((rows, 1), lambda i, j: (chunk, 0)),
            pl.BlockSpec((1, bn), lambda i, j: (0, j)),
        ]
        + [ANY] * len(more),
        [
            there(cols),
            pl.BlockSpec((bt, bn), lambda i, j: (i, j)),
            pl.BlockSpec((1, 1, bt), lambda i, j: (i, 0, 0)),
            pl.BlockSpec((1, 1, bn), lambda i, j: (i, 0, j)),
            row,
            row,
        ],
        [
            shape((total, cols), BF16),
            shape((rows, width), BF16),
            shape((rows // bt, 1, bt), F32),
            shape((rows // bt, 1, width), F32),
            shape((rows // bt, 1, dim), F32),
            shape((rows // bt, 1, dim), F32),
        ],
        (rows // bt, width // bn),
        "back_qkv",
        (2 * rows * width * cols, rows * width * 4 + rows * cols * 10, 0),
        alias={12: 0} if more else None,
        carry=carry,
    )


def pair_kernel(low_ref, high_ref, first_ref, second_ref, out_ref):
    out_ref[...] = (dot_tn(low_ref[...], first_ref[...]) + dot_tn(high_ref[...], second_ref[...])).astype(BF16)


def weight_grad_pair(launch, lefts, rights, rows_at, carry=()):
    rows, cols = rights[0].shape
    width = lefts[0].shape[1]
    bm = next(size for size in (1024, 768, 512, 256, 128) if width % size == 0)
    bn = tile_of(cols, 512)

    def left(k):
        return pl.BlockSpec((rows, bm), lambda i, j: (rows_at[k], i))

    right = pl.BlockSpec((rows, bn), lambda i, j: (0, j))
    return launch(
        pair_kernel,
        (*lefts, *rights),
        [left(0), left(1), right, right],
        [pl.BlockSpec((bm, bn), lambda i, j: (i, j))],
        [shape((width, cols), BF16)],
        (width // bm, cols // bn),
        "weight_grad",
        (4 * rows * width * cols, rows * (width + cols) * 4 + width * cols * 2, 0),
        carry=carry,
    )[0]


def grad_kernel(tiles, left_ref, *refs):
    rights, out_ref = refs[:-1], refs[-1]
    for k, right in enumerate(rights):
        @pl.when(pl.program_id(1) // tiles == k)
        def _():
            out_ref[...] = dot_tn(left_ref[...], right[...]).astype(BF16)


def weight_grad(launch, left, *rights, carry=()):
    rows, width = left.shape
    cols = rights[0].shape[1]
    bm = next(size for size in (1024, 768, 512, 256, 128) if width % size == 0)
    bn = next(size for size in (512, 384, 256, 128) if cols % size == 0)
    tiles = cols // bn

    def part(k):
        return pl.BlockSpec((rows, bn), lambda i, j: (0, jnp.clip(j - k * tiles, 0, tiles - 1)))

    return launch(
        functools.partial(grad_kernel, tiles),
        (left, *rights),
        [pl.BlockSpec((rows, bm), lambda i, j: (0, i))] + [part(k) for k in range(len(rights))],
        [pl.BlockSpec((bm, bn), lambda i, j: (i, j))],
        [shape((width, cols * len(rights)), BF16)],
        (width // bm, tiles * len(rights)),
        "weight_grad",
        (2 * rows * width * cols * len(rights), rows * (width + cols) * 2 + width * cols * 4, 0),
        carry=carry,
    )[0]


def out_kernel(left_ref, right_ref, out_ref):
    out_ref[...] = dot_nt(left_ref[...], right_ref[...]).astype(BF16)


def project_out(launch, left, weights, chunk, rows, carry=()):
    width, hidden = weights.shape[0], left.shape[1]
    bn = tile_of(width, 512)
    last = weights.shape[1] // hidden - 1
    return launch(
        out_kernel,
        (left, weights),
        [Held((rows, hidden), chunk * rows), pl.BlockSpec((bn, hidden), lambda i, j: (j, last))],
        [pl.BlockSpec((rows, bn), lambda i, j: (0, j))],
        [shape((rows, width), BF16)],
        (1, width // bn),
        "project_out",
        (2 * rows * width * hidden, rows * (width + hidden) * 2 + width * hidden * 2, 0),
        carry=carry,
    )[0]


def mix_kernel(left_ref, right_ref, out_ref):
    out_ref[...] = dot_nn(left_ref[...], right_ref[...]).astype(BF16)


def grad_mix(launch, grads, weights, cols):
    rows, width = grads.shape
    bt = tile_of(rows, 512)
    return launch(
        mix_kernel,
        (grads, weights),
        [pl.BlockSpec((bt, width), lambda i: (i, 0)), Held((width, cols), 0, weights.shape[1] - cols)],
        [pl.BlockSpec((bt, cols), lambda i: (i, 0))],
        [shape((rows, cols), BF16)],
        (rows // bt,),
        "grad_mix",
        (2 * rows * width * cols, (rows * width + rows * cols + width * cols) * 2, 0),
    )[0]


def tables_kernel(position_ref, segment_ref, inverse_ref, cos_ref, sin_ref, wide_ref):
    def column(row):
        return jnp.broadcast_to(row.astype(F32), (128, row.shape[1])).T

    angle = column(position_ref[...]) * inverse_ref[...]
    half = lax.broadcasted_iota(jnp.int32, angle.shape, 1) < angle.shape[1] // 2
    sine = jnp.sin(angle)
    cos_ref[...] = jnp.cos(angle)
    sin_ref[...] = jnp.where(half, -sine, sine)
    wide_ref[...] = column(segment_ref[...]).astype(jnp.int32)


def tables(launch, positions, segments, dim, carry=()):
    rows = positions.shape[0]
    bt = tile_of(rows, 512)
    inverse = THETA ** (-(jnp.arange(dim // 2, dtype=F32) * 2.0 / dim))
    row = pl.BlockSpec((1, bt), lambda i: (0, i))
    wide = pl.BlockSpec((bt, 128), lambda i: (i, 0))
    return launch(
        tables_kernel,
        (positions[None], segments[None], jnp.concatenate([inverse, inverse])[None]),
        [row, row, resident((1, dim))],
        [wide, wide, wide],
        [shape((rows, dim), F32), shape((rows, dim), F32), shape((rows, 128), jnp.int32)],
        (rows // bt,),
        "tables",
        (0, rows * dim * 12, rows * dim * 2),
        carry=carry,
    )


def side(first, low, high):
    return jnp.where(first, low[...].astype(F32), high[...].astype(F32))


def grad_block(factor, first, base, term, t0, t1, t2, t3, values, scale, inner, others, gain):
    row = inner[0] + jnp.sum(others[:, 0, 0, :], axis=0, keepdims=True)
    inner = jnp.broadcast_to(row, (128, row.shape[1])).T[:, :1]
    scales = scale[...]
    total = term[...].astype(F32) + side(first, t0, t1) + side(first, t2, t3)
    return base[...].astype(F32) + scales * (
        total * gain[...] - values[...].astype(F32) * (scales * scales * inner * factor)
    )


def grad_operands(base, summed, values, scale, gain, base_at, values_at, scale_at, start=0):
    local = base.shape[1]
    bt = summed.half // 2

    def step(i):
        return jnp.clip(i - start, 0, 3)

    def at(chunk, wide):
        return pl.BlockSpec((bt, wide), lambda i: (step(i) + 4 * chunk, 0))

    mine = pl.BlockSpec((bt, local), lambda i: (step(i), lax.axis_index("col")))
    low = pl.BlockSpec((bt, local), lambda i: (jnp.minimum(step(i), 1), 0))
    high = pl.BlockSpec((bt, local), lambda i: (jnp.maximum(step(i) - 2, 0), 0))
    others = summed.inner_others
    args = (base, summed.partial, *summed.pieces(), values, scale, summed.inner, others, gain[None])
    specs = [at(base_at, local), mine, low, high, low, high, at(values_at, local), at(scale_at, 1)]
    specs += [
        pl.BlockSpec((1, 1, bt), lambda i: (0, 0, step(i))),
        pl.BlockSpec((others.shape[0], 1, 1, bt), lambda i: (0, 0, 0, step(i))),
        resident((1, local)),
    ]
    return args, specs, at


def hidden_kernel(factor, *refs):
    grad = grad_block(factor, pl.program_id(0) < 2, *refs[:-2])
    refs[-2][...] = grad
    refs[-1][...] = grad.astype(BF16)


def hidden_grad(launch, base, summed, values, scale, gain, chunk):
    args, specs, at = grad_operands(base, summed, values, scale, gain, chunk, 0, 0)
    rows, local = summed.rows, base.shape[1]
    return launch(
        functools.partial(hidden_kernel, 1.0 / (local * launch.ring.size)),
        args,
        specs,
        [at(0, local), at(0, local)],
        [shape((rows, local), F32), shape((rows, local), BF16)],
        (4,),
        "hidden_grad",
        (0, rows * local * 18, 0),
    )


def settle_kernel(*refs):
    step = pl.program_id(0)
    output = refs[-1]

    def one(hidden, down, p0, p1, p2, p3):
        first = step % 2 == 0
        output[...] = (hidden[...] + (down[...].astype(F32) + side(first, p0, p1) + side(first, p2, p3))).astype(BF16)

    pl.when(step < 2)(lambda: one(*refs[:6]))
    pl.when(step >= 2)(lambda: one(*refs[6:12]))


def settle(launch, hidden, sums, carry=()):
    rows, local = hidden[0].shape
    bt = rows // 2
    args, specs = [], []
    for c in (0, 1):
        here = pl.BlockSpec((bt, local), lambda i, c=c: (jnp.clip(i - 2 * c, 0, 1), 0))
        mine = pl.BlockSpec((bt, local), lambda i, c=c: (jnp.clip(i - 2 * c, 0, 1), lax.axis_index("col")))
        args += [hidden[c], sums[c].partial, *sums[c].pieces()]
        specs += [here, mine] + [Held((bt, local))] * 4
    return launch(
        settle_kernel,
        args,
        specs,
        [pl.BlockSpec((bt, local), lambda i: (i, 0))],
        [shape((2 * rows, local), BF16)],
        (4,),
        "settle",
        (0, rows * local * 24, 0),
        carry=carry,
    )[0]


def last_kernel(factor, *refs):
    step = pl.program_id(0)
    count = (len(refs) - 1) // 2

    @pl.when(step < 4)
    def _():
        refs[-1][...] = grad_block(factor, step < 2, *refs[:count])

    @pl.when(step >= 4)
    def _():
        refs[-1][...] = grad_block(factor, step < 6, *refs[count:-1])


def settle_last(launch, grad_hidden, sums, tokens, scale, gain, carry=()):
    args, specs = [], []
    for c in (0, 1):
        more, more_specs, _ = grad_operands(grad_hidden[c], sums[c], tokens, scale, gain, 0, c, c, 4 * c)
        args += more
        specs += more_specs
    total, local = tokens.shape
    return launch(
        functools.partial(last_kernel, 1.0 / (local * launch.ring.size)),
        args,
        specs,
        [pl.BlockSpec((total // 8, local), lambda i: (i, 0))],
        [shape((total, local), F32)],
        (8,),
        "settle_last",
        (0, total * local * 24, 0),
        carry=carry,
    )[0]


def hand_on_kernel(*refs):
    half = len(refs) // 2
    for source, target in zip(refs[:half], refs[half:]):
        target[...] = source[...]


def hand_on(launch, *arrays):
    steps = 4
    specs = [pl.BlockSpec((a.shape[0] // steps, a.shape[1]), lambda i: (i, 0)) for a in arrays]
    return launch(
        hand_on_kernel, arrays, specs, specs, [shape(a.shape, a.dtype) for a in arrays], (steps,), "hand_on",
        (0, sum(a.size * a.dtype.itemsize * 2 for a in arrays), 0),
    )


def widen_kernel(source, *targets):
    at = 0
    for target in targets:
        target[...] = source[:, at : at + target.shape[1]].astype(F32)
        at += target.shape[1]


def widen(launch, source, *cols):
    rows = source.shape[0]
    whole = [pl.BlockSpec((rows, n), lambda i: (0, 0)) for n in (source.shape[1], *cols)]
    return launch(
        widen_kernel, [source], whole[:1], whole[1:], [shape((rows, n), F32) for n in cols], (1,), "widen",
        (0, source.size * 6, 0),
    )


def after(value, *others):
    return lax.optimization_barrier((value, *jax.tree.leaves(others)))[0]


def body(
    tokens,
    segments,
    positions,
    gain_attn,
    w_query,
    key_weight_matrix,
    value_weight_matrix,
    gain_query,
    gain_key,
    w_out,
    gain_mlp,
    w_gate,
    w_up,
    w_down,
    cotangent,
):
    total, local = tokens.shape
    dim = gain_query.shape[0]
    query_cols, key_cols = w_query.shape[1], key_weight_matrix.shape[1]
    kv = key_cols // dim
    hidden_units = w_gate.shape[1]
    ring = Ring(lax.axis_size("col"))
    launch = Launcher(ring)
    width = local * ring.size
    rows = total // 2
    parts = [slice(0, rows), slice(rows, total)]
    offset = lax.axis_index("col") * local
    gain_attn_local = lax.dynamic_slice_in_dim(gain_attn, offset, local)
    gain_mlp_local = lax.dynamic_slice_in_dim(gain_mlp, offset, local)
    gain_q, gain_k = gain_query[None], gain_key[None]
    bq = tile_of(rows, 512)

    def gathered(weights, axis):
        return lax.all_gather(weights, "row", axis=axis, tiled=True)

    def scattered(partial, axis):
        return lax.psum_scatter(partial, "row", scatter_dimension=axis, tiled=True)

    def carried(*stages):
        for stage in stages:
            for _ in range(ring.stages - 2):
                launch.alone(stage)

    pair = lambda: [None] * 2
    mixed, logs, hidden, mid_low, scale_mid = pair(), pair(), pair(), pair(), pair()
    get_cot, get_mid, get_grad = pair(), pair(), pair()
    sum_out, sum_down, sum_mid, sum_in = pair(), pair(), pair(), pair()
    gain_mlp_part, grad_hidden, gains_in = pair(), pair(), pair()

    qkv_cols = query_cols + 2 * key_cols
    w_attn = gathered(jnp.concatenate([w_query, key_weight_matrix, value_weight_matrix, w_out.T], axis=1), 0)

    get_tok = Gather(ring, tokens, 0, total)
    launch.alone(get_tok)
    w_mlp = gathered(jnp.concatenate([after(w_gate, get_tok.full), w_up, w_down.T], axis=1), 0)
    seg_row = segments[None]
    for _ in range(ring.stages - 2):
        launch.alone(get_tok)
    cosine, sine, seg_wide = tables(launch, positions, segments, dim, [get_tok])
    x_full = get_tok.full

    for c in (0, 1):
        get_cot[c] = Gather(ring, cotangent, c * rows, rows, split=c == 0)
    normed, scale_attn, proj, queries, keys, values = project_qkv(
        launch, x_full, gain_attn[None], w_attn, qkv_cols, gain_q, gain_k, cosine, sine, kv, carry=[get_cot[1]]
    )

    def attention(c, at, carry):
        mixed[c], logs[c] = attend(
            launch, queries, keys, values, after(seg_row, at), seg_wide, c * rows, rows, dim, bq, bq, carry=carry
        )
        return logs[c]

    def start_out(c, at, carry):
        partial = project_out(launch, after(mixed[c], at), w_attn, 0, rows, carry=carry)
        sum_out[c] = Scatter(ring, partial)
        return partial

    def end_out(c):
        hidden[c] = tokens[parts[c]].astype(F32) + sum_out[c].total()
        mid_low[c] = hidden[c].astype(BF16)
        get_mid[c] = Gather(ring, mid_low[c], 0, rows)

    carried(get_cot[1])
    at = attention(1, normed, [get_cot[1]])
    at = start_out(1, at, [get_cot[0]])
    at = attention(0, at, [sum_out[1]])
    carried(sum_out[1])
    launch.alone(sum_out[1])
    end_out(1)
    launch.alone(get_mid[1])
    carried(get_mid[1])
    start_out(0, get_mid[1].full, [get_mid[1]])
    launch.alone(sum_out[0])
    carried(sum_out[0])
    launch.alone(sum_out[0], get_cot[0])
    end_out(0)

    def feed_forward(c, kept, at, carry):
        nm, scale_mid[c], *rest = mlp(
            launch, get_mid[c].full, after(gain_mlp[None], at), w_mlp, get_cot[c].full, c, total, kept,
            carry=carry,
        )
        return (nm, *rest)

    def back_middle(c, kept, at, carry):
        partial, inner, gain_part = back_mid(
            launch, kept[2], kept[3], w_mlp, get_mid[c].full, scale_mid[c], after(gain_mlp[None], at), c, carry=carry
        )
        gain_mlp_part[c] = jnp.sum(gain_part, axis=(0, 1))
        sum_mid[c] = Scatter(ring, partial, inner)
        return partial

    def end_mid(c):
        grad_hidden[c], low = hidden_grad(
            launch, cotangent, sum_mid[c], mid_low[c], scale_mid[c], gain_mlp_local, c
        )
        get_grad[c] = Gather(ring, low, 0, rows)
        return low

    def start_down(c, active, at, carry=()):
        partial = project_out(launch, after(active, at), w_mlp, c, rows, carry=carry)
        sum_down[c] = Scatter(ring, partial, split=True)
        return partial

    kept = feed_forward(1, None, get_mid[1].full, [get_mid[0]])
    carried(get_mid[0], get_cot[0])
    at = start_down(1, kept[1], kept[0], [get_mid[0]])
    at = back_middle(1, kept, at, [get_cot[0], sum_down[1]])
    kept = feed_forward(0, kept, at, [sum_mid[1]])
    normed_mid, active, grad_gate, grad_up = kept
    carried(sum_mid[1])
    partial = weight_grad_pair(
        launch, (active, active), (get_cot[0].full, get_cot[1].full), (0, 1), carry=[sum_mid[1], sum_down[1].near]
    )
    rs_down = scattered(partial, 1)
    low = end_mid(1)
    at = back_middle(0, kept, (partial, low), [get_grad[1]])
    carried(get_grad[1])
    partial = weight_grad(launch, after(normed_mid, at), grad_gate, grad_up, carry=[get_grad[1], sum_mid[0]])
    rs_gate_up = scattered(partial, 0)
    carried(sum_mid[0])
    at = start_down(0, active, partial, [sum_mid[0]])
    low = end_mid(0)

    def mix(c):
        return jnp.dot(get_grad[c].full, w_attn[:, qkv_cols:], preferred_element_type=F32).astype(BF16)

    def attention_back(c, grad_mixed, sums, at, carry):
        return attend_back(
            launch, queries, keys, values, grad_mixed, mixed[c], logs[c], after(seg_row, at), seg_wide, c * rows, dim,
            bq, bq, sums, carry=carry,
        )

    def projection_back(c, grads, low_all, at, carry):
        low_all, partial, inner, *gains_in[c] = back_qkv(
            launch, *grads, proj, cosine, sine, gain_q, gain_k, w_attn, qkv_cols, x_full, scale_attn, after(gain_attn[None], at),
            kv, c, low_all, carry=carry,
        )
        sum_in[c] = Scatter(ring, partial, inner, split=True)
        return low_all, partial

    grads = attention_back(1, mix(1), None, (at, low), [get_grad[0], sum_down[0]])
    carried(get_grad[0])
    low_all, at = projection_back(1, grads, None, None, [get_grad[0], sum_down[0].near])
    grad_mixed = mix(0)
    early = Share("col", *gains_in[1], (gain_mlp_part[0] + gain_mlp_part[1])[None])
    grads = attention_back(0, grad_mixed, grads[1:], (at, rs_down), [sum_in[1], early])
    carried(sum_down[1])
    grad_out = weight_grad_pair(
        launch, (after(mixed[0], grads[0]), mixed[1]), (get_grad[0].full, get_grad[1].full), (0, 0), carry=[sum_down[1]]
    )
    rs_out = scattered(grad_out, 1)
    carried(sum_in[1], sum_down[0])
    low_all, at = projection_back(0, grads, low_all, grad_out, [sum_in[1], sum_down[0]])
    gains = Share("col", *gains_in[0])
    partial = weight_grad(launch, after(normed, at, rs_gate_up), low_all, carry=[sum_in[0], sum_in[1].near, gains])

    grad_qkv = scattered(after(partial, rs_out), 0)
    gains = jnp.concatenate([part.reshape(-1) for part in (*gains.sums, *early.sums)])[None]
    gains = Share("row", gains)
    carried(sum_in[0])
    output = settle(launch, hidden, sum_down, [sum_in[0], sum_in[0].near])
    grad_tokens = settle_last(launch, grad_hidden, sum_in, tokens, scale_attn, gain_attn_local, [gains])
    sum_attn, sum_q, sum_k, more_attn, more_q, more_k, sum_mlp = jnp.split(
        gains.sums[0][0], list(itertools.accumulate([width, dim, dim, width, dim, dim]))
    )
    output, grad_tokens = hand_on(launch, output, grad_tokens)
    grad_query, grad_key, grad_value = widen(launch, grad_qkv, query_cols, key_cols, key_cols)
    return (
        output,
        grad_tokens,
        sum_attn + more_attn,
        grad_query,
        grad_key,
        grad_value,
        sum_q + more_q,
        sum_k + more_k,
        rs_out.astype(F32),
        sum_mlp,
        rs_gate_up[:, :hidden_units].astype(F32),
        rs_gate_up[:, hidden_units:].astype(F32),
        rs_down.astype(F32),
    )


def solution(mesh):
    both, split = P("row", "col"), P("col", "row")
    in_specs = (both, P("row"), P("row"), P(), both, both, both, P(), P(), split, P(), both, both, split, both)
    out_specs = (both, both, P(), both, both, both, P(), P(), split, P(), both, both, split)
    return jax.shard_map(body, mesh=mesh, in_specs=in_specs, out_specs=out_specs, check_vma=False)
```

```python
import functools
import itertools
import math

import jax
import jax.numpy as jnp
from jax import lax
from jax.experimental import pallas as pl
from jax.experimental.pallas import tpu as pltpu
from jax.sharding import PartitionSpec as P

BF16 = jnp.bfloat16
F32 = jnp.float32
EPS = 1e-06
THETA = 1000000.0
LOG2E = 1.4426950408889634
VMEM_LIMIT = 60 * 1024 * 1024
ANY = pl.BlockSpec(memory_space=pl.ANY)


def dot_nt(left, right):
    return lax.dot_general(left, right, (((1,), (1,)), ((), ())), preferred_element_type=F32)


def dot_nn(left, right):
    return jnp.dot(left, right, preferred_element_type=F32)


def dot_tn(left, right):
    return lax.dot_general(left, right, (((0,), (0,)), ((), ())), preferred_element_type=F32)


def shape(dims, dtype):
    return jax.ShapeDtypeStruct(tuple(dims), dtype)


def resident(dims):
    return pl.BlockSpec(dims, lambda *_: (0,) * len(dims), pipeline_mode=pl.Buffered(1))


def held(dims, index):
    return pl.BlockSpec(dims, index, pipeline_mode=pl.Buffered(1))


def tile_of(size, most):
    tile = most
    while size % tile:
        tile //= 2
    return tile


def swap(values):
    half = values.shape[-1] // 2
    return jnp.concatenate([values[:, half:], values[:, :half]], axis=1)


def row_scale(values):
    return lax.rsqrt(jnp.mean(values * values, axis=-1, keepdims=True) + EPS)


def row_of(column):
    return jnp.broadcast_to(column, (column.shape[0], 128)).T[:1]


class Held:
    def __init__(self, dims, row=0, col=0):
        self.dims, self.row, self.col = dims, row, col

    def of(self, ref):
        return ref.at[pl.ds(self.row, self.dims[0]), pl.ds(self.col, self.dims[1])]


class Ring:
    def __init__(self, size):
        self.size = size
        self.stages = size // 2

    def place(self, index):
        half = self.size // 2
        return jnp.where(index < half, index, self.size + half - 1 - index)

    def owner(self, offset):
        return self.place(lax.rem(self.place(lax.axis_index("col")) + offset + self.size, self.size))

    def cols(self, offset, width):
        return pl.ds(pl.multiple_of(self.owner(offset) * width, 128), width)


class Gather:
    def __init__(self, ring, local, row, rows, split=False):
        self.ring, self.local, self.row, self.rows = ring, local, row, rows
        self.width = local.shape[1]
        self.stage, self.full, self.part = 0, None, 2 if split else 0
        self.out = [shape((rows, self.width * ring.size), BF16)]
        self.offsets = [-1, 1]

    def prepare(self):
        if self.stage == 0 or self.part == 0:
            self.stage += 1
        self.ins = [self.full] if self.full is not None else []
        self.alias = {0: 0} if self.ins else {}
        self.count, self.bounce, self.span = 2, [], None
        if self.stage == 1:
            start, size = self.row, self.rows
            if self.part:
                size //= 2
                start += (2 - self.part) * size
                self.part -= 1
            self.span = start, size
            self.ins = self.ins + [self.local]
            self.count, self.bounce = 3, [(size, self.width)]
        return self

    def copies(self, ins, outs):
        ring, full, width, half = self.ring, outs[0], self.width, self.rows // 2
        if self.stage == 1:
            start, size = self.span
            source = ins[-1].at[pl.ds(start, size), :]
            mine = full.at[pl.ds(start - self.row, size), ring.cols(0, width)]
            return [(source, mine, 1), (source, mine, -1), (source, mine, None)]
        from_left, from_right = ring.cols(1 - self.stage, width), ring.cols(self.stage - 1, width)
        if self.stage < ring.stages:
            left, right = full.at[:, from_left], full.at[:, from_right]
        else:
            left, right = full.at[pl.ds(0, half), from_left], full.at[pl.ds(half, half), from_right]
        return [(left, left, 1), (right, right, -1)]

    def finish(self, outs):
        self.full = outs[0]


class Scatter:
    def __init__(self, ring, partial, inner=None, split=False):
        self.ring, self.partial, self.inner = ring, partial, inner
        self.split = split and ring.stages == 2
        self.rows, self.half = partial.shape[0], partial.shape[0] // 2
        self.width = partial.shape[1] // ring.size
        self.stage, self.inner_others, self.bounce, self.alias = 0, None, [], {}
        self.near = Near(self)
        self.scratch = []

    def block(self, offset, low):
        start = (self.half if low else 0, self.ring.owner(offset) * self.width)
        return lax.dynamic_slice(self.partial, start, (self.half, self.width)).astype(F32)

    def prepare(self):
        self.stage += 1
        stage, stages = self.stage, self.ring.stages
        whole = stage < stages
        self.offsets = [-1, 1]
        if stage == 1:
            self.ins = [self.partial]
        elif stages == 2:
            self.ins, self.scratch = [self.partial, *self.got[:2]], [(self.half, self.width)] * 4
            if not self.split:
                self.kept = self.got[2:]
        else:
            top = self.block(stages + 1 - stage, False) + self.got[0].astype(F32)
            bottom = self.block(stage - 1 - stages, True) + self.got[1].astype(F32)
            self.ins = [top.astype(BF16), bottom.astype(BF16)]
            if whole:
                low = self.block(stages - stage, True) + self.got[2].astype(F32)
                high = self.block(stage - stages, False) + self.got[3].astype(F32)
                self.ins += [low.astype(BF16), high.astype(BF16)]
            elif not self.split:
                self.kept = self.got[2:]
        self.out = [shape((self.half, self.width), BF16)] * (4 if whole and not self.split else 2)
        self.count = len(self.out)
        if stage == 1 and not self.split:
            self.near.add_inner(self)
        return self

    def far_copies(self, ins, outs):
        top, bottom = pl.ds(0, self.half), pl.ds(self.half, self.half)
        far = self.ring.cols(self.ring.stages, self.width)
        return [(ins[0].at[top, far], outs[0], 1), (ins[0].at[bottom, far], outs[1], -1)]

    def loads(self, ins, held):
        top, bottom = pl.ds(0, self.half), pl.ds(self.half, self.half)
        right, left = self.ring.cols(1, self.width), self.ring.cols(-1, self.width)
        sources = [ins[0].at[top, right], ins[0].at[bottom, left], ins[1], ins[2]]
        self.held = held
        return list(zip(sources, held))

    def combine(self):
        for term, others in zip(self.held[:2], self.held[2:]):
            term[...] = (term[...].astype(F32) + others[...].astype(F32)).astype(BF16)

    def copies(self, ins, outs):
        if self.scratch:
            return [(self.held[0], outs[0], 1), (self.held[1], outs[1], -1)]
        if self.stage > 1:
            return [(ref, out, way) for ref, out, way in zip(ins, outs, (1, -1, 1, -1))]
        made = self.far_copies(ins, outs)
        if not self.split:
            made += self.near.near_copies(ins, outs[2:])
        return made

    def finish(self, outs):
        if self.stage == 1 and not self.split:
            outs = [*outs[:2], *self.near.take(outs[2:])]
        self.got = outs

    def pieces(self):
        return self.got[0], self.kept[0], self.kept[1], self.got[1]

    def total(self):
        mine = lax.dynamic_slice_in_dim(self.partial, lax.axis_index("col") * self.width, self.width, 1)
        left = jnp.concatenate([self.got[0], self.kept[0]]).astype(F32)
        right = jnp.concatenate([self.kept[1], self.got[1]]).astype(F32)
        return mine.astype(F32) + left + right


class Near:
    def __init__(self, whole):
        self.whole = whole
        self.bounce, self.alias = [], {}

    @property
    def empty(self):
        return not self.whole.split

    def add_inner(self, stage):
        whole = self.whole
        if whole.inner is not None:
            others = whole.ring.size - 1
            stage.ins = stage.ins + [whole.inner]
            stage.out = stage.out + [shape((others, *whole.inner.shape), F32)]
            stage.count += others
            stage.offsets = list(range(1, whole.ring.size))

    def prepare(self):
        whole = self.whole
        self.ins, self.offsets, self.count = [whole.partial], [-1, 1], 2
        self.out = [shape((whole.half, whole.width), BF16)] * 2
        self.add_inner(self)
        return self

    def near_copies(self, ins, outs):
        whole, ring = self.whole, self.whole.ring
        top, bottom = pl.ds(0, whole.half), pl.ds(whole.half, whole.half)
        made = [
            (ins[0].at[bottom, ring.cols(ring.stages - 1, whole.width)], outs[0], 1),
            (ins[0].at[top, ring.cols(1 - ring.stages, whole.width)], outs[1], -1),
        ]
        if whole.inner is not None:
            made += [(ins[1], outs[2].at[k - 1], k) for k in range(1, ring.size)]
        return made

    def copies(self, ins, outs):
        return self.near_copies(ins, outs)

    def take(self, outs):
        whole = self.whole
        if whole.inner is not None:
            whole.inner_others = outs[2]
        return outs[:2]

    def finish(self, outs):
        self.whole.kept = self.take(outs)


class Share:
    def __init__(self, axis, *arrays):
        self.axis, self.arrays = axis, arrays
        self.size = lax.axis_size(axis)
        self.bounce, self.alias = [], {}
        self.offsets = [(axis, k) for k in range(1, self.size)]

    def prepare(self):
        self.ins, self.out = list(self.arrays), [shape((self.size, *a.shape), F32) for a in self.arrays]
        self.count = (self.size - 1) * len(self.arrays)
        return self

    def copies(self, ins, outs):
        here = lax.axis_index(self.axis)
        return [(a, out.at[here], offset) for a, out in zip(ins, outs) for offset in self.offsets]

    def finish(self, outs):
        self.sums = []
        for mine, out in zip(self.arrays, outs):
            here = lax.broadcasted_iota(jnp.int32, out.shape, 0) == lax.axis_index(self.axis)
            self.sums.append(jnp.sum(jnp.where(here, mine[None], out), axis=0))


class Launcher:
    def __init__(self, ring):
        self.ring = ring
        self.ids = itertools.count()

    def __call__(self, kernel, args, in_specs, out_specs, out_shape, grid, name, cost, alias=None, scratch=(), carry=()):
        stages = [stage.prepare() for stage in carry if not getattr(stage, "empty", False)]
        own_in, own_out = len(args), len(out_shape)
        held_in = [(i, spec) for i, spec in enumerate(in_specs) if isinstance(spec, Held)]
        held_out = [(i, spec) for i, spec in enumerate(out_specs) if isinstance(spec, Held)]
        held_types = [args[i].dtype for i, _ in held_in] + [out_shape[i].dtype for i, _ in held_out]
        in_specs = [ANY if isinstance(spec, Held) else spec for spec in in_specs]
        out_specs = [ANY if isinstance(spec, Held) else spec for spec in out_specs]
        args, in_specs, out_specs, out_shape = list(args), list(in_specs), list(out_specs), list(out_shape)
        alias, scratch = dict(alias or {}), list(scratch)
        own_scratch = len(scratch)
        scratch += [pltpu.VMEM(spec.dims, kind) for (_, spec), kind in zip(held_in + held_out, held_types)]
        if held_types:
            scratch.append(pltpu.SemaphoreType.DMA((len(held_types),)))
        spans = []
        for stage in stages:
            ins, outs = len(args), len(out_shape)
            alias.update({ins + i: outs + o for i, o in stage.alias.items()})
            args += stage.ins
            out_shape += stage.out
            spans.append((ins, len(args), outs, len(out_shape)))
        in_specs += [ANY] * (len(args) - own_in)
        out_specs += [ANY] * (len(out_shape) - own_out)
        more = {}
        if stages:
            count = sum(stage.count for stage in stages)
            scratch += [pltpu.SemaphoreType.DMA((count,)), pltpu.SemaphoreType.DMA((count,))]
            more = dict(collective_id=next(self.ids), has_side_effects=True)
            scratch += [pltpu.VMEM(dims, BF16) for stage in stages for dims in stage.bounce]
        summed = [stage for stage in stages if getattr(stage, "scratch", None)]
        if summed:
            scratch += [pltpu.VMEM(dims, BF16) for stage in summed for dims in stage.scratch]
            scratch.append(pltpu.SemaphoreType.DMA((4 * len(summed),)))
        offsets = {o if isinstance(o, tuple) else ("col", o % self.ring.size) for stage in stages for o in stage.offsets}
        offsets = sorted(offsets)
        ring = self.ring

        def device(way):
            if not isinstance(way, tuple):
                way = ("col", way)
            axis, offset = way
            if axis == "col":
                return {axis: ring.owner(offset)}
            return {axis: lax.rem(lax.axis_index(axis) + offset, lax.axis_size(axis))}

        total_in, total_out = len(args), len(out_shape)

        def body(*refs):
            ins, outs, rest = refs[:total_in], refs[total_in : total_in + total_out], refs[total_in + total_out :]
            own_ins, own_outs = list(ins[:own_in]), list(outs[:own_out])
            own, rest = rest[:own_scratch], rest[own_scratch:]
            inward, outward = [], []
            if held_types:
                buffers, sems, rest = rest[: len(held_types)], rest[len(held_types)], rest[len(held_types) + 1 :]
                for k, (at, spec) in enumerate(held_in):
                    inward.append((spec.of(own_ins[at]), buffers[k], sems.at[k]))
                    own_ins[at] = buffers[k]
                for k, (at, spec) in enumerate(held_out, len(held_in)):
                    outward.append((buffers[k], spec.of(own_outs[at]), sems.at[k]))
                    own_outs[at] = buffers[k]
            own = (*own_ins, *own_outs, *own)
            loads = []
            if summed:
                *rest, buffers, sems = (*rest[: -4 * len(summed) - 1], rest[-4 * len(summed) - 1 : -1], rest[-1])
                for stage, (a, b, _, _) in zip(stages, spans):
                    if stage in summed:
                        k = 4 * summed.index(stage)
                        for at, pair in enumerate(stage.loads(ins[a:b], buffers[k : k + 4]), k):
                            loads.append((*pair, sems.at[at]))
            send, receive, *bounce = rest if stages else (None, None)

            def copies(part, which=(False, True)):
                made, at, held = [], 0, 0
                for stage, (a, b, c, d) in zip(stages, spans):
                    for source, target, way in stage.copies(ins[a:b], outs[c:d]):
                        if way is None:
                            if part == "in":
                                made.append(pltpu.make_async_copy(source, bounce[held], receive.at[at]))
                            elif part == "out":
                                made.append(pltpu.make_async_copy(bounce[held], target, send.at[at]))
                            held += 1
                        elif part == "remote" and (stage in summed) in which:
                            made.append(
                                pltpu.make_async_remote_copy(
                                    source, target, send.at[at], receive.at[at], device_id=device(way),
                                    device_id_type=pl.DeviceIdType.MESH,
                                )
                            )
                        at += 1
                return made

            first = last = True
            for axis, size in enumerate(grid):
                first &= pl.program_id(axis) == 0
                last &= pl.program_id(axis) == size - 1
            @pl.when(first)
            def _():
                if stages:
                    barrier = pltpu.get_barrier_semaphore()
                    for offset in offsets:
                        pl.semaphore_signal(
                            barrier, 1, device_id=device(offset), device_id_type=pl.DeviceIdType.MESH
                        )
                for copy in inward:
                    pltpu.make_async_copy(*copy).start()
                if stages:
                    for copy in copies("in"):
                        copy.start()
                    for copy in loads:
                        pltpu.make_async_copy(*copy).start()
                    pl.semaphore_wait(barrier, len(offsets))
                    for copy in copies("remote", (False,)):
                        copy.start()
                    for copy in loads:
                        pltpu.make_async_copy(*copy).wait()
                    for stage in summed:
                        stage.combine()
                    for copy in copies("remote", (True,)):
                        copy.start()
                for copy in inward:
                    pltpu.make_async_copy(*copy).wait()

            kernel(*own)

            @pl.when(first)
            def _():
                for copy in outward:
                    pltpu.make_async_copy(*copy).start()
                if stages:
                    for here, there in zip(copies("in"), copies("out")):
                        here.wait()
                        there.start()

            @pl.when(last)
            def _():
                for copy in outward:
                    pltpu.make_async_copy(*copy).wait()
                if stages:
                    for copy in copies("out") + copies("remote"):
                        copy.wait()

        flops, moved, exps = cost
        made = pl.pallas_call(
            body,
            grid=grid,
            in_specs=in_specs,
            out_specs=out_specs,
            out_shape=out_shape,
            input_output_aliases=alias,
            scratch_shapes=scratch,
            compiler_params=pltpu.CompilerParams(vmem_limit_bytes=VMEM_LIMIT, **more),
            cost_estimate=pl.CostEstimate(flops=int(flops), bytes_accessed=int(moved), transcendentals=int(exps)),
            name=name,
        )(*args)
        for stage, (_, _, c, d) in zip(stages, spans):
            stage.finish(made[c:d])
        return made[:own_out]

    def alone(self, *stages):
        self(lambda *_: None, [], [], [], [], (1,), "exchange", (0, 0, 0), carry=stages)


def lane_repeat(column, width):
    return jnp.concatenate([column] * (width // column.shape[1]), axis=1)


def causal(bk, bq, shift):
    key_at = lax.broadcasted_iota(jnp.int32, (bk, bq), 0)
    query_at = lax.broadcasted_iota(jnp.int32, (bk, bq), 1)
    return key_at + shift <= query_at


def fwd_kernel(q0, bk, q_ref, k_ref, v_ref, seg_q_ref, seg_k_ref, out_ref, log_ref, vt):
    bq, wide = q_ref.shape
    dim = k_ref.shape[1]
    group = wide // dim
    step = pl.program_id(1)
    factor = LOG2E / math.sqrt(dim)

    @pl.when(step == 0)
    def _():
        for j in range(vt.shape[0]):
            vt[j] = v_ref[pl.ds(j * bk, bk), :].astype(F32).T.astype(BF16)

    seg_q = seg_q_ref[...]
    queries = [q_ref[:, h * dim : (h + 1) * dim] for h in range(group)]

    def block(j, carry, shift):
        key_rows = k_ref[pl.ds(pl.multiple_of(j * bk, bk), bk), :]
        seg_k = seg_k_ref[pl.ds(pl.multiple_of(j * bk, bk), bk), :]
        allowed = lane_repeat(seg_k, bq) == seg_q
        if shift is not None:
            allowed &= causal(bk, bq, shift)
        value_cols = vt[j]
        new = []
        for h in range(group):
            total, acc = carry[2 * h], carry[2 * h + 1]
            scores = dot_nt(key_rows, queries[h])
            weights = jnp.where(allowed, jnp.exp2(scores * factor), 0.0)
            total = total + jnp.sum(weights.reshape(bk // 8, 8, bq), axis=0)
            acc = acc + dot_nn(value_cols, weights.astype(BF16))
            new += [total, acc]
        return tuple(new)

    carry = (jnp.zeros((8, bq), F32), jnp.zeros((dim, bq), F32)) * group
    diag = bq // bk
    whole = q0 // bk + step * diag
    carry = lax.fori_loop(0, whole, lambda j, c: block(j, c, None), carry)
    for d in range(diag):
        carry = block(whole + d, carry, d * bk)
    for h in range(group):
        total = jnp.sum(carry[2 * h], axis=0, keepdims=True)
        mixed = carry[2 * h + 1] * (1.0 / total)
        out_ref[:, h * dim : (h + 1) * dim] = mixed.T.astype(BF16)
        log_ref[0, h : h + 1, :] = jnp.log2(total)


def attend(launch, queries, keys, values, seg_row, seg_wide, q0, rows, dim, bq, bk, carry=()):
    width = queries.shape[1]
    span = q0 + rows
    kv = keys.shape[1] // dim
    group = width // dim // kv
    pairs = group * kv * rows * (span - rows / 2)
    base = q0 // bq
    whole = pl.BlockSpec((span, dim), lambda k, i: (0, k))
    return launch(
        functools.partial(fwd_kernel, q0, bk),
        (queries, keys, values, seg_row, seg_wide),
        [
            pl.BlockSpec((bq, group * dim), lambda k, i: (i + base, k)),
            whole,
            whole,
            pl.BlockSpec((1, bq), lambda k, i: (0, i + base)),
            pl.BlockSpec((span, 128), lambda k, i: (0, 0)),
        ],
        [
            pl.BlockSpec((bq, group * dim), lambda k, i: (i, k)),
            pl.BlockSpec((1, group, bq), lambda k, i: (k, 0, i)),
        ],
        [shape((rows, width), BF16), shape((kv, group, rows), F32)],
        (kv, rows // bq),
        "attend",
        (pairs * dim * 8, rows * width * 4, pairs),
        scratch=[pltpu.VMEM((span // bk, dim, bk), BF16)],
        carry=carry,
    )


def bwd_kernel(q0, bk, first, *refs):
    q_ref, k_ref, v_ref, g_ref, o_ref, log_ref, seg_q_ref, seg_k_ref = refs[:8]
    dk_in, dv_in = (None, None) if first else refs[8:10]
    dq_ref, dk_ref, dv_ref, kt = refs[-4:]
    bq, wide = q_ref.shape
    dim = k_ref.shape[1]
    group = wide // dim
    step = pl.program_id(1)
    scale = 1.0 / math.sqrt(dim)
    factor = LOG2E * scale

    @pl.when(step == 0)
    def _():
        for j in range(kt.shape[0]):
            kt[j] = k_ref[pl.ds(j * bk, bk), :].astype(F32).T.astype(BF16)
        if first:
            dk_ref[...] = jnp.zeros_like(dk_ref)
            dv_ref[...] = jnp.zeros_like(dv_ref)
        else:
            dk_ref[...] = dk_in[...]
            dv_ref[...] = dv_in[...]

    seg_q = seg_q_ref[...]
    queries = [q_ref[:, h * dim : (h + 1) * dim] for h in range(group)]
    grads = [g_ref[:, h * dim : (h + 1) * dim] for h in range(group)]
    logs = [log_ref[0, h : h + 1, :] for h in range(group)]
    inner = []
    for h in range(group):
        product = grads[h].astype(F32) * o_ref[:, h * dim : (h + 1) * dim].astype(F32)
        inner.append(jnp.sum(product.T, axis=0, keepdims=True))

    def block(j, carry, shift):
        at = pl.ds(pl.multiple_of(j * bk, bk), bk)
        key_rows = k_ref[at, :]
        value_rows = v_ref[at, :]
        allowed = lane_repeat(seg_k_ref[at, :], bq) == seg_q
        if shift is not None:
            allowed &= causal(bk, bq, shift)
        key_cols = kt[j]
        new = []
        dk, dv = dk_ref[at, :], dv_ref[at, :]
        for h in range(group):
            scores = dot_nt(key_rows, queries[h])
            probs = jnp.where(allowed, jnp.exp2(scores * factor - logs[h]), 0.0)
            grad_probs = dot_nt(value_rows, grads[h])
            grad_scores = (probs * (grad_probs - inner[h])).astype(BF16)
            dv = dv + dot_nn(probs.astype(BF16), grads[h])
            dk = dk + dot_nn(grad_scores, queries[h])
            new.append(carry[h] + dot_nn(key_cols, grad_scores))
        dk_ref[at, :] = dk
        dv_ref[at, :] = dv
        return tuple(new)

    carry = (jnp.zeros((dim, bq), F32),) * group
    diag = bq // bk
    whole = q0 // bk + step * diag
    carry = lax.fori_loop(0, whole, lambda j, c: block(j, c, None), carry)
    for d in range(diag):
        carry = block(whole + d, carry, d * bk)
    for h in range(group):
        dq_ref[:, h * dim : (h + 1) * dim] = (carry[h] * scale).T


def attend_back(launch, queries, keys, values, grads, mixed, logs, seg_row, seg_wide, q0, dim, bq, bk, sums, carry=()):
    rows, width = grads.shape
    span = q0 + rows
    kv = keys.shape[1] // dim
    group = width // dim // kv
    pairs = group * kv * rows * (span - rows / 2)
    base = q0 // bq
    whole = pl.BlockSpec((span, dim), lambda k, i: (0, k))
    part = pl.BlockSpec((bq, group * dim), lambda k, i: (i, k))
    more = [] if sums is None else list(sums)
    return launch(
        functools.partial(bwd_kernel, q0, bk, sums is None),
        (queries, keys, values, grads, mixed, logs, seg_row, seg_wide, *more),
        [
            pl.BlockSpec((bq, group * dim), lambda k, i: (i + base, k)),
            whole,
            whole,
            part,
            part,
            pl.BlockSpec((1, group, bq), lambda k, i: (k, 0, i)),
            pl.BlockSpec((1, bq), lambda k, i: (0, i + base)),
            pl.BlockSpec((span, 128), lambda k, i: (0, 0)),
        ]
        + [whole] * len(more),
        [part, whole, whole],
        [shape((rows, width), F32), shape((span, kv * dim), F32), shape((span, kv * dim), F32)],
        (kv, rows // bq),
        "attend_back",
        (pairs * dim * 20, rows * width * 10, pairs),
        scratch=[pltpu.VMEM((span // bk, dim, bk), BF16)],
        carry=carry,
    )


def qkv_kernel(kv, x_ref, gain_ref, w_ref, gq_ref, gk_ref, cos_ref, sin_ref, *refs):
    normed_ref, scale_ref, proj_ref, q_ref, k_ref, v_ref = refs[-6:]
    dim = gq_ref.shape[1]
    heads = q_ref.shape[1] // dim
    values = x_ref[...].astype(F32)
    scale = row_scale(values)
    normed = (values * scale * gain_ref[...]).astype(BF16)
    normed_ref[...] = normed
    scale_ref[...] = scale
    projected = dot_nn(normed, w_ref[...])
    cosine, sine = cos_ref[...], sin_ref[...]
    wide = (heads + kv) * dim
    proj_ref[...] = projected[:, :wide]
    for h in range(heads + kv):
        part = projected[:, h * dim : (h + 1) * dim]
        gain = gq_ref[...] if h < heads else gk_ref[...]
        part = part * row_scale(part) * gain
        turned = (part * cosine + swap(part) * sine).astype(BF16)
        if h < heads:
            q_ref[:, h * dim : (h + 1) * dim] = turned
        else:
            k_ref[:, (h - heads) * dim : (h - heads + 1) * dim] = turned
    v_ref[...] = projected[:, wide:].astype(BF16)


def project_qkv(launch, x, gain, weights, cols, gain_q, gain_k, cosine, sine, kv, carry=()):
    rows, width = x.shape
    dim = gain_q.shape[1]
    heads = cols // dim - 2 * kv
    bt = tile_of(rows, 512)
    wide = (heads + kv) * dim

    def part(w):
        return pl.BlockSpec((bt, w), lambda i: (i, 0))

    return launch(
        functools.partial(qkv_kernel, kv),
        (x, gain, weights, gain_q, gain_k, cosine, sine),
        [
            part(width),
            resident((1, width)),
            Held((width, cols)),
            resident((1, dim)),
            resident((1, dim)),
            part(dim),
            part(dim),
        ],
        [part(width), part(1), part(wide), part(heads * dim), part(kv * dim), part(kv * dim)],
        [
            shape((rows, width), BF16),
            shape((rows, 1), F32),
            shape((rows, wide), F32),
            shape((rows, heads * dim), BF16),
            shape((rows, kv * dim), BF16),
            shape((rows, kv * dim), BF16),
        ],
        (rows // bt,),
        "project_qkv",
        (2 * rows * width * cols, rows * width * 4 + width * cols * 2, 0),
        carry=carry,
    )


def mlp_kernel(x_ref, gain_ref, wg_ref, wu_ref, wd_ref, cot_ref, *refs):
    normed_ref, scale_ref, active_ref, gg_ref, gu_ref = refs[-5:]

    @pl.when(pl.program_id(1) == 0)
    def _():
        values = x_ref[...].astype(F32)
        scale = row_scale(values)
        normed_ref[...] = (values * scale * gain_ref[...]).astype(BF16)
        scale_ref[...] = scale

    normed = normed_ref[...]
    gate = dot_nn(normed, wg_ref[...])
    up = dot_nn(normed, wu_ref[...])
    grad = dot_nn(cot_ref[...], wd_ref[...])
    sig = jax.nn.sigmoid(gate)
    silu = gate * sig
    active_ref[...] = (silu * up).astype(BF16)
    gu_ref[...] = (grad * silu).astype(BF16)
    gg_ref[...] = (grad * up * (sig + silu * (1.0 - sig))).astype(BF16)


def mlp(launch, x, gain, weights, cot, chunk, total, kept, carry=()):
    rows, width = x.shape
    hidden = weights.shape[1] // 3
    bn = tile_of(hidden, 256)
    tiles = hidden // bn
    more = [] if kept is None else list(kept)
    tile = pl.BlockSpec((rows, bn), lambda i, j: (chunk, j))
    low = shape((total, hidden), BF16)
    return launch(
        mlp_kernel,
        (x, gain, weights, weights, weights, cot, *more),
        [
            Held((rows, width)),
            resident((1, width)),
            pl.BlockSpec((width, bn), lambda i, j: (0, j)),
            pl.BlockSpec((width, bn), lambda i, j: (0, j + tiles)),
            pl.BlockSpec((width, bn), lambda i, j: (0, j + 2 * tiles)),
            Held((rows, width)),
        ]
        + [ANY] * len(more),
        [Held((rows, width), chunk * rows), pl.BlockSpec((rows, 1), lambda i, j: (0, 0)), tile, tile, tile],
        [shape((total, width), BF16), shape((rows, 1), F32), low, low, low],
        (1, tiles),
        "mlp",
        (6 * rows * width * hidden, rows * (width + hidden) * 6 + 6 * width * hidden, rows * hidden),
        alias={6: 0, 7: 2, 8: 3, 9: 4} if more else None,
        carry=carry,
    )


def mid_kernel(gg_ref, gu_ref, w_ref, v_ref, scale_ref, gain_ref, part_ref, inner_ref, gain_out):
    hidden = gg_ref.shape[1]
    partial = dot_nt(gg_ref[...], w_ref[:, :hidden]) + dot_nt(gu_ref[...], w_ref[:, hidden:])
    part_ref[...] = partial.astype(BF16)
    product = partial * v_ref[...].astype(F32)
    gain_out[0] = jnp.sum(product * scale_ref[...], axis=0, keepdims=True)
    inner = row_of(jnp.sum(product * gain_ref[...], axis=1, keepdims=True))

    @pl.when(pl.program_id(1) == 0)
    def _():
        inner_ref[0] = inner

    @pl.when(pl.program_id(1) > 0)
    def _():
        inner_ref[0] += inner


def back_mid(launch, gg, gu, weights, values, scale, gain, chunk, carry=()):
    rows, width = values.shape
    hidden = gg.shape[1]
    bn = tile_of(width, 512)
    return launch(
        mid_kernel,
        (gg, gu, weights, values, scale, gain),
        [
            Held((rows, hidden), chunk * rows),
            Held((rows, hidden), chunk * rows),
            pl.BlockSpec((bn, 2 * hidden), lambda i, j: (j, 0)),
            pl.BlockSpec((rows, bn), lambda i, j: (0, j)),
            pl.BlockSpec((rows, 1), lambda i, j: (0, 0)),
            pl.BlockSpec((1, bn), lambda i, j: (0, j)),
        ],
        [
            pl.BlockSpec((rows, bn), lambda i, j: (0, j)),
            pl.BlockSpec((1, 1, rows), lambda i, j: (0, 0, 0)),
            pl.BlockSpec((1, 1, bn), lambda i, j: (0, 0, j)),
        ],
        [shape((rows, width), BF16), shape((1, 1, rows), F32), shape((1, 1, width), F32)],
        (1, width // bn),
        "back_mid",
        (4 * rows * width * hidden, rows * (width + hidden) * 4 + 4 * width * hidden, 0),
        carry=carry,
    )


def qkv_back_kernel(
    kv, dq_ref, dk_ref, dv_ref, proj_ref, cos_ref, sin_ref, gq_ref, gk_ref, w_ref, v_ref, scale_ref, gain_ref, *refs
):
    low_ref, part_ref, inner_ref, gain_out, gq_out, gk_out = refs[-6:]
    dim = gq_ref.shape[1]
    heads = dq_ref.shape[1] // dim
    wide = (heads + kv) * dim

    @pl.when(pl.program_id(1) == 0)
    def _():
        cosine, sine = cos_ref[...], sin_ref[...]
        sums = [jnp.zeros((1, dim), F32), jnp.zeros((1, dim), F32)]
        for h in range(heads + kv):
            is_key = h >= heads
            if is_key:
                grad = dk_ref[:, (h - heads) * dim : (h - heads + 1) * dim] * (1.0 / math.sqrt(dim))
            else:
                grad = dq_ref[:, h * dim : (h + 1) * dim]
            grad = grad * cosine + swap(grad * sine)
            value = proj_ref[:, h * dim : (h + 1) * dim]
            scale = row_scale(value)
            sums[is_key] += jnp.sum(grad * value * scale, axis=0, keepdims=True)
            weighted = grad * (gk_ref[...] if is_key else gq_ref[...])
            mean = jnp.mean(weighted * value, axis=-1, keepdims=True)
            low_ref[:, h * dim : (h + 1) * dim] = (scale * (weighted - value * scale * scale * mean)).astype(BF16)
        low_ref[:, wide:] = dv_ref[...].astype(BF16)
        gq_out[0] = sums[0]
        gk_out[0] = sums[1]

    partial = dot_nt(low_ref[...], w_ref[...])
    part_ref[...] = partial.astype(BF16)
    product = partial * v_ref[...].astype(F32)
    gain_out[0] = jnp.sum(product * scale_ref[...], axis=0, keepdims=True)
    inner = row_of(jnp.sum(product * gain_ref[...], axis=1, keepdims=True))

    @pl.when(pl.program_id(1) == 0)
    def _():
        inner_ref[0] = inner

    @pl.when(pl.program_id(1) > 0)
    def _():
        inner_ref[0] += inner


def back_qkv(launch, dq, dk, dv, proj, cosine, sine, gain_q, gain_k, weights, cols, values, scale, gain, kv, chunk, kept, carry=()):
    total, width = values.shape
    rows = dq.shape[0]
    dim = gain_q.shape[1]
    bt = rows
    bn = tile_of(width, 512)
    base = chunk

    def here(w):
        return Held((rows, w))

    def there(w):
        return Held((rows, w), chunk * rows)

    row = pl.BlockSpec((1, 1, dim), lambda i, j: (i, 0, 0))
    more = [] if kept is None else [kept]
    return launch(
        functools.partial(qkv_back_kernel, kv),
        (dq, dk, dv, proj, cosine, sine, gain_q, gain_k, weights, values, scale, gain, *more),
        [
            here(dq.shape[1]),
            there(dk.shape[1]),
            there(dv.shape[1]),
            there(proj.shape[1]),
            there(dim),
            there(dim),
            resident((1, dim)),
            resident((1, dim)),
            pl.BlockSpec((bn, cols), lambda i, j: (j, 0)),
            pl.BlockSpec((bt, bn), lambda i, j: (i + base, j)),
            pl.BlockSpec((rows, 1), lambda i, j: (chunk, 0)),
            pl.BlockSpec((1, bn), lambda i, j: (0, j)),
        ]
        + [ANY] * len(more),
        [
            there(cols),
            pl.BlockSpec((bt, bn), lambda i, j: (i, j)),
            pl.BlockSpec((1, 1, bt), lambda i, j: (i, 0, 0)),
            pl.BlockSpec((1, 1, bn), lambda i, j: (i, 0, j)),
            row,
            row,
        ],
        [
            shape((total, cols), BF16),
            shape((rows, width), BF16),
            shape((rows // bt, 1, bt), F32),
            shape((rows // bt, 1, width), F32),
            shape((rows // bt, 1, dim), F32),
            shape((rows // bt, 1, dim), F32),
        ],
        (rows // bt, width // bn),
        "back_qkv",
        (2 * rows * width * cols, rows * width * 4 + rows * cols * 10, 0),
        alias={12: 0} if more else None,
        carry=carry,
    )


def pair_kernel(low_ref, high_ref, first_ref, second_ref, out_ref):
    out_ref[...] = (dot_tn(low_ref[...], first_ref[...]) + dot_tn(high_ref[...], second_ref[...])).astype(BF16)


def weight_grad_pair(launch, lefts, rights, rows_at, carry=()):
    rows, cols = rights[0].shape
    width = lefts[0].shape[1]
    bm = next(size for size in (1024, 768, 512, 256, 128) if width % size == 0)
    bn = tile_of(cols, 512)

    def left(k):
        return pl.BlockSpec((rows, bm), lambda i, j: (rows_at[k], i))

    right = pl.BlockSpec((rows, bn), lambda i, j: (0, j))
    return launch(
        pair_kernel,
        (*lefts, *rights),
        [left(0), left(1), right, right],
        [pl.BlockSpec((bm, bn), lambda i, j: (i, j))],
        [shape((width, cols), BF16)],
        (width // bm, cols // bn),
        "weight_grad",
        (4 * rows * width * cols, rows * (width + cols) * 4 + width * cols * 2, 0),
        carry=carry,
    )[0]


def grad_kernel(tiles, left_ref, *refs):
    rights, out_ref = refs[:-1], refs[-1]
    for k, right in enumerate(rights):
        @pl.when(pl.program_id(1) // tiles == k)
        def _():
            out_ref[...] = dot_tn(left_ref[...], right[...]).astype(BF16)


def weight_grad(launch, left, *rights, carry=()):
    rows, width = left.shape
    cols = rights[0].shape[1]
    bm = next(size for size in (1024, 768, 512, 256, 128) if width % size == 0)
    bn = next(size for size in (512, 384, 256, 128) if cols % size == 0)
    tiles = cols // bn

    def part(k):
        return pl.BlockSpec((rows, bn), lambda i, j: (0, jnp.clip(j - k * tiles, 0, tiles - 1)))

    return launch(
        functools.partial(grad_kernel, tiles),
        (left, *rights),
        [pl.BlockSpec((rows, bm), lambda i, j: (0, i))] + [part(k) for k in range(len(rights))],
        [pl.BlockSpec((bm, bn), lambda i, j: (i, j))],
        [shape((width, cols * len(rights)), BF16)],
        (width // bm, tiles * len(rights)),
        "weight_grad",
        (2 * rows * width * cols * len(rights), rows * (width + cols) * 2 + width * cols * 4, 0),
        carry=carry,
    )[0]


def out_kernel(left_ref, right_ref, out_ref):
    out_ref[...] = dot_nt(left_ref[...], right_ref[...]).astype(BF16)


def project_out(launch, left, weights, chunk, rows, carry=()):
    width, hidden = weights.shape[0], left.shape[1]
    bn = tile_of(width, 512)
    last = weights.shape[1] // hidden - 1
    return launch(
        out_kernel,
        (left, weights),
        [Held((rows, hidden), chunk * rows), pl.BlockSpec((bn, hidden), lambda i, j: (j, last))],
        [pl.BlockSpec((rows, bn), lambda i, j: (0, j))],
        [shape((rows, width), BF16)],
        (1, width // bn),
        "project_out",
        (2 * rows * width * hidden, rows * (width + hidden) * 2 + width * hidden * 2, 0),
        carry=carry,
    )[0]


def mix_kernel(left_ref, right_ref, out_ref):
    out_ref[...] = dot_nn(left_ref[...], right_ref[...]).astype(BF16)


def grad_mix(launch, grads, weights, cols):
    rows, width = grads.shape
    bt = tile_of(rows, 512)
    return launch(
        mix_kernel,
        (grads, weights),
        [pl.BlockSpec((bt, width), lambda i: (i, 0)), Held((width, cols), 0, weights.shape[1] - cols)],
        [pl.BlockSpec((bt, cols), lambda i: (i, 0))],
        [shape((rows, cols), BF16)],
        (rows // bt,),
        "grad_mix",
        (2 * rows * width * cols, (rows * width + rows * cols + width * cols) * 2, 0),
    )[0]


def tables_kernel(position_ref, segment_ref, inverse_ref, cos_ref, sin_ref, wide_ref):
    def column(row):
        return jnp.broadcast_to(row.astype(F32), (128, row.shape[1])).T

    angle = column(position_ref[...]) * inverse_ref[...]
    half = lax.broadcasted_iota(jnp.int32, angle.shape, 1) < angle.shape[1] // 2
    sine = jnp.sin(angle)
    cos_ref[...] = jnp.cos(angle)
    sin_ref[...] = jnp.where(half, -sine, sine)
    wide_ref[...] = column(segment_ref[...]).astype(jnp.int32)


def tables(launch, positions, segments, dim, carry=()):
    rows = positions.shape[0]
    bt = tile_of(rows, 512)
    inverse = THETA ** (-(jnp.arange(dim // 2, dtype=F32) * 2.0 / dim))
    row = pl.BlockSpec((1, bt), lambda i: (0, i))
    wide = pl.BlockSpec((bt, 128), lambda i: (i, 0))
    return launch(
        tables_kernel,
        (positions[None], segments[None], jnp.concatenate([inverse, inverse])[None]),
        [row, row, resident((1, dim))],
        [wide, wide, wide],
        [shape((rows, dim), F32), shape((rows, dim), F32), shape((rows, 128), jnp.int32)],
        (rows // bt,),
        "tables",
        (0, rows * dim * 12, rows * dim * 2),
        carry=carry,
    )


def side(first, low, high):
    return jnp.where(first, low[...].astype(F32), high[...].astype(F32))


def grad_block(factor, first, base, term, t0, t1, t2, t3, values, scale, inner, others, gain):
    row = inner[0] + jnp.sum(others[:, 0, 0, :], axis=0, keepdims=True)
    inner = jnp.broadcast_to(row, (128, row.shape[1])).T[:, :1]
    scales = scale[...]
    total = term[...].astype(F32) + side(first, t0, t1) + side(first, t2, t3)
    return base[...].astype(F32) + scales * (
        total * gain[...] - values[...].astype(F32) * (scales * scales * inner * factor)
    )


def grad_operands(base, summed, values, scale, gain, base_at, values_at, scale_at, start=0):
    local = base.shape[1]
    bt = summed.half // 2

    def step(i):
        return jnp.clip(i - start, 0, 3)

    def at(chunk, wide):
        return pl.BlockSpec((bt, wide), lambda i: (step(i) + 4 * chunk, 0))

    mine = pl.BlockSpec((bt, local), lambda i: (step(i), lax.axis_index("col")))
    low = pl.BlockSpec((bt, local), lambda i: (jnp.minimum(step(i), 1), 0))
    high = pl.BlockSpec((bt, local), lambda i: (jnp.maximum(step(i) - 2, 0), 0))
    others = summed.inner_others
    args = (base, summed.partial, *summed.pieces(), values, scale, summed.inner, others, gain[None])
    specs = [at(base_at, local), mine, low, high, low, high, at(values_at, local), at(scale_at, 1)]
    specs += [
        pl.BlockSpec((1, 1, bt), lambda i: (0, 0, step(i))),
        pl.BlockSpec((others.shape[0], 1, 1, bt), lambda i: (0, 0, 0, step(i))),
        resident((1, local)),
    ]
    return args, specs, at


def hidden_kernel(factor, *refs):
    grad = grad_block(factor, pl.program_id(0) < 2, *refs[:-2])
    refs[-2][...] = grad
    refs[-1][...] = grad.astype(BF16)


def hidden_grad(launch, base, summed, values, scale, gain, chunk):
    args, specs, at = grad_operands(base, summed, values, scale, gain, chunk, 0, 0)
    rows, local = summed.rows, base.shape[1]
    return launch(
        functools.partial(hidden_kernel, 1.0 / (local * launch.ring.size)),
        args,
        specs,
        [at(0, local), at(0, local)],
        [shape((rows, local), F32), shape((rows, local), BF16)],
        (4,),
        "hidden_grad",
        (0, rows * local * 18, 0),
    )


def settle_kernel(*refs):
    step = pl.program_id(0)
    output = refs[-1]

    def one(hidden, down, p0, p1, p2, p3):
        first = step % 2 == 0
        output[...] = (hidden[...] + (down[...].astype(F32) + side(first, p0, p1) + side(first, p2, p3))).astype(BF16)

    pl.when(step < 2)(lambda: one(*refs[:6]))
    pl.when(step >= 2)(lambda: one(*refs[6:12]))


def settle(launch, hidden, sums, carry=()):
    rows, local = hidden[0].shape
    bt = rows // 2
    args, specs = [], []
    for c in (0, 1):
        here = pl.BlockSpec((bt, local), lambda i, c=c: (jnp.clip(i - 2 * c, 0, 1), 0))
        mine = pl.BlockSpec((bt, local), lambda i, c=c: (jnp.clip(i - 2 * c, 0, 1), lax.axis_index("col")))
        args += [hidden[c], sums[c].partial, *sums[c].pieces()]
        specs += [here, mine] + [Held((bt, local))] * 4
    return launch(
        settle_kernel,
        args,
        specs,
        [pl.BlockSpec((bt, local), lambda i: (i, 0))],
        [shape((2 * rows, local), BF16)],
        (4,),
        "settle",
        (0, rows * local * 24, 0),
        carry=carry,
    )[0]


def last_kernel(factor, *refs):
    step = pl.program_id(0)
    count = (len(refs) - 1) // 2

    @pl.when(step < 4)
    def _():
        refs[-1][...] = grad_block(factor, step < 2, *refs[:count])

    @pl.when(step >= 4)
    def _():
        refs[-1][...] = grad_block(factor, step < 6, *refs[count:-1])


def settle_last(launch, grad_hidden, sums, tokens, scale, gain, carry=()):
    args, specs = [], []
    for c in (0, 1):
        more, more_specs, _ = grad_operands(grad_hidden[c], sums[c], tokens, scale, gain, 0, c, c, 4 * c)
        args += more
        specs += more_specs
    total, local = tokens.shape
    return launch(
        functools.partial(last_kernel, 1.0 / (local * launch.ring.size)),
        args,
        specs,
        [pl.BlockSpec((total // 8, local), lambda i: (i, 0))],
        [shape((total, local), F32)],
        (8,),
        "settle_last",
        (0, total * local * 24, 0),
        carry=carry,
    )[0]


def hand_on_kernel(*refs):
    half = len(refs) // 2
    for source, target in zip(refs[:half], refs[half:]):
        target[...] = source[...]


def hand_on(launch, *arrays):
    steps = 4
    specs = [pl.BlockSpec((a.shape[0] // steps, a.shape[1]), lambda i: (i, 0)) for a in arrays]
    return launch(
        hand_on_kernel, arrays, specs, specs, [shape(a.shape, a.dtype) for a in arrays], (steps,), "hand_on",
        (0, sum(a.size * a.dtype.itemsize * 2 for a in arrays), 0),
    )


def widen_kernel(source, *targets):
    at = 0
    for target in targets:
        target[...] = source[:, at : at + target.shape[1]].astype(F32)
        at += target.shape[1]


def widen(launch, source, *cols):
    rows = source.shape[0]
    whole = [pl.BlockSpec((rows, n), lambda i: (0, 0)) for n in (source.shape[1], *cols)]
    return launch(
        widen_kernel, [source], whole[:1], whole[1:], [shape((rows, n), F32) for n in cols], (1,), "widen",
        (0, source.size * 6, 0),
    )


def after(value, *others):
    return lax.optimization_barrier((value, *jax.tree.leaves(others)))[0]


def body(
    tokens,
    segments,
    positions,
    gain_attn,
    w_query,
    key_weight_matrix,
    value_weight_matrix,
    gain_query,
    gain_key,
    w_out,
    gain_mlp,
    w_gate,
    w_up,
    w_down,
    cotangent,
):
    total, local = tokens.shape
    dim = gain_query.shape[0]
    query_cols, key_cols = w_query.shape[1], key_weight_matrix.shape[1]
    kv = key_cols // dim
    hidden_units = w_gate.shape[1]
    ring = Ring(lax.axis_size("col"))
    launch = Launcher(ring)
    width = local * ring.size
    rows = total // 2
    parts = [slice(0, rows), slice(rows, total)]
    offset = lax.axis_index("col") * local
    gain_attn_local = lax.dynamic_slice_in_dim(gain_attn, offset, local)
    gain_mlp_local = lax.dynamic_slice_in_dim(gain_mlp, offset, local)
    gain_q, gain_k = gain_query[None], gain_key[None]
    bq = tile_of(rows, 512)

    def gathered(weights, axis):
        return lax.all_gather(weights, "row", axis=axis, tiled=True)

    def scattered(partial, axis):
        return lax.psum_scatter(partial, "row", scatter_dimension=axis, tiled=True)

    def carried(*stages):
        for stage in stages:
            for _ in range(ring.stages - 2):
                launch.alone(stage)

    pair = lambda: [None] * 2
    mixed, logs, hidden, mid_low, scale_mid = pair(), pair(), pair(), pair(), pair()
    get_cot, get_mid, get_grad = pair(), pair(), pair()
    sum_out, sum_down, sum_mid, sum_in = pair(), pair(), pair(), pair()
    gain_mlp_part, grad_hidden, gains_in = pair(), pair(), pair()

    qkv_cols = query_cols + 2 * key_cols
    w_attn = gathered(jnp.concatenate([w_query, key_weight_matrix, value_weight_matrix, w_out.T], axis=1), 0)

    get_tok = Gather(ring, tokens, 0, total)
    launch.alone(get_tok)
    w_mlp = gathered(jnp.concatenate([after(w_gate, get_tok.full), w_up, w_down.T], axis=1), 0)
    seg_row = segments[None]
    for _ in range(ring.stages - 2):
        launch.alone(get_tok)
    cosine, sine, seg_wide = tables(launch, positions, segments, dim, [get_tok])
    x_full = get_tok.full

    for c in (0, 1):
        get_cot[c] = Gather(ring, cotangent, c * rows, rows, split=c == 0)
    normed, scale_attn, proj, queries, keys, values = project_qkv(
        launch, x_full, gain_attn[None], w_attn, qkv_cols, gain_q, gain_k, cosine, sine, kv, carry=[get_cot[1]]
    )

    def attention(c, at, carry):
        mixed[c], logs[c] = attend(
            launch, queries, keys, values, after(seg_row, at), seg_wide, c * rows, rows, dim, bq, bq, carry=carry
        )
        return logs[c]

    def start_out(c, at, carry):
        partial = project_out(launch, after(mixed[c], at), w_attn, 0, rows, carry=carry)
        sum_out[c] = Scatter(ring, partial)
        return partial

    def end_out(c):
        hidden[c] = tokens[parts[c]].astype(F32) + sum_out[c].total()
        mid_low[c] = hidden[c].astype(BF16)
        get_mid[c] = Gather(ring, mid_low[c], 0, rows)

    carried(get_cot[1])
    at = attention(1, normed, [get_cot[1]])
    at = start_out(1, at, [get_cot[0]])
    at = attention(0, at, [sum_out[1]])
    carried(sum_out[1])
    launch.alone(sum_out[1])
    end_out(1)
    launch.alone(get_mid[1])
    carried(get_mid[1])
    start_out(0, get_mid[1].full, [get_mid[1]])
    launch.alone(sum_out[0])
    carried(sum_out[0])
    launch.alone(sum_out[0], get_cot[0])
    end_out(0)

    def feed_forward(c, kept, at, carry):
        nm, scale_mid[c], *rest = mlp(
            launch, get_mid[c].full, after(gain_mlp[None], at), w_mlp, get_cot[c].full, c, total, kept,
            carry=carry,
        )
        return (nm, *rest)

    def back_middle(c, kept, at, carry):
        partial, inner, gain_part = back_mid(
            launch, kept[2], kept[3], w_mlp, get_mid[c].full, scale_mid[c], after(gain_mlp[None], at), c, carry=carry
        )
        gain_mlp_part[c] = jnp.sum(gain_part, axis=(0, 1))
        sum_mid[c] = Scatter(ring, partial, inner)
        return partial

    def end_mid(c):
        grad_hidden[c], low = hidden_grad(
            launch, cotangent, sum_mid[c], mid_low[c], scale_mid[c], gain_mlp_local, c
        )
        get_grad[c] = Gather(ring, low, 0, rows)
        return low

    def start_down(c, active, at, carry=()):
        partial = project_out(launch, after(active, at), w_mlp, c, rows, carry=carry)
        sum_down[c] = Scatter(ring, partial, split=True)
        return partial

    kept = feed_forward(1, None, get_mid[1].full, [get_mid[0]])
    carried(get_mid[0], get_cot[0])
    at = start_down(1, kept[1], kept[0], [get_mid[0]])
    at = back_middle(1, kept, at, [get_cot[0], sum_down[1]])
    kept = feed_forward(0, kept, at, [sum_mid[1]])
    normed_mid, active, grad_gate, grad_up = kept
    carried(sum_mid[1])
    partial = weight_grad_pair(
        launch, (active, active), (get_cot[0].full, get_cot[1].full), (0, 1), carry=[sum_mid[1], sum_down[1].near]
    )
    rs_down = scattered(partial, 1)
    low = end_mid(1)
    at = back_middle(0, kept, (partial, low), [get_grad[1]])
    carried(get_grad[1])
    partial = weight_grad(launch, after(normed_mid, at), grad_gate, grad_up, carry=[get_grad[1], sum_mid[0]])
    rs_gate_up = scattered(partial, 0)
    carried(sum_mid[0])
    at = start_down(0, active, partial, [sum_mid[0]])
    low = end_mid(0)

    def mix(c):
        return jnp.dot(get_grad[c].full, w_attn[:, qkv_cols:], preferred_element_type=F32).astype(BF16)

    def attention_back(c, grad_mixed, sums, at, carry):
        return attend_back(
            launch, queries, keys, values, grad_mixed, mixed[c], logs[c], after(seg_row, at), seg_wide, c * rows, dim,
            bq, bq, sums, carry=carry,
        )

    def projection_back(c, grads, low_all, at, carry):
        low_all, partial, inner, *gains_in[c] = back_qkv(
            launch, *grads, proj, cosine, sine, gain_q, gain_k, w_attn, qkv_cols, x_full, scale_attn, after(gain_attn[None], at),
            kv, c, low_all, carry=carry,
        )
        sum_in[c] = Scatter(ring, partial, inner, split=True)
        return low_all, partial

    grads = attention_back(1, mix(1), None, (at, low), [get_grad[0], sum_down[0]])
    carried(get_grad[0])
    low_all, at = projection_back(1, grads, None, None, [get_grad[0], sum_down[0].near])
    grad_mixed = mix(0)
    early = Share("col", *gains_in[1], (gain_mlp_part[0] + gain_mlp_part[1])[None])
    grads = attention_back(0, grad_mixed, grads[1:], (at, rs_down), [sum_in[1]])
    carried(sum_down[1])
    grad_out = weight_grad_pair(
        launch, (after(mixed[0], grads[0]), mixed[1]), (get_grad[0].full, get_grad[1].full), (0, 0), carry=[sum_down[1], early]
    )
    rs_out = scattered(grad_out, 1)
    carried(sum_in[1], sum_down[0])
    low_all, at = projection_back(0, grads, low_all, grad_out, [sum_in[1], sum_down[0]])
    gains = Share("col", *gains_in[0])
    partial = weight_grad(launch, after(normed, at, rs_gate_up), low_all, carry=[sum_in[0], sum_in[1].near, gains])

    grad_qkv = scattered(after(partial, rs_out), 0)
    gains = jnp.concatenate([part.reshape(-1) for part in (*gains.sums, *early.sums)])[None]
    gains = Share("row", gains)
    carried(sum_in[0])
    output = settle(launch, hidden, sum_down, [sum_in[0], sum_in[0].near])
    grad_tokens = settle_last(launch, grad_hidden, sum_in, tokens, scale_attn, gain_attn_local, [gains])
    sum_attn, sum_q, sum_k, more_attn, more_q, more_k, sum_mlp = jnp.split(
        gains.sums[0][0], list(itertools.accumulate([width, dim, dim, width, dim, dim]))
    )
    output, grad_tokens = hand_on(launch, output, grad_tokens)
    grad_query, grad_key, grad_value = widen(launch, grad_qkv, query_cols, key_cols, key_cols)
    return (
        output,
        grad_tokens,
        sum_attn + more_attn,
        grad_query,
        grad_key,
        grad_value,
        sum_q + more_q,
        sum_k + more_k,
        rs_out.astype(F32),
        sum_mlp,
        rs_gate_up[:, :hidden_units].astype(F32),
        rs_gate_up[:, hidden_units:].astype(F32),
        rs_down.astype(F32),
    )


def solution(mesh):
    both, split = P("row", "col"), P("col", "row")
    in_specs = (both, P("row"), P("row"), P(), both, both, both, P(), P(), split, P(), both, both, split, both)
    out_specs = (both, both, P(), both, both, both, P(), P(), split, P(), both, both, split)
    return jax.shard_map(body, mesh=mesh, in_specs=in_specs, out_specs=out_specs, check_vma=False)
```
